32 devices in a mesh: blk: 4 (over x, core), tp: 8 (over z, y).
Axes of the slice: x: 2, y: 2, z: 4, core: 2. Of those that a mesh axis runs over, the one named last changes fastest.
Arguments:
- tokens: bfloat16 [4, 1024, 2048], P(None, 'blk'), may hold values from -6 to 6
- lengths: int32 [4, 4], replicated, may hold values from 1 to 769, 1024 in all within a row
- head_count: int32 [4, 1024], P(None, 'blk'), may hold values from 1 to 16
- width_index: int32 [4, 1024], P(None, 'blk'), may hold values from 0 to 3
- router_prob: float32 [4, 1024], P(None, 'blk'), may hold values from 0.25 to 1
- norm_gain: float32 [2048], replicated, may hold values from 0.5 to 1.5
- w_query: bfloat16 [2048, 2048], P(None, 'tp'), may hold values from -0.125 to 0.125
- w_key: bfloat16 [2048, 2048], P(None, 'tp'), may hold values from -0.125 to 0.125
- w_value: bfloat16 [2048, 2048], P(None, 'tp'), may hold values from -0.125 to 0.125
- w_out: bfloat16 [2048, 2048], P('tp'), may hold values from -1.5 to 1.5
- ln_gain: float32 [2048], replicated, may hold values from 0.5 to 1.5
- ln_bias: float32 [2048], replicated, may hold values from -3 to 3
- w_up: bfloat16 [2048, 8192], P(None, 'tp'), may hold values from -0.125 to 0.125
- w_down: bfloat16 [8192, 2048], P('tp'), may hold values from -0.0625 to 0.0625
- grad_out: bfloat16 [4, 1024, 2048], P(None, 'blk'), may hold values from -6 to 6
Outputs:
- mixed_out: bfloat16 [4, 1024, 2048], P(None, 'blk')
- grad_in: bfloat16 [4, 1024, 2048], P(None, 'blk')
- grad_norm_gain: float32 [2048], P('blk')
- grad_w_query: float32 [2048, 2048], P('blk', 'tp')
- grad_w_key: float32 [2048, 2048], P('blk', 'tp')
- grad_w_value: float32 [2048, 2048], P('blk', 'tp')
- grad_w_out: float32 [2048, 2048], P('tp', 'blk')
- grad_ln_gain: float32 [2048], P('blk')
- grad_ln_bias: float32 [2048], P('blk')
- grad_w_up: float32 [2048, 8192], P('blk', 'tp')
- grad_w_down: float32 [8192, 2048], P('tp', 'blk')
The draws below stay inside these ranges and needn't reach their ends.
Inputs may be any that keep to these rules, and one draw needn't show every extreme that they name: `lengths`: each row sums to 1024; its longest sequence has exactly 769 rows, so it begins on the first index of blk and ends on the last. A token uses heads 0 to head_count - 1. A token uses feed-forward units 0 to (width_index + 1) * 2048 - 1.
All inputs are finite; a program needn't handle non-finite values.
Results may differ from the reference program's by a relative error of at most 0.024.
Values may be sent and summed in bfloat16 or wider, within the bound.
A program may use at most 256 MiB of HBM per device.

```python
import math
import jax
import jax.numpy as jnp
import numpy as np
from jax import lax

D = 2048
H = 16
HD = 128
FF = 8192
MB = 4
NSEQ = 4
TOKENS = 1024
LONGEST = 769


def set_ends(array, own_key, smallest, high):
    longest = array.shape.index(max(array.shape))
    spots = []
    for shift in (0, 1):
        where = [jax.random.randint(jax.random.fold_in(own_key, axis), (), 0, length) for axis, length in enumerate(array.shape)]
        where[longest] = (where[longest] + shift) % array.shape[longest]
        spots.append(tuple(where))
    return array.at[spots[0]].set(smallest).at[spots[1]].set(high)


def shard_levels(rng, dims, cuts, smallest, largest):
    def one(axis_at, blocks):
        heights = jax.random.uniform(jax.random.fold_in(jax.random.fold_in(rng, 6), axis_at), (blocks,), jnp.float32, smallest / len(cuts), largest / len(cuts))
        return jnp.repeat(jnp.exp(heights), dims[axis_at] // blocks).reshape((-1,) + (1,) * (len(dims) - axis_at - 1))

    factor_of = one(*cuts[0])
    for cut in cuts[1:]:
        factor_of = factor_of * one(*cut)
    return factor_of


def split_up(count, total, bound, slope):
    portions = [(1 << 20) // math.isqrt(grade ** slope) + 1 for grade in range(2, count + 1)]
    surplus, counts = total - bound - (count - 1), [1] * (count - 1)
    while surplus > 0:
        movable = [i for i in range(count - 1) if counts[i] < bound]
        mass, budget = sum([portions[i] for i in movable]), surplus
        for i in movable:
            addition = min(bound - counts[i], max(1, budget * portions[i] // mass), surplus)
            counts[i] = counts[i] + addition
            surplus = surplus - addition
    return np.array([bound] + counts)


def ragged(stream_key, amount, total, reach, lean):
    if amount == 2:
        one = jax.random.randint(stream_key, (), max(1, total - reach), min(reach, total - 1) + 1)
        return jnp.stack([one, total - one])
    tallies = jnp.asarray(split_up(amount, total, reach, lean), jnp.int32)
    pairs = (amount - 1) // 2
    giver, sink = tallies[1:1 + 2 * pairs:2], tallies[2:2 + 2 * pairs:2]
    room = jnp.minimum(giver - 1, reach - sink)
    moved = jax.random.randint(jax.random.fold_in(stream_key, 1), (pairs,), 0, 1 << 20) % (room + 1)
    tallies = tallies.at[1:1 + 2 * pairs:2].set(giver - moved).at[2:2 + 2 * pairs:2].set(sink + moved)
    return tallies[jax.random.permutation(jax.random.fold_in(stream_key, 2), amount)]


def noise(key, extent, spread, bound, shards=(), kind=jnp.bfloat16):
    result = spread * jax.random.normal(key, extent, jnp.float32)
    if shards:
        result = result * shard_levels(key, extent, shards, -0.22, 0.18)
    return jnp.clip(result, -bound, bound).astype(kind)


def setup_inputs(seed: int = 0) -> dict:
    streams_of = jax.random.split(jax.random.key(seed), 16)
    tokens = noise(streams_of[0], (MB, TOKENS, D), 1.0, 6.0, ((1, 4),))
    lengths = jax.vmap(lambda own: ragged(own, NSEQ, TOKENS, LONGEST, 2))(jax.random.split(streams_of[1], MB)).reshape((MB, NSEQ)).astype(jnp.int32)
    head_count = set_ends(jax.random.randint(streams_of[2], (MB, TOKENS), 1, H + 1), jax.random.fold_in(streams_of[2], 1), 1, H).astype(jnp.int32)
    width_index = set_ends(jax.random.randint(streams_of[3], (MB, TOKENS), 0, 4), jax.random.fold_in(streams_of[3], 1), 0, 3).astype(jnp.int32)
    router_prob = jnp.clip(0.25 + 0.75 * jax.random.uniform(streams_of[4], (MB, TOKENS), jnp.float32) ** shard_levels(streams_of[4], (MB, TOKENS), ((1, 4),), -0.2, 0.2), 0.25, 1.0)
    norm_gain = jnp.clip(1.0 + 0.1 * jax.random.normal(streams_of[5], (D,), jnp.float32), 0.5, 1.5)
    w_query = noise(streams_of[6], (D, H * HD), D ** -0.5, 0.125, ((1, 8),))
    w_key = noise(streams_of[7], (D, H * HD), D ** -0.5, 0.125, ((1, 8),))
    w_value = noise(streams_of[8], (D, H * HD), D ** -0.5, 0.125, ((1, 8),))
    w_out = noise(streams_of[9], (H * HD, D), 16 ** -0.5, 1.5, ((0, 8),))
    ln_gain = jnp.clip(1.0 + 0.1 * jax.random.normal(streams_of[10], (D,), jnp.float32), 0.5, 1.5)
    ln_bias = noise(streams_of[11], (D,), 0.5, 3.0, (), jnp.float32)
    w_up = noise(streams_of[12], (D, FF), D ** -0.5, 0.125, ((1, 8),))
    w_down = noise(streams_of[13], (FF, D), FF ** -0.5, 0.0625, ((0, 8),))
    grad_out = noise(streams_of[14], (MB, TOKENS, D), 1.0, 6.0, ((1, 4),))
    return dict(tokens=tokens, lengths=lengths, head_count=head_count, width_index=width_index, router_prob=router_prob, norm_gain=norm_gain, w_query=w_query, w_key=w_key, w_value=w_value, w_out=w_out, ln_gain=ln_gain, ln_bias=ln_bias, w_up=w_up, w_down=w_down, grad_out=grad_out)


EPS = 1e-05
NEG = -1e+30
HIGH = lax.Precision.HIGHEST

@jax.custom_vjp
def low(v):
    return lax.optimization_barrier(v.astype(jnp.bfloat16)).astype(jnp.float32)

@jax.custom_vjp
def low_back(v):
    return v

def low_keep(v):
    return (low(v), None)

def low_pass(kept, grad):
    return (grad,)

def back_keep(v):
    return (v, None)

def back_low(kept, grad):
    return (low(grad),)
low.defvjp(low_keep, low_pass)
low_back.defvjp(back_keep, back_low)

def seq_begin(lengths, rows):
    seq_ends = jnp.cumsum(lengths, axis=1)
    past_end = rows[None, :, None] >= seq_ends[:, None, :]
    return lax.optimization_barrier(jnp.sum(jnp.where(past_end, lengths[:, None, :], 0), axis=2)).astype(jnp.int32)

def turn_table(positions, dim_size):
    half_dim = dim_size // 2
    frequency = jnp.exp(jnp.arange(half_dim, dtype=jnp.float32) * (-math.log(10000.0) / half_dim))
    angles = positions.astype(jnp.float32)[..., None] * frequency
    return (jnp.cos(angles)[..., None, :], jnp.sin(angles)[..., None, :])

def rotate(values_in, cos_table, sine_table):
    half_dim = values_in.shape[-1] // 2
    first_half = values_in[..., :half_dim]
    second_half = values_in[..., half_dim:]
    return jnp.concatenate([first_half * cos_table - second_half * sine_table, first_half * sine_table + second_half * cos_table], axis=-1)

def layer(params, item_x, item_begin, item_heads, item_width, item_prob):
    gain_rms, w_query, w_key, w_value, w_out, gain_ln, bias_ln, w_up, w_down = params
    row_ids = jnp.arange(TOKENS, dtype=jnp.int32)
    cos_table, sine_table = turn_table(row_ids - item_begin, HD)
    inv_rms = lax.rsqrt(lax.optimization_barrier(jnp.mean(item_x * item_x, axis=-1, keepdims=True)) + EPS)
    normed = low(item_x * inv_rms * gain_rms)
    q_pre = low_back(jnp.dot(normed, w_query, precision=HIGH)).reshape(TOKENS, H, HD)
    k_pre = low_back(jnp.dot(normed, w_key, precision=HIGH)).reshape(TOKENS, H, HD)
    v_pre = low_back(jnp.dot(normed, w_value, precision=HIGH)).reshape(TOKENS, H, HD)
    query = low(rotate(q_pre, cos_table, sine_table))
    key_all = low(rotate(k_pre, cos_table, sine_table))
    value_all = low(v_pre)
    allowed = (row_ids[None, :] <= row_ids[:, None]) & (row_ids[None, :] >= item_begin[:, None])
    score_scale = 1.0 / math.sqrt(HD)

    def head_attend(items):
        q_head, k_head, v_head = items
        raw_score = low_back(jnp.dot(q_head, k_head.T, precision=HIGH))
        score = jnp.where(allowed, raw_score * score_scale, NEG)
        row_max = lax.optimization_barrier(jnp.max(score, axis=-1, keepdims=True))
        expo = jnp.where(allowed, jnp.exp(score - row_max), 0.0)
        prob_rows = low(expo / lax.optimization_barrier(jnp.sum(expo, axis=-1, keepdims=True)))
        return jnp.dot(prob_rows, v_head, precision=HIGH)
    per_head = lax.map(jax.checkpoint(head_attend), (jnp.transpose(query, (1, 0, 2)), jnp.transpose(key_all, (1, 0, 2)), jnp.transpose(value_all, (1, 0, 2))))
    attended = jnp.transpose(per_head, (1, 0, 2))
    head_mask = (jnp.arange(H, dtype=jnp.int32)[None, :] < item_heads[:, None]).astype(jnp.float32)
    heads_out = low(low_back(attended * head_mask[:, :, None])).reshape(TOKENS, H * HD)
    branch = low_back(jnp.dot(heads_out, w_out, precision=HIGH))
    residual = item_x + branch
    center = residual - lax.optimization_barrier(jnp.mean(residual, axis=-1, keepdims=True))
    inv_std = lax.rsqrt(lax.optimization_barrier(jnp.mean(center * center, axis=-1, keepdims=True)) + EPS)
    lifted = low(center * inv_std * gain_ln + bias_ln)
    hidden = low_back(jnp.dot(lifted, w_up, precision=HIGH))
    unit_mask = (jnp.arange(FF, dtype=jnp.int32)[None, :] < ((item_width + 1) * (FF // 4))[:, None]).astype(jnp.float32)
    active = jnp.maximum(hidden, 0.0)
    squared = low(active * active * unit_mask)
    feed_out = low_back(jnp.dot(squared, w_down, precision=HIGH))
    return residual + item_prob[:, None] * feed_out

def reference(tokens, lengths, head_count, width_index, router_prob, norm_gain, w_query, w_key, w_value, w_out, ln_gain, ln_bias, w_up, w_down, grad_out):
    begin_all = seq_begin(lengths, jnp.arange(TOKENS, dtype=jnp.int32))
    prob_all = router_prob.astype(jnp.float32)

    def forward(inputs, *params):

        def one_batch(items):
            return layer(params, *items)
        return lax.map(jax.checkpoint(one_batch), (inputs, begin_all, head_count, width_index, prob_all))
    primals = (tokens.astype(jnp.float32), norm_gain.astype(jnp.float32), w_query.astype(jnp.float32), w_key.astype(jnp.float32), w_value.astype(jnp.float32), w_out.astype(jnp.float32), ln_gain.astype(jnp.float32), ln_bias.astype(jnp.float32), w_up.astype(jnp.float32), w_down.astype(jnp.float32))
    output, pullback = jax.vjp(forward, *primals)
    grads = pullback(grad_out.astype(jnp.float32))
    return (output.astype(jnp.bfloat16), grads[0].astype(jnp.bfloat16), grads[1], grads[2], grads[3], grads[4], grads[5], grads[6], grads[7], grads[8], grads[9])
```

```python
import functools
import math

import jax
import jax.numpy as jnp
from jax import lax
from jax.experimental import pallas as pl
from jax.experimental.pallas import tpu as pltpu
from jax.sharding import PartitionSpec as P

HD = 128
FF = 8192


EPS = 1e-05
NEG = -1e30
CHUNK_ROWS = 128
CUT = 1280
VMEM_LIMIT = 60 * 2**20


MESH = pl.DeviceIdType.MESH
VMEM = pltpu.VMEM
LANE = 128


def remote(src, dst, send, recv, device):
    return pltpu.make_async_remote_copy(
        src_ref=src, dst_ref=dst, send_sem=send, recv_sem=recv, device_id=device, device_id_type=MESH
    )


class Place:
    def __init__(self, lines):
        blk, tp = lax.axis_index("blk"), lax.axis_index("tp")
        self.lines, self.tp = lines, tp
        self.z, self.y = tp // 2, tp % 2
        self.other = 1 - self.y
        self.across = (blk, self.z * 2 + self.other)
        self.right = (blk, jnp.minimum(self.z + 1, lines - 1) * 2 + self.y)
        self.left = (blk, jnp.maximum(self.z - 1, 0) * 2 + self.y)
        self.has_right, self.has_left = self.z < lines - 1, self.z > 0

    def greet(self):
        barrier = pltpu.get_barrier_semaphore()
        pl.semaphore_signal(barrier, inc=1, device_id=self.across, device_id_type=MESH)

        @pl.when(self.has_right)
        def _():
            pl.semaphore_signal(barrier, inc=1, device_id=self.right, device_id_type=MESH)

        @pl.when(self.has_left)
        def _():
            pl.semaphore_signal(barrier, inc=1, device_id=self.left, device_id_type=MESH)

        peers = 1 + self.has_right.astype(jnp.int32) + self.has_left.astype(jnp.int32)
        pl.semaphore_wait(barrier, peers)


class Scatter:
    def __init__(self, place, cut, part, across_a, line_a, line_b, across_b, send, recv):
        self.at, self.cut, self.part = place, cut, part
        self.across_a, self.line_a, self.line_b, self.across_b = across_a, line_a, line_b, across_b
        self.send, self.recv = send, recv

    @staticmethod
    def scratch(chunks, lines, rows, width, cut):
        return [
            VMEM((chunks, 2, lines, rows, width), jnp.bfloat16),
            VMEM((chunks, lines, rows, cut), jnp.bfloat16),
            VMEM((chunks, lines + 1, rows, cut), jnp.bfloat16),
            VMEM((chunks, lines + 1, 2, rows, width - cut), jnp.bfloat16),
            VMEM((chunks, rows, width - cut), jnp.bfloat16),
            pltpu.SemaphoreType.DMA((chunks, 2 * lines + 2)),
            pltpu.SemaphoreType.DMA((chunks, 2 * lines + 4)),
        ]

    def low(self, c, j):
        return self.part.at[c, self.at.y, j, :, : self.cut]

    def high(self, c, j):
        return self.part.at[c, :, j, :, self.cut :]

    def copy_across_a(self, c):
        return remote(
            self.part.at[c, self.at.other, :, :, : self.cut],
            self.across_a.at[c],
            self.send.at[c, 0],
            self.recv.at[c, 0],
            self.at.across,
        )

    def copy_across_b(self, c):
        return remote(
            self.part.at[c, self.at.other, self.at.z, :, self.cut :],
            self.across_b.at[c],
            self.send.at[c, 1],
            self.recv.at[c, 1],
            self.at.across,
        )

    def copy_line(self, c, j, slot, device, first):
        lines = self.at.lines
        if first:
            source, target, send, recv = self.low(c, j), self.line_a, 2, 2
        else:
            source, target, send, recv = self.high(c, j), self.line_b, 2 + lines, 3 + lines
        return remote(
            source, target.at[c, slot], self.send.at[c, send + j], self.recv.at[c, recv + slot], device
        )

    def to_right(self, c, j, first):
        return self.copy_line(c, j, j + 1, self.at.right, first)

    def to_left(self, c, j, first):
        return self.copy_line(c, j, j, self.at.left, first)

    def take(self, c, j, slot, first):
        self.copy_line(c, j, slot, self.at.right, first).wait_recv()
        view = self.low(c, j) if first else self.high(c, j)
        came = (self.line_a if first else self.line_b)[c, slot]
        view[...] = (view[...].astype(jnp.float32) + came.astype(jnp.float32)).astype(jnp.bfloat16)

    def line_starts(self, c, first):
        lines = self.at.lines

        @pl.when(self.at.z == 0)
        def _():
            for j in range(lines - 1, 0, -1):
                self.to_right(c, j, first).start()

        @pl.when(self.at.z == lines - 1)
        def _():
            for j in range(lines - 1):
                self.to_left(c, j, first).start()

    def line_hop(self, c, step, first):
        lines = self.at.lines

        @pl.when(self.at.z == step)
        def _():
            for j in range(lines - 1, step, -1):
                self.take(c, j, j + 1, first)
                self.to_right(c, j, first).start()

        @pl.when(self.at.z == lines - 1 - step)
        def _():
            for j in range(lines - 1 - step):
                self.take(c, j, j, first)
                self.to_left(c, j, first).start()

    def line_end(self, c, total, first):
        z = self.at.z
        buffer = self.line_a if first else self.line_b

        @pl.when(self.at.has_left)
        def _():
            self.copy_line(c, z, z + 1, self.at.right, first).wait_recv()
            total[...] += buffer[c, z + 1].astype(jnp.float32)

        @pl.when(self.at.has_right)
        def _():
            self.copy_line(c, z, z, self.at.right, first).wait_recv()
            total[...] += buffer[c, z].astype(jnp.float32)

    def step0(self, c):
        self.copy_across_a(c).start()
        self.line_starts(c, False)

    def step(self, c, k, total_b):
        lines = self.at.lines
        if k == 1:
            self.copy_across_a(c).wait_recv()
            mine = self.part.at[c, self.at.y, :, :, : self.cut]
            mine[...] = (
                mine[...].astype(jnp.float32) + self.across_a[c].astype(jnp.float32)
            ).astype(jnp.bfloat16)
            self.line_starts(c, True)
        elif k - 1 <= lines - 2:
            self.line_hop(c, k - 1, True)
        if k <= lines - 2:
            self.line_hop(c, k, False)
        elif k == lines - 1:
            mine = self.high(c, self.at.z)
            total_b[...] = mine[...].astype(jnp.float32)
            self.line_end(c, total_b, False)
            mine[...] = total_b[...].astype(jnp.bfloat16)
            self.copy_across_b(c).start()

    def finish(self, c, total):
        y, z = self.at.y, self.at.z
        low, high = total.at[:, : self.cut], total.at[:, self.cut :]
        low[...] = self.low(c, z)[...].astype(jnp.float32)
        self.line_end(c, low, True)
        self.copy_across_b(c).wait_recv()
        high[...] = self.part[c, y, z, :, self.cut :].astype(jnp.float32) + self.across_b[c].astype(
            jnp.float32
        )

    def drain(self, c):
        self.copy_across_a(c).wait_send()
        self.copy_across_b(c).wait_send()
        for first in (True, False):
            for j in range(self.at.lines):

                @pl.when(self.at.z != j)
                def _(j=j, first=first):
                    self.to_right(c, j, first).wait_send()


class Gather:
    def __init__(self, place, cut, own, full, local, send, recv):
        self.at, self.cut, self.own, self.full = place, cut, own, full
        self.local, self.send, self.recv = local, send, recv

    @staticmethod
    def scratch(chunks, lines):
        return [
            pltpu.SemaphoreType.DMA((chunks,)),
            pltpu.SemaphoreType.DMA((chunks, 5 * lines + 1)),
            pltpu.SemaphoreType.DMA((chunks, 3 * lines + 1)),
        ]

    def low(self, c, j):
        target = self.full.at[c, self.at.y, j, :, : self.cut]
        return target, target

    def copy_low(self, c, j, way, mine):
        lines = self.at.lines
        target = self.full.at[c, self.at.y, j, :, : self.cut]
        source = self.own(c).at[:, : self.cut] if mine else target
        device = (self.at.right, self.at.left, self.at.across)[way]
        recv = j + (lines if way == 2 else 0)
        return remote(source, target, self.send.at[c, way * lines + j], self.recv.at[c, recv], device)

    def copy_high(self, c, j, way):
        lines = self.at.lines
        view = self.full.at[c, :, j, :, self.cut :]
        device = (self.at.right, self.at.left)[way]
        return remote(
            view, view, self.send.at[c, (3 + way) * lines + j], self.recv.at[c, 2 * lines + j], device
        )

    def copy_high_across(self, c):
        lines = self.at.lines
        return remote(
            self.own(c).at[:, self.cut :],
            self.full.at[c, self.at.y, self.at.z, :, self.cut :],
            self.send.at[c, 5 * lines],
            self.recv.at[c, 3 * lines],
            self.at.across,
        )

    def copy_local(self, c):
        return pltpu.make_async_copy(
            self.own(c), self.full.at[c, self.at.y, self.at.z], self.local.at[c]
        )

    def step0(self, c):
        z = self.at.z
        if self.local is not None:
            self.copy_local(c).start()

        @pl.when(self.at.has_right)
        def _():
            self.copy_low(c, z, 0, True).start()

        @pl.when(self.at.has_left)
        def _():
            self.copy_low(c, z, 1, True).start()

        self.copy_high_across(c).start()
        self.copy_low(c, z, 2, True).start()

    def low_hop(self, c, k):
        z, lines = self.at.z, self.at.lines

        @pl.when(z >= k)
        def _():
            self.copy_low(c, z - k, 0, False).wait_recv()

            @pl.when(self.at.has_right)
            def _():
                self.copy_low(c, z - k, 0, False).start()

            self.copy_low(c, z - k, 2, False).start()

        @pl.when(z + k < lines)
        def _():
            self.copy_low(c, z + k, 0, False).wait_recv()

            @pl.when(self.at.has_left)
            def _():
                self.copy_low(c, z + k, 1, False).start()

            self.copy_low(c, z + k, 2, False).start()

    def high_hop(self, c, k):
        z, lines = self.at.z, self.at.lines

        @pl.when(z >= k)
        def _():
            self.copy_high(c, z - k, 0).wait_recv()

            @pl.when(self.at.has_right)
            def _():
                self.copy_high(c, z - k, 0).start()

        @pl.when(z + k < lines)
        def _():
            self.copy_high(c, z + k, 0).wait_recv()

            @pl.when(self.at.has_left)
            def _():
                self.copy_high(c, z + k, 1).start()

    def step(self, c, k):
        lines, z = self.at.lines, self.at.z
        if k == 1:
            if self.local is not None:
                self.copy_local(c).wait()
            self.copy_high_across(c).wait_recv()

            @pl.when(self.at.has_right)
            def _():
                self.copy_high(c, z, 0).start()

            @pl.when(self.at.has_left)
            def _():
                self.copy_high(c, z, 1).start()

        if k <= lines - 1:
            self.low_hop(c, k)
        if k > 1:
            self.high_hop(c, k - 1)
        if k == lines:
            for j in range(lines):
                target = self.full.at[c, self.at.other, j, :, : self.cut]
                remote(
                    target, target, self.send.at[c, 2 * lines + j], self.recv.at[c, lines + j], self.at.across
                ).wait_recv()

    def drain(self, c):
        lines, z = self.at.lines, self.at.z
        self.copy_high_across(c).wait_send()
        for j in range(lines):

            @pl.when(self.at.has_right & (z >= j))
            def _(j=j):
                self.copy_low(c, j, 0, False).wait_send()
                self.copy_high(c, j, 0).wait_send()

            @pl.when(self.at.has_left & (z <= j))
            def _(j=j):
                self.copy_low(c, j, 1, False).wait_send()
                self.copy_high(c, j, 1).wait_send()

            self.copy_low(c, j, 2, False).wait_send()


def rows_sum(values):
    return jnp.sum(values, axis=0, keepdims=True)


def mean_last(values):
    return jnp.mean(values, axis=-1, keepdims=True)


def dot_nn(a, b):
    return jnp.dot(a, b, preferred_element_type=jnp.float32)


def dot_nt(a, b):
    return lax.dot_general(a, b, (((1,), (1,)), ((), ())), preferred_element_type=jnp.float32)


TILE = 256


def middle_kernel(
    lines, chunks, cut, chunk_rows, tokens_hbm, grad_hbm, heads_ref, wo_ref, gain_ref, bias_ref, up_ref, down_ref,
    prob_ref, width_ref, mixed_hbm, branch_hbm, lifted_ref, squared_ref, hidden_ref, resid_ref, sums_ref,
    x_own, g_own, g_chunk, own_mixed, own_branch, normal_ref, resid_own, inv_own, total, total_b, sem_in, *rest,
):
    place = Place(lines)
    y, z, tp = place.y, place.z, place.tp
    spot = y * lines + z
    rows = chunk_rows // (2 * lines)
    width = gain_ref.shape[-1]
    units = up_ref.shape[1]
    s1, s2, s3 = (Scatter(place, cut, *rest[7 * i : 7 * i + 7]) for i in range(3))
    rest = rest[21:]
    a1 = Gather(place, cut, lambda c: lifted_ref.at[c, y, z], lifted_ref, None, *rest[1:3])
    a2 = Gather(place, cut, lambda c: own_branch.at[c], branch_hbm, *rest[3:6])
    a3 = Gather(place, cut, lambda c: own_mixed.at[c], mixed_hbm, *rest[6:9])

    get_x = pltpu.make_async_copy(tokens_hbm.at[:, spot], x_own, sem_in.at[0])
    get_g = pltpu.make_async_copy(grad_hbm.at[:, spot], g_own, sem_in.at[1])
    get_x.start()
    get_g.start()
    place.greet()
    get_x.wait()
    get_g.wait()
    sums_ref[...] = jnp.zeros_like(sums_ref)

    def own_rows(c):
        return pl.ds(pl.multiple_of(c * chunk_rows + spot * rows, rows), rows)

    def all_rows(c):
        return pl.ds(pl.multiple_of(c * chunk_rows, chunk_rows), chunk_rows)

    def tiled(n, body):
        @pl.loop(0, n // TILE)
        def _(i):
            body(pl.ds(pl.multiple_of(i * TILE, TILE), TILE))

    def put(part, c, cols, values):
        part[c, :, :, :, cols] = values.astype(jnp.bfloat16).reshape(2, lines, rows, TILE)

    def project(c):
        heads = heads_ref[all_rows(c), :]

        def one(cols):
            put(s1.part, c, cols, dot_nn(heads, wo_ref[:, cols]))

        tiled(width, one)
        s1.step0(c)

    def norm(c):
        s1.finish(c, total)
        residual = x_own[c].astype(jnp.float32) + total[...]
        center = residual - mean_last(residual)
        inv_std = lax.rsqrt(mean_last(center * center) + EPS)
        normal = center * inv_std
        resid_own[c] = residual
        normal_ref[c] = normal
        inv_own[c] = jnp.broadcast_to(inv_std, (rows, LANE))
        lifted_ref[c, y, z] = (normal * gain_ref[...] + bias_ref[...]).astype(jnp.bfloat16)
        a1.step0(c)

    def feed(c):
        get = pltpu.make_async_copy(grad_hbm.at[c], g_chunk, sem_in.at[2])
        get.start()
        lifted = lifted_ref[c].reshape(chunk_rows, width)
        span = all_rows(c)
        prob, limit = prob_ref[span, :], (width_ref[span, :] + 1) * (FF // 4)
        get.wait()
        g_chunk[...] = (g_chunk[...].astype(jnp.float32) * prob.reshape(2 * lines, rows, 1)).astype(
            jnp.bfloat16
        )

        def units_of(cols):
            active = jnp.maximum(dot_nn(lifted, up_ref[:, cols]), 0.0)
            ids = tp * units + cols.start + lax.broadcasted_iota(jnp.int32, (chunk_rows, TILE), 1)
            mask = (ids < limit).astype(jnp.float32)
            squared_ref[span, cols] = (active * active * mask).astype(jnp.bfloat16)
            back = dot_nt(g_chunk[...].reshape(chunk_rows, width), down_ref[cols, :])
            hidden_ref[span, cols] = (back * mask * 2.0 * active).astype(jnp.bfloat16)

        tiled(units, units_of)
        hidden = hidden_ref[span, :]

        def lift(cols):
            put(s2.part, c, cols, dot_nt(hidden, up_ref[cols, :]))

        tiled(width, lift)
        s2.step0(c)
        squared = squared_ref[span, :]

        def out(cols):
            put(s3.part, c, cols, dot_nn(squared, down_ref[:, cols]))

        tiled(width, out)
        s3.step0(c)

    def norm_back(c):
        s2.finish(c, total)
        grad_lifted, normal = total[...], normal_ref[c]
        sums_ref[0:1, :] += rows_sum(grad_lifted * normal)
        sums_ref[1:2, :] += rows_sum(grad_lifted)
        g = grad_lifted * gain_ref[...]
        grad_resid = g_own[c].astype(jnp.float32) + inv_own[c][:, 0:1] * (
            g - mean_last(g) - normal * mean_last(g * normal)
        )
        resid_ref[c] = grad_resid
        own_branch[c] = grad_resid.astype(jnp.bfloat16)
        a2.step0(c)

    def mix(c):
        s3.finish(c, total)
        own_mixed[c] = (resid_own[c] + prob_ref[own_rows(c), :] * total[...]).astype(jnp.bfloat16)
        a3.step0(c)

    @pl.loop(0, chunks + 4 * lines)
    def _(r):
        def at(offset, task):
            c = r - offset

            @pl.when((c >= 0) & (c < chunks))
            def _():
                task(c)

        for k in range(1, lines):
            at(2 * lines + k, lambda c, k=k: s2.step(c, k, total_b))
        for k in range(1, lines):
            at(k, lambda c, k=k: s1.step(c, k, total_b))
        for k in range(1, lines + 1):
            at(lines + k, lambda c, k=k: a1.step(c, k))
        for k in range(1, lines + 1):
            at(3 * lines + k, lambda c, k=k: a2.step(c, k))
        for k in range(1, lines):
            at(2 * lines + k, lambda c, k=k: s3.step(c, k, total_b))
        for k in range(1, lines + 1):
            at(3 * lines + k, lambda c, k=k: a3.step(c, k))
        at(3 * lines, norm_back)
        at(lines, norm)
        at(3 * lines, mix)
        at(2 * lines, feed)
        at(0, project)

    @pl.loop(0, chunks)
    def _(c):
        for part in (s1, s2, s3, a1, a2, a3):
            part.drain(c)


def middle(tokens, grad_out, heads_out, w_out, ln_gain, ln_bias, w_up, w_down, router_prob, width_index):
    lines = lax.axis_size("tp") // 2
    count, width = tokens.shape
    units = w_up.shape[1]
    chunk_rows = CHUNK_ROWS
    chunks, rows = count // chunk_rows, chunk_rows // (2 * lines)
    cut = CUT
    split = (chunks, 2 * lines, rows, width)
    full = (chunks, 2, lines, rows, width)
    any_space, vmem = pl.BlockSpec(memory_space=pl.ANY), pl.BlockSpec(memory_space=VMEM)
    bf16, f32 = jnp.bfloat16, jnp.float32
    scatter = Scatter.scratch(chunks, lines, rows, width, cut)
    gather = Gather.scratch(chunks, lines)
    outs = pl.pallas_call(
        functools.partial(middle_kernel, lines, chunks, cut, chunk_rows),
        out_shape=[
            jax.ShapeDtypeStruct(full, bf16),
            jax.ShapeDtypeStruct(full, bf16),
            jax.ShapeDtypeStruct(full, bf16),
            jax.ShapeDtypeStruct((count, units), bf16),
            jax.ShapeDtypeStruct((count, units), bf16),
            jax.ShapeDtypeStruct((chunks, rows, width), f32),
            jax.ShapeDtypeStruct((2, width), f32),
        ],
        in_specs=[any_space, any_space] + [vmem] * 8,
        out_specs=[any_space, any_space] + [vmem] * 5,
        scratch_shapes=[
            VMEM((chunks, rows, width), bf16),
            VMEM((chunks, rows, width), bf16),
            VMEM((2 * lines, rows, width), bf16),
            VMEM((chunks, rows, width), bf16),
            VMEM((chunks, rows, width), bf16),
            VMEM((chunks, rows, width), f32),
            VMEM((chunks, rows, width), f32),
            VMEM((chunks, rows, LANE), f32),
            VMEM((rows, width), f32),
            VMEM((2, rows, width - cut), f32),
            pltpu.SemaphoreType.DMA((3,)),
        ]
        + scatter * 3
        + gather * 3,
        compiler_params=pltpu.CompilerParams(
            collective_id=1, has_side_effects=True, vmem_limit_bytes=VMEM_LIMIT
        ),
        cost_estimate=pl.CostEstimate(
            flops=2 * count * width * (w_out.shape[0] + 4 * units), bytes_accessed=40 * 2**20, transcendentals=0
        ),
    )(
        tokens.reshape(split),
        grad_out.reshape(split),
        heads_out,
        w_out,
        ln_gain[None],
        ln_bias[None],
        w_up,
        w_down,
        router_prob.reshape(count, 1),
        width_index.reshape(count, 1),
    )
    mixed, branch, lifted, squared, hidden, resid, sums = outs
    return (
        mixed.reshape(count, width),
        branch.reshape(count, width),
        lifted.reshape(count, width),
        squared,
        hidden,
        resid,
        sums,
    )


def as_sent(array):
    return jax.tree.map(lambda a: a.astype(jnp.bfloat16) if a.dtype == jnp.float32 else a, array)


def seq_begin(lengths, rows):
    seq_ends = jnp.cumsum(lengths, axis=1)
    past_end = rows[None, :, None] >= seq_ends[:, None, :]
    return jnp.sum(jnp.where(past_end, lengths[:, None, :], 0), axis=2)


def turn_table(positions, dim_size):
    half_dim = dim_size // 2
    frequency = jnp.exp(jnp.arange(half_dim, dtype=jnp.float32) * (-math.log(10000.0) / half_dim))
    angles = positions.astype(jnp.float32)[..., None] * frequency
    return (jnp.cos(angles)[..., None, :], jnp.sin(angles)[..., None, :])


def rotate(values_in, cos_table, sine_table):
    half_dim = values_in.shape[-1] // 2
    first_half = values_in[..., :half_dim]
    second_half = values_in[..., half_dim:]
    return jnp.concatenate(
        [
            first_half * cos_table - second_half * sine_table,
            first_half * sine_table + second_half * cos_table,
        ],
        axis=-1,
    )


def rotate_back(grad_rot, cos_table, sine_table):
    half_dim = grad_rot.shape[-1] // 2
    first_half = grad_rot[..., :half_dim]
    second_half = grad_rot[..., half_dim:]
    return jnp.concatenate(
        [
            first_half * cos_table + second_half * sine_table,
            second_half * cos_table - first_half * sine_table,
        ],
        axis=-1,
    )


def allowed_pairs(q_rows, q_begin, k_rows):
    causal_ok = k_rows[None, None, :] <= q_rows[None, :, None]
    inside_seq = k_rows[None, None, :] >= q_begin[:, :, None]
    return (causal_ok & inside_seq)[:, None]


def pair_grads(
    q_block, grad_block, logsum, row_delta, q_rows, q_begin, k_block, v_block, k_rows, score_scale
):
    raw_score = jnp.einsum("mqhd,mkhd->mhqk", q_block, k_block, preferred_element_type=jnp.float32)
    allowed = allowed_pairs(q_rows, q_begin, k_rows)
    prob_rows = jnp.where(allowed, jnp.exp(raw_score * score_scale - logsum[..., None]), 0.0)
    grad_prob = jnp.einsum(
        "mqhd,mkhd->mhqk", grad_block, v_block, preferred_element_type=jnp.float32
    )
    grad_score = (prob_rows * (grad_prob - row_delta[..., None]) * score_scale).astype(jnp.bfloat16)
    result = []
    result.append(
        jnp.einsum("mhqk,mkhd->mqhd", grad_score, k_block, preferred_element_type=jnp.float32)
    )
    result.append(
        jnp.einsum("mhqk,mqhd->mkhd", grad_score, q_block, preferred_element_type=jnp.float32)
    )
    result.append(
        jnp.einsum(
            "mhqk,mqhd->mkhd",
            prob_rows.astype(jnp.bfloat16),
            grad_block,
            preferred_element_type=jnp.float32,
        )
    )
    return tuple(result)


def local(
    tokens,
    lengths,
    head_count,
    width_index,
    router_prob,
    norm_gain,
    w_query,
    w_key,
    w_value,
    w_out,
    ln_gain,
    ln_bias,
    w_up,
    w_down,
    grad_out,
):
    batches, rows_dev, features = tokens.shape
    local_heads = w_query.shape[1] // HD
    unit_count = w_up.shape[1]
    blocks = lax.axis_size("blk")
    first_row = lax.axis_index("blk") * rows_dev
    last_row = first_row + rows_dev - 1
    local_rows = first_row + jnp.arange(rows_dev, dtype=jnp.int32)
    local_begin = seq_begin(lengths, local_rows)
    cos_table, sine_table = turn_table(local_rows[None, :] - local_begin, HD)
    score_scale = 1.0 / math.sqrt(HD)
    head_ids = lax.axis_index("tp") * local_heads + jnp.arange(local_heads, dtype=jnp.int32)
    head_mask = (head_ids[None, None, :] < head_count[:, :, None]).astype(jnp.float32)
    unit_ids = lax.axis_index("tp") * unit_count + jnp.arange(unit_count, dtype=jnp.int32)
    unit_mask = (unit_ids[None, None, :] < (width_index[:, :, None] + 1) * (FF // 4)).astype(
        jnp.float32
    )
    block_shape = (batches, rows_dev, local_heads, HD)
    inputs = tokens.astype(jnp.float32)
    inv_rms = lax.rsqrt(jnp.mean(inputs * inputs, axis=-1, keepdims=True) + EPS)
    scaled = inputs * inv_rms
    normed = (scaled * norm_gain).astype(jnp.bfloat16)

    def project(matrix):
        return jnp.einsum(
            "mtd,de->mte", normed, matrix, preferred_element_type=jnp.float32
        ).reshape(block_shape)

    query_local = rotate(project(w_query), cos_table, sine_table).astype(jnp.bfloat16)
    key_local = rotate(project(w_key), cos_table, sine_table).astype(jnp.bfloat16)
    value_local = project(w_value).astype(jnp.bfloat16)
    start_state = (
        jnp.full((batches, local_heads, rows_dev), NEG, jnp.float32),
        jnp.zeros((batches, local_heads, rows_dev), jnp.float32),
        jnp.zeros((batches, local_heads, rows_dev, HD), jnp.float32),
    )
    key_piece = lax.all_gather(key_local, "blk", axis=1, tiled=True)
    value_piece = lax.all_gather(value_local, "blk", axis=1, tiled=True)
    k_rows = jnp.arange(key_piece.shape[1], dtype=jnp.int32)

    def attend_compute_part(state_now):
        row_max, row_sum, weighted = state_now
        raw_score = jnp.einsum(
            "mqhd,mkhd->mhqk", query_local, key_piece, preferred_element_type=jnp.float32
        )
        allowed = allowed_pairs(local_rows, local_begin, k_rows)
        score = jnp.where(allowed, raw_score * score_scale, NEG)
        new_max = jnp.maximum(row_max, jnp.max(score, axis=-1))
        weights = jnp.where(allowed, jnp.exp(score - new_max[..., None]), 0.0)
        new_sum = jnp.sum(weights, axis=-1)
        new_weighted = jnp.einsum(
            "mhqk,mkhd->mhqd",
            weights.astype(jnp.bfloat16),
            value_piece,
            preferred_element_type=jnp.float32,
        )
        return (new_max, new_sum, new_weighted)

    row_max, row_sum, weighted = lax.cond(
        jnp.int32(0) > last_row, lambda state_now: state_now, attend_compute_part, start_state
    )
    logsum = row_max + jnp.log(row_sum)
    attended = jnp.transpose(weighted / row_sum[..., None], (0, 2, 1, 3)) * head_mask[..., None]
    heads_out = attended.astype(jnp.bfloat16).reshape(batches, rows_dev, local_heads * HD)
    router_col = router_prob[..., None]
    upstream = grad_out.astype(jnp.float32)
    count = batches * rows_dev
    mixed_out, grad_branch, lifted, squared, grad_hidden, own_resid, ln_sums = middle(
        tokens.reshape(count, features),
        grad_out.reshape(count, features),
        heads_out.reshape(count, -1),
        w_out,
        ln_gain,
        ln_bias,
        w_up,
        w_down,
        router_prob,
        width_index,
    )
    mixed_out = mixed_out.reshape(tokens.shape)
    grad_branch = grad_branch.reshape(tokens.shape)
    grad_feed = (router_col * upstream).astype(jnp.bfloat16).reshape(count, features)
    grad_down = jnp.einsum("tf,td->fd", squared, grad_feed, preferred_element_type=jnp.float32)
    grad_upw = jnp.einsum("td,tf->df", lifted, grad_hidden, preferred_element_type=jnp.float32)
    grad_outw = jnp.einsum(
        "mte,mtd->ed", heads_out, grad_branch, preferred_element_type=jnp.float32
    )
    grad_heads = (
        jnp.einsum("mtd,ed->mte", grad_branch, w_out, preferred_element_type=jnp.float32)
        .astype(jnp.bfloat16)
        .reshape(block_shape)
    )
    grad_block = grad_heads * head_mask[..., None].astype(jnp.bfloat16)
    row_delta = jnp.sum(grad_block.astype(jnp.float32) * attended, axis=-1)
    delta_heads = jnp.transpose(row_delta, (0, 2, 1))
    key_all, value_all = (
        lax.all_gather(key_local, "blk", axis=1, tiled=True),
        lax.all_gather(value_local, "blk", axis=1, tiled=True),
    )

    def key_step(grad_query, piece_index):
        row_start = piece_index * rows_dev
        key_piece = lax.dynamic_slice_in_dim(key_all, row_start, rows_dev, 1)
        value_piece = lax.dynamic_slice_in_dim(value_all, row_start, rows_dev, 1)
        k_rows = row_start + jnp.arange(rows_dev, dtype=jnp.int32)

        def key_compute_part(running):
            pair_parts = pair_grads(
                query_local,
                grad_block,
                logsum,
                delta_heads,
                local_rows,
                local_begin,
                key_piece,
                value_piece,
                k_rows,
                score_scale,
            )
            return (running + pair_parts[0], pair_parts[1:])

        def skip_part(running):
            zero_block = jnp.zeros(block_shape, jnp.float32)
            return (running, (zero_block, zero_block))

        return lax.cond(row_start > last_row, skip_part, key_compute_part, grad_query)

    grad_query, key_terms = lax.scan(
        key_step, jnp.zeros(block_shape, jnp.float32), jnp.arange(blocks, dtype=jnp.int32)
    )
    summed_keys, summed_values = jax.tree.map(
        lambda part: part.astype(jnp.float32),
        lax.psum_scatter(as_sent(key_terms), "blk", scatter_dimension=0, tiled=True),
    )
    grad_keys = summed_keys[0]
    grad_values = summed_values[0]
    flat_shape = (batches, rows_dev, local_heads * HD)
    grad_q_pre = (
        rotate_back(grad_query, cos_table, sine_table).astype(jnp.bfloat16).reshape(flat_shape)
    )
    grad_k_pre = (
        rotate_back(grad_keys, cos_table, sine_table).astype(jnp.bfloat16).reshape(flat_shape)
    )
    grad_v_pre = grad_values.astype(jnp.bfloat16).reshape(flat_shape)
    grad_wq = jnp.einsum("mtd,mte->de", normed, grad_q_pre, preferred_element_type=jnp.float32)
    grad_wk = jnp.einsum("mtd,mte->de", normed, grad_k_pre, preferred_element_type=jnp.float32)
    grad_wv = jnp.einsum("mtd,mte->de", normed, grad_v_pre, preferred_element_type=jnp.float32)
    normed_part = (
        jnp.einsum("mte,de->mtd", grad_q_pre, w_query, preferred_element_type=jnp.float32)
        + jnp.einsum("mte,de->mtd", grad_k_pre, w_key, preferred_element_type=jnp.float32)
        + jnp.einsum("mte,de->mtd", grad_v_pre, w_value, preferred_element_type=jnp.float32)
    )
    ranks = lax.axis_size("tp")
    tp = lax.axis_index("tp")
    chunks = own_resid.shape[0]
    split = (chunks, ranks, own_resid.shape[1], features)
    grad_normed = lax.psum_scatter(
        normed_part.astype(jnp.bfloat16)
        .reshape(chunks, 2, ranks // 2, -1, features)
        .swapaxes(1, 2)
        .reshape(split),
        "tp",
        scatter_dimension=1,
    ).astype(jnp.float32)

    def own(array):
        return lax.dynamic_index_in_dim(array.reshape(split[:-1] + (-1,)), tp % 2 * (ranks // 2) + tp // 2, 1, keepdims=False)

    own_scaled = own(tokens).astype(jnp.float32) * own(inv_rms)
    gain_part = jnp.sum(grad_normed * own_scaled, axis=(0, 1))
    grad_scaled = grad_normed * norm_gain
    grad_input = own_resid + own(inv_rms) * (
        grad_scaled - own_scaled * jnp.mean(grad_scaled * own_scaled, axis=-1, keepdims=True)
    )
    grad_in = lax.all_gather(grad_input.astype(jnp.bfloat16), "tp", axis=1)
    grad_in = grad_in.reshape(chunks, ranks // 2, 2, -1, features).swapaxes(1, 2).reshape(tokens.shape)
    sums = lax.psum(jnp.concatenate([gain_part[None], ln_sums]), ("blk", "tp"))
    sums = lax.dynamic_slice_in_dim(sums, lax.axis_index("blk") * (features // blocks), features // blocks, 1)
    def share(array, dim):
        return lax.psum_scatter(
            array.astype(jnp.bfloat16), "blk", scatter_dimension=dim, tiled=True
        ).astype(jnp.float32)

    return (
        mixed_out,
        grad_in,
        sums[0],
        share(grad_wq, 0),
        share(grad_wk, 0),
        share(grad_wv, 0),
        share(grad_outw, 1),
        sums[1],
        sums[2],
        share(grad_upw, 0),
        share(grad_down, 1),
    )


def solution(mesh):
    return jax.shard_map(
        local,
        mesh=mesh,
        in_specs=(
            P(None, "blk", None),
            P(),
            P(None, "blk"),
            P(None, "blk"),
            P(None, "blk"),
            P(),
            P(None, "tp"),
            P(None, "tp"),
            P(None, "tp"),
            P("tp", None),
            P(),
            P(),
            P(None, "tp"),
            P("tp", None),
            P(None, "blk", None),
        ),
        out_specs=(
            P(None, "blk", None),
            P(None, "blk", None),
            P("blk"),
            P("blk", "tp"),
            P("blk", "tp"),
            P("blk", "tp"),
            P("tp", "blk"),
            P("blk"),
            P("blk"),
            P("blk", "tp"),
            P("tp", "blk"),
        ),
        check_vma=False,
    )
```

```python
import functools
import math

import jax
import jax.numpy as jnp
from jax import lax
from jax.experimental import pallas as pl
from jax.experimental.pallas import tpu as pltpu
from jax.sharding import PartitionSpec as P

HD = 128
FF = 8192


EPS = 1e-05
NEG = -1e30
CHUNK_ROWS = 128
CUT = 1280
VMEM_LIMIT = 60 * 2**20
RING = 4


MESH = pl.DeviceIdType.MESH
VMEM = pltpu.VMEM
LANE = 128


def remote(src, dst, send, recv, device):
    return pltpu.make_async_remote_copy(
        src_ref=src, dst_ref=dst, send_sem=send, recv_sem=recv, device_id=device, device_id_type=MESH
    )


class Place:
    def __init__(self, lines):
        blk, tp = lax.axis_index("blk"), lax.axis_index("tp")
        self.lines, self.tp = lines, tp
        self.z, self.y = tp // 2, tp % 2
        self.other = 1 - self.y
        self.across = (blk, self.z * 2 + self.other)
        self.right = (blk, jnp.minimum(self.z + 1, lines - 1) * 2 + self.y)
        self.left = (blk, jnp.maximum(self.z - 1, 0) * 2 + self.y)
        self.has_right, self.has_left = self.z < lines - 1, self.z > 0


def greet(*axes):
    place = {axis: lax.axis_index(axis) for axis in ("blk", "tp")}
    peers = 0
    for axis in axes:
        size = lax.axis_size(axis)
        for k in range(1, size):
            peer = dict(place)
            peer[axis] = (place[axis] + k) % size
            pl.semaphore_signal(
                pltpu.get_barrier_semaphore(),
                inc=1,
                device_id=(peer["blk"], peer["tp"]),
                device_id_type=MESH,
            )
        peers += size - 1
    pl.semaphore_wait(pltpu.get_barrier_semaphore(), peers)


class Scatter:
    def __init__(self, place, cut, part, across_a, line_a, line_b, across_b, send, recv):
        self.at, self.cut, self.part = place, cut, part
        self.across_a, self.line_a, self.line_b, self.across_b = across_a, line_a, line_b, across_b
        self.send, self.recv = send, recv

    @staticmethod
    def scratch(chunks, lines, rows, width, cut):
        return [
            VMEM((chunks, 2, lines, rows, width), jnp.bfloat16),
            VMEM((chunks, lines, rows, cut), jnp.bfloat16),
            VMEM((chunks, lines + 1, rows, cut), jnp.bfloat16),
            VMEM((chunks, lines + 1, 2, rows, width - cut), jnp.bfloat16),
            VMEM((chunks, rows, width - cut), jnp.bfloat16),
        ]

    @staticmethod
    def semaphores(chunks, lines):
        return [
            pltpu.SemaphoreType.DMA((chunks, 2 * lines + 2)),
            pltpu.SemaphoreType.DMA((chunks, 2 * lines + 4)),
        ]

    def low(self, c, j):
        return self.part.at[c, self.at.y, j, :, : self.cut]

    def high(self, c, j):
        return self.part.at[c, :, j, :, self.cut :]

    def copy_across_a(self, c):
        return remote(
            self.part.at[c, self.at.other, :, :, : self.cut],
            self.across_a.at[c],
            self.send.at[c, 0],
            self.recv.at[c, 0],
            self.at.across,
        )

    def copy_across_b(self, c):
        return remote(
            self.part.at[c, self.at.other, self.at.z, :, self.cut :],
            self.across_b.at[c],
            self.send.at[c, 1],
            self.recv.at[c, 1],
            self.at.across,
        )

    def copy_line(self, c, j, slot, device, first):
        lines = self.at.lines
        if first:
            source, target, send, recv = self.low(c, j), self.line_a, 2, 2
        else:
            source, target, send, recv = self.high(c, j), self.line_b, 2 + lines, 3 + lines
        return remote(
            source, target.at[c, slot], self.send.at[c, send + j], self.recv.at[c, recv + slot], device
        )

    def to_right(self, c, j, first):
        return self.copy_line(c, j, j + 1, self.at.right, first)

    def to_left(self, c, j, first):
        return self.copy_line(c, j, j, self.at.left, first)

    def take(self, c, j, slot, first):
        self.copy_line(c, j, slot, self.at.right, first).wait_recv()
        view = self.low(c, j) if first else self.high(c, j)
        came = (self.line_a if first else self.line_b)[c, slot]
        view[...] = (view[...].astype(jnp.float32) + came.astype(jnp.float32)).astype(jnp.bfloat16)

    def line_starts(self, c, first):
        lines = self.at.lines

        @pl.when(self.at.z == 0)
        def _():
            for j in range(lines - 1, 0, -1):
                self.to_right(c, j, first).start()

        @pl.when(self.at.z == lines - 1)
        def _():
            for j in range(lines - 1):
                self.to_left(c, j, first).start()

    def line_hop(self, c, step, first):
        lines = self.at.lines

        @pl.when(self.at.z == step)
        def _():
            for j in range(lines - 1, step, -1):
                self.take(c, j, j + 1, first)
                self.to_right(c, j, first).start()

        @pl.when(self.at.z == lines - 1 - step)
        def _():
            for j in range(lines - 1 - step):
                self.take(c, j, j, first)
                self.to_left(c, j, first).start()

    def line_end(self, c, total, first):
        z = self.at.z
        buffer = self.line_a if first else self.line_b

        @pl.when(self.at.has_left)
        def _():
            self.copy_line(c, z, z + 1, self.at.right, first).wait_recv()
            total[...] += buffer[c, z + 1].astype(jnp.float32)

        @pl.when(self.at.has_right)
        def _():
            self.copy_line(c, z, z, self.at.right, first).wait_recv()
            total[...] += buffer[c, z].astype(jnp.float32)

    def step0(self, c):
        self.copy_across_a(c).start()
        self.line_starts(c, False)

    def step(self, c, k, total_b):
        lines = self.at.lines
        if k == 1:
            self.copy_across_a(c).wait_recv()
            mine = self.part.at[c, self.at.y, :, :, : self.cut]
            mine[...] = (
                mine[...].astype(jnp.float32) + self.across_a[c].astype(jnp.float32)
            ).astype(jnp.bfloat16)
            self.line_starts(c, True)
        elif k - 1 <= lines - 2:
            self.line_hop(c, k - 1, True)
        if k <= lines - 2:
            self.line_hop(c, k, False)
        elif k == lines - 1:
            mine = self.high(c, self.at.z)
            total_b[...] = mine[...].astype(jnp.float32)
            self.line_end(c, total_b, False)
            mine[...] = total_b[...].astype(jnp.bfloat16)
            self.copy_across_b(c).start()

    def finish(self, c, total):
        y, z = self.at.y, self.at.z
        low, high = total.at[:, : self.cut], total.at[:, self.cut :]
        low[...] = self.low(c, z)[...].astype(jnp.float32)
        self.line_end(c, low, True)
        self.copy_across_b(c).wait_recv()
        high[...] = self.part[c, y, z, :, self.cut :].astype(jnp.float32) + self.across_b[c].astype(
            jnp.float32
        )

    def drain(self, c):
        self.copy_across_a(c).wait_send()
        self.copy_across_b(c).wait_send()
        for first in (True, False):
            for j in range(self.at.lines):

                @pl.when(self.at.z != j)
                def _(j=j, first=first):
                    self.to_right(c, j, first).wait_send()


class Gather:
    def __init__(self, place, cut, own, full, local, send, recv):
        self.at, self.cut, self.own, self.full = place, cut, own, full
        self.local, self.send, self.recv = local, send, recv

    @staticmethod
    def scratch(chunks, lines):
        return [
            pltpu.SemaphoreType.DMA((chunks,)),
            pltpu.SemaphoreType.DMA((chunks, 5 * lines + 1)),
            pltpu.SemaphoreType.DMA((chunks, 3 * lines + 1)),
        ]

    def low(self, c, j):
        target = self.full.at[c, self.at.y, j, :, : self.cut]
        return target, target

    def copy_low(self, c, j, way, mine):
        lines = self.at.lines
        target = self.full.at[c, self.at.y, j, :, : self.cut]
        source = self.own(c).at[:, : self.cut] if mine else target
        device = (self.at.right, self.at.left, self.at.across)[way]
        recv = j + (lines if way == 2 else 0)
        return remote(source, target, self.send.at[c, way * lines + j], self.recv.at[c, recv], device)

    def copy_high(self, c, j, way):
        lines = self.at.lines
        view = self.full.at[c, :, j, :, self.cut :]
        device = (self.at.right, self.at.left)[way]
        return remote(
            view, view, self.send.at[c, (3 + way) * lines + j], self.recv.at[c, 2 * lines + j], device
        )

    def copy_high_across(self, c):
        lines = self.at.lines
        return remote(
            self.own(c).at[:, self.cut :],
            self.full.at[c, self.at.y, self.at.z, :, self.cut :],
            self.send.at[c, 5 * lines],
            self.recv.at[c, 3 * lines],
            self.at.across,
        )

    def copy_local(self, c):
        return pltpu.make_async_copy(
            self.own(c), self.full.at[c, self.at.y, self.at.z], self.local.at[c]
        )

    def step0(self, c):
        z = self.at.z
        if self.local is not None:
            self.copy_local(c).start()

        @pl.when(self.at.has_right)
        def _():
            self.copy_low(c, z, 0, True).start()

        @pl.when(self.at.has_left)
        def _():
            self.copy_low(c, z, 1, True).start()

        self.copy_high_across(c).start()
        self.copy_low(c, z, 2, True).start()

    def low_hop(self, c, k):
        z, lines = self.at.z, self.at.lines

        @pl.when(z >= k)
        def _():
            self.copy_low(c, z - k, 0, False).wait_recv()

            @pl.when(self.at.has_right)
            def _():
                self.copy_low(c, z - k, 0, False).start()

            self.copy_low(c, z - k, 2, False).start()

        @pl.when(z + k < lines)
        def _():
            self.copy_low(c, z + k, 0, False).wait_recv()

            @pl.when(self.at.has_left)
            def _():
                self.copy_low(c, z + k, 1, False).start()

            self.copy_low(c, z + k, 2, False).start()

    def high_hop(self, c, k):
        z, lines = self.at.z, self.at.lines

        @pl.when(z >= k)
        def _():
            self.copy_high(c, z - k, 0).wait_recv()

            @pl.when(self.at.has_right)
            def _():
                self.copy_high(c, z - k, 0).start()

        @pl.when(z + k < lines)
        def _():
            self.copy_high(c, z + k, 0).wait_recv()

            @pl.when(self.at.has_left)
            def _():
                self.copy_high(c, z + k, 1).start()

    def step(self, c, k):
        lines, z = self.at.lines, self.at.z
        if k == 1:
            if self.local is not None:
                self.copy_local(c).wait()
            self.copy_high_across(c).wait_recv()

            @pl.when(self.at.has_right)
            def _():
                self.copy_high(c, z, 0).start()

            @pl.when(self.at.has_left)
            def _():
                self.copy_high(c, z, 1).start()

        if k <= lines - 1:
            self.low_hop(c, k)
        if k > 1:
            self.high_hop(c, k - 1)
        if k == lines:
            for j in range(lines):
                target = self.full.at[c, self.at.other, j, :, : self.cut]
                remote(
                    target, target, self.send.at[c, 2 * lines + j], self.recv.at[c, lines + j], self.at.across
                ).wait_recv()

    def drain(self, c):
        lines, z = self.at.lines, self.at.z
        self.copy_high_across(c).wait_send()
        for j in range(lines):

            @pl.when(self.at.has_right & (z >= j))
            def _(j=j):
                self.copy_low(c, j, 0, False).wait_send()
                self.copy_high(c, j, 0).wait_send()

            @pl.when(self.at.has_left & (z <= j))
            def _(j=j):
                self.copy_low(c, j, 1, False).wait_send()
                self.copy_high(c, j, 1).wait_send()

            self.copy_low(c, j, 2, False).wait_send()


class BlockScatter:
    def __init__(self, blocks, slice_of, part, from_core, from_chip, send, recv):
        self.blk, self.tp = lax.axis_index("blk"), lax.axis_index("tp")
        self.chips, self.chip, self.core = blocks // 2, self.blk // 2, self.blk % 2
        self.slice_of, self.part = slice_of, part
        self.from_core, self.from_chip, self.send, self.recv = from_core, from_chip, send, recv

    @staticmethod
    def scratch(blocks, shape):
        chips = blocks // 2
        return [
            VMEM((blocks,) + shape, jnp.bfloat16),
            VMEM((chips,) + shape, jnp.bfloat16),
            VMEM((max(chips - 1, 1),) + shape, jnp.bfloat16),
            pltpu.SemaphoreType.DMA((2, chips)),
            pltpu.SemaphoreType.DMA((2, chips)),
        ]

    def to_core(self, k):
        return remote(
            self.part.at[k * 2 + 1 - self.core],
            self.from_core.at[k],
            self.send.at[0, k],
            self.recv.at[0, k],
            (self.chip * 2 + 1 - self.core, self.tp),
        )

    def to_chip(self, k):
        return remote(
            self.part.at[k * 2 + self.core],
            self.from_chip.at[(self.chip - k + self.chips) % self.chips - 1],
            self.send.at[1, k],
            self.recv.at[1, (self.chip - k + self.chips) % self.chips],
            (k * 2 + self.core, self.tp),
        )

    def came_chip(self, i):
        k = (self.chip + i) % self.chips
        return remote(
            self.part.at[k * 2 + self.core],
            self.from_chip.at[i - 1],
            self.send.at[1, k],
            self.recv.at[1, i],
            (k * 2 + self.core, self.tp),
        )

    def all_first(self):
        @pl.loop(0, self.chips)
        def _(i):
            self.first(i)

    def all_second(self):
        @pl.loop(0, self.chips)
        def _(i):
            self.second(i)

    def first(self, i):
        k = (self.chip + 1 + i) % self.chips
        self.slice_of(k * 2 + 1 - self.core, self.part.at[k * 2 + 1 - self.core])
        self.to_core(k).start()

    def second(self, i):
        k = (self.chip + 1 + i) % self.chips
        mine = self.part.at[k * 2 + self.core]
        self.slice_of(k * 2 + self.core, mine)
        self.to_core(k).wait_recv()
        mine[...] = (mine[...].astype(jnp.float32) + self.from_core[k].astype(jnp.float32)).astype(
            jnp.bfloat16
        )

        @pl.when(k != self.chip)
        def _():
            self.to_chip(k).start()

    def third(self, out):
        out[...] = self.part[self.blk].astype(jnp.float32)

        @pl.loop(1, self.chips)
        def _(i):
            self.came_chip(i).wait_recv()
            out[...] += self.from_chip[i - 1].astype(jnp.float32)

    def drain(self):
        @pl.loop(0, self.chips)
        def _(k):
            self.to_core(k).wait_send()

            @pl.when(k != self.chip)
            def _():
                self.to_chip(k).wait_send()


def rows_sum(values):
    return jnp.sum(values, axis=0, keepdims=True)


def mean_last(values):
    return jnp.mean(values, axis=-1, keepdims=True)


def dot_nn(a, b):
    return jnp.dot(a, b, preferred_element_type=jnp.float32)


def dot_nt(a, b):
    return lax.dot_general(a, b, (((1,), (1,)), ((), ())), preferred_element_type=jnp.float32)


def dot_tn(a, b):
    return lax.dot_general(a, b, (((0,), (0,)), ((), ())), preferred_element_type=jnp.float32)


TILE = 256


def middle_kernel(
    lines, chunks, cut, chunk_rows, tokens_hbm, grad_hbm, heads_ref, wo_ref, gain_ref, bias_ref, up_ref, down_ref,
    prob_ref, width_ref, branch_hbm, feed_hbm, input_ref, resid_ref, sums_ref, grad_up_ref, grad_down_ref,
    x_own, g_own, g_all, own_branch, feed_part, lifted_ref, squared_ref, hidden_ref, normal_ref, inv_own, total,
    total_b, sem_in, sem_g, sem_feed, *rest,
):
    place = Place(lines)
    y, z, tp = place.y, place.z, place.tp
    spot = y * lines + z
    rows = chunk_rows // (2 * lines)
    width = gain_ref.shape[-1]
    units = up_ref.shape[1]
    blocks = lax.axis_size("blk")
    s1, s2 = Scatter(place, cut, *rest[:5], *rest[5:7]), Scatter(place, cut, *rest[:5], *rest[7:9])
    a1 = Gather(place, cut, lambda c: lifted_ref.at[c, y, z], lifted_ref, None, *rest[10:12])
    a2 = Gather(place, cut, lambda c: own_branch.at[c], branch_hbm, *rest[12:15])
    share = width // blocks

    def up_slice(target, out):
        step = min(TILE, share)

        @pl.loop(0, share // step)
        def _(i):
            lanes = pl.ds(pl.multiple_of(target * share + i * step, step), step)
            lifted = lifted_ref[:, :, :, :, lanes].reshape(chunks * chunk_rows, step)
            out[pl.ds(pl.multiple_of(i * step, step), step), :] = dot_tn(lifted, hidden_ref[...]).astype(
                jnp.bfloat16
            )

    def down_slice(target, out):
        lanes = pl.ds(pl.multiple_of(target * share, share), share)

        @pl.loop(0, units // TILE)
        def _(i):
            cols = pl.ds(pl.multiple_of(i * TILE, TILE), TILE)
            grad = g_all[:, :, :, lanes].reshape(chunks * chunk_rows, share)
            out[cols, :] = dot_tn(squared_ref[:, cols], grad).astype(jnp.bfloat16)

    grad_up = BlockScatter(blocks, up_slice, *rest[15:20])
    grad_down = BlockScatter(blocks, down_slice, *rest[20:25])

    get_x = pltpu.make_async_copy(tokens_hbm.at[:, spot], x_own, sem_in.at[0])
    get_g = pltpu.make_async_copy(grad_hbm.at[:, spot], g_own, sem_in.at[1])
    get_x.start()
    get_g.start()

    def get_grad(c):
        return pltpu.make_async_copy(grad_hbm.at[c], g_all.at[c], sem_g.at[c])

    def put_feed(c):
        return pltpu.make_async_copy(feed_part.at[c % 2], feed_hbm.at[c], sem_feed.at[c])

    @pl.loop(0, chunks)
    def _(c):
        get_grad(c).start()

    greet("tp", "blk")
    get_x.wait()
    get_g.wait()
    sums_ref[...] = jnp.zeros_like(sums_ref)

    def own_rows(c):
        return pl.ds(pl.multiple_of(c * chunk_rows + spot * rows, rows), rows)

    def all_rows(c):
        return pl.ds(pl.multiple_of(c * chunk_rows, chunk_rows), chunk_rows)

    def tiled(n, body):
        @pl.loop(0, n // TILE)
        def _(i):
            body(pl.ds(pl.multiple_of(i * TILE, TILE), TILE))

    def put(part, c, cols, values):
        part[c, :, :, :, cols] = values.astype(jnp.bfloat16).reshape(2, lines, rows, TILE)

    def project(c):
        heads = heads_ref[all_rows(c), :]

        def one(cols):
            put(s1.part, c, cols, dot_nn(heads, wo_ref[:, cols]))

        tiled(width, one)
        s1.step0(c)

    def norm(c):
        s1.finish(c, total)
        residual = x_own[c].astype(jnp.float32) + total[...]
        center = residual - mean_last(residual)
        inv_std = lax.rsqrt(mean_last(center * center) + EPS)
        normal = center * inv_std
        input_ref[c] = residual
        normal_ref[c] = normal
        inv_own[c] = jnp.broadcast_to(inv_std, (rows, LANE))
        lifted_ref[c, y, z] = (normal * gain_ref[...] + bias_ref[...]).astype(jnp.bfloat16)
        a1.step0(c)

    def feed(c):
        s1.drain(c)
        lifted = lifted_ref[c].reshape(chunk_rows, width)
        span = all_rows(c)
        prob, limit = prob_ref[span, :], (width_ref[span, :] + 1) * (FF // 4)
        get_grad(c).wait()
        g_all[c] = (g_all[c].astype(jnp.float32) * prob.reshape(2 * lines, rows, 1)).astype(jnp.bfloat16)

        def units_of(cols):
            active = jnp.maximum(dot_nn(lifted, up_ref[:, cols]), 0.0)
            ids = tp * units + cols.start + lax.broadcasted_iota(jnp.int32, (chunk_rows, TILE), 1)
            mask = (ids < limit).astype(jnp.float32)
            squared_ref[span, cols] = (active * active * mask).astype(jnp.bfloat16)
            back = dot_nt(g_all[c].reshape(chunk_rows, width), down_ref[cols, :])
            hidden_ref[span, cols] = (back * mask * 2.0 * active).astype(jnp.bfloat16)

        tiled(units, units_of)
        hidden = hidden_ref[span, :]

        def lift(cols):
            put(s2.part, c, cols, dot_nt(hidden, up_ref[cols, :]))

        tiled(width, lift)
        s2.step0(c)
        squared = squared_ref[span, :]

        @pl.when(c >= 2)
        def _():
            put_feed(c - 2).wait()

        def out(cols):
            put(feed_part, c % 2, cols, dot_nn(squared, down_ref[:, cols]))

        tiled(width, out)
        put_feed(c).start()

    def norm_back(c):
        s2.finish(c, total)
        grad_lifted, normal = total[...], normal_ref[c]
        sums_ref[0:1, :] += rows_sum(grad_lifted * normal)
        sums_ref[1:2, :] += rows_sum(grad_lifted)
        g = grad_lifted * gain_ref[...]
        grad_resid = g_own[c].astype(jnp.float32) + inv_own[c][:, 0:1] * (
            g - mean_last(g) - normal * mean_last(g * normal)
        )
        resid_ref[c] = grad_resid
        own_branch[c] = grad_resid.astype(jnp.bfloat16)
        a2.step0(c)

    @pl.loop(0, chunks + 4 * lines)
    def _(r):
        def at(offset, task):
            c = r - offset

            @pl.when((c >= 0) & (c < chunks))
            def _():
                task(c)

        for k in range(1, lines):
            at(2 * lines + k, lambda c, k=k: s2.step(c, k, total_b))
        for k in range(1, lines):
            at(k, lambda c, k=k: s1.step(c, k, total_b))
        for k in range(1, lines + 1):
            at(lines + k, lambda c, k=k: a1.step(c, k))
        for k in range(1, lines + 1):
            at(3 * lines + k, lambda c, k=k: a2.step(c, k))
        at(3 * lines, norm_back)
        at(lines, norm)
        at(2 * lines, feed)
        at(0, project)
        for k, task in enumerate((grad_up.all_first, grad_down.all_first, grad_up.all_second, grad_down.all_second)):
            pl.when(r == chunks + 2 * lines + k)(task)

    grad_up.third(grad_up_ref)
    grad_down.third(grad_down_ref)
    for c in range(max(chunks - 2, 0), chunks):
        put_feed(c).wait()

    @pl.loop(0, chunks)
    def _(c):
        for part in (s2, a1, a2):
            part.drain(c)

    grad_up.drain()
    grad_down.drain()


def middle(tokens, grad_out, heads_out, w_out, ln_gain, ln_bias, w_up, w_down, router_prob, width_index):
    lines = lax.axis_size("tp") // 2
    count, width = tokens.shape
    units = w_up.shape[1]
    chunk_rows = CHUNK_ROWS
    chunks, rows = count // chunk_rows, chunk_rows // (2 * lines)
    cut = CUT
    split = (chunks, 2 * lines, rows, width)
    full = (chunks, 2, lines, rows, width)
    any_space, vmem = pl.BlockSpec(memory_space=pl.ANY), pl.BlockSpec(memory_space=VMEM)
    bf16, f32 = jnp.bfloat16, jnp.float32
    dma = pltpu.SemaphoreType.DMA
    blocks = lax.axis_size("blk")
    share = width // blocks
    outs = pl.pallas_call(
        functools.partial(middle_kernel, lines, chunks, cut, chunk_rows),
        out_shape=[
            jax.ShapeDtypeStruct(full, bf16),
            jax.ShapeDtypeStruct(full, bf16),
            jax.ShapeDtypeStruct((chunks, rows, width), f32),
            jax.ShapeDtypeStruct((chunks, rows, width), f32),
            jax.ShapeDtypeStruct((2, width), f32),
            jax.ShapeDtypeStruct((share, units), f32),
            jax.ShapeDtypeStruct((units, share), f32),
        ],
        in_specs=[any_space, any_space] + [vmem] * 8,
        out_specs=[any_space, any_space] + [vmem] * 5,
        scratch_shapes=[
            VMEM((chunks, rows, width), bf16),
            VMEM((chunks, rows, width), bf16),
            VMEM(split, bf16),
            VMEM((chunks, rows, width), bf16),
            VMEM((2,) + full[1:], bf16),
            VMEM(full, bf16),
            VMEM((count, units), bf16),
            VMEM((count, units), bf16),
            VMEM((chunks, rows, width), f32),
            VMEM((chunks, rows, LANE), f32),
            VMEM((rows, width), f32),
            VMEM((2, rows, width - cut), f32),
            dma((2,)),
            dma((chunks,)),
            dma((chunks,)),
        ]
        + Scatter.scratch(chunks, lines, rows, width, cut)
        + Scatter.semaphores(chunks, lines) * 2
        + Gather.scratch(chunks, lines) * 2
        + BlockScatter.scratch(blocks, (share, units))
        + BlockScatter.scratch(blocks, (units, share)),
        compiler_params=pltpu.CompilerParams(
            collective_id=1, has_side_effects=True, vmem_limit_bytes=VMEM_LIMIT
        ),
        cost_estimate=pl.CostEstimate(
            flops=2 * count * width * (w_out.shape[0] + 6 * units), bytes_accessed=40 * 2**20, transcendentals=0
        ),
    )(
        tokens.reshape(split),
        grad_out.reshape(split),
        heads_out,
        w_out,
        ln_gain[None],
        ln_bias[None],
        w_up,
        w_down,
        router_prob.reshape(count, 1),
        width_index.reshape(count, 1),
    )
    return (outs[0].reshape(count, width),) + tuple(outs[1:])


def turn_back(grad, cos_rows, sin_rows):
    return grad * cos_rows - pltpu.roll(grad, HD // 2, 1) * sin_rows


def back_kernel(
    lines, blocks, batches, chunks, cut, chunk_rows, tokens_hbm, keys_hbm, values_hbm, feed_hbm, input_ref,
    resid_ref, branch_ref, query_ref, heads_ref, normed_ref, wq_ref, wk_ref, wv_ref, wo_ref, gain_ref, lse_ref,
    begin_ref, count_ref, prob_ref, cos_ref, sin_ref, sums_ref, mixed_hbm, in_hbm, gq_ref, gk_ref, gv_ref, go_ref,
    small_ref, x_own, own_in, own_mixed, key_mb, value_mb, grad_mb, delta_mb, dq_mb, stage, own, came, pre, total, total_b,
    grad_w, small, small_blk, small_part, small_tp, sem_in, sem_feed, sem_kv, sem_send, sem_recv, sem_free, sem_blk, sem_tp,
    *rest,
):
    place = Place(lines)
    blk, tp, y, z = lax.axis_index("blk"), place.tp, place.y, place.z
    spot = y * lines + z
    rows = chunk_rows // (2 * lines)
    width = gain_ref.shape[-1]
    wide = query_ref.shape[1]
    heads = wide // HD
    span = query_ref.shape[0] // batches
    per = span // chunk_rows
    scale = 1.0 / math.sqrt(HD)
    s3, s4 = Scatter(place, cut, *rest[0:7]), Scatter(place, cut, *rest[7:14])
    a3 = Gather(place, cut, lambda c: own_mixed.at[c], mixed_hbm, *rest[14:17])
    a4 = Gather(place, cut, lambda c: own_in.at[c], in_hbm, *rest[17:20])

    get_x = pltpu.make_async_copy(tokens_hbm.at[:, spot], x_own, sem_in)
    get_x.start()

    def get_kv(step):
        m, keys = step // (blk + 1), pl.ds(pl.multiple_of(step % (blk + 1) * span, span), span)
        return (
            pltpu.make_async_copy(keys_hbm.at[m, keys], key_mb.at[step % 2], sem_kv.at[0, step % 2]),
            pltpu.make_async_copy(values_hbm.at[m, keys], value_mb.at[step % 2], sem_kv.at[1, step % 2]),
        )

    def get_feed(c):
        return pltpu.make_async_copy(feed_hbm.at[c], s3.part.at[c], sem_feed.at[c])

    @pl.loop(0, chunks)
    def _(c):
        get_feed(c).start()

    for copy in get_kv(0):
        copy.start()
    greet("tp", "blk")
    get_x.wait()
    small[...] = jnp.zeros_like(small)
    small[1:3, :] = sums_ref[...]

    def slab(m):
        return pl.ds(pl.multiple_of(m * span, span), span)

    ring = stage.shape[0]

    def to_owner(m, k):
        slot = (m * blk + k) % ring
        return remote(
            stage.at[slot], came.at[m % 2, blk], sem_send.at[slot], sem_recv.at[m % 2, blk], (k, tp)
        )

    def from_peer(m, k):
        return remote(stage.at[0], came.at[m % 2, k], sem_send.at[0], sem_recv.at[m % 2, k], (k, tp))

    def attend_back(m):
        here = slab(m)
        grad = dot_nt(branch_ref[here, :], wo_ref[...]).astype(jnp.bfloat16)
        for h in range(heads):
            cols = slice(h * HD, (h + 1) * HD)
            head = tp * heads + h
            masked = jnp.where(head < count_ref[here, :], grad[:, cols].astype(jnp.float32), 0.0)
            grad_mb[:, cols] = masked.astype(jnp.bfloat16)
            delta = jnp.sum(masked * heads_ref[here, cols].astype(jnp.float32), axis=-1, keepdims=True)
            delta_mb[h] = jnp.broadcast_to(delta, (span, LANE))
        dq_mb[...] = jnp.zeros_like(dq_mb)
        q_rows = blk * span + lax.broadcasted_iota(jnp.int32, (span, span), 0)
        begin = begin_ref[here, :]

        def pairs(k, out):
            step = m * (blk + 1) + k
            for copy in get_kv(step):
                copy.wait()

            @pl.when(step + 1 < batches * (blk + 1))
            def _():
                for copy in get_kv(step + 1):
                    copy.start()

            k_rows = k * span + lax.broadcasted_iota(jnp.int32, (span, span), 1)
            allowed = (k_rows <= q_rows) & (k_rows >= begin)
            for h in range(heads):
                cols = slice(h * HD, (h + 1) * HD)
                q, g = query_ref[here, cols], grad_mb[:, cols]
                key, value = key_mb[step % 2, :, cols], value_mb[step % 2, :, cols]
                raw = dot_nt(q, key)
                prob = jnp.where(allowed, jnp.exp(raw * scale - lse_ref[here, h : h + 1]), 0.0)
                grad_prob = dot_nt(g, value)
                grad_score = (prob * (grad_prob - delta_mb[h][:, 0:1]) * scale).astype(jnp.bfloat16)
                dq_mb[:, cols] += dot_nn(grad_score, key)
                out[:, cols] = dot_tn(grad_score, q).astype(jnp.bfloat16)
                out[:, wide + h * HD : wide + (h + 1) * HD] = dot_tn(prob.astype(jnp.bfloat16), g).astype(
                    jnp.bfloat16
                )

        @pl.loop(0, blk)
        def _(k):
            sent = m * blk + k

            @pl.when(sent >= ring)
            def _():
                to_owner((sent - ring) // blk, (sent - ring) % blk).wait_send()

            pairs(k, stage.at[sent % ring])

            @pl.when(m >= 2)
            def _():
                pl.semaphore_wait(sem_free.at[k], 1)

            to_owner(m, k).start()

        pairs(blk, own.at[m % 2])
        for h in range(heads):
            cols = slice(h * HD, (h + 1) * HD)
            pre[here, cols] = turn_back(dq_mb[:, cols], cos_ref[here, :], sin_ref[here, :]).astype(
                jnp.bfloat16
            )

    def gather_kv(m):
        here = slab(m)
        grad_w[...] = own[m % 2].astype(jnp.float32)

        @pl.loop(blk + 1, blocks)
        def _(k):
            from_peer(m, k).wait_recv()
            grad_w[...] += came[m % 2, k].astype(jnp.float32)

            @pl.when(m + 2 < batches)
            def _():
                pl.semaphore_signal(sem_free.at[blk], inc=1, device_id=(k, tp), device_id_type=MESH)

        for h in range(heads):
            cols = slice(h * HD, (h + 1) * HD)
            pre[here, wide + h * HD : wide + (h + 1) * HD] = turn_back(
                grad_w[:, cols], cos_ref[here, :], sin_ref[here, :]
            ).astype(jnp.bfloat16)
        pre[here, 2 * wide :] = grad_w[:, wide:].astype(jnp.bfloat16)

    def spread(c):
        here = pl.ds(pl.multiple_of(c * chunk_rows, chunk_rows), chunk_rows)

        @pl.loop(0, width // TILE)
        def _(i):
            cols = pl.ds(pl.multiple_of(i * TILE, TILE), TILE)
            grad = dot_nt(pre[here, :wide], wq_ref[cols, :])
            grad += dot_nt(pre[here, wide : 2 * wide], wk_ref[cols, :])
            grad += dot_nt(pre[here, 2 * wide :], wv_ref[cols, :])
            s4.part[c, :, :, :, cols] = grad.astype(jnp.bfloat16).reshape(2, lines, rows, TILE)

        s4.step0(c)

    def feed(c):
        get_feed(c).wait()
        s3.step0(c)

    def mix(c):
        s3.finish(c, total)
        prob = prob_ref[pl.ds(pl.multiple_of(c * chunk_rows + spot * rows, rows), rows), :]
        own_mixed[c] = (input_ref[c] + prob * total[...]).astype(jnp.bfloat16)
        a3.step0(c)

    def last(c):
        s4.finish(c, total)
        grad_normed, x = total[...], x_own[c].astype(jnp.float32)
        inv_rms = lax.rsqrt(mean_last(x * x) + EPS)
        scaled = x * inv_rms
        small[0:1, :] += rows_sum(grad_normed * scaled)
        s = grad_normed * gain_ref[...]
        grad_in = resid_ref[c] + inv_rms * (s - scaled * mean_last(s * scaled))
        own_in[c] = grad_in.astype(jnp.bfloat16)
        a4.step0(c)

    share = width // blocks

    def slice_of(target, out):
        step = min(TILE, share)

        @pl.loop(0, share // step)
        def _(i):
            lanes = pl.ds(pl.multiple_of(target * share + i * step, step), step)
            out[pl.ds(pl.multiple_of(i * step, step), step), :] = dot_tn(
                normed_ref[:, lanes], pre[...]
            ).astype(jnp.bfloat16)

    def out_slice(target, out):
        lanes = pl.ds(pl.multiple_of(target * share, share), share)
        out[...] = dot_tn(heads_ref[...], branch_ref[:, lanes]).astype(jnp.bfloat16)

    weights = BlockScatter(blocks, slice_of, *rest[20:25])
    w_out = rest[25]
    out_weights = BlockScatter(blocks, out_slice, *rest[26:31])
    ranks = 2 * lines

    def small_to_blk(k):
        peer = (blk + k) % blocks
        lanes = pl.ds(pl.multiple_of(peer * share, share), share)
        return remote(
            small.at[:, lanes], small_blk.at[k - 1], sem_blk.at[0, k], sem_blk.at[1, k], (peer, tp)
        )

    def small_to_tp(k):
        return remote(
            small_part, small_tp.at[k - 1], sem_tp.at[0, k], sem_tp.at[1, k], (blk, (tp + k) % ranks)
        )

    def small_first():
        for k in range(1, blocks):
            small_to_blk(k).start()

    def small_second():
        small_part[...] = small[:, pl.ds(pl.multiple_of(blk * share, share), share)]
        for k in range(1, blocks):
            small_to_blk(k).wait()
            small_part[...] += small_blk[k - 1]
        for k in range(1, ranks):
            small_to_tp(k).start()

    def small_third():
        small_ref[...] = small_part[...]
        for k in range(1, ranks):
            small_to_tp(k).wait()
            small_ref[...] += small_tp[k - 1]

    pre_done = batches * per + 2

    @pl.loop(0, batches * per + 2 + 2 * lines + 1)
    def _(r):
        def at(offset, task):
            c = r - offset

            @pl.when((c >= 0) & (c < chunks))
            def _():
                task(c)

        def at_batch(offset, task):
            c = r - offset

            @pl.when((c >= 0) & (c < chunks) & (c % per == 0))
            def _():
                task(c // per)

        for k in range(1, lines):
            at(k, lambda c, k=k: s3.step(c, k, total_b))
        for k in range(1, lines):
            at(2 + k, lambda c, k=k: s4.step(c, k, total_b))
        for k in range(1, lines + 1):
            at(lines + k, lambda c, k=k: a3.step(c, k))
        for k in range(1, lines + 1):
            at(2 + lines + k, lambda c, k=k: a4.step(c, k))
        at(2 + lines, last)
        at(lines, mix)
        at(0, feed)
        at_batch(2, gather_kv)
        at(2, spread)
        at_batch(0, attend_back)

        pl.when(r == 0)(out_weights.all_first)
        pl.when(r == 1)(out_weights.all_second)
        pl.when(r == pre_done)(weights.all_first)
        pl.when(r == pre_done + 1)(weights.all_second)
        pl.when(r == chunks + 2 + lines)(small_first)
        pl.when(r == chunks + 3 + lines)(small_second)
        pl.when(r == chunks + 5 + lines)(small_third)

    out_weights.third(go_ref)
    weights.third(w_out)
    gq_ref[...] = w_out[:, :wide]
    gk_ref[...] = w_out[:, wide : 2 * wide]
    gv_ref[...] = w_out[:, 2 * wide :]

    @pl.loop(0, chunks)
    def _(c):
        for part in (s3, s4, a3, a4):
            part.drain(c)

    @pl.loop(jnp.maximum(batches * blk - ring, 0), batches * blk)
    def _(sent):
        to_owner(sent // blk, sent % blk).wait_send()

    weights.drain()
    out_weights.drain()


def back(tokens, keys, values, feed_part, own_input, own_resid, grad_branch, query, heads_out, normed, w_query, w_key, w_value, w_out,
         norm_gain, lse, begin, head_count, router_prob, cos_rows, sin_rows, ln_sums):
    lines, blocks = lax.axis_size("tp") // 2, lax.axis_size("blk")
    count, width = tokens.shape
    batches, key_count, wide = keys.shape
    chunk_rows = CHUNK_ROWS
    chunks, rows = count // chunk_rows, chunk_rows // (2 * lines)
    cut = CUT
    span = count // batches
    heads = wide // HD
    share = width // blocks
    any_space, vmem = pl.BlockSpec(memory_space=pl.ANY), pl.BlockSpec(memory_space=VMEM)
    bf16, f32 = jnp.bfloat16, jnp.float32
    dma = pltpu.SemaphoreType.DMA
    full = (chunks, 2, lines, rows, width)
    outs = pl.pallas_call(
        functools.partial(back_kernel, lines, blocks, batches, chunks, cut, chunk_rows),
        out_shape=[jax.ShapeDtypeStruct(full, bf16)] * 2
        + [jax.ShapeDtypeStruct((share, wide), f32)] * 3
        + [jax.ShapeDtypeStruct((wide, share), f32), jax.ShapeDtypeStruct((8, share), f32)],
        in_specs=[any_space] * 4 + [vmem] * 18,
        out_specs=[any_space] * 2 + [vmem] * 5,
        scratch_shapes=[
            VMEM((chunks, rows, width), bf16),
            VMEM((chunks, rows, width), bf16),
            VMEM((chunks, rows, width), bf16),
            VMEM((2, span, wide), bf16),
            VMEM((2, span, wide), bf16),
            VMEM((span, wide), bf16),
            VMEM((heads, span, LANE), f32),
            VMEM((span, wide), f32),
            VMEM((RING, span, 2 * wide), bf16),
            VMEM((2, span, 2 * wide), bf16),
            VMEM((2, blocks, span, 2 * wide), bf16),
            VMEM((count, 3 * wide), bf16),
            VMEM((rows, width), f32),
            VMEM((2, rows, width - cut), f32),
            VMEM((span, 2 * wide), f32),
            VMEM((8, width), f32),
            VMEM((blocks - 1, 8, share), f32),
            VMEM((8, share), f32),
            VMEM((2 * lines - 1, 8, share), f32),
            dma(()),
            dma((chunks,)),
            dma((2, 2)),
            dma((RING,)),
            dma((2, blocks)),
            pltpu.SemaphoreType.REGULAR((blocks,)),
            dma((2, blocks)),
            dma((2, 2 * lines)),
        ]
        + (Scatter.scratch(chunks, lines, rows, width, cut) + Scatter.semaphores(chunks, lines)) * 2
        + Gather.scratch(chunks, lines) * 2
        + BlockScatter.scratch(blocks, (share, 3 * wide))
        + [VMEM((share, 3 * wide), f32)]
        + BlockScatter.scratch(blocks, (wide, share)),
        compiler_params=pltpu.CompilerParams(
            collective_id=2, has_side_effects=True, vmem_limit_bytes=VMEM_LIMIT
        ),
        cost_estimate=pl.CostEstimate(
            flops=2 * count * width * wide * 7, bytes_accessed=40 * 2**20, transcendentals=0
        ),
    )(
        tokens.reshape(chunks, 2 * lines, rows, width), keys, values, feed_part, own_input, own_resid, grad_branch, query,
        heads_out, normed, w_query, w_key, w_value, w_out, norm_gain[None], lse, begin.reshape(count, 1),
        head_count.reshape(count, 1), router_prob.reshape(count, 1), cos_rows, sin_rows, ln_sums,
    )
    return outs


def seq_begin(lengths, rows):
    seq_ends = jnp.cumsum(lengths, axis=1)
    past_end = rows[None, :, None] >= seq_ends[:, None, :]
    return jnp.sum(jnp.where(past_end, lengths[:, None, :], 0), axis=2)


def turn_table(positions, dim_size):
    half_dim = dim_size // 2
    frequency = jnp.exp(jnp.arange(half_dim, dtype=jnp.float32) * (-math.log(10000.0) / half_dim))
    angles = positions.astype(jnp.float32)[..., None] * frequency
    return (jnp.cos(angles)[..., None, :], jnp.sin(angles)[..., None, :])


def rotate(values_in, cos_table, sine_table):
    half_dim = values_in.shape[-1] // 2
    first_half = values_in[..., :half_dim]
    second_half = values_in[..., half_dim:]
    return jnp.concatenate(
        [
            first_half * cos_table - second_half * sine_table,
            first_half * sine_table + second_half * cos_table,
        ],
        axis=-1,
    )


def allowed_pairs(q_rows, q_begin, k_rows):
    causal_ok = k_rows[None, None, :] <= q_rows[None, :, None]
    inside_seq = k_rows[None, None, :] >= q_begin[:, :, None]
    return (causal_ok & inside_seq)[:, None]


def local(
    tokens,
    lengths,
    head_count,
    width_index,
    router_prob,
    norm_gain,
    w_query,
    w_key,
    w_value,
    w_out,
    ln_gain,
    ln_bias,
    w_up,
    w_down,
    grad_out,
):
    batches, rows_dev, features = tokens.shape
    local_heads = w_query.shape[1] // HD
    unit_count = w_up.shape[1]
    blocks = lax.axis_size("blk")
    first_row = lax.axis_index("blk") * rows_dev
    last_row = first_row + rows_dev - 1
    local_rows = first_row + jnp.arange(rows_dev, dtype=jnp.int32)
    local_begin = seq_begin(lengths, local_rows)
    cos_table, sine_table = turn_table(local_rows[None, :] - local_begin, HD)
    score_scale = 1.0 / math.sqrt(HD)
    head_ids = lax.axis_index("tp") * local_heads + jnp.arange(local_heads, dtype=jnp.int32)
    head_mask = (head_ids[None, None, :] < head_count[:, :, None]).astype(jnp.float32)
    block_shape = (batches, rows_dev, local_heads, HD)
    inputs = tokens.astype(jnp.float32)
    inv_rms = lax.rsqrt(jnp.mean(inputs * inputs, axis=-1, keepdims=True) + EPS)
    scaled = inputs * inv_rms
    normed = (scaled * norm_gain).astype(jnp.bfloat16)

    def project(matrix):
        return jnp.einsum(
            "mtd,de->mte", normed, matrix, preferred_element_type=jnp.float32
        ).reshape(block_shape)

    query_local = rotate(project(w_query), cos_table, sine_table).astype(jnp.bfloat16)
    key_local = rotate(project(w_key), cos_table, sine_table).astype(jnp.bfloat16)
    value_local = project(w_value).astype(jnp.bfloat16)
    start_state = (
        jnp.full((batches, local_heads, rows_dev), NEG, jnp.float32),
        jnp.zeros((batches, local_heads, rows_dev), jnp.float32),
        jnp.zeros((batches, local_heads, rows_dev, HD), jnp.float32),
    )
    key_piece = lax.all_gather(key_local, "blk", axis=1, tiled=True)
    value_piece = lax.all_gather(value_local, "blk", axis=1, tiled=True)
    k_rows = jnp.arange(key_piece.shape[1], dtype=jnp.int32)

    def attend_compute_part(state_now):
        row_max, row_sum, weighted = state_now
        raw_score = jnp.einsum(
            "mqhd,mkhd->mhqk", query_local, key_piece, preferred_element_type=jnp.float32
        )
        allowed = allowed_pairs(local_rows, local_begin, k_rows)
        score = jnp.where(allowed, raw_score * score_scale, NEG)
        new_max = jnp.maximum(row_max, jnp.max(score, axis=-1))
        weights = jnp.where(allowed, jnp.exp(score - new_max[..., None]), 0.0)
        new_sum = jnp.sum(weights, axis=-1)
        new_weighted = jnp.einsum(
            "mhqk,mkhd->mhqd",
            weights.astype(jnp.bfloat16),
            value_piece,
            preferred_element_type=jnp.float32,
        )
        return (new_max, new_sum, new_weighted)

    row_max, row_sum, weighted = lax.cond(
        jnp.int32(0) > last_row, lambda state_now: state_now, attend_compute_part, start_state
    )
    logsum = row_max + jnp.log(row_sum)
    attended = jnp.transpose(weighted / row_sum[..., None], (0, 2, 1, 3)) * head_mask[..., None]
    heads_out = attended.astype(jnp.bfloat16).reshape(batches, rows_dev, local_heads * HD)
    count = batches * rows_dev
    wide = local_heads * HD
    grad_branch, feed_part, own_input, own_resid, ln_sums, grad_upw, grad_down = middle(
        tokens.reshape(count, features),
        grad_out.reshape(count, features),
        heads_out.reshape(count, wide),
        w_out,
        ln_gain,
        ln_bias,
        w_up,
        w_down,
        router_prob,
        width_index,
    )
    cos_rows = jnp.concatenate([cos_table, cos_table], axis=-1).reshape(count, HD)
    sin_rows = jnp.concatenate([-sine_table, sine_table], axis=-1).reshape(count, HD)
    mixed_out, grad_in, grad_wq, grad_wk, grad_wv, grad_outw, sums = back(
        tokens.reshape(count, features),
        key_piece.reshape(batches, -1, wide),
        value_piece.reshape(batches, -1, wide),
        feed_part,
        own_input,
        own_resid,
        grad_branch,
        query_local.reshape(count, wide),
        heads_out.reshape(count, wide),
        normed.reshape(count, features),
        w_query,
        w_key,
        w_value,
        w_out,
        norm_gain,
        jnp.transpose(logsum, (0, 2, 1)).reshape(count, local_heads),
        local_begin,
        head_count,
        router_prob,
        cos_rows,
        sin_rows,
        ln_sums,
    )
    return (
        mixed_out.reshape(tokens.shape),
        grad_in.reshape(tokens.shape),
        sums[0],
        grad_wq,
        grad_wk,
        grad_wv,
        grad_outw,
        sums[1],
        sums[2],
        grad_upw,
        grad_down,
    )


def solution(mesh):
    return jax.shard_map(
        local,
        mesh=mesh,
        in_specs=(
            P(None, "blk", None),
            P(),
            P(None, "blk"),
            P(None, "blk"),
            P(None, "blk"),
            P(),
            P(None, "tp"),
            P(None, "tp"),
            P(None, "tp"),
            P("tp", None),
            P(),
            P(),
            P(None, "tp"),
            P("tp", None),
            P(None, "blk", None),
        ),
        out_specs=(
            P(None, "blk", None),
            P(None, "blk", None),
            P("blk"),
            P("blk", "tp"),
            P("blk", "tp"),
            P("blk", "tp"),
            P("tp", "blk"),
            P("blk"),
            P("blk"),
            P("blk", "tp"),
            P("tp", "blk"),
        ),
        check_vma=False,
    )
```

```python
import functools
import math

import jax
import jax.numpy as jnp
from jax import lax
from jax.experimental import pallas as pl
from jax.experimental.pallas import tpu as pltpu
from jax.sharding import PartitionSpec as P

HD = 128
FF = 8192


EPS = 1e-05
NEG = -1e30
CHUNK_ROWS = 128
CUT = 1280
VMEM_LIMIT = 63 * 2**20
RING = 4
TILE = 512
NAMES = ("P", "A1", "A2", "A3", "B1", "B2", "B3", "F", "l1", "l2", "l3", "h0", "h1", "h2", "h3", "E", "W", "T", "K", "O", "V", "M", "Z", "Q", "X", "S")
MIDDLE_ORDER = (
    920, 921, 922, 960, 1000, 8, 961, 9, 1001, 10, 168, 169, 923, 48, 11, 209, 50, 962, 49, 208,
    170, 248, 88, 1002, 128, 210, 288, 249, 963, 90, 51, 89, 250, 12, 448, 13, 130, 129, 171, 289,
    91, 172, 328, 290, 488, 131, 1003, 211, 52, 212, 368, 53, 173, 330, 251, 528, 408, 449, 92, 329,
    450, 14, 15, 568, 213, 252, 16, 490, 93, 370, 369, 54, 132, 489, 530, 409, 291, 292, 176, 175,
    529, 55, 253, 174, 56, 410, 133, 569, 216, 94, 17, 332, 134, 451, 452, 214, 96, 570, 331, 256,
    18, 492, 491, 371, 57, 136, 293, 372, 177, 411, 296, 531, 254, 178, 58, 97, 412, 453, 571, 217,
    19, 532, 218, 572, 98, 95, 258, 257, 294, 333, 215, 138, 137, 179, 59, 135, 298, 255, 334, 373,
    493, 336, 219, 20, 259, 99, 374, 413, 454, 295, 533, 139, 297, 456, 573, 299, 414, 455, 494,
    335, 21, 375, 534, 459, 339, 415, 458, 495, 574, 22, 535, 496, 575, 23, 180, 640, 498, 220, 60,
    337, 457, 182, 181, 338, 376, 641, 379, 62, 61, 260, 538, 642, 378, 221, 100, 102, 101, 140,
    300, 222, 418, 142, 63, 261, 377, 460, 141, 262, 301, 419, 103, 497, 417, 340, 536, 499, 380,
    183, 643, 578, 143, 461, 341, 500, 223, 302, 537, 263, 416, 381, 501, 342, 303, 541, 462, 420,
    540, 539, 382, 463, 576, 502, 577, 343, 580, 616, 542, 620, 422, 581, 579, 618, 421, 619, 621,
    503, 543, 582, 617, 383, 622, 423, 583, 623, 880,
)
BACK_ORDER = (
    24, 25, 680, 64, 26, 184, 681, 185, 65, 27, 66, 186, 760, 104, 28, 224, 105, 264, 226, 225, 720,
    32, 187, 33, 145, 265, 682, 106, 144, 72, 192, 305, 304, 67, 193, 266, 721, 73, 465, 227, 464,
    112, 34, 146, 306, 113, 232, 152, 272, 345, 68, 233, 267, 107, 35, 194, 344, 188, 466, 273, 761,
    153, 505, 504, 385, 312, 234, 74, 29, 108, 346, 722, 384, 506, 147, 195, 313, 30, 544, 472, 75,
    114, 228, 545, 683, 352, 473, 546, 189, 235, 36, 148, 274, 386, 307, 229, 69, 512, 426, 115,
    424, 37, 552, 190, 196, 154, 268, 314, 467, 70, 76, 275, 513, 353, 109, 230, 392, 723, 197, 236,
    155, 354, 269, 553, 149, 38, 347, 393, 110, 270, 507, 116, 315, 309, 308, 394, 31, 584, 77, 276,
    237, 78, 474, 277, 198, 547, 156, 475, 800, 150, 624, 348, 310, 355, 39, 117, 388, 238, 118,
    157, 395, 316, 158, 515, 514, 71, 191, 554, 278, 199, 349, 231, 387, 468, 239, 79, 356, 119,
    427, 476, 428, 469, 470, 159, 435, 350, 433, 318, 434, 801, 396, 592, 510, 508, 358, 594, 317,
    111, 516, 587, 555, 279, 319, 478, 550, 593, 359, 432, 398, 271, 151, 436, 556, 357, 518, 311,
    390, 548, 351, 477, 438, 558, 425, 634, 517, 590, 471, 389, 585, 399, 509, 596, 625, 636, 557,
    430, 595, 479, 632, 598, 586, 630, 439, 391, 638, 397, 549, 626, 431, 511, 429, 597, 840, 627,
    437, 841, 637, 551, 635, 589, 842, 588, 519, 633, 629, 591, 631, 628, 559, 599, 639, 880,
)


MESH = pl.DeviceIdType.MESH
VMEM = pltpu.VMEM
LANE = 128


def remote(src, dst, send, recv, device):
    return pltpu.make_async_remote_copy(
        src_ref=src, dst_ref=dst, send_sem=send, recv_sem=recv, device_id=device, device_id_type=MESH
    )


class Place:
    def __init__(self, lines):
        blk, tp = lax.axis_index("blk"), lax.axis_index("tp")
        self.lines, self.tp = lines, tp
        self.z, self.y = tp // 2, tp % 2
        self.other = 1 - self.y
        self.across = (blk, self.z * 2 + self.other)
        self.right = (blk, jnp.minimum(self.z + 1, lines - 1) * 2 + self.y)
        self.left = (blk, jnp.maximum(self.z - 1, 0) * 2 + self.y)
        self.has_right, self.has_left = self.z < lines - 1, self.z > 0


def greet(*axes):
    place = {axis: lax.axis_index(axis) for axis in ("blk", "tp")}
    peers = 0
    for axis in axes:
        size = lax.axis_size(axis)
        for k in range(1, size):
            peer = dict(place)
            peer[axis] = (place[axis] + k) % size
            pl.semaphore_signal(
                pltpu.get_barrier_semaphore(),
                inc=1,
                device_id=(peer["blk"], peer["tp"]),
                device_id_type=MESH,
            )
        peers += size - 1
    pl.semaphore_wait(pltpu.get_barrier_semaphore(), peers)


class Scatter:
    def __init__(self, place, cut, part, across_a, line_a, line_b, across_b, send, recv):
        self.at, self.cut, self.part = place, cut, part
        self.across_a, self.line_a, self.line_b, self.across_b = across_a, line_a, line_b, across_b
        self.send, self.recv = send, recv

    @staticmethod
    def scratch(chunks, lines, rows, width, cut):
        return [
            VMEM((chunks, 2, lines, rows, width), jnp.bfloat16),
            VMEM((chunks, lines, rows, cut), jnp.bfloat16),
            VMEM((chunks, lines + 1, rows, cut), jnp.bfloat16),
            VMEM((chunks, lines + 1, 2, rows, width - cut), jnp.bfloat16),
            VMEM((chunks, rows, width - cut), jnp.bfloat16),
        ]

    @staticmethod
    def semaphores(chunks, lines):
        return [
            pltpu.SemaphoreType.DMA((chunks, 2 * lines + 2)),
            pltpu.SemaphoreType.DMA((chunks, 2 * lines + 4)),
        ]

    def low(self, c, j):
        return self.part.at[c, self.at.y, j, :, : self.cut]

    def high(self, c, j):
        return self.part.at[c, :, j, :, self.cut :]

    def copy_across_a(self, c):
        return remote(
            self.part.at[c, self.at.other, :, :, : self.cut],
            self.across_a.at[c],
            self.send.at[c, 0],
            self.recv.at[c, 0],
            self.at.across,
        )

    def copy_across_b(self, c):
        return remote(
            self.part.at[c, self.at.other, self.at.z, :, self.cut :],
            self.across_b.at[c],
            self.send.at[c, 1],
            self.recv.at[c, 1],
            self.at.across,
        )

    def copy_line(self, c, j, slot, device, first):
        lines = self.at.lines
        if first:
            source, target, send, recv = self.low(c, j), self.line_a, 2, 2
        else:
            source, target, send, recv = self.high(c, j), self.line_b, 2 + lines, 3 + lines
        return remote(
            source, target.at[c, slot], self.send.at[c, send + j], self.recv.at[c, recv + slot], device
        )

    def to_right(self, c, j, first):
        return self.copy_line(c, j, j + 1, self.at.right, first)

    def to_left(self, c, j, first):
        return self.copy_line(c, j, j, self.at.left, first)

    def take(self, c, j, slot, first):
        self.copy_line(c, j, slot, self.at.right, first).wait_recv()
        view = self.low(c, j) if first else self.high(c, j)
        came = (self.line_a if first else self.line_b)[c, slot]
        view[...] = (view[...].astype(jnp.float32) + came.astype(jnp.float32)).astype(jnp.bfloat16)

    def line_starts(self, c, first):
        lines = self.at.lines

        @pl.when(self.at.z == 0)
        def _():
            for j in range(lines - 1, 0, -1):
                self.to_right(c, j, first).start()

        @pl.when(self.at.z == lines - 1)
        def _():
            for j in range(lines - 1):
                self.to_left(c, j, first).start()

    def line_hop(self, c, step, first):
        lines = self.at.lines

        @pl.when(self.at.z == step)
        def _():
            for j in range(lines - 1, step, -1):
                self.take(c, j, j + 1, first)
                self.to_right(c, j, first).start()

        @pl.when(self.at.z == lines - 1 - step)
        def _():
            for j in range(lines - 1 - step):
                self.take(c, j, j, first)
                self.to_left(c, j, first).start()

    def line_end(self, c, total, first):
        z = self.at.z
        buffer = self.line_a if first else self.line_b

        @pl.when(self.at.has_left)
        def _():
            self.copy_line(c, z, z + 1, self.at.right, first).wait_recv()
            total[...] += buffer[c, z + 1].astype(jnp.float32)

        @pl.when(self.at.has_right)
        def _():
            self.copy_line(c, z, z, self.at.right, first).wait_recv()
            total[...] += buffer[c, z].astype(jnp.float32)

    def begin(self, c):
        self.copy_across_a(c).start()
        self.line_starts(c, False)

    def low_step(self, c, k):
        if k > 1:
            return self.line_hop(c, k - 1, True)
        self.copy_across_a(c).wait_recv()
        mine = self.part.at[c, self.at.y, :, :, : self.cut]
        mine[...] = (mine[...].astype(jnp.float32) + self.across_a[c].astype(jnp.float32)).astype(
            jnp.bfloat16
        )
        self.line_starts(c, True)

    def high_step(self, c, k, total_b):
        if k < self.at.lines - 1:
            return self.line_hop(c, k, False)
        mine = self.high(c, self.at.z)
        total_b[...] = mine[...].astype(jnp.float32)
        self.line_end(c, total_b, False)
        mine[...] = total_b[...].astype(jnp.bfloat16)
        self.copy_across_b(c).start()

    def finish(self, c, total):
        y, z = self.at.y, self.at.z
        low, high = total.at[:, : self.cut], total.at[:, self.cut :]
        low[...] = self.low(c, z)[...].astype(jnp.float32)
        self.line_end(c, low, True)
        self.copy_across_b(c).wait_recv()
        high[...] = self.part[c, y, z, :, self.cut :].astype(jnp.float32) + self.across_b[c].astype(
            jnp.float32
        )

    def drain(self, c):
        self.copy_across_a(c).wait_send()
        self.copy_across_b(c).wait_send()
        for first in (True, False):
            for j in range(self.at.lines):

                @pl.when(self.at.z != j)
                def _(j=j, first=first):
                    self.to_right(c, j, first).wait_send()


class Gather:
    def __init__(self, place, cut, own, full, local, send, recv):
        self.at, self.cut, self.own, self.full = place, cut, own, full
        self.local, self.send, self.recv = local, send, recv

    @staticmethod
    def scratch(chunks, lines):
        return [
            pltpu.SemaphoreType.DMA((chunks,)),
            pltpu.SemaphoreType.DMA((chunks, 5 * lines + 1)),
            pltpu.SemaphoreType.DMA((chunks, 3 * lines + 1)),
        ]

    def low(self, c, j):
        target = self.full.at[c, self.at.y, j, :, : self.cut]
        return target, target

    def copy_low(self, c, j, way, mine):
        lines = self.at.lines
        target = self.full.at[c, self.at.y, j, :, : self.cut]
        source = self.own(c).at[:, : self.cut] if mine else target
        device = (self.at.right, self.at.left, self.at.across)[way]
        recv = j + (lines if way == 2 else 0)
        return remote(source, target, self.send.at[c, way * lines + j], self.recv.at[c, recv], device)

    def copy_high(self, c, j, way):
        lines = self.at.lines
        view = self.full.at[c, :, j, :, self.cut :]
        device = (self.at.right, self.at.left)[way]
        return remote(
            view, view, self.send.at[c, (3 + way) * lines + j], self.recv.at[c, 2 * lines + j], device
        )

    def copy_high_across(self, c):
        lines = self.at.lines
        return remote(
            self.own(c).at[:, self.cut :],
            self.full.at[c, self.at.y, self.at.z, :, self.cut :],
            self.send.at[c, 5 * lines],
            self.recv.at[c, 3 * lines],
            self.at.across,
        )

    def copy_local(self, c):
        return pltpu.make_async_copy(
            self.own(c), self.full.at[c, self.at.y, self.at.z], self.local.at[c]
        )

    def begin(self, c):
        z = self.at.z
        if self.local is not None:
            self.copy_local(c).start()

        @pl.when(self.at.has_right)
        def _():
            self.copy_low(c, z, 0, True).start()

        @pl.when(self.at.has_left)
        def _():
            self.copy_low(c, z, 1, True).start()

        self.copy_high_across(c).start()
        self.copy_low(c, z, 2, True).start()

    def low_step(self, c, k):
        z, lines = self.at.z, self.at.lines

        @pl.when(z >= k)
        def _():
            self.copy_low(c, z - k, 0, False).wait_recv()

            @pl.when(self.at.has_right)
            def _():
                self.copy_low(c, z - k, 0, False).start()

            self.copy_low(c, z - k, 2, False).start()

        @pl.when(z + k < lines)
        def _():
            self.copy_low(c, z + k, 0, False).wait_recv()

            @pl.when(self.at.has_left)
            def _():
                self.copy_low(c, z + k, 1, False).start()

            self.copy_low(c, z + k, 2, False).start()

    def high_step(self, c, k):
        z, lines = self.at.z, self.at.lines
        if k == 0:
            if self.local is not None:
                self.copy_local(c).wait()
            self.copy_high_across(c).wait_recv()

            @pl.when(self.at.has_right)
            def _():
                self.copy_high(c, z, 0).start()

            @pl.when(self.at.has_left)
            def _():
                self.copy_high(c, z, 1).start()

            return

        @pl.when(z >= k)
        def _():
            self.copy_high(c, z - k, 0).wait_recv()

            @pl.when(self.at.has_right)
            def _():
                self.copy_high(c, z - k, 0).start()

        @pl.when(z + k < lines)
        def _():
            self.copy_high(c, z + k, 0).wait_recv()

            @pl.when(self.at.has_left)
            def _():
                self.copy_high(c, z + k, 1).start()

    def end(self, c):
        for j in range(self.at.lines):
            target = self.full.at[c, self.at.other, j, :, : self.cut]
            remote(
                target,
                target,
                self.send.at[c, 2 * self.at.lines + j],
                self.recv.at[c, self.at.lines + j],
                self.at.across,
            ).wait_recv()

    def drain(self, c):
        lines, z = self.at.lines, self.at.z
        self.copy_high_across(c).wait_send()
        for j in range(lines):

            @pl.when(self.at.has_right & (z >= j))
            def _(j=j):
                self.copy_low(c, j, 0, False).wait_send()
                self.copy_high(c, j, 0).wait_send()

            @pl.when(self.at.has_left & (z <= j))
            def _(j=j):
                self.copy_low(c, j, 1, False).wait_send()
                self.copy_high(c, j, 1).wait_send()

            self.copy_low(c, j, 2, False).wait_send()


class BlockScatter:
    def __init__(self, blocks, slice_of, part, from_core, from_chip, send, recv):
        self.blk, self.tp = lax.axis_index("blk"), lax.axis_index("tp")
        self.chips, self.chip, self.core = blocks // 2, self.blk // 2, self.blk % 2
        self.slice_of, self.part = slice_of, part
        self.from_core, self.from_chip, self.send, self.recv = from_core, from_chip, send, recv

    @staticmethod
    def scratch(blocks, shape):
        chips = blocks // 2
        return [
            VMEM((chips,) + shape, jnp.bfloat16),
            VMEM((max(chips - 1, 1),) + shape, jnp.bfloat16),
            pltpu.SemaphoreType.DMA((2, chips)),
            pltpu.SemaphoreType.DMA((2, chips)),
        ]

    def to_core(self, k):
        return remote(
            self.part(k * 2 + 1 - self.core),
            self.from_core.at[k],
            self.send.at[0, k],
            self.recv.at[0, k],
            (self.chip * 2 + 1 - self.core, self.tp),
        )

    def to_chip(self, k):
        return remote(
            self.part(k * 2 + self.core),
            self.from_chip.at[(self.chip - k + self.chips) % self.chips - 1],
            self.send.at[1, k],
            self.recv.at[1, (self.chip - k + self.chips) % self.chips],
            (k * 2 + self.core, self.tp),
        )

    def came_chip(self, i):
        k = (self.chip + i) % self.chips
        return remote(
            self.part(k * 2 + self.core),
            self.from_chip.at[i - 1],
            self.send.at[1, k],
            self.recv.at[1, i],
            (k * 2 + self.core, self.tp),
        )

    def all_first(self):
        @pl.loop(0, self.chips)
        def _(i):
            self.first(i)

    def all_second(self):
        @pl.loop(0, self.chips)
        def _(i):
            self.second(i)

    def first(self, i):
        k = (self.chip + 1 + i) % self.chips
        self.slice_of(k * 2 + 1 - self.core, self.part(k * 2 + 1 - self.core))
        self.to_core(k).start()

    def second(self, i):
        k = (self.chip + 1 + i) % self.chips
        mine = self.part(k * 2 + self.core)
        self.slice_of(k * 2 + self.core, mine)
        self.to_core(k).wait_recv()
        mine[...] = (mine[...].astype(jnp.float32) + self.from_core[k].astype(jnp.float32)).astype(
            jnp.bfloat16
        )

        @pl.when(k != self.chip)
        def _():
            self.to_chip(k).start()

    def third(self, out):
        out[...] = self.part(self.blk)[...].astype(jnp.float32)

        @pl.loop(1, self.chips)
        def _(i):
            self.came_chip(i).wait_recv()
            out[...] += self.from_chip[i - 1].astype(jnp.float32)

    def drain(self):
        @pl.loop(0, self.chips)
        def _(k):
            self.to_core(k).wait_send()

            @pl.when(k != self.chip)
            def _():
                self.to_chip(k).wait_send()


class Tasks:
    def __init__(self):
        self.by_name = {}

    def add(self, name, phase, task):
        self.by_name[name, phase] = task

    def sum_and_share(self, phase, scatter, gather, total_b, finish):
        lines = scatter.at.lines
        for k in range(1, lines):
            self.add(f"A{k}", phase, functools.partial(scatter.low_step, k=k))
            self.add(f"B{k}", phase, functools.partial(scatter.high_step, k=k, total_b=total_b))
            self.add(f"l{k}", phase, functools.partial(gather.low_step, k=k))
        self.add("F", phase, finish)
        for k in range(lines):
            self.add(f"h{k}", phase, functools.partial(gather.high_step, k=k))
        self.add("E", phase, gather.end)

    def run(self, order):
        for name, phase, c in order:
            self.by_name[name, phase](c)


def phase_rounds(phase, lines, offset):
    steps = [(offset + k, f"{half}{k}") for k in range(1, lines) for half in "AB"]
    steps += [(offset + lines, "F")]
    steps += [(offset + lines + k, f"l{k}") for k in range(1, lines)]
    steps += [(offset + lines + 1 + k, f"h{k}") for k in range(lines)]
    return [(at, name, phase) for at, name in steps]


def in_rounds(chunks, steps, extra=()):
    tasks = [(at + c, -at, name, phase, c) for at, name, phase in steps for c in range(chunks)]
    tasks += [(at, 1, name, phase, c) for at, name, phase, c in extra]
    return [task[2:] for task in sorted(tasks, key=lambda task: task[:2])]


def unpack(order):
    return [(NAMES[code // 40], code // 8 % 5, code % 8) for code in order]


def rows_sum(values):
    return jnp.sum(values, axis=0, keepdims=True)


def mean_last(values):
    return jnp.mean(values, axis=-1, keepdims=True)


def dot_nn(a, b):
    return jnp.dot(a, b, preferred_element_type=jnp.float32)


def dot_nt(a, b):
    return lax.dot_general(a, b, (((1,), (1,)), ((), ())), preferred_element_type=jnp.float32)


def dot_tn(a, b):
    return lax.dot_general(a, b, (((0,), (0,)), ((), ())), preferred_element_type=jnp.float32)


def turn(values, cos_rows, sin_rows):
    return values * cos_rows + pltpu.roll(values, HD // 2, 1) * sin_rows


def front_tasks(
    tasks, batches, blocks, lengths_ref, x_hbm, gain_ref, wq_ref, wk_ref, wv_ref, count_ref, width_ref, prob_ref,
    normed_hbm, query_ref, kv_hbm, heads_ref, ints_ref, floats_ref, cos_ref, sin_ref,
    x_mb, kv_own, kv_in, acc,
    sem_x, sem_normed, sem_own, sem_in, sem_send, sem_pass, sem_recv,
):
    blk, tp = lax.axis_index("blk"), lax.axis_index("tp")
    chips, chip, core = blocks // 2, blk // 2, blk % 2
    span, wide = x_hbm.shape[1], wq_ref.shape[1]
    heads = wide // HD
    scale = 1.0 / math.sqrt(HD)

    def slab(m):
        return pl.ds(pl.multiple_of(m * span, span), span)

    def get_x(m):
        return pltpu.make_async_copy(x_hbm.at[m], x_mb.at[m % 2], sem_x.at[m % 2])

    def put_normed(m):
        return pltpu.make_async_copy(x_mb.at[m % 2], normed_hbm.at[m], sem_normed.at[m % 2])

    def put_own(m):
        return pltpu.make_async_copy(kv_own.at[m], kv_hbm.at[m, blk], sem_own.at[m])

    def to_chip(m, k):
        return remote(
            kv_own.at[m], kv_hbm.at[m, blk], sem_send.at[m, k], sem_recv.at[m, blk], (k * 2 + core, tp)
        )

    def to_core(m):
        return remote(
            kv_own.at[m], kv_hbm.at[m, blk], sem_send.at[m, chip], sem_recv.at[m, blk], (chip * 2 + 1 - core, tp)
        )

    def pass_on(m, k):
        block = kv_hbm.at[m, k * 2 + core]
        return remote(
            block, block, sem_pass.at[m, k], sem_recv.at[m, k * 2 + core], (chip * 2 + 1 - core, tp)
        )

    def arrived(m, k):
        block = kv_hbm.at[m, k]
        return remote(block, block, sem_pass.at[m, 0], sem_recv.at[m, k], (blk, tp))

    def column(row):
        across = lax.broadcasted_iota(jnp.int32, (span, span), 1)
        down = lax.broadcasted_iota(jnp.int32, (span, span), 0)
        return jnp.sum(jnp.where(across == down, row.astype(jnp.float32), 0.0), axis=1, keepdims=True)

    def project(m):
        get_x(m).wait()
        if m + 1 < batches:
            if m >= 1:
                put_normed(m - 1).wait()
            get_x(m + 1).start()
        here = slab(m)
        x = x_mb[m % 2].astype(jnp.float32)
        scaled = x * lax.rsqrt(mean_last(x * x) + EPS)
        x_mb[m % 2] = (scaled * gain_ref[...]).astype(jnp.bfloat16)
        put_normed(m).start()
        rows = blk * span + lax.broadcasted_iota(jnp.int32, (span, 1), 0)
        begin, end = jnp.zeros((span, 1), jnp.int32), jnp.int32(0)
        for s in range(lengths_ref.shape[1]):
            length = lengths_ref[m, s]
            end = end + length
            begin = begin + jnp.where(rows >= end, length, 0)
        ints_ref[here, 0:1] = column(count_ref[m : m + 1, :]).astype(jnp.int32)
        ints_ref[here, 1:2] = column(width_ref[m : m + 1, :]).astype(jnp.int32)
        ints_ref[here, 2:3] = begin
        floats_ref[here, 0:1] = column(prob_ref[m : m + 1, :])
        lanes = lax.broadcasted_iota(jnp.int32, (1, HD), 1)
        half = HD // 2
        frequency = jnp.exp((lanes % half).astype(jnp.float32) * (-math.log(10000.0) / half))
        angles = (rows - begin).astype(jnp.float32) * frequency
        cos_rows = jnp.cos(angles)
        sin_rows = jnp.sin(angles) * jnp.where(lanes < half, -1.0, 1.0)
        cos_ref[here, :] = cos_rows
        sin_ref[here, :] = sin_rows
        normed = x_mb[m % 2]
        query, key = dot_nn(normed, wq_ref[...]), dot_nn(normed, wk_ref[...])
        for h in range(heads):
            cols = slice(h * HD, (h + 1) * HD)
            query_ref[here, cols] = turn(query[:, cols], cos_rows, sin_rows).astype(jnp.bfloat16)
            kv_own[m, :, cols] = turn(key[:, cols], cos_rows, sin_rows).astype(jnp.bfloat16)
        kv_own[m, :, wide:] = dot_nn(normed, wv_ref[...]).astype(jnp.bfloat16)
        put_own(m).start()

        @pl.loop(chip + 1, chips)
        def _(k):
            to_chip(m, k).start()

        @pl.when(core == 0)
        def _():
            to_core(m).start()

    def pass_blocks(m):
        @pl.loop(0, chip)
        def _(k):
            arrived(m, k * 2 + core).wait_recv()
            pass_on(m, k).start()

    def get_kv(m, k):
        return pltpu.make_async_copy(kv_hbm.at[m, k], kv_in.at[k], sem_in.at[k])

    def attend(m):
        here = slab(m)
        q_rows = blk * span + lax.broadcasted_iota(jnp.int32, (span, span), 0)
        begin = ints_ref[here, 2:3]

        @pl.loop(0, blk)
        def _(k):
            @pl.when(k % 2 != core)
            def _():
                arrived(m, k).wait_recv()

            get_kv(m, k).start()

        def raw_scores(k, kv):
            k_rows = k * span + lax.broadcasted_iota(jnp.int32, (span, span), 1)
            allowed = (k_rows <= q_rows) & (k_rows >= begin)
            result = []
            for h in range(heads):
                cols = slice(h * HD, (h + 1) * HD)
                raw = dot_nt(query_ref[here, cols], kv[:, cols])
                result.append(jnp.where(allowed, raw * scale, NEG))
            return result

        def highest_of(k, kv):
            return tuple(functools.reduce(jnp.maximum, lane_tiles(score)) for score in raw_scores(k, kv))

        def weigh(k, kv, tops, sums):
            result, scores = [], raw_scores(k, kv)
            for h in range(heads):
                weights = jnp.exp(scores[h] - tops[h])
                result.append(sums[h] + sum(lane_tiles(weights)))
                acc[:, h * HD : (h + 1) * HD] += dot_nn(
                    weights.astype(jnp.bfloat16), kv[:, wide + h * HD : wide + (h + 1) * HD]
                )
            return tuple(result)

        highest = highest_of(blk, kv_own.at[m])

        def first(k, highest):
            get_kv(m, k).wait()
            return tuple(map(jnp.maximum, highest, highest_of(k, kv_in.at[k])))

        highest = lax.fori_loop(0, blk, first, highest)
        tops = [jnp.max(high, axis=-1, keepdims=True) for high in highest]
        acc[...] = jnp.zeros_like(acc)
        sums = weigh(blk, kv_own.at[m], tops, (jnp.zeros((span, LANE), jnp.float32),) * heads)
        sums = lax.fori_loop(0, blk, lambda k, sums: weigh(k, kv_in.at[k], tops, sums), sums)
        for h in range(heads):
            cols = slice(h * HD, (h + 1) * HD)
            row_sum = jnp.sum(sums[h], axis=-1, keepdims=True)
            floats_ref[here, 1 + h : 2 + h] = tops[h] + jnp.log(row_sum)
            heads_ref[here, cols] = jnp.where(
                tp * heads + h < ints_ref[here, 0:1], acc[:, cols] / row_sum, 0.0
            ).astype(jnp.bfloat16)

    def end():
        for m in range(batches):
            put_own(m).wait()
            if m >= batches - 2:
                put_normed(m).wait()

            @pl.loop(chip + 1, chips)
            def _(k):
                to_chip(m, k).wait_send()

            @pl.when(core == 0)
            def _():
                to_core(m).wait_send()

            @pl.loop(0, chip)
            def _(k):
                pass_on(m, k).wait_send()

    tasks.add("Q", 0, project)
    tasks.add("X", 0, pass_blocks)
    tasks.add("S", 0, attend)
    get_x(0).start()
    return end


def lane_tiles(values):
    return [values[:, i : i + LANE] for i in range(0, values.shape[1], LANE)]


def middle_kernel(
    lines, blocks, batches, chunks, cut, chunk_rows, lengths_ref, tokens_hbm, x_hbm, grad_hbm, up_hbm, down_hbm, wo_ref,
    gain_ref, bias_ref, rms_ref, wq_ref, wk_ref, wv_ref, count_ref, width_ref, prob_ref, normed_hbm, kv_hbm, branch_hbm, feed_hbm, input_ref, resid_ref, sums_ref, grad_up_ref, grad_down_ref,
    query_ref, heads_ref, ints_ref, floats_ref, cos_ref, sin_ref,
    up_ref, down_ref, x_own, g_own, g_all, own_branch, feed_part, lifted_ref, squared_ref, hidden_ref, normal_ref, inv_own, total,
    total_b, sem_in, sem_g, sem_feed, *rest,
):
    place = Place(lines)
    y, z, tp = place.y, place.z, place.tp
    spot = y * lines + z
    rows = chunk_rows // (2 * lines)
    width = gain_ref.shape[-1]
    units = up_ref.shape[1]
    s1, s2 = Scatter(place, cut, *rest[:5], *rest[5:7]), Scatter(place, cut, *rest[:5], *rest[7:9])
    a1 = Gather(place, cut, lambda c: lifted_ref.at[c, y, z], lifted_ref, None, *rest[10:12])
    a2 = Gather(place, cut, lambda c: own_branch.at[c], branch_hbm, *rest[12:15])
    share = width // blocks

    def up_slice(target, out):
        step = min(TILE, share)

        @pl.loop(0, share // step)
        def _(i):
            lanes = pl.ds(pl.multiple_of(target * share + i * step, step), step)
            lifted = lifted_ref[:, :, :, :, lanes].reshape(chunks * chunk_rows, step)
            out[pl.ds(pl.multiple_of(i * step, step), step), :] = dot_tn(lifted, hidden_ref[...]).astype(
                jnp.bfloat16
            )

    def down_slice(target, out):
        lanes = pl.ds(pl.multiple_of(target * share, share), share)

        @pl.loop(0, units // TILE)
        def _(i):
            cols = pl.ds(pl.multiple_of(i * TILE, TILE), TILE)
            grad = g_all[:, :, :, lanes].reshape(chunks * chunk_rows, share)
            out[cols, :] = dot_tn(squared_ref[:, cols], grad).astype(jnp.bfloat16)

    grad_up = BlockScatter(
        blocks, up_slice, lambda k: up_ref.at[pl.ds(pl.multiple_of(k * share, share), share), :], *rest[15:19]
    )
    grad_down = BlockScatter(
        blocks, down_slice, lambda k: down_ref.at[:, pl.ds(pl.multiple_of(k * share, share), share)], *rest[19:23]
    )

    get_x = pltpu.make_async_copy(tokens_hbm.at[:, spot], x_own, sem_in.at[0])
    get_g = pltpu.make_async_copy(grad_hbm.at[:, spot], g_own, sem_in.at[1])
    get_up = pltpu.make_async_copy(up_hbm, up_ref, sem_in.at[2])
    get_down = pltpu.make_async_copy(down_hbm, down_ref, sem_in.at[3])
    for copy in (get_x, get_g, get_up, get_down):
        copy.start()

    def get_grad(c):
        return pltpu.make_async_copy(grad_hbm.at[c], g_all.at[c], sem_g.at[c])

    def put_feed(c):
        return pltpu.make_async_copy(feed_part.at[c % 2], feed_hbm.at[c], sem_feed.at[c])

    @pl.loop(0, chunks)
    def _(c):
        get_grad(c).start()

    greet("tp", "blk")
    get_x.wait()
    get_g.wait()
    sums_ref[...] = jnp.zeros_like(sums_ref)

    def own_rows(c):
        return pl.ds(pl.multiple_of(c * chunk_rows + spot * rows, rows), rows)

    def all_rows(c):
        return pl.ds(pl.multiple_of(c * chunk_rows, chunk_rows), chunk_rows)

    def tiled(n, body):
        @pl.loop(0, n // TILE)
        def _(i):
            body(pl.ds(pl.multiple_of(i * TILE, TILE), TILE))

    def put(part, c, cols, values):
        part[c, :, :, :, cols] = values.astype(jnp.bfloat16).reshape(2, lines, rows, TILE)

    def project(c):
        heads = heads_ref[all_rows(c), :]

        def one(cols):
            put(s1.part, c, cols, dot_nn(heads, wo_ref[:, cols]))

        tiled(width, one)
        s1.begin(c)

    def norm(c):
        s1.finish(c, total)
        residual = x_own[c].astype(jnp.float32) + total[...]
        center = residual - mean_last(residual)
        inv_std = lax.rsqrt(mean_last(center * center) + EPS)
        normal = center * inv_std
        input_ref[c] = residual
        normal_ref[c] = normal
        inv_own[c] = jnp.broadcast_to(inv_std, (rows, LANE))
        lifted_ref[c, y, z] = (normal * gain_ref[...] + bias_ref[...]).astype(jnp.bfloat16)
        a1.begin(c)

    def feed(c):
        if c == 0:
            get_up.wait()
            get_down.wait()
        a1.end(c)
        s1.drain(c)
        lifted = lifted_ref[c].reshape(chunk_rows, width)
        span = all_rows(c)
        prob, limit = floats_ref[span, 0:1], (ints_ref[span, 1:2] + 1) * (FF // 4)
        get_grad(c).wait()
        g_all[c] = (g_all[c].astype(jnp.float32) * prob.reshape(2 * lines, rows, 1)).astype(jnp.bfloat16)

        def units_of(cols):
            active = jnp.maximum(dot_nn(lifted, up_ref[:, cols]), 0.0)
            ids = tp * units + cols.start + lax.broadcasted_iota(jnp.int32, (chunk_rows, TILE), 1)
            mask = (ids < limit).astype(jnp.float32)
            squared_ref[span, cols] = (active * active * mask).astype(jnp.bfloat16)
            back = dot_nt(g_all[c].reshape(chunk_rows, width), down_ref[cols, :])
            hidden_ref[span, cols] = (back * mask * 2.0 * active).astype(jnp.bfloat16)

        tiled(units, units_of)
        hidden = hidden_ref[span, :]

        def lift(cols):
            put(s2.part, c, cols, dot_nt(hidden, up_ref[cols, :]))

        tiled(width, lift)
        s2.begin(c)
        squared = squared_ref[span, :]

        @pl.when(c >= 2)
        def _():
            put_feed(c - 2).wait()

        def out(cols):
            put(feed_part, c % 2, cols, dot_nn(squared, down_ref[:, cols]))

        tiled(width, out)
        put_feed(c).start()

    def norm_back(c):
        s2.finish(c, total)
        grad_lifted, normal = total[...], normal_ref[c]
        sums_ref[0:1, :] += rows_sum(grad_lifted * normal)
        sums_ref[1:2, :] += rows_sum(grad_lifted)
        g = grad_lifted * gain_ref[...]
        grad_resid = g_own[c].astype(jnp.float32) + inv_own[c][:, 0:1] * (
            g - mean_last(g) - normal * mean_last(g * normal)
        )
        resid_ref[c] = grad_resid
        own_branch[c] = grad_resid.astype(jnp.bfloat16)
        a2.begin(c)

    tasks = Tasks()
    front_end = front_tasks(
        tasks, batches, blocks, lengths_ref, x_hbm, rms_ref, wq_ref, wk_ref, wv_ref, count_ref, width_ref, prob_ref,
        normed_hbm, query_ref, kv_hbm, heads_ref, ints_ref, floats_ref, cos_ref, sin_ref, *rest[23:],
    )
    tasks.add("P", 1, project)
    tasks.sum_and_share(1, s1, a1, total_b, norm)
    tasks.add("P", 2, feed)
    tasks.sum_and_share(2, s2, a2, total_b, norm_back)
    steps = (grad_up.all_first, grad_down.all_first, grad_up.all_second, grad_down.all_second)
    tasks.add("W", 0, lambda k: steps[k]())
    tasks.add("Z", 0, lambda k: None)
    tasks.run(middle_order(lines, chunks, batches))
    front_end()

    grad_up.third(grad_up_ref)
    grad_down.third(grad_down_ref)
    for c in range(max(chunks - 2, 0), chunks):
        put_feed(c).wait()

    @pl.loop(0, chunks)
    def _(c):
        for part in (s2, a1, a2):
            part.drain(c)

    grad_up.drain()
    grad_down.drain()


def middle_order(lines, chunks, batches):
    if (lines, chunks, batches) == (4, 8, 4):
        return unpack(MIDDLE_ORDER)
    steps = phase_rounds(1, lines, 0) + phase_rounds(2, lines, 2 * lines)
    steps += [(0, "P", 1), (2 * lines, "P", 2), (4 * lines, "E", 2)]
    order = in_rounds(chunks, steps, [(chunks + 2 * lines + k, "W", 0, k) for k in range(4)])
    for m in range(batches):
        at = order.index(("P", 1, m * (chunks // batches)))
        order[at:at] = [(name, 0, m) for name in "QXS"]
    return order


def middle(tokens, lengths, head_count, width_index, router_prob, norm_gain, w_query, w_key, w_value, grad_out, w_out,
           ln_gain, ln_bias, w_up, w_down):
    lines, blocks = lax.axis_size("tp") // 2, lax.axis_size("blk")
    batches, span, width = tokens.shape
    count, units, wide = batches * span, w_up.shape[1], w_query.shape[1]
    heads = wide // HD
    chunk_rows = CHUNK_ROWS
    chunks, rows = count // chunk_rows, chunk_rows // (2 * lines)
    cut = CUT
    share = width // blocks
    split = (chunks, 2 * lines, rows, width)
    full = (chunks, 2, lines, rows, width)
    any_space, vmem = pl.BlockSpec(memory_space=pl.ANY), pl.BlockSpec(memory_space=VMEM)
    bf16, f32 = jnp.bfloat16, jnp.float32
    dma = pltpu.SemaphoreType.DMA
    outs = pl.pallas_call(
        functools.partial(middle_kernel, lines, blocks, batches, chunks, cut, chunk_rows),
        out_shape=[
            jax.ShapeDtypeStruct((batches, span, width), bf16),
            jax.ShapeDtypeStruct((batches, blocks, span, 2 * wide), bf16),
            jax.ShapeDtypeStruct(full, bf16),
            jax.ShapeDtypeStruct(full, bf16),
            jax.ShapeDtypeStruct((chunks, rows, width), f32),
            jax.ShapeDtypeStruct((chunks, rows, width), f32),
            jax.ShapeDtypeStruct((2, width), f32),
            jax.ShapeDtypeStruct((share, units), f32),
            jax.ShapeDtypeStruct((units, share), f32),
            jax.ShapeDtypeStruct((count, wide), bf16),
            jax.ShapeDtypeStruct((count, wide), bf16),
            jax.ShapeDtypeStruct((count, 3), jnp.int32),
            jax.ShapeDtypeStruct((count, 1 + heads), f32),
            jax.ShapeDtypeStruct((count, HD), f32),
            jax.ShapeDtypeStruct((count, HD), f32),
        ],
        in_specs=[pl.BlockSpec(memory_space=pltpu.SMEM)] + [any_space] * 5 + [vmem] * 10,
        out_specs=[any_space] * 4 + [vmem] * 11,
        scratch_shapes=[
            VMEM(w_up.shape, bf16),
            VMEM(w_down.shape, bf16),
            VMEM((chunks, rows, width), bf16),
            VMEM((chunks, rows, width), bf16),
            VMEM(split, bf16),
            VMEM((chunks, rows, width), bf16),
            VMEM((2,) + full[1:], bf16),
            VMEM(full, bf16),
            VMEM((count, units), bf16),
            VMEM((count, units), bf16),
            VMEM((chunks, rows, width), f32),
            VMEM((chunks, rows, LANE), f32),
            VMEM((rows, width), f32),
            VMEM((2, rows, width - cut), f32),
            dma((4,)),
            dma((chunks,)),
            dma((chunks,)),
        ]
        + Scatter.scratch(chunks, lines, rows, width, cut)
        + Scatter.semaphores(chunks, lines) * 2
        + Gather.scratch(chunks, lines) * 2
        + BlockScatter.scratch(blocks, (share, units))
        + BlockScatter.scratch(blocks, (units, share))
        + [
            VMEM((2, span, width), bf16),
            VMEM((batches, span, 2 * wide), bf16),
            VMEM((blocks, span, 2 * wide), bf16),
            VMEM((span, wide), f32),
            dma((2,)),
            dma((2,)),
            dma((batches,)),
            dma((blocks,)),
            dma((batches, blocks // 2)),
            dma((batches, blocks // 2)),
            dma((batches, blocks)),
        ],
        compiler_params=pltpu.CompilerParams(
            collective_id=1, has_side_effects=True, vmem_limit_bytes=VMEM_LIMIT
        ),
        cost_estimate=pl.CostEstimate(
            flops=2 * count * width * (4 * wide + 6 * units), bytes_accessed=40 * 2**20, transcendentals=0
        ),
    )(
        lengths, tokens.reshape(split), tokens, grad_out.reshape(split), w_up, w_down, w_out, ln_gain[None],
        ln_bias[None], norm_gain[None], w_query, w_key, w_value, head_count, width_index, router_prob,
    )
    return outs


def turn_back(grad, cos_rows, sin_rows):
    return grad * cos_rows - pltpu.roll(grad, HD // 2, 1) * sin_rows


def back_kernel(
    lines, blocks, batches, chunks, cut, chunk_rows, tokens_hbm, kv_hbm, feed_hbm, branch_hbm,
    normed_hbm, input_ref, resid_ref, query_ref, heads_ref, wq_ref, wk_ref, wv_ref, wo_ref, gain_ref, ints_ref,
    floats_ref, cos_ref, sin_ref, sums_ref, mixed_hbm, in_hbm, gq_ref, gk_ref, gv_ref, go_ref,
    small_ref, branch_ref, x_own, own_in, own_mixed, kv_mb, grad_mb, delta_mb, dq_mb, stage, own, came, pre, total, total_b,
    grad_w, small, small_blk, small_part, small_tp, sem_in, sem_branch, sem_feed, sem_kv, sem_send, sem_recv, sem_free, sem_blk, sem_tp,
    *rest,
):
    place = Place(lines)
    blk, tp, y, z = lax.axis_index("blk"), place.tp, place.y, place.z
    spot = y * lines + z
    rows = chunk_rows // (2 * lines)
    width = gain_ref.shape[-1]
    wide = query_ref.shape[1]
    heads = wide // HD
    span = query_ref.shape[0] // batches
    per = span // chunk_rows
    scale = 1.0 / math.sqrt(HD)
    s3, s4 = Scatter(place, cut, *rest[0:7]), Scatter(place, cut, *rest[7:14])
    a3 = Gather(place, cut, lambda c: own_mixed.at[c], mixed_hbm, *rest[14:17])
    a4 = Gather(place, cut, lambda c: own_in.at[c], in_hbm, *rest[17:20])

    get_x = pltpu.make_async_copy(tokens_hbm.at[:, spot], x_own, sem_in)
    get_x.start()

    def get_kv(step):
        source = kv_hbm.at[step // (blk + 1), step % (blk + 1)]
        return pltpu.make_async_copy(source, kv_mb.at[step % 2], sem_kv.at[step % 2])

    def get_feed(c):
        return pltpu.make_async_copy(feed_hbm.at[c], s3.part.at[c], sem_feed.at[c])

    def slab(m):
        return pl.ds(pl.multiple_of(m * span, span), span)

    ring = stage.shape[0]

    def get_branch(m):
        return pltpu.make_async_copy(branch_hbm.at[slab(m), :], branch_ref.at[slab(m), :], sem_branch.at[m])

    get_normed = pltpu.make_async_copy(normed_hbm, branch_ref, sem_branch.at[batches])
    waited = set()

    def need_branch(*which):
        for m in which:
            if m not in waited:
                waited.add(m)
                get_branch(m).wait()

    def to_owner(m, k):
        slot = (m * blk + k) % ring
        return remote(
            stage.at[slot], came.at[m % 2, blk], sem_send.at[slot], sem_recv.at[m % 2, blk], (k, tp)
        )

    def from_peer(m, k):
        return remote(stage.at[0], came.at[m % 2, k], sem_send.at[0], sem_recv.at[m % 2, k], (k, tp))

    def attend_back(m):
        need_branch(m)
        here = slab(m)
        grad = dot_nt(branch_ref[here, :], wo_ref[...]).astype(jnp.bfloat16)
        for h in range(heads):
            cols = slice(h * HD, (h + 1) * HD)
            head = tp * heads + h
            masked = jnp.where(head < ints_ref[here, 0:1], grad[:, cols].astype(jnp.float32), 0.0)
            grad_mb[:, cols] = masked.astype(jnp.bfloat16)
            delta = jnp.sum(masked * heads_ref[here, cols].astype(jnp.float32), axis=-1, keepdims=True)
            delta_mb[h] = jnp.broadcast_to(delta, (span, LANE))
        dq_mb[...] = jnp.zeros_like(dq_mb)
        q_rows = blk * span + lax.broadcasted_iota(jnp.int32, (span, span), 0)
        begin = ints_ref[here, 2:3]

        def pairs(k, out):
            step = m * (blk + 1) + k
            get_kv(step).wait()

            @pl.when(step + 1 < batches * (blk + 1))
            def _():
                get_kv(step + 1).start()

            k_rows = k * span + lax.broadcasted_iota(jnp.int32, (span, span), 1)
            allowed = (k_rows <= q_rows) & (k_rows >= begin)
            for h in range(heads):
                cols = slice(h * HD, (h + 1) * HD)
                q, g = query_ref[here, cols], grad_mb[:, cols]
                key = kv_mb[step % 2, :, cols]
                value = kv_mb[step % 2, :, wide + h * HD : wide + (h + 1) * HD]
                raw = dot_nt(q, key)
                prob = jnp.where(allowed, jnp.exp(raw * scale - floats_ref[here, 1 + h : 2 + h]), 0.0)
                grad_prob = dot_nt(g, value)
                grad_score = (prob * (grad_prob - delta_mb[h][:, 0:1]) * scale).astype(jnp.bfloat16)
                dq_mb[:, cols] += dot_nn(grad_score, key)
                out[:, cols] = dot_tn(grad_score, q).astype(jnp.bfloat16)
                out[:, wide + h * HD : wide + (h + 1) * HD] = dot_tn(prob.astype(jnp.bfloat16), g).astype(
                    jnp.bfloat16
                )

        @pl.loop(0, blk)
        def _(k):
            sent = m * blk + k

            @pl.when(sent >= ring)
            def _():
                to_owner((sent - ring) // blk, (sent - ring) % blk).wait_send()

            pairs(k, stage.at[sent % ring])

            @pl.when(m >= 2)
            def _():
                pl.semaphore_wait(sem_free.at[k], 1)

            to_owner(m, k).start()

        pairs(blk, own.at[m % 2])
        if m == batches - 1:
            get_normed.start()
        for h in range(heads):
            cols = slice(h * HD, (h + 1) * HD)
            pre[here, cols] = turn_back(dq_mb[:, cols], cos_ref[here, :], sin_ref[here, :]).astype(
                jnp.bfloat16
            )

    def gather_kv(m):
        here = slab(m)
        grad_w[...] = own[m % 2].astype(jnp.float32)

        @pl.loop(blk + 1, blocks)
        def _(k):
            from_peer(m, k).wait_recv()
            grad_w[...] += came[m % 2, k].astype(jnp.float32)

            @pl.when(m + 2 < batches)
            def _():
                pl.semaphore_signal(sem_free.at[blk], inc=1, device_id=(k, tp), device_id_type=MESH)

        for h in range(heads):
            cols = slice(h * HD, (h + 1) * HD)
            pre[here, wide + h * HD : wide + (h + 1) * HD] = turn_back(
                grad_w[:, cols], cos_ref[here, :], sin_ref[here, :]
            ).astype(jnp.bfloat16)
        pre[here, 2 * wide :] = grad_w[:, wide:].astype(jnp.bfloat16)

    def spread(c):
        here = pl.ds(pl.multiple_of(c * chunk_rows, chunk_rows), chunk_rows)

        @pl.loop(0, width // TILE)
        def _(i):
            cols = pl.ds(pl.multiple_of(i * TILE, TILE), TILE)
            grad = dot_nt(pre[here, :wide], wq_ref[cols, :])
            grad += dot_nt(pre[here, wide : 2 * wide], wk_ref[cols, :])
            grad += dot_nt(pre[here, 2 * wide :], wv_ref[cols, :])
            s4.part[c, :, :, :, cols] = grad.astype(jnp.bfloat16).reshape(2, lines, rows, TILE)

        s4.begin(c)

    def feed(c):
        get_feed(c).wait()
        s3.begin(c)

    def mix(c):
        s3.finish(c, total)
        prob = floats_ref[pl.ds(pl.multiple_of(c * chunk_rows + spot * rows, rows), rows), 0:1]
        own_mixed[c] = (input_ref[c] + prob * total[...]).astype(jnp.bfloat16)
        a3.begin(c)

    def last(c):
        s4.finish(c, total)
        grad_normed, x = total[...], x_own[c].astype(jnp.float32)
        inv_rms = lax.rsqrt(mean_last(x * x) + EPS)
        scaled = x * inv_rms
        small[0:1, :] += rows_sum(grad_normed * scaled)
        s = grad_normed * gain_ref[...]
        grad_in = resid_ref[c] + inv_rms * (s - scaled * mean_last(s * scaled))
        own_in[c] = grad_in.astype(jnp.bfloat16)
        a4.begin(c)

    share = width // blocks

    def slice_of(target, out):
        step = min(TILE, share)

        @pl.loop(0, share // step)
        def _(i):
            lanes = pl.ds(pl.multiple_of(target * share + i * step, step), step)
            out[pl.ds(pl.multiple_of(i * step, step), step), :] = dot_tn(
                branch_ref[:, lanes], pre[...]
            ).astype(jnp.bfloat16)

    def out_slice(target, out):
        lanes = pl.ds(pl.multiple_of(target * share, share), share)
        out[...] = dot_tn(heads_ref[...], branch_ref[:, lanes]).astype(jnp.bfloat16)

    part, out_part = rest[20], rest[26]
    weights = BlockScatter(blocks, slice_of, lambda k: part.at[k], *rest[21:25])
    w_out = rest[25]
    out_weights = BlockScatter(blocks, out_slice, lambda k: out_part.at[k], *rest[27:31])
    ranks = 2 * lines

    def small_to_blk(k):
        peer = (blk + k) % blocks
        lanes = pl.ds(pl.multiple_of(peer * share, share), share)
        return remote(
            small.at[:, lanes], small_blk.at[k - 1], sem_blk.at[0, k], sem_blk.at[1, k], (peer, tp)
        )

    def small_to_tp(k):
        return remote(
            small_part, small_tp.at[k - 1], sem_tp.at[0, k], sem_tp.at[1, k], (blk, (tp + k) % ranks)
        )

    def small_first():
        for k in range(1, blocks):
            small_to_blk(k).start()

    def small_second():
        small_part[...] = small[:, pl.ds(pl.multiple_of(blk * share, share), share)]
        for k in range(1, blocks):
            small_to_blk(k).wait()
            small_part[...] += small_blk[k - 1]
        for k in range(1, ranks):
            small_to_tp(k).start()

    def small_third():
        small_ref[...] = small_part[...]
        for k in range(1, ranks):
            small_to_tp(k).wait()
            small_ref[...] += small_tp[k - 1]

    for m in range(batches):
        get_branch(m).start()

    @pl.loop(0, chunks)
    def _(c):
        get_feed(c).start()

    get_kv(0).start()
    greet("tp", "blk")
    get_x.wait()
    small[...] = jnp.zeros_like(small)
    small[1:3, :] = sums_ref[...]

    tasks = Tasks()
    tasks.add("P", 3, feed)
    tasks.sum_and_share(3, s3, a3, total_b, mix)
    tasks.add("T", 0, attend_back)
    tasks.add("K", 0, gather_kv)
    tasks.add("P", 4, spread)
    tasks.sum_and_share(4, s4, a4, total_b, last)

    def out_gradient(k):
        need_branch(*range(batches))
        (out_weights.all_first, out_weights.all_second)[k]()

    def weight_gradients(k):
        if k == 0:
            get_normed.wait()
        (weights.all_first, weights.all_second)[k]()

    tasks.add("O", 0, out_gradient)
    tasks.add("V", 0, weight_gradients)
    tasks.add("M", 0, lambda k: (small_first, small_second, small_third)[k]())
    tasks.add("Z", 0, lambda k: None)
    tasks.run(back_order(lines, chunks, batches))

    out_weights.third(go_ref)
    weights.third(w_out)
    gq_ref[...] = w_out[:, :wide]
    gk_ref[...] = w_out[:, wide : 2 * wide]
    gv_ref[...] = w_out[:, 2 * wide :]

    @pl.loop(0, chunks)
    def _(c):
        for part in (s3, s4, a3, a4):
            part.drain(c)

    @pl.loop(jnp.maximum(batches * blk - ring, 0), batches * blk)
    def _(sent):
        to_owner(sent // blk, sent % blk).wait_send()

    weights.drain()
    out_weights.drain()


def back_order(lines, chunks, batches):
    if (lines, chunks, batches) == (4, 8, 4):
        return unpack(BACK_ORDER)
    per = chunks // batches
    steps = phase_rounds(3, lines, 0) + phase_rounds(4, lines, per)
    steps += [(0, "P", 3), (2 * lines, "E", 3), (per, "P", 4), (per + 2 * lines, "E", 4)]
    extra = [(k, "O", 0, k) for k in range(2)] + [(chunks + per + k, "V", 0, k) for k in range(2)]
    extra += [(chunks + per + lines + 1 + k, "M", 0, k) for k in range(3)]
    order = in_rounds(chunks, steps, extra)
    for m in range(batches):
        at = order.index(("P", 4, m * per))
        order[at:at] = [("T", 0, m), ("K", 0, m)]
    return order


def back(tokens, kv, feed_part, grad_branch, normed, own_input, own_resid, query, heads_out, w_query, w_key, w_value,
         w_out, norm_gain, ints, floats, cos_rows, sin_rows, ln_sums):
    lines, blocks = lax.axis_size("tp") // 2, lax.axis_size("blk")
    count, width = tokens.shape
    batches, wide = kv.shape[0], query.shape[1]
    chunk_rows = CHUNK_ROWS
    chunks, rows = count // chunk_rows, chunk_rows // (2 * lines)
    cut = CUT
    span = count // batches
    heads = wide // HD
    share = width // blocks
    any_space, vmem = pl.BlockSpec(memory_space=pl.ANY), pl.BlockSpec(memory_space=VMEM)
    bf16, f32 = jnp.bfloat16, jnp.float32
    dma = pltpu.SemaphoreType.DMA
    full = (chunks, 2, lines, rows, width)
    outs = pl.pallas_call(
        functools.partial(back_kernel, lines, blocks, batches, chunks, cut, chunk_rows),
        out_shape=[jax.ShapeDtypeStruct(full, bf16)] * 2
        + [jax.ShapeDtypeStruct((share, wide), f32)] * 3
        + [jax.ShapeDtypeStruct((wide, share), f32), jax.ShapeDtypeStruct((8, share), f32)],
        in_specs=[any_space] * 5 + [vmem] * 14,
        out_specs=[any_space] * 2 + [vmem] * 5,
        scratch_shapes=[
            VMEM((count, width), bf16),
            VMEM((chunks, rows, width), bf16),
            VMEM((chunks, rows, width), bf16),
            VMEM((chunks, rows, width), bf16),
            VMEM((2, span, 2 * wide), bf16),
            VMEM((span, wide), bf16),
            VMEM((heads, span, LANE), f32),
            VMEM((span, wide), f32),
            VMEM((RING, span, 2 * wide), bf16),
            VMEM((2, span, 2 * wide), bf16),
            VMEM((2, blocks, span, 2 * wide), bf16),
            VMEM((count, 3 * wide), bf16),
            VMEM((rows, width), f32),
            VMEM((2, rows, width - cut), f32),
            VMEM((span, 2 * wide), f32),
            VMEM((8, width), f32),
            VMEM((blocks - 1, 8, share), f32),
            VMEM((8, share), f32),
            VMEM((2 * lines - 1, 8, share), f32),
            dma(()),
            dma((batches + 1,)),
            dma((chunks,)),
            dma((2,)),
            dma((RING,)),
            dma((2, blocks)),
            pltpu.SemaphoreType.REGULAR((blocks,)),
            dma((2, blocks)),
            dma((2, 2 * lines)),
        ]
        + (Scatter.scratch(chunks, lines, rows, width, cut) + Scatter.semaphores(chunks, lines)) * 2
        + Gather.scratch(chunks, lines) * 2
        + [VMEM((blocks, share, 3 * wide), bf16)]
        + BlockScatter.scratch(blocks, (share, 3 * wide))
        + [VMEM((share, 3 * wide), f32)]
        + [VMEM((blocks, wide, share), bf16)]
        + BlockScatter.scratch(blocks, (wide, share)),
        compiler_params=pltpu.CompilerParams(
            collective_id=2, has_side_effects=True, vmem_limit_bytes=VMEM_LIMIT
        ),
        cost_estimate=pl.CostEstimate(
            flops=2 * count * width * wide * 7, bytes_accessed=40 * 2**20, transcendentals=0
        ),
    )(
        tokens.reshape(chunks, 2 * lines, rows, width), kv, feed_part, grad_branch, normed, own_input, own_resid, query,
        heads_out, w_query, w_key, w_value, w_out, norm_gain[None], ints, floats, cos_rows, sin_rows, ln_sums,
    )
    return outs


def local(
    tokens,
    lengths,
    head_count,
    width_index,
    router_prob,
    norm_gain,
    w_query,
    w_key,
    w_value,
    w_out,
    ln_gain,
    ln_bias,
    w_up,
    w_down,
    grad_out,
):
    batches, rows_dev, features = tokens.shape
    count = batches * rows_dev
    (
        normed, kv, grad_branch, feed_part, own_input, own_resid, ln_sums, grad_upw, grad_down, query, heads_out, ints,
        floats, cos_rows, sin_rows,
    ) = middle(
        tokens, lengths, head_count, width_index, router_prob, norm_gain, w_query, w_key, w_value,
        grad_out.reshape(count, features), w_out, ln_gain, ln_bias, w_up, w_down,
    )
    flat = tokens.reshape(count, features)
    mixed_out, grad_in, grad_wq, grad_wk, grad_wv, grad_outw, sums = back(
        flat,
        kv,
        feed_part,
        grad_branch.reshape(count, features),
        normed.reshape(count, features),
        own_input,
        own_resid,
        query,
        heads_out,
        w_query,
        w_key,
        w_value,
        w_out,
        norm_gain,
        ints,
        floats,
        cos_rows,
        sin_rows,
        ln_sums,
    )
    return (
        mixed_out.reshape(tokens.shape),
        grad_in.reshape(tokens.shape),
        sums[0],
        grad_wq,
        grad_wk,
        grad_wv,
        grad_outw,
        sums[1],
        sums[2],
        grad_upw,
        grad_down,
    )


def solution(mesh):
    return jax.shard_map(
        local,
        mesh=mesh,
        in_specs=(
            P(None, "blk", None),
            P(),
            P(None, "blk"),
            P(None, "blk"),
            P(None, "blk"),
            P(),
            P(None, "tp"),
            P(None, "tp"),
            P(None, "tp"),
            P("tp", None),
            P(),
            P(),
            P(None, "tp"),
            P("tp", None),
            P(None, "blk", None),
        ),
        out_specs=(
            P(None, "blk", None),
            P(None, "blk", None),
            P("blk"),
            P("blk", "tp"),
            P("blk", "tp"),
            P("blk", "tp"),
            P("tp", "blk"),
            P("blk"),
            P("blk"),
            P("blk", "tp"),
            P("tp", "blk"),
        ),
        check_vma=False,
    )
```

```python
import functools
import math

import jax
import jax.numpy as jnp
from jax import lax
from jax.experimental import pallas as pl
from jax.experimental.pallas import tpu as pltpu
from jax.sharding import PartitionSpec as P

HD = 128
FF = 8192


EPS = 1e-05
NEG = -1e30
CHUNK_ROWS = 128
CUT = 1408
VMEM_LIMIT = 63 * 2**20
RING = 4
TILE = 512
FEED = 2
NAMES = ("P", "A1", "A2", "A3", "B1", "B2", "B3", "F", "l1", "l2", "l3", "h0", "h1", "h2", "h3", "E", "W", "T", "K", "O", "V", "M", "Z", "Q", "X", "S")
MIDDLE_ORDER = (
    920, 921, 922, 960, 1000, 961, 8, 9, 1001, 10, 48, 168, 923, 962, 170, 169, 49, 11, 1002, 12,
    88, 208, 209, 89, 963, 13, 50, 249, 171, 1003, 172, 211, 51, 173, 128, 210, 248, 14, 129, 90,
    213, 288, 130, 212, 91, 289, 448, 251, 250, 252, 52, 131, 449, 253, 328, 329, 53, 488, 15, 174,
    368, 92, 369, 290, 214, 254, 132, 528, 93, 408, 292, 489, 133, 55, 291, 175, 529, 293, 54, 215,
    409, 568, 330, 95, 450, 569, 255, 452, 453, 332, 451, 331, 370, 333, 135, 16, 491, 94, 492, 371,
    490, 134, 176, 531, 295, 493, 56, 294, 177, 96, 571, 216, 411, 372, 410, 373, 530, 335, 57, 256,
    412, 334, 455, 413, 570, 533, 217, 97, 532, 454, 18, 374, 375, 257, 573, 495, 414, 136, 572,
    137, 494, 415, 20, 178, 534, 58, 574, 179, 296, 535, 297, 575, 22, 98, 219, 181, 640, 336, 457,
    138, 337, 456, 221, 59, 641, 218, 180, 376, 61, 496, 183, 377, 642, 536, 258, 60, 497, 101, 223,
    220, 99, 259, 537, 298, 100, 141, 63, 261, 458, 139, 299, 338, 301, 140, 498, 182, 577, 260,
    459, 461, 576, 62, 263, 538, 300, 339, 341, 378, 222, 501, 103, 643, 460, 102, 381, 262, 416,
    417, 143, 379, 303, 142, 578, 499, 541, 419, 302, 581, 421, 539, 340, 500, 380, 579, 420, 343,
    462, 418, 621, 342, 463, 618, 540, 502, 619, 382, 580, 616, 383, 422, 620, 503, 542, 617, 423,
    543, 582, 622, 583, 623, 880,
)
BACK_ORDER = (
    24, 25, 26, 680, 64, 184, 185, 27, 681, 28, 104, 760, 65, 224, 66, 225, 186, 29, 187, 265, 264,
    144, 30, 188, 226, 720, 67, 227, 105, 682, 106, 189, 304, 228, 145, 266, 32, 190, 146, 229, 107,
    305, 68, 464, 230, 306, 267, 268, 147, 192, 465, 70, 345, 33, 466, 232, 108, 307, 72, 346, 385,
    270, 761, 148, 110, 344, 505, 308, 504, 467, 721, 73, 150, 347, 310, 545, 384, 112, 272, 386,
    34, 348, 468, 544, 193, 31, 507, 113, 387, 470, 506, 152, 683, 547, 233, 508, 69, 74, 191, 312,
    269, 510, 548, 546, 273, 350, 35, 109, 231, 550, 388, 472, 114, 722, 71, 352, 149, 271, 195,
    154, 153, 426, 36, 512, 194, 235, 587, 309, 111, 390, 313, 234, 196, 75, 275, 349, 151, 392,
    723, 552, 424, 115, 585, 469, 311, 584, 432, 274, 76, 353, 236, 155, 473, 37, 509, 116, 315,
    276, 471, 393, 38, 156, 197, 389, 433, 549, 39, 513, 237, 314, 277, 553, 475, 511, 355, 198,
    316, 77, 238, 354, 351, 515, 395, 199, 592, 117, 800, 78, 589, 425, 555, 239, 79, 429, 394, 428,
    427, 430, 278, 157, 118, 593, 279, 474, 625, 391, 119, 158, 317, 586, 588, 476, 514, 431, 590,
    435, 627, 356, 551, 159, 801, 633, 357, 396, 516, 629, 595, 624, 318, 477, 319, 626, 358, 840,
    591, 556, 517, 554, 436, 359, 635, 628, 557, 632, 841, 479, 399, 397, 398, 630, 478, 596, 439,
    519, 437, 518, 597, 594, 434, 842, 631, 637, 438, 636, 559, 599, 634, 558, 639, 598, 638, 880,
)


MESH = pl.DeviceIdType.MESH
VMEM = pltpu.VMEM
LANE = 128


def remote(src, dst, send, recv, device):
    return pltpu.make_async_remote_copy(
        src_ref=src, dst_ref=dst, send_sem=send, recv_sem=recv, device_id=device, device_id_type=MESH
    )


class Place:
    def __init__(self, lines):
        blk, tp = lax.axis_index("blk"), lax.axis_index("tp")
        self.lines, self.tp = lines, tp
        self.z, self.y = tp // 2, tp % 2
        self.other = 1 - self.y
        self.across = (blk, self.z * 2 + self.other)
        self.right = (blk, jnp.minimum(self.z + 1, lines - 1) * 2 + self.y)
        self.left = (blk, jnp.maximum(self.z - 1, 0) * 2 + self.y)
        self.has_right, self.has_left = self.z < lines - 1, self.z > 0


def greet(*axes):
    place = {axis: lax.axis_index(axis) for axis in ("blk", "tp")}
    peers = 0
    for axis in axes:
        size = lax.axis_size(axis)
        for k in range(1, size):
            peer = dict(place)
            peer[axis] = (place[axis] + k) % size
            pl.semaphore_signal(
                pltpu.get_barrier_semaphore(),
                inc=1,
                device_id=(peer["blk"], peer["tp"]),
                device_id_type=MESH,
            )
        peers += size - 1
    pl.semaphore_wait(pltpu.get_barrier_semaphore(), peers)


class Scatter:
    def __init__(self, place, cut, part, across_a, line_a, line_b, across_b, send, recv):
        self.at, self.cut, self.part = place, cut, part
        self.across_a, self.line_a, self.line_b, self.across_b = across_a, line_a, line_b, across_b
        self.send, self.recv = send, recv

    @staticmethod
    def scratch(chunks, lines, rows, width, cut):
        return [
            VMEM((chunks, 2, lines, rows, width), jnp.bfloat16),
            VMEM((chunks, lines, rows, cut), jnp.bfloat16),
            VMEM((chunks, lines + 1, rows, cut), jnp.bfloat16),
            VMEM((chunks, lines + 1, 2, rows, width - cut), jnp.bfloat16),
            VMEM((chunks, rows, width - cut), jnp.bfloat16),
        ]

    @staticmethod
    def semaphores(chunks, lines):
        return [
            pltpu.SemaphoreType.DMA((chunks, 2 * lines + 2)),
            pltpu.SemaphoreType.DMA((chunks, 2 * lines + 4)),
        ]

    def low(self, c, j):
        return self.part.at[c, self.at.y, j, :, : self.cut]

    def high(self, c, j):
        return self.part.at[c, :, j, :, self.cut :]

    def copy_across_a(self, c):
        return remote(
            self.part.at[c, self.at.other, :, :, : self.cut],
            self.across_a.at[c],
            self.send.at[c, 0],
            self.recv.at[c, 0],
            self.at.across,
        )

    def copy_across_b(self, c):
        return remote(
            self.part.at[c, self.at.other, self.at.z, :, self.cut :],
            self.across_b.at[c],
            self.send.at[c, 1],
            self.recv.at[c, 1],
            self.at.across,
        )

    def copy_line(self, c, j, slot, device, first):
        lines = self.at.lines
        if first:
            source, target, send, recv = self.low(c, j), self.line_a, 2, 2
        else:
            source, target, send, recv = self.high(c, j), self.line_b, 2 + lines, 3 + lines
        return remote(
            source, target.at[c, slot], self.send.at[c, send + j], self.recv.at[c, recv + slot], device
        )

    def to_right(self, c, j, first):
        return self.copy_line(c, j, j + 1, self.at.right, first)

    def to_left(self, c, j, first):
        return self.copy_line(c, j, j, self.at.left, first)

    def take(self, c, j, slot, first):
        self.copy_line(c, j, slot, self.at.right, first).wait_recv()
        view = self.low(c, j) if first else self.high(c, j)
        came = (self.line_a if first else self.line_b)[c, slot]
        view[...] = (view[...].astype(jnp.float32) + came.astype(jnp.float32)).astype(jnp.bfloat16)

    def line_starts(self, c, first):
        lines = self.at.lines

        @pl.when(self.at.z == 0)
        def _():
            for j in range(lines - 1, 0, -1):
                self.to_right(c, j, first).start()

        @pl.when(self.at.z == lines - 1)
        def _():
            for j in range(lines - 1):
                self.to_left(c, j, first).start()

    def line_hop(self, c, step, first):
        lines = self.at.lines

        @pl.when(self.at.z == step)
        def _():
            for j in range(lines - 1, step, -1):
                self.take(c, j, j + 1, first)
                self.to_right(c, j, first).start()

        @pl.when(self.at.z == lines - 1 - step)
        def _():
            for j in range(lines - 1 - step):
                self.take(c, j, j, first)
                self.to_left(c, j, first).start()

    def line_end(self, c, total, first):
        z = self.at.z
        buffer = self.line_a if first else self.line_b

        @pl.when(self.at.has_left)
        def _():
            self.copy_line(c, z, z + 1, self.at.right, first).wait_recv()
            total[...] += buffer[c, z + 1].astype(jnp.float32)

        @pl.when(self.at.has_right)
        def _():
            self.copy_line(c, z, z, self.at.right, first).wait_recv()
            total[...] += buffer[c, z].astype(jnp.float32)

    def begin(self, c):
        self.copy_across_a(c).start()
        self.line_starts(c, False)

    def low_step(self, c, k):
        if k > 1:
            return self.line_hop(c, k - 1, True)
        self.copy_across_a(c).wait_recv()
        mine = self.part.at[c, self.at.y, :, :, : self.cut]
        mine[...] = (mine[...].astype(jnp.float32) + self.across_a[c].astype(jnp.float32)).astype(
            jnp.bfloat16
        )
        self.line_starts(c, True)

    def high_step(self, c, k, total_b):
        if k < self.at.lines - 1:
            return self.line_hop(c, k, False)
        mine = self.high(c, self.at.z)
        total_b[...] = mine[...].astype(jnp.float32)
        self.line_end(c, total_b, False)
        mine[...] = total_b[...].astype(jnp.bfloat16)
        self.copy_across_b(c).start()

    def finish(self, c, total):
        y, z = self.at.y, self.at.z
        low, high = total.at[:, : self.cut], total.at[:, self.cut :]
        low[...] = self.low(c, z)[...].astype(jnp.float32)
        self.line_end(c, low, True)
        self.copy_across_b(c).wait_recv()
        high[...] = self.part[c, y, z, :, self.cut :].astype(jnp.float32) + self.across_b[c].astype(
            jnp.float32
        )

    def drain(self, c):
        self.copy_across_a(c).wait_send()
        self.copy_across_b(c).wait_send()
        for first in (True, False):
            for j in range(self.at.lines):

                @pl.when(self.at.z != j)
                def _(j=j, first=first):
                    self.to_right(c, j, first).wait_send()


class Gather:
    def __init__(self, place, cut, own, full, local, send, recv):
        self.at, self.cut, self.own, self.full = place, cut, own, full
        self.local, self.send, self.recv = local, send, recv

    @staticmethod
    def scratch(chunks, lines):
        return [
            pltpu.SemaphoreType.DMA((chunks,)),
            pltpu.SemaphoreType.DMA((chunks, 5 * lines + 1)),
            pltpu.SemaphoreType.DMA((chunks, 3 * lines + 1)),
        ]

    def low(self, c, j):
        target = self.full.at[c, self.at.y, j, :, : self.cut]
        return target, target

    def copy_low(self, c, j, way, mine):
        lines = self.at.lines
        target = self.full.at[c, self.at.y, j, :, : self.cut]
        source = self.own(c).at[:, : self.cut] if mine else target
        device = (self.at.right, self.at.left, self.at.across)[way]
        recv = j + (lines if way == 2 else 0)
        return remote(source, target, self.send.at[c, way * lines + j], self.recv.at[c, recv], device)

    def copy_high(self, c, j, way):
        lines = self.at.lines
        view = self.full.at[c, :, j, :, self.cut :]
        device = (self.at.right, self.at.left)[way]
        return remote(
            view, view, self.send.at[c, (3 + way) * lines + j], self.recv.at[c, 2 * lines + j], device
        )

    def copy_high_across(self, c):
        lines = self.at.lines
        return remote(
            self.own(c).at[:, self.cut :],
            self.full.at[c, self.at.y, self.at.z, :, self.cut :],
            self.send.at[c, 5 * lines],
            self.recv.at[c, 3 * lines],
            self.at.across,
        )

    def copy_local(self, c):
        return pltpu.make_async_copy(
            self.own(c), self.full.at[c, self.at.y, self.at.z], self.local.at[c]
        )

    def begin(self, c):
        z = self.at.z
        if self.local is not None:
            self.copy_local(c).start()

        @pl.when(self.at.has_right)
        def _():
            self.copy_low(c, z, 0, True).start()

        @pl.when(self.at.has_left)
        def _():
            self.copy_low(c, z, 1, True).start()

        self.copy_high_across(c).start()
        self.copy_low(c, z, 2, True).start()

    def low_step(self, c, k):
        z, lines = self.at.z, self.at.lines

        @pl.when(z >= k)
        def _():
            self.copy_low(c, z - k, 0, False).wait_recv()

            @pl.when(self.at.has_right)
            def _():
                self.copy_low(c, z - k, 0, False).start()

            self.copy_low(c, z - k, 2, False).start()

        @pl.when(z + k < lines)
        def _():
            self.copy_low(c, z + k, 0, False).wait_recv()

            @pl.when(self.at.has_left)
            def _():
                self.copy_low(c, z + k, 1, False).start()

            self.copy_low(c, z + k, 2, False).start()

    def high_step(self, c, k):
        z, lines = self.at.z, self.at.lines
        if k == 0:
            if self.local is not None:
                self.copy_local(c).wait()
            self.copy_high_across(c).wait_recv()

            @pl.when(self.at.has_right)
            def _():
                self.copy_high(c, z, 0).start()

            @pl.when(self.at.has_left)
            def _():
                self.copy_high(c, z, 1).start()

            return

        @pl.when(z >= k)
        def _():
            self.copy_high(c, z - k, 0).wait_recv()

            @pl.when(self.at.has_right)
            def _():
                self.copy_high(c, z - k, 0).start()

        @pl.when(z + k < lines)
        def _():
            self.copy_high(c, z + k, 0).wait_recv()

            @pl.when(self.at.has_left)
            def _():
                self.copy_high(c, z + k, 1).start()

    def end(self, c):
        for j in range(self.at.lines):
            target = self.full.at[c, self.at.other, j, :, : self.cut]
            remote(
                target,
                target,
                self.send.at[c, 2 * self.at.lines + j],
                self.recv.at[c, self.at.lines + j],
                self.at.across,
            ).wait_recv()

    def drain(self, c):
        lines, z = self.at.lines, self.at.z
        self.copy_high_across(c).wait_send()
        for j in range(lines):

            @pl.when(self.at.has_right & (z >= j))
            def _(j=j):
                self.copy_low(c, j, 0, False).wait_send()
                self.copy_high(c, j, 0).wait_send()

            @pl.when(self.at.has_left & (z <= j))
            def _(j=j):
                self.copy_low(c, j, 1, False).wait_send()
                self.copy_high(c, j, 1).wait_send()

            self.copy_low(c, j, 2, False).wait_send()


class BlockScatter:
    def __init__(self, blocks, slice_of, part, from_core, from_chip, send, recv):
        self.blk, self.tp = lax.axis_index("blk"), lax.axis_index("tp")
        self.chips, self.chip, self.core = blocks // 2, self.blk // 2, self.blk % 2
        self.slice_of, self.part = slice_of, part
        self.from_core, self.from_chip, self.send, self.recv = from_core, from_chip, send, recv

    @staticmethod
    def scratch(blocks, shape):
        chips = blocks // 2
        return [
            VMEM((chips,) + shape, jnp.bfloat16),
            VMEM((max(chips - 1, 1),) + shape, jnp.bfloat16),
            pltpu.SemaphoreType.DMA((2, chips)),
            pltpu.SemaphoreType.DMA((2, chips)),
        ]

    def to_core(self, k):
        return remote(
            self.part(k * 2 + 1 - self.core),
            self.from_core.at[k],
            self.send.at[0, k],
            self.recv.at[0, k],
            (self.chip * 2 + 1 - self.core, self.tp),
        )

    def to_chip(self, k):
        return remote(
            self.part(k * 2 + self.core),
            self.from_chip.at[(self.chip - k + self.chips) % self.chips - 1],
            self.send.at[1, k],
            self.recv.at[1, (self.chip - k + self.chips) % self.chips],
            (k * 2 + self.core, self.tp),
        )

    def came_chip(self, i):
        k = (self.chip + i) % self.chips
        return remote(
            self.part(k * 2 + self.core),
            self.from_chip.at[i - 1],
            self.send.at[1, k],
            self.recv.at[1, i],
            (k * 2 + self.core, self.tp),
        )

    def all_first(self):
        @pl.loop(0, self.chips)
        def _(i):
            self.first(i)

    def all_second(self):
        @pl.loop(0, self.chips)
        def _(i):
            self.second(i)

    def first(self, i):
        k = (self.chip + 1 + i) % self.chips
        self.slice_of(k * 2 + 1 - self.core, self.part(k * 2 + 1 - self.core))
        self.to_core(k).start()

    def second(self, i):
        k = (self.chip + 1 + i) % self.chips
        mine = self.part(k * 2 + self.core)
        self.slice_of(k * 2 + self.core, mine)
        self.to_core(k).wait_recv()
        mine[...] = (mine[...].astype(jnp.float32) + self.from_core[k].astype(jnp.float32)).astype(
            jnp.bfloat16
        )

        @pl.when(k != self.chip)
        def _():
            self.to_chip(k).start()

    def third(self, out):
        out[...] = self.part(self.blk)[...].astype(jnp.float32)

        @pl.loop(1, self.chips)
        def _(i):
            self.came_chip(i).wait_recv()
            out[...] += self.from_chip[i - 1].astype(jnp.float32)

    def drain(self):
        @pl.loop(0, self.chips)
        def _(k):
            self.to_core(k).wait_send()

            @pl.when(k != self.chip)
            def _():
                self.to_chip(k).wait_send()


class Tasks:
    def __init__(self):
        self.by_name = {}

    def add(self, name, phase, task):
        self.by_name[name, phase] = task

    def sum_and_share(self, phase, scatter, gather, total_b, finish):
        lines = scatter.at.lines
        for k in range(1, lines):
            self.add(f"A{k}", phase, functools.partial(scatter.low_step, k=k))
            self.add(f"B{k}", phase, functools.partial(scatter.high_step, k=k, total_b=total_b))
            self.add(f"l{k}", phase, functools.partial(gather.low_step, k=k))
        self.add("F", phase, finish)
        for k in range(lines):
            self.add(f"h{k}", phase, functools.partial(gather.high_step, k=k))
        self.add("E", phase, gather.end)

    def run(self, order):
        for name, phase, c in order:
            self.by_name[name, phase](c)


def in_turn(phase, lines, chunks):
    names = [f"{half}{k}" for k in range(1, lines) for half in "AB"] + ["F"]
    names += [f"l{k}" for k in range(1, lines)] + [f"h{k}" for k in range(lines)] + ["E"]
    return [(name, phase, c) for name in names for c in range(chunks)]


def unpack(order):
    return [(NAMES[code // 40], code // 8 % 5, code % 8) for code in order]


def rows_sum(values):
    return jnp.sum(values, axis=0, keepdims=True)


def mean_last(values):
    return jnp.mean(values, axis=-1, keepdims=True)


def dot_nn(a, b):
    return jnp.dot(a, b, preferred_element_type=jnp.float32)


def dot_nt(a, b):
    return lax.dot_general(a, b, (((1,), (1,)), ((), ())), preferred_element_type=jnp.float32)


def dot_tn(a, b):
    return lax.dot_general(a, b, (((0,), (0,)), ((), ())), preferred_element_type=jnp.float32)


def turn(values, cos_rows, sin_rows):
    return values * cos_rows + pltpu.roll(values, HD // 2, 1) * sin_rows


def front_tasks(
    tasks, batches, blocks, lengths_ref, x_hbm, gain_ref, wq_ref, wk_ref, wv_ref, count_ref, width_ref, prob_ref,
    normed_hbm, query_ref, kv_hbm, heads_ref, ints_ref, floats_ref, cos_ref, sin_ref,
    x_mb, kv_own, kv_in, acc,
    sem_x, sem_normed, sem_own, sem_in, sem_send, sem_pass, sem_recv,
):
    blk, tp = lax.axis_index("blk"), lax.axis_index("tp")
    chips, chip, core = blocks // 2, blk // 2, blk % 2
    span, wide = x_hbm.shape[1], wq_ref.shape[1]
    heads = wide // HD
    scale = 1.0 / math.sqrt(HD)

    def slab(m):
        return pl.ds(pl.multiple_of(m * span, span), span)

    def get_x(m):
        return pltpu.make_async_copy(x_hbm.at[m], x_mb.at[m % 2], sem_x.at[m % 2])

    def put_normed(m):
        return pltpu.make_async_copy(x_mb.at[m % 2], normed_hbm.at[m], sem_normed.at[m % 2])

    def put_own(m):
        return pltpu.make_async_copy(kv_own.at[m], kv_hbm.at[m, blk], sem_own.at[m])

    def to_chip(m, k):
        return remote(
            kv_own.at[m], kv_hbm.at[m, blk], sem_send.at[m, k], sem_recv.at[m, blk], (k * 2 + core, tp)
        )

    def to_core(m):
        return remote(
            kv_own.at[m], kv_hbm.at[m, blk], sem_send.at[m, chip], sem_recv.at[m, blk], (chip * 2 + 1 - core, tp)
        )

    def pass_on(m, k):
        block = kv_hbm.at[m, k * 2 + core]
        return remote(
            block, block, sem_pass.at[m, k], sem_recv.at[m, k * 2 + core], (chip * 2 + 1 - core, tp)
        )

    def arrived(m, k):
        block = kv_hbm.at[m, k]
        return remote(block, block, sem_pass.at[m, 0], sem_recv.at[m, k], (blk, tp))

    def column(row):
        across = lax.broadcasted_iota(jnp.int32, (span, span), 1)
        down = lax.broadcasted_iota(jnp.int32, (span, span), 0)
        return jnp.sum(jnp.where(across == down, row.astype(jnp.float32), 0.0), axis=1, keepdims=True)

    def project(m):
        get_x(m).wait()
        if m + 1 < batches:
            if m >= 1:
                put_normed(m - 1).wait()
            get_x(m + 1).start()
        here = slab(m)
        x = x_mb[m % 2].astype(jnp.float32)
        scaled = x * lax.rsqrt(mean_last(x * x) + EPS)
        x_mb[m % 2] = (scaled * gain_ref[...]).astype(jnp.bfloat16)
        put_normed(m).start()
        rows = blk * span + lax.broadcasted_iota(jnp.int32, (span, 1), 0)
        begin, end = jnp.zeros((span, 1), jnp.int32), jnp.int32(0)
        for s in range(lengths_ref.shape[1]):
            length = lengths_ref[m, s]
            end = end + length
            begin = begin + jnp.where(rows >= end, length, 0)
        ints_ref[here, 0:1] = column(count_ref[m : m + 1, :]).astype(jnp.int32)
        ints_ref[here, 1:2] = column(width_ref[m : m + 1, :]).astype(jnp.int32)
        ints_ref[here, 2:3] = begin
        floats_ref[here, 0:1] = column(prob_ref[m : m + 1, :])
        lanes = lax.broadcasted_iota(jnp.int32, (1, HD), 1)
        half = HD // 2
        frequency = jnp.exp((lanes % half).astype(jnp.float32) * (-math.log(10000.0) / half))
        angles = (rows - begin).astype(jnp.float32) * frequency
        cos_rows = jnp.cos(angles)
        sin_rows = jnp.sin(angles) * jnp.where(lanes < half, -1.0, 1.0)
        cos_ref[here, :] = cos_rows
        sin_ref[here, :] = sin_rows
        normed = x_mb[m % 2]
        query, key = dot_nn(normed, wq_ref[...]), dot_nn(normed, wk_ref[...])
        for h in range(heads):
            cols = slice(h * HD, (h + 1) * HD)
            query_ref[here, cols] = turn(query[:, cols], cos_rows, sin_rows).astype(jnp.bfloat16)
            kv_own[m, :, cols] = turn(key[:, cols], cos_rows, sin_rows).astype(jnp.bfloat16)
        kv_own[m, :, wide:] = dot_nn(normed, wv_ref[...]).astype(jnp.bfloat16)
        put_own(m).start()

        @pl.loop(chip + 1, chips)
        def _(k):
            to_chip(m, k).start()

        @pl.when(core == 0)
        def _():
            to_core(m).start()

    def pass_blocks(m):
        @pl.loop(0, chip)
        def _(k):
            arrived(m, k * 2 + core).wait_recv()
            pass_on(m, k).start()

    def get_kv(m, k):
        return pltpu.make_async_copy(kv_hbm.at[m, k], kv_in.at[k], sem_in.at[k])

    def attend(m):
        here = slab(m)
        q_rows = blk * span + lax.broadcasted_iota(jnp.int32, (span, span), 0)
        begin = ints_ref[here, 2:3]

        @pl.loop(0, blk)
        def _(k):
            @pl.when(k % 2 != core)
            def _():
                arrived(m, k).wait_recv()

            get_kv(m, k).start()

        def raw_scores(k, kv):
            k_rows = k * span + lax.broadcasted_iota(jnp.int32, (span, span), 1)
            allowed = (k_rows <= q_rows) & (k_rows >= begin)
            result = []
            for h in range(heads):
                cols = slice(h * HD, (h + 1) * HD)
                raw = dot_nt(query_ref[here, cols], kv[:, cols])
                result.append(jnp.where(allowed, raw * scale, NEG))
            return result

        def highest_of(k, kv):
            return tuple(functools.reduce(jnp.maximum, lane_tiles(score)) for score in raw_scores(k, kv))

        def weigh(k, kv, tops, sums):
            result, scores = [], raw_scores(k, kv)
            for h in range(heads):
                weights = jnp.exp(scores[h] - tops[h])
                result.append(sums[h] + sum(lane_tiles(weights)))
                acc[:, h * HD : (h + 1) * HD] += dot_nn(
                    weights.astype(jnp.bfloat16), kv[:, wide + h * HD : wide + (h + 1) * HD]
                )
            return tuple(result)

        highest = highest_of(blk, kv_own.at[m])

        def first(k, highest):
            get_kv(m, k).wait()
            return tuple(map(jnp.maximum, highest, highest_of(k, kv_in.at[k])))

        highest = lax.fori_loop(0, blk, first, highest)
        tops = [jnp.max(high, axis=-1, keepdims=True) for high in highest]
        acc[...] = jnp.zeros_like(acc)
        sums = weigh(blk, kv_own.at[m], tops, (jnp.zeros((span, LANE), jnp.float32),) * heads)
        sums = lax.fori_loop(0, blk, lambda k, sums: weigh(k, kv_in.at[k], tops, sums), sums)
        for h in range(heads):
            cols = slice(h * HD, (h + 1) * HD)
            row_sum = jnp.sum(sums[h], axis=-1, keepdims=True)
            floats_ref[here, 1 + h : 2 + h] = tops[h] + jnp.log(row_sum)
            heads_ref[here, cols] = jnp.where(
                tp * heads + h < ints_ref[here, 0:1], acc[:, cols] / row_sum, 0.0
            ).astype(jnp.bfloat16)

    def end():
        for m in range(batches):
            put_own(m).wait()
            if m >= batches - 2:
                put_normed(m).wait()

            @pl.loop(chip + 1, chips)
            def _(k):
                to_chip(m, k).wait_send()

            @pl.when(core == 0)
            def _():
                to_core(m).wait_send()

            @pl.loop(0, chip)
            def _(k):
                pass_on(m, k).wait_send()

    tasks.add("Q", 0, project)
    tasks.add("X", 0, pass_blocks)
    tasks.add("S", 0, attend)
    get_x(0).start()
    return end


def lane_tiles(values):
    return [values[:, i : i + LANE] for i in range(0, values.shape[1], LANE)]


def middle_kernel(
    lines, blocks, batches, chunks, cut, chunk_rows, lengths_ref, tokens_hbm, x_hbm, grad_hbm, up_hbm, down_hbm, wo_ref,
    gain_ref, bias_ref, rms_ref, wq_ref, wk_ref, wv_ref, count_ref, width_ref, prob_ref, normed_hbm, kv_hbm, branch_hbm, feed_hbm, input_ref, resid_ref, sums_ref, grad_up_ref, grad_down_ref,
    query_ref, heads_ref, ints_ref, floats_ref, cos_ref, sin_ref,
    up_ref, down_ref, x_own, g_own, g_all, own_branch, feed_part, lifted_ref, squared_ref, hidden_ref, normal_ref, inv_own, total,
    total_b, sem_in, sem_g, sem_feed, *rest,
):
    place = Place(lines)
    y, z, tp = place.y, place.z, place.tp
    spot = y * lines + z
    rows = chunk_rows // (2 * lines)
    width = gain_ref.shape[-1]
    units = up_ref.shape[1]
    s1, s2 = Scatter(place, cut, *rest[:5], *rest[5:7]), Scatter(place, cut, *rest[:5], *rest[7:9])
    a1 = Gather(place, cut, lambda c: lifted_ref.at[c, y, z], lifted_ref, None, *rest[10:12])
    a2 = Gather(place, cut, lambda c: own_branch.at[c], branch_hbm, *rest[12:15])
    share = width // blocks

    def up_slice(target, out):
        step = min(TILE, share)

        @pl.loop(0, share // step)
        def _(i):
            lanes = pl.ds(pl.multiple_of(target * share + i * step, step), step)
            lifted = lifted_ref[:, :, :, :, lanes].reshape(chunks * chunk_rows, step)
            out[pl.ds(pl.multiple_of(i * step, step), step), :] = dot_tn(lifted, hidden_ref[...]).astype(
                jnp.bfloat16
            )

    def down_slice(target, out):
        lanes = pl.ds(pl.multiple_of(target * share, share), share)

        @pl.loop(0, units // TILE)
        def _(i):
            cols = pl.ds(pl.multiple_of(i * TILE, TILE), TILE)
            grad = g_all[:, :, :, lanes].reshape(chunks * chunk_rows, share)
            out[cols, :] = dot_tn(squared_ref[:, cols], grad).astype(jnp.bfloat16)

    grad_up = BlockScatter(
        blocks, up_slice, lambda k: up_ref.at[pl.ds(pl.multiple_of(k * share, share), share), :], *rest[15:19]
    )
    grad_down = BlockScatter(
        blocks, down_slice, lambda k: down_ref.at[:, pl.ds(pl.multiple_of(k * share, share), share)], *rest[19:23]
    )

    get_x = pltpu.make_async_copy(tokens_hbm.at[:, spot], x_own, sem_in.at[0])
    get_g = pltpu.make_async_copy(grad_hbm.at[:, spot], g_own, sem_in.at[1])
    get_up = pltpu.make_async_copy(up_hbm, up_ref, sem_in.at[2])
    get_down = pltpu.make_async_copy(down_hbm, down_ref, sem_in.at[3])
    for copy in (get_x, get_g, get_up, get_down):
        copy.start()

    def get_grad(c):
        return pltpu.make_async_copy(grad_hbm.at[c], g_all.at[c], sem_g.at[c])

    def put_feed(c):
        return pltpu.make_async_copy(feed_part.at[c % FEED], feed_hbm.at[c], sem_feed.at[c])

    @pl.loop(0, chunks)
    def _(c):
        get_grad(c).start()

    greet("tp", "blk")
    get_x.wait()
    get_g.wait()
    sums_ref[...] = jnp.zeros_like(sums_ref)

    def own_rows(c):
        return pl.ds(pl.multiple_of(c * chunk_rows + spot * rows, rows), rows)

    def all_rows(c):
        return pl.ds(pl.multiple_of(c * chunk_rows, chunk_rows), chunk_rows)

    def tiled(n, body):
        @pl.loop(0, n // TILE)
        def _(i):
            body(pl.ds(pl.multiple_of(i * TILE, TILE), TILE))

    def put(part, c, cols, values):
        n = values.shape[0] // chunk_rows
        part[c : c + n, :, :, :, cols] = values.astype(jnp.bfloat16).reshape(n, 2, lines, rows, TILE)

    def project(c):
        heads = heads_ref[all_rows(c), :]

        def one(cols):
            put(s1.part, c, cols, dot_nn(heads, wo_ref[:, cols]))

        tiled(width, one)
        s1.begin(c)

    def norm(c):
        s1.finish(c, total)
        residual = x_own[c].astype(jnp.float32) + total[...]
        center = residual - mean_last(residual)
        inv_std = lax.rsqrt(mean_last(center * center) + EPS)
        normal = center * inv_std
        input_ref[c] = residual
        normal_ref[c] = normal
        inv_own[c] = jnp.broadcast_to(inv_std, (rows, LANE))
        lifted_ref[c, y, z] = (normal * gain_ref[...] + bias_ref[...]).astype(jnp.bfloat16)
        a1.begin(c)

    def feed(c):
        group = range(c, c + FEED)
        if c == 0:
            get_up.wait()
            get_down.wait()
        for i in group:
            a1.end(i)
            s1.drain(i)
            get_grad(i).wait()
        size = FEED * chunk_rows
        lifted = lifted_ref[c : c + FEED].reshape(size, width)
        span = pl.ds(c * chunk_rows, size)
        prob, limit = floats_ref[span, 0:1], (ints_ref[span, 1:2] + 1) * (FF // 4)
        g_all[c : c + FEED] = (
            g_all[c : c + FEED].astype(jnp.float32) * prob.reshape(FEED, 2 * lines, rows, 1)
        ).astype(jnp.bfloat16)

        def units_of(cols):
            active = jnp.maximum(dot_nn(lifted, up_ref[:, cols]), 0.0)
            ids = tp * units + cols.start + lax.broadcasted_iota(jnp.int32, (size, TILE), 1)
            mask = (ids < limit).astype(jnp.float32)
            squared_ref[span, cols] = (active * active * mask).astype(jnp.bfloat16)
            back = dot_nt(g_all[c : c + FEED].reshape(size, width), down_ref[cols, :])
            hidden_ref[span, cols] = (back * mask * 2.0 * active).astype(jnp.bfloat16)

        tiled(units, units_of)
        hidden = hidden_ref[span, :]

        def lift(cols):
            put(s2.part, c, cols, dot_nt(hidden, up_ref[cols, :]))

        tiled(width, lift)
        for i in group:
            s2.begin(i)
        squared = squared_ref[span, :]
        if c > 0:
            for i in range(FEED):
                put_feed(c - FEED + i).wait()

        def out(cols):
            put(feed_part, 0, cols, dot_nn(squared, down_ref[:, cols]))

        tiled(width, out)
        for i in group:
            put_feed(i).start()

    def norm_back(c):
        s2.finish(c, total)
        grad_lifted, normal = total[...], normal_ref[c]
        sums_ref[0:1, :] += rows_sum(grad_lifted * normal)
        sums_ref[1:2, :] += rows_sum(grad_lifted)
        g = grad_lifted * gain_ref[...]
        grad_resid = g_own[c].astype(jnp.float32) + inv_own[c][:, 0:1] * (
            g - mean_last(g) - normal * mean_last(g * normal)
        )
        resid_ref[c] = grad_resid
        own_branch[c] = grad_resid.astype(jnp.bfloat16)
        a2.begin(c)

    tasks = Tasks()
    front_end = front_tasks(
        tasks, batches, blocks, lengths_ref, x_hbm, rms_ref, wq_ref, wk_ref, wv_ref, count_ref, width_ref, prob_ref,
        normed_hbm, query_ref, kv_hbm, heads_ref, ints_ref, floats_ref, cos_ref, sin_ref, *rest[23:],
    )
    tasks.add("P", 1, project)
    tasks.sum_and_share(1, s1, a1, total_b, norm)
    tasks.add("P", 2, feed)
    tasks.sum_and_share(2, s2, a2, total_b, norm_back)
    steps = (grad_up.all_first, grad_down.all_first, grad_up.all_second, grad_down.all_second)
    tasks.add("W", 0, lambda k: steps[k]())
    tasks.add("Z", 0, lambda k: None)
    tasks.run(middle_order(lines, chunks, batches))
    front_end()

    grad_up.third(grad_up_ref)
    grad_down.third(grad_down_ref)
    for c in range(chunks - FEED, chunks):
        put_feed(c).wait()

    @pl.loop(0, chunks)
    def _(c):
        for part in (s2, a1, a2):
            part.drain(c)

    grad_up.drain()
    grad_down.drain()


def middle_order(lines, chunks, batches):
    if (lines, chunks, batches) == (4, 8, 4):
        return unpack(MIDDLE_ORDER)
    order = [(name, 0, m) for name in "QXS" for m in range(batches)]
    order += [("P", 1, c) for c in range(chunks)] + in_turn(1, lines, chunks)[:-chunks]
    order += [("P", 2, c) for c in range(0, chunks, FEED)] + in_turn(2, lines, chunks)
    return order + [("W", 0, k) for k in range(4)]


def middle(tokens, lengths, head_count, width_index, router_prob, norm_gain, w_query, w_key, w_value, grad_out, w_out,
           ln_gain, ln_bias, w_up, w_down):
    lines, blocks = lax.axis_size("tp") // 2, lax.axis_size("blk")
    batches, span, width = tokens.shape
    count, units, wide = batches * span, w_up.shape[1], w_query.shape[1]
    heads = wide // HD
    chunk_rows = CHUNK_ROWS
    chunks, rows = count // chunk_rows, chunk_rows // (2 * lines)
    cut = CUT
    share = width // blocks
    split = (chunks, 2 * lines, rows, width)
    full = (chunks, 2, lines, rows, width)
    any_space, vmem = pl.BlockSpec(memory_space=pl.ANY), pl.BlockSpec(memory_space=VMEM)
    bf16, f32 = jnp.bfloat16, jnp.float32
    dma = pltpu.SemaphoreType.DMA
    outs = pl.pallas_call(
        functools.partial(middle_kernel, lines, blocks, batches, chunks, cut, chunk_rows),
        out_shape=[
            jax.ShapeDtypeStruct((batches, span, width), bf16),
            jax.ShapeDtypeStruct((batches, blocks, span, 2 * wide), bf16),
            jax.ShapeDtypeStruct(full, bf16),
            jax.ShapeDtypeStruct(full, bf16),
            jax.ShapeDtypeStruct((chunks, rows, width), f32),
            jax.ShapeDtypeStruct((chunks, rows, width), f32),
            jax.ShapeDtypeStruct((2, width), f32),
            jax.ShapeDtypeStruct((share, units), f32),
            jax.ShapeDtypeStruct((units, share), f32),
            jax.ShapeDtypeStruct((count, wide), bf16),
            jax.ShapeDtypeStruct((count, wide), bf16),
            jax.ShapeDtypeStruct((count, 3), jnp.int32),
            jax.ShapeDtypeStruct((count, 1 + heads), f32),
            jax.ShapeDtypeStruct((count, HD), f32),
            jax.ShapeDtypeStruct((count, HD), f32),
        ],
        in_specs=[pl.BlockSpec(memory_space=pltpu.SMEM)] + [any_space] * 5 + [vmem] * 10,
        out_specs=[any_space] * 4 + [vmem] * 11,
        scratch_shapes=[
            VMEM(w_up.shape, bf16),
            VMEM(w_down.shape, bf16),
            VMEM((chunks, rows, width), bf16),
            VMEM((chunks, rows, width), bf16),
            VMEM(split, bf16),
            VMEM((chunks, rows, width), bf16),
            VMEM((FEED,) + full[1:], bf16),
            VMEM(full, bf16),
            VMEM((count, units), bf16),
            VMEM((count, units), bf16),
            VMEM((chunks, rows, width), f32),
            VMEM((chunks, rows, LANE), f32),
            VMEM((rows, width), f32),
            VMEM((2, rows, width - cut), f32),
            dma((4,)),
            dma((chunks,)),
            dma((chunks,)),
        ]
        + Scatter.scratch(chunks, lines, rows, width, cut)
        + Scatter.semaphores(chunks, lines) * 2
        + Gather.scratch(chunks, lines) * 2
        + BlockScatter.scratch(blocks, (share, units))
        + BlockScatter.scratch(blocks, (units, share))
        + [
            VMEM((2, span, width), bf16),
            VMEM((batches, span, 2 * wide), bf16),
            VMEM((blocks, span, 2 * wide), bf16),
            VMEM((span, wide), f32),
            dma((2,)),
            dma((2,)),
            dma((batches,)),
            dma((blocks,)),
            dma((batches, blocks // 2)),
            dma((batches, blocks // 2)),
            dma((batches, blocks)),
        ],
        compiler_params=pltpu.CompilerParams(
            collective_id=1, has_side_effects=True, vmem_limit_bytes=VMEM_LIMIT
        ),
        cost_estimate=pl.CostEstimate(
            flops=2 * count * width * (4 * wide + 6 * units), bytes_accessed=40 * 2**20, transcendentals=0
        ),
    )(
        lengths, tokens.reshape(split), tokens, grad_out.reshape(split), w_up, w_down, w_out, ln_gain[None],
        ln_bias[None], norm_gain[None], w_query, w_key, w_value, head_count, width_index, router_prob,
    )
    return outs


def turn_back(grad, cos_rows, sin_rows):
    return grad * cos_rows - pltpu.roll(grad, HD // 2, 1) * sin_rows


def back_kernel(
    lines, blocks, batches, chunks, cut, chunk_rows, tokens_hbm, kv_hbm, feed_hbm, branch_hbm,
    normed_hbm, input_ref, resid_ref, query_ref, heads_ref, wq_ref, wk_ref, wv_ref, wo_ref, gain_ref, ints_ref,
    floats_ref, cos_ref, sin_ref, sums_ref, mixed_hbm, in_hbm, gq_ref, gk_ref, gv_ref, go_ref,
    small_ref, branch_ref, x_own, own_in, own_mixed, kv_mb, grad_mb, delta_mb, dq_mb, stage, own, came, pre, total, total_b,
    grad_w, small, small_blk, small_part, small_tp, sem_in, sem_branch, sem_feed, sem_kv, sem_send, sem_recv, sem_free, sem_blk, sem_tp,
    *rest,
):
    place = Place(lines)
    blk, tp, y, z = lax.axis_index("blk"), place.tp, place.y, place.z
    spot = y * lines + z
    rows = chunk_rows // (2 * lines)
    width = gain_ref.shape[-1]
    wide = query_ref.shape[1]
    heads = wide // HD
    span = query_ref.shape[0] // batches
    per = span // chunk_rows
    scale = 1.0 / math.sqrt(HD)
    s3, s4 = Scatter(place, cut, *rest[0:7]), Scatter(place, cut, *rest[7:14])
    a3 = Gather(place, cut, lambda c: own_mixed.at[c], mixed_hbm, *rest[14:17])
    a4 = Gather(place, cut, lambda c: own_in.at[c], in_hbm, *rest[17:20])

    get_x = pltpu.make_async_copy(tokens_hbm.at[:, spot], x_own, sem_in)
    get_x.start()

    def get_kv(step):
        source = kv_hbm.at[step // (blk + 1), step % (blk + 1)]
        return pltpu.make_async_copy(source, kv_mb.at[step % 2], sem_kv.at[step % 2])

    def get_feed(c):
        return pltpu.make_async_copy(feed_hbm.at[c], s3.part.at[c], sem_feed.at[c])

    def slab(m):
        return pl.ds(pl.multiple_of(m * span, span), span)

    ring = stage.shape[0]

    def get_branch(m):
        return pltpu.make_async_copy(branch_hbm.at[slab(m), :], branch_ref.at[slab(m), :], sem_branch.at[m])

    get_normed = pltpu.make_async_copy(normed_hbm, branch_ref, sem_branch.at[batches])
    waited = set()

    def need_branch(*which):
        for m in which:
            if m not in waited:
                waited.add(m)
                get_branch(m).wait()

    def to_owner(m, k):
        slot = (m * blk + k) % ring
        return remote(
            stage.at[slot], came.at[m % 2, blk], sem_send.at[slot], sem_recv.at[m % 2, blk], (k, tp)
        )

    def from_peer(m, k):
        return remote(stage.at[0], came.at[m % 2, k], sem_send.at[0], sem_recv.at[m % 2, k], (k, tp))

    def attend_back(m):
        need_branch(m)
        here = slab(m)
        grad = dot_nt(branch_ref[here, :], wo_ref[...]).astype(jnp.bfloat16)
        for h in range(heads):
            cols = slice(h * HD, (h + 1) * HD)
            head = tp * heads + h
            masked = jnp.where(head < ints_ref[here, 0:1], grad[:, cols].astype(jnp.float32), 0.0)
            grad_mb[:, cols] = masked.astype(jnp.bfloat16)
            delta = jnp.sum(masked * heads_ref[here, cols].astype(jnp.float32), axis=-1, keepdims=True)
            delta_mb[h] = jnp.broadcast_to(delta, (span, LANE))
        dq_mb[...] = jnp.zeros_like(dq_mb)
        q_rows = blk * span + lax.broadcasted_iota(jnp.int32, (span, span), 0)
        begin = ints_ref[here, 2:3]

        def pairs(k, out):
            step = m * (blk + 1) + k
            get_kv(step).wait()

            @pl.when(step + 1 < batches * (blk + 1))
            def _():
                get_kv(step + 1).start()

            k_rows = k * span + lax.broadcasted_iota(jnp.int32, (span, span), 1)
            allowed = (k_rows <= q_rows) & (k_rows >= begin)
            for h in range(heads):
                cols = slice(h * HD, (h + 1) * HD)
                q, g = query_ref[here, cols], grad_mb[:, cols]
                key = kv_mb[step % 2, :, cols]
                value = kv_mb[step % 2, :, wide + h * HD : wide + (h + 1) * HD]
                raw = dot_nt(q, key)
                prob = jnp.where(allowed, jnp.exp(raw * scale - floats_ref[here, 1 + h : 2 + h]), 0.0)
                grad_prob = dot_nt(g, value)
                grad_score = (prob * (grad_prob - delta_mb[h][:, 0:1]) * scale).astype(jnp.bfloat16)
                dq_mb[:, cols] += dot_nn(grad_score, key)
                out[:, cols] = dot_tn(grad_score, q).astype(jnp.bfloat16)
                out[:, wide + h * HD : wide + (h + 1) * HD] = dot_tn(prob.astype(jnp.bfloat16), g).astype(
                    jnp.bfloat16
                )

        @pl.loop(0, blk)
        def _(k):
            sent = m * blk + k

            @pl.when(sent >= ring)
            def _():
                to_owner((sent - ring) // blk, (sent - ring) % blk).wait_send()

            pairs(k, stage.at[sent % ring])

            @pl.when(m >= 2)
            def _():
                pl.semaphore_wait(sem_free.at[k], 1)

            to_owner(m, k).start()

        pairs(blk, own.at[m % 2])
        if m == batches - 1:
            get_normed.start()
        for h in range(heads):
            cols = slice(h * HD, (h + 1) * HD)
            pre[here, cols] = turn_back(dq_mb[:, cols], cos_ref[here, :], sin_ref[here, :]).astype(
                jnp.bfloat16
            )

    def gather_kv(m):
        here = slab(m)
        grad_w[...] = own[m % 2].astype(jnp.float32)

        @pl.loop(blk + 1, blocks)
        def _(k):
            from_peer(m, k).wait_recv()
            grad_w[...] += came[m % 2, k].astype(jnp.float32)

            @pl.when(m + 2 < batches)
            def _():
                pl.semaphore_signal(sem_free.at[blk], inc=1, device_id=(k, tp), device_id_type=MESH)

        for h in range(heads):
            cols = slice(h * HD, (h + 1) * HD)
            pre[here, wide + h * HD : wide + (h + 1) * HD] = turn_back(
                grad_w[:, cols], cos_ref[here, :], sin_ref[here, :]
            ).astype(jnp.bfloat16)
        pre[here, 2 * wide :] = grad_w[:, wide:].astype(jnp.bfloat16)

    def spread(c):
        here = pl.ds(pl.multiple_of(c * chunk_rows, chunk_rows), chunk_rows)

        @pl.loop(0, width // TILE)
        def _(i):
            cols = pl.ds(pl.multiple_of(i * TILE, TILE), TILE)
            grad = dot_nt(pre[here, :wide], wq_ref[cols, :])
            grad += dot_nt(pre[here, wide : 2 * wide], wk_ref[cols, :])
            grad += dot_nt(pre[here, 2 * wide :], wv_ref[cols, :])
            s4.part[c, :, :, :, cols] = grad.astype(jnp.bfloat16).reshape(2, lines, rows, TILE)

        s4.begin(c)

    def feed(c):
        get_feed(c).wait()
        s3.begin(c)

    def mix(c):
        s3.finish(c, total)
        prob = floats_ref[pl.ds(pl.multiple_of(c * chunk_rows + spot * rows, rows), rows), 0:1]
        own_mixed[c] = (input_ref[c] + prob * total[...]).astype(jnp.bfloat16)
        a3.begin(c)

    def last(c):
        s4.finish(c, total)
        grad_normed, x = total[...], x_own[c].astype(jnp.float32)
        inv_rms = lax.rsqrt(mean_last(x * x) + EPS)
        scaled = x * inv_rms
        small[0:1, :] += rows_sum(grad_normed * scaled)
        s = grad_normed * gain_ref[...]
        grad_in = resid_ref[c] + inv_rms * (s - scaled * mean_last(s * scaled))
        own_in[c] = grad_in.astype(jnp.bfloat16)
        a4.begin(c)

    share = width // blocks

    def slice_of(target, out):
        step = min(TILE, share)

        @pl.loop(0, share // step)
        def _(i):
            lanes = pl.ds(pl.multiple_of(target * share + i * step, step), step)
            out[pl.ds(pl.multiple_of(i * step, step), step), :] = dot_tn(
                branch_ref[:, lanes], pre[...]
            ).astype(jnp.bfloat16)

    def out_slice(target, out):
        lanes = pl.ds(pl.multiple_of(target * share, share), share)
        out[...] = dot_tn(heads_ref[...], branch_ref[:, lanes]).astype(jnp.bfloat16)

    part, out_part = rest[20], rest[26]
    weights = BlockScatter(blocks, slice_of, lambda k: part.at[k], *rest[21:25])
    w_out = rest[25]
    out_weights = BlockScatter(blocks, out_slice, lambda k: out_part.at[k], *rest[27:31])
    ranks = 2 * lines

    def small_to_blk(k):
        peer = (blk + k) % blocks
        lanes = pl.ds(pl.multiple_of(peer * share, share), share)
        return remote(
            small.at[:, lanes], small_blk.at[k - 1], sem_blk.at[0, k], sem_blk.at[1, k], (peer, tp)
        )

    def small_to_tp(k):
        return remote(
            small_part, small_tp.at[k - 1], sem_tp.at[0, k], sem_tp.at[1, k], (blk, (tp + k) % ranks)
        )

    def small_first():
        for k in range(1, blocks):
            small_to_blk(k).start()

    def small_second():
        small_part[...] = small[:, pl.ds(pl.multiple_of(blk * share, share), share)]
        for k in range(1, blocks):
            small_to_blk(k).wait()
            small_part[...] += small_blk[k - 1]
        for k in range(1, ranks):
            small_to_tp(k).start()

    def small_third():
        small_ref[...] = small_part[...]
        for k in range(1, ranks):
            small_to_tp(k).wait()
            small_ref[...] += small_tp[k - 1]

    for m in range(batches):
        get_branch(m).start()

    @pl.loop(0, chunks)
    def _(c):
        get_feed(c).start()

    get_kv(0).start()
    greet("tp", "blk")
    get_x.wait()
    small[...] = jnp.zeros_like(small)
    small[1:3, :] = sums_ref[...]

    tasks = Tasks()
    tasks.add("P", 3, feed)
    tasks.sum_and_share(3, s3, a3, total_b, mix)
    tasks.add("T", 0, attend_back)
    tasks.add("K", 0, gather_kv)
    tasks.add("P", 4, spread)
    tasks.sum_and_share(4, s4, a4, total_b, last)

    def out_gradient(k):
        need_branch(*range(batches))
        (out_weights.all_first, out_weights.all_second)[k]()

    def weight_gradients(k):
        if k == 0:
            get_normed.wait()
        (weights.all_first, weights.all_second)[k]()

    tasks.add("O", 0, out_gradient)
    tasks.add("V", 0, weight_gradients)
    tasks.add("M", 0, lambda k: (small_first, small_second, small_third)[k]())
    tasks.add("Z", 0, lambda k: None)
    tasks.run(back_order(lines, chunks, batches))

    out_weights.third(go_ref)
    weights.third(w_out)
    gq_ref[...] = w_out[:, :wide]
    gk_ref[...] = w_out[:, wide : 2 * wide]
    gv_ref[...] = w_out[:, 2 * wide :]

    @pl.loop(0, chunks)
    def _(c):
        for part in (s3, s4, a3, a4):
            part.drain(c)

    @pl.loop(jnp.maximum(batches * blk - ring, 0), batches * blk)
    def _(sent):
        to_owner(sent // blk, sent % blk).wait_send()

    weights.drain()
    out_weights.drain()


def back_order(lines, chunks, batches):
    if (lines, chunks, batches) == (4, 8, 4):
        return unpack(BACK_ORDER)
    order = [("O", 0, 0), ("O", 0, 1)] + [("P", 3, c) for c in range(chunks)] + in_turn(3, lines, chunks)
    order += [(name, 0, m) for m in range(batches) for name in "TK"]
    order += [("V", 0, 0), ("V", 0, 1)] + [("P", 4, c) for c in range(chunks)] + in_turn(4, lines, chunks)
    return order + [("M", 0, k) for k in range(3)]


def back(tokens, kv, feed_part, grad_branch, normed, own_input, own_resid, query, heads_out, w_query, w_key, w_value,
         w_out, norm_gain, ints, floats, cos_rows, sin_rows, ln_sums):
    lines, blocks = lax.axis_size("tp") // 2, lax.axis_size("blk")
    count, width = tokens.shape
    batches, wide = kv.shape[0], query.shape[1]
    chunk_rows = CHUNK_ROWS
    chunks, rows = count // chunk_rows, chunk_rows // (2 * lines)
    cut = CUT
    span = count // batches
    heads = wide // HD
    share = width // blocks
    any_space, vmem = pl.BlockSpec(memory_space=pl.ANY), pl.BlockSpec(memory_space=VMEM)
    bf16, f32 = jnp.bfloat16, jnp.float32
    dma = pltpu.SemaphoreType.DMA
    full = (chunks, 2, lines, rows, width)
    outs = pl.pallas_call(
        functools.partial(back_kernel, lines, blocks, batches, chunks, cut, chunk_rows),
        out_shape=[jax.ShapeDtypeStruct(full, bf16)] * 2
        + [jax.ShapeDtypeStruct((share, wide), f32)] * 3
        + [jax.ShapeDtypeStruct((wide, share), f32), jax.ShapeDtypeStruct((8, share), f32)],
        in_specs=[any_space] * 5 + [vmem] * 14,
        out_specs=[any_space] * 2 + [vmem] * 5,
        scratch_shapes=[
            VMEM((count, width), bf16),
            VMEM((chunks, rows, width), bf16),
            VMEM((chunks, rows, width), bf16),
            VMEM((chunks, rows, width), bf16),
            VMEM((2, span, 2 * wide), bf16),
            VMEM((span, wide), bf16),
            VMEM((heads, span, LANE), f32),
            VMEM((span, wide), f32),
            VMEM((RING, span, 2 * wide), bf16),
            VMEM((2, span, 2 * wide), bf16),
            VMEM((2, blocks, span, 2 * wide), bf16),
            VMEM((count, 3 * wide), bf16),
            VMEM((rows, width), f32),
            VMEM((2, rows, width - cut), f32),
            VMEM((span, 2 * wide), f32),
            VMEM((8, width), f32),
            VMEM((blocks - 1, 8, share), f32),
            VMEM((8, share), f32),
            VMEM((2 * lines - 1, 8, share), f32),
            dma(()),
            dma((batches + 1,)),
            dma((chunks,)),
            dma((2,)),
            dma((RING,)),
            dma((2, blocks)),
            pltpu.SemaphoreType.REGULAR((blocks,)),
            dma((2, blocks)),
            dma((2, 2 * lines)),
        ]
        + (Scatter.scratch(chunks, lines, rows, width, cut) + Scatter.semaphores(chunks, lines)) * 2
        + Gather.scratch(chunks, lines) * 2
        + [VMEM((blocks, share, 3 * wide), bf16)]
        + BlockScatter.scratch(blocks, (share, 3 * wide))
        + [VMEM((share, 3 * wide), f32)]
        + [VMEM((blocks, wide, share), bf16)]
        + BlockScatter.scratch(blocks, (wide, share)),
        compiler_params=pltpu.CompilerParams(
            collective_id=2, has_side_effects=True, vmem_limit_bytes=VMEM_LIMIT
        ),
        cost_estimate=pl.CostEstimate(
            flops=2 * count * width * wide * 7, bytes_accessed=40 * 2**20, transcendentals=0
        ),
    )(
        tokens.reshape(chunks, 2 * lines, rows, width), kv, feed_part, grad_branch, normed, own_input, own_resid, query,
        heads_out, w_query, w_key, w_value, w_out, norm_gain[None], ints, floats, cos_rows, sin_rows, ln_sums,
    )
    return outs


def local(
    tokens,
    lengths,
    head_count,
    width_index,
    router_prob,
    norm_gain,
    w_query,
    w_key,
    w_value,
    w_out,
    ln_gain,
    ln_bias,
    w_up,
    w_down,
    grad_out,
):
    batches, rows_dev, features = tokens.shape
    count = batches * rows_dev
    (
        normed, kv, grad_branch, feed_part, own_input, own_resid, ln_sums, grad_upw, grad_down, query, heads_out, ints,
        floats, cos_rows, sin_rows,
    ) = middle(
        tokens, lengths, head_count, width_index, router_prob, norm_gain, w_query, w_key, w_value,
        grad_out.reshape(count, features), w_out, ln_gain, ln_bias, w_up, w_down,
    )
    flat = tokens.reshape(count, features)
    mixed_out, grad_in, grad_wq, grad_wk, grad_wv, grad_outw, sums = back(
        flat,
        kv,
        feed_part,
        grad_branch.reshape(count, features),
        normed.reshape(count, features),
        own_input,
        own_resid,
        query,
        heads_out,
        w_query,
        w_key,
        w_value,
        w_out,
        norm_gain,
        ints,
        floats,
        cos_rows,
        sin_rows,
        ln_sums,
    )
    return (
        mixed_out.reshape(tokens.shape),
        grad_in.reshape(tokens.shape),
        sums[0],
        grad_wq,
        grad_wk,
        grad_wv,
        grad_outw,
        sums[1],
        sums[2],
        grad_upw,
        grad_down,
    )


def solution(mesh):
    return jax.shard_map(
        local,
        mesh=mesh,
        in_specs=(
            P(None, "blk", None),
            P(),
            P(None, "blk"),
            P(None, "blk"),
            P(None, "blk"),
            P(),
            P(None, "tp"),
            P(None, "tp"),
            P(None, "tp"),
            P("tp", None),
            P(),
            P(),
            P(None, "tp"),
            P("tp", None),
            P(None, "blk", None),
        ),
        out_specs=(
            P(None, "blk", None),
            P(None, "blk", None),
            P("blk"),
            P("blk", "tp"),
            P("blk", "tp"),
            P("blk", "tp"),
            P("tp", "blk"),
            P("blk"),
            P("blk"),
            P("blk", "tp"),
            P("tp", "blk"),
        ),
        check_vma=False,
    )
```

```python
import functools
import math

import jax
import jax.numpy as jnp
from jax import lax
from jax.experimental import pallas as pl
from jax.experimental.pallas import tpu as pltpu
from jax.sharding import PartitionSpec as P

HD = 128
FF = 8192


EPS = 1e-05
NEG = -1e30
CHUNK_ROWS = 128
CUT_SUM = 1408
CUT_SHARE = 1408
VMEM_LIMIT = 63 * 2**20
RING = 4
TILE = 512
FEED = 2
NAMES = ("P", "A1", "A2", "A3", "B1", "B2", "B3", "F", "l1", "l2", "l3", "h0", "h1", "h2", "h3", "E", "W", "T", "K", "O", "V", "M", "Z", "Q", "X", "S")
MIDDLE_ORDER = (
    920, 921, 922, 960, 1000, 8, 961, 9, 1001, 48, 10, 962, 168, 923, 88, 11, 208, 169, 1002, 171,
    12, 248, 49, 963, 13, 209, 128, 172, 170, 1003, 89, 288, 249, 173, 14, 129, 211, 212, 328, 51,
    448, 174, 50, 213, 252, 210, 91, 289, 251, 214, 131, 53, 488, 368, 90, 15, 449, 253, 528, 130,
    329, 93, 291, 250, 52, 133, 175, 369, 293, 215, 409, 489, 408, 54, 255, 254, 92, 331, 290, 132,
    568, 55, 333, 529, 451, 292, 94, 453, 371, 450, 373, 330, 569, 16, 370, 95, 134, 491, 490, 410,
    176, 411, 294, 135, 56, 530, 531, 295, 332, 216, 452, 96, 413, 177, 334, 256, 57, 372, 570, 454,
    493, 335, 492, 455, 571, 136, 412, 18, 374, 217, 257, 375, 414, 533, 532, 97, 415, 296, 573,
    495, 494, 572, 137, 20, 178, 535, 575, 179, 534, 297, 574, 22, 180, 219, 640, 456, 59, 58, 457,
    337, 218, 336, 181, 641, 377, 220, 376, 182, 496, 99, 642, 221, 98, 536, 61, 259, 260, 222, 183,
    261, 139, 497, 258, 138, 63, 101, 223, 299, 537, 298, 416, 459, 141, 458, 103, 301, 417, 499,
    60, 263, 339, 461, 498, 643, 143, 341, 577, 539, 100, 262, 62, 538, 579, 379, 338, 303, 501,
    102, 576, 140, 541, 300, 581, 142, 381, 421, 378, 578, 340, 460, 343, 302, 383, 463, 616, 418,
    423, 342, 462, 380, 617, 382, 420, 500, 419, 621, 502, 422, 618, 619, 503, 543, 540, 580, 583,
    542, 620, 623, 582, 622, 880,
)
BACK_ORDER = (
    24, 25, 26, 27, 680, 28, 64, 185, 184, 681, 225, 224, 186, 187, 265, 188, 66, 760, 226, 104,
    264, 266, 65, 227, 29, 720, 106, 67, 32, 30, 105, 144, 33, 189, 145, 146, 306, 228, 229, 107,
    682, 190, 147, 305, 192, 230, 304, 267, 346, 232, 466, 68, 345, 721, 465, 506, 108, 72, 344, 69,
    385, 307, 268, 505, 464, 272, 761, 112, 386, 148, 109, 546, 384, 545, 467, 269, 308, 270, 31,
    34, 149, 152, 504, 309, 312, 191, 468, 70, 347, 424, 194, 348, 544, 35, 73, 507, 352, 193, 231,
    387, 586, 349, 234, 110, 469, 508, 71, 472, 683, 388, 113, 233, 392, 547, 150, 74, 274, 722,
    584, 111, 509, 273, 310, 271, 153, 75, 114, 195, 548, 587, 426, 151, 389, 36, 588, 512, 154,
    425, 313, 470, 311, 235, 314, 115, 552, 37, 549, 353, 510, 196, 723, 471, 473, 155, 800, 236,
    275, 428, 474, 354, 76, 511, 351, 513, 38, 315, 514, 393, 427, 276, 550, 198, 77, 553, 592, 197,
    39, 117, 551, 593, 238, 355, 391, 116, 237, 78, 199, 624, 554, 801, 394, 475, 277, 156, 626,
    316, 585, 239, 594, 627, 350, 157, 278, 279, 395, 79, 515, 118, 435, 433, 555, 590, 158, 317,
    434, 429, 356, 119, 318, 477, 634, 159, 432, 476, 589, 319, 357, 390, 840, 633, 595, 517, 478,
    397, 359, 625, 430, 591, 557, 841, 518, 358, 431, 479, 632, 396, 630, 398, 597, 436, 399, 516,
    558, 519, 437, 438, 629, 631, 842, 439, 556, 596, 636, 598, 635, 638, 628, 637, 559, 599, 639,
    880,
)


MESH = pl.DeviceIdType.MESH
VMEM = pltpu.VMEM
LANE = 128


def remote(src, dst, send, recv, device):
    return pltpu.make_async_remote_copy(
        src_ref=src, dst_ref=dst, send_sem=send, recv_sem=recv, device_id=device, device_id_type=MESH
    )


class Place:
    def __init__(self, lines):
        blk, tp = lax.axis_index("blk"), lax.axis_index("tp")
        self.lines, self.tp = lines, tp
        self.z, self.y = tp // 2, tp % 2
        self.other = 1 - self.y
        self.across = (blk, self.z * 2 + self.other)
        self.right = (blk, jnp.minimum(self.z + 1, lines - 1) * 2 + self.y)
        self.left = (blk, jnp.maximum(self.z - 1, 0) * 2 + self.y)
        self.has_right, self.has_left = self.z < lines - 1, self.z > 0


def greet(*axes):
    place = {axis: lax.axis_index(axis) for axis in ("blk", "tp")}
    peers = 0
    for axis in axes:
        size = lax.axis_size(axis)
        for k in range(1, size):
            peer = dict(place)
            peer[axis] = (place[axis] + k) % size
            pl.semaphore_signal(
                pltpu.get_barrier_semaphore(),
                inc=1,
                device_id=(peer["blk"], peer["tp"]),
                device_id_type=MESH,
            )
        peers += size - 1
    pl.semaphore_wait(pltpu.get_barrier_semaphore(), peers)


class Scatter:
    def __init__(self, place, cut, part, across_a, line_a, line_b, across_b, send, recv):
        self.at, self.cut, self.part = place, cut, part
        self.across_a, self.line_a, self.line_b, self.across_b = across_a, line_a, line_b, across_b
        self.send, self.recv = send, recv

    @staticmethod
    def scratch(chunks, lines, rows, width, cut):
        return [
            VMEM((chunks, 2, lines, rows, width), jnp.bfloat16),
            VMEM((chunks, lines, rows, cut), jnp.bfloat16),
            VMEM((chunks, lines + 1, rows, cut), jnp.bfloat16),
            VMEM((chunks, lines + 1, 2, rows, width - cut), jnp.bfloat16),
            VMEM((chunks, rows, width - cut), jnp.bfloat16),
        ]

    @staticmethod
    def semaphores(chunks, lines):
        return [
            pltpu.SemaphoreType.DMA((chunks, 2 * lines + 2)),
            pltpu.SemaphoreType.DMA((chunks, 2 * lines + 4)),
        ]

    def low(self, c, j):
        return self.part.at[c, self.at.y, j, :, : self.cut]

    def high(self, c, j):
        return self.part.at[c, :, j, :, self.cut :]

    def copy_across_a(self, c):
        return remote(
            self.part.at[c, self.at.other, :, :, : self.cut],
            self.across_a.at[c],
            self.send.at[c, 0],
            self.recv.at[c, 0],
            self.at.across,
        )

    def copy_across_b(self, c):
        return remote(
            self.part.at[c, self.at.other, self.at.z, :, self.cut :],
            self.across_b.at[c],
            self.send.at[c, 1],
            self.recv.at[c, 1],
            self.at.across,
        )

    def copy_line(self, c, j, slot, device, first):
        lines = self.at.lines
        if first:
            source, target, send, recv = self.low(c, j), self.line_a, 2, 2
        else:
            source, target, send, recv = self.high(c, j), self.line_b, 2 + lines, 3 + lines
        return remote(
            source, target.at[c, slot], self.send.at[c, send + j], self.recv.at[c, recv + slot], device
        )

    def to_right(self, c, j, first):
        return self.copy_line(c, j, j + 1, self.at.right, first)

    def to_left(self, c, j, first):
        return self.copy_line(c, j, j, self.at.left, first)

    def take(self, c, j, slot, first):
        self.copy_line(c, j, slot, self.at.right, first).wait_recv()
        view = self.low(c, j) if first else self.high(c, j)
        came = (self.line_a if first else self.line_b)[c, slot]
        view[...] = (view[...].astype(jnp.float32) + came.astype(jnp.float32)).astype(jnp.bfloat16)

    def line_starts(self, c, first):
        lines = self.at.lines

        @pl.when(self.at.z == 0)
        def _():
            for j in range(lines - 1, 0, -1):
                self.to_right(c, j, first).start()

        @pl.when(self.at.z == lines - 1)
        def _():
            for j in range(lines - 1):
                self.to_left(c, j, first).start()

    def line_hop(self, c, step, first):
        lines = self.at.lines

        @pl.when(self.at.z == step)
        def _():
            for j in range(lines - 1, step, -1):
                self.take(c, j, j + 1, first)
                self.to_right(c, j, first).start()

        @pl.when(self.at.z == lines - 1 - step)
        def _():
            for j in range(lines - 1 - step):
                self.take(c, j, j, first)
                self.to_left(c, j, first).start()

    def line_end(self, c, total, first):
        z = self.at.z
        buffer = self.line_a if first else self.line_b

        @pl.when(self.at.has_left)
        def _():
            self.copy_line(c, z, z + 1, self.at.right, first).wait_recv()
            total[...] += buffer[c, z + 1].astype(jnp.float32)

        @pl.when(self.at.has_right)
        def _():
            self.copy_line(c, z, z, self.at.right, first).wait_recv()
            total[...] += buffer[c, z].astype(jnp.float32)

    def begin(self, c):
        self.copy_across_a(c).start()
        self.line_starts(c, False)

    def low_step(self, c, k):
        if k > 1:
            return self.line_hop(c, k - 1, True)
        self.copy_across_a(c).wait_recv()
        mine = self.part.at[c, self.at.y, :, :, : self.cut]
        mine[...] = (mine[...].astype(jnp.float32) + self.across_a[c].astype(jnp.float32)).astype(
            jnp.bfloat16
        )
        self.line_starts(c, True)

    def high_step(self, c, k, total_b):
        if k < self.at.lines - 1:
            return self.line_hop(c, k, False)
        mine = self.high(c, self.at.z)
        total_b[...] = mine[...].astype(jnp.float32)
        self.line_end(c, total_b, False)
        mine[...] = total_b[...].astype(jnp.bfloat16)
        self.copy_across_b(c).start()

    def finish(self, c, total):
        y, z = self.at.y, self.at.z
        low, high = total.at[:, : self.cut], total.at[:, self.cut :]
        low[...] = self.low(c, z)[...].astype(jnp.float32)
        self.line_end(c, low, True)
        self.copy_across_b(c).wait_recv()
        high[...] = self.part[c, y, z, :, self.cut :].astype(jnp.float32) + self.across_b[c].astype(
            jnp.float32
        )

    def drain(self, c):
        self.copy_across_a(c).wait_send()
        self.copy_across_b(c).wait_send()
        for first in (True, False):
            for j in range(self.at.lines):

                @pl.when(self.at.z != j)
                def _(j=j, first=first):
                    self.to_right(c, j, first).wait_send()


class Gather:
    def __init__(self, place, cut, own, full, local, send, recv):
        self.at, self.cut, self.own, self.full = place, cut, own, full
        self.local, self.send, self.recv = local, send, recv

    @staticmethod
    def scratch(chunks, lines):
        return [
            pltpu.SemaphoreType.DMA((chunks,)),
            pltpu.SemaphoreType.DMA((chunks, 5 * lines + 1)),
            pltpu.SemaphoreType.DMA((chunks, 3 * lines + 1)),
        ]

    def low(self, c, j):
        target = self.full.at[c, self.at.y, j, :, : self.cut]
        return target, target

    def copy_low(self, c, j, way, mine):
        lines = self.at.lines
        target = self.full.at[c, self.at.y, j, :, : self.cut]
        source = self.own(c).at[:, : self.cut] if mine else target
        device = (self.at.right, self.at.left, self.at.across)[way]
        recv = j + (lines if way == 2 else 0)
        return remote(source, target, self.send.at[c, way * lines + j], self.recv.at[c, recv], device)

    def copy_high(self, c, j, way):
        lines = self.at.lines
        view = self.full.at[c, :, j, :, self.cut :]
        device = (self.at.right, self.at.left)[way]
        return remote(
            view, view, self.send.at[c, (3 + way) * lines + j], self.recv.at[c, 2 * lines + j], device
        )

    def copy_high_across(self, c):
        lines = self.at.lines
        return remote(
            self.own(c).at[:, self.cut :],
            self.full.at[c, self.at.y, self.at.z, :, self.cut :],
            self.send.at[c, 5 * lines],
            self.recv.at[c, 3 * lines],
            self.at.across,
        )

    def copy_local(self, c):
        return pltpu.make_async_copy(
            self.own(c), self.full.at[c, self.at.y, self.at.z], self.local.at[c]
        )

    def begin(self, c):
        z = self.at.z
        if self.local is not None:
            self.copy_local(c).start()

        @pl.when(self.at.has_right)
        def _():
            self.copy_low(c, z, 0, True).start()

        @pl.when(self.at.has_left)
        def _():
            self.copy_low(c, z, 1, True).start()

        self.copy_high_across(c).start()
        self.copy_low(c, z, 2, True).start()

    def low_step(self, c, k):
        z, lines = self.at.z, self.at.lines

        @pl.when(z >= k)
        def _():
            self.copy_low(c, z - k, 0, False).wait_recv()

            @pl.when(self.at.has_right)
            def _():
                self.copy_low(c, z - k, 0, False).start()

            self.copy_low(c, z - k, 2, False).start()

        @pl.when(z + k < lines)
        def _():
            self.copy_low(c, z + k, 0, False).wait_recv()

            @pl.when(self.at.has_left)
            def _():
                self.copy_low(c, z + k, 1, False).start()

            self.copy_low(c, z + k, 2, False).start()

    def high_step(self, c, k):
        z, lines = self.at.z, self.at.lines
        if k == 0:
            if self.local is not None:
                self.copy_local(c).wait()
            self.copy_high_across(c).wait_recv()

            @pl.when(self.at.has_right)
            def _():
                self.copy_high(c, z, 0).start()

            @pl.when(self.at.has_left)
            def _():
                self.copy_high(c, z, 1).start()

            return

        @pl.when(z >= k)
        def _():
            self.copy_high(c, z - k, 0).wait_recv()

            @pl.when(self.at.has_right)
            def _():
                self.copy_high(c, z - k, 0).start()

        @pl.when(z + k < lines)
        def _():
            self.copy_high(c, z + k, 0).wait_recv()

            @pl.when(self.at.has_left)
            def _():
                self.copy_high(c, z + k, 1).start()

    def end(self, c):
        for j in range(self.at.lines):
            target = self.full.at[c, self.at.other, j, :, : self.cut]
            remote(
                target,
                target,
                self.send.at[c, 2 * self.at.lines + j],
                self.recv.at[c, self.at.lines + j],
                self.at.across,
            ).wait_recv()

    def drain(self, c):
        lines, z = self.at.lines, self.at.z
        self.copy_high_across(c).wait_send()
        for j in range(lines):

            @pl.when(self.at.has_right & (z >= j))
            def _(j=j):
                self.copy_low(c, j, 0, False).wait_send()
                self.copy_high(c, j, 0).wait_send()

            @pl.when(self.at.has_left & (z <= j))
            def _(j=j):
                self.copy_low(c, j, 1, False).wait_send()
                self.copy_high(c, j, 1).wait_send()

            self.copy_low(c, j, 2, False).wait_send()


class BlockScatter:
    def __init__(self, blocks, slice_of, part, own_hbm, from_chip, from_core, send, recv, sem_own):
        self.blk, self.tp = lax.axis_index("blk"), lax.axis_index("tp")
        self.chips, self.chip, self.core = blocks // 2, self.blk // 2, self.blk % 2
        self.slice_of, self.part = slice_of, part
        self.from_core, self.from_chip, self.send, self.recv = from_core, from_chip, send, recv
        self.put_own = pltpu.make_async_copy(part(self.blk), own_hbm, sem_own)

    @staticmethod
    def scratch(blocks, shape):
        chips = blocks // 2
        return [
            VMEM((chips,) + shape, jnp.bfloat16),
            pltpu.SemaphoreType.DMA((2, chips)),
            pltpu.SemaphoreType.DMA((2, chips)),
            pltpu.SemaphoreType.DMA(()),
        ]

    @staticmethod
    def outs(blocks, shape):
        return [
            jax.ShapeDtypeStruct(shape, jnp.bfloat16),
            jax.ShapeDtypeStruct((blocks // 2 - 1,) + shape, jnp.bfloat16),
        ]

    def to_core(self, k):
        return remote(
            self.part(k * 2 + 1 - self.core),
            self.from_core.at[k],
            self.send.at[0, k],
            self.recv.at[0, k],
            (self.chip * 2 + 1 - self.core, self.tp),
        )

    def to_chip(self, k):
        return remote(
            self.part(k * 2 + self.core),
            self.from_chip.at[(self.chip - k + self.chips) % self.chips - 1],
            self.send.at[1, k],
            self.recv.at[1, (self.chip - k + self.chips) % self.chips],
            (k * 2 + self.core, self.tp),
        )

    def came_chip(self, i):
        k = (self.chip + i) % self.chips
        return remote(
            self.part(k * 2 + self.core),
            self.from_chip.at[i - 1],
            self.send.at[1, k],
            self.recv.at[1, i],
            (k * 2 + self.core, self.tp),
        )

    def all_first(self):
        @pl.loop(0, self.chips)
        def _(i):
            self.first(i)

    def all_second(self):
        @pl.loop(0, self.chips)
        def _(i):
            self.second(i)

        self.put_own.start()

    def first(self, i):
        k = (self.chip + 1 + i) % self.chips
        self.slice_of(k * 2 + 1 - self.core, self.part(k * 2 + 1 - self.core))
        self.to_core(k).start()

    def second(self, i):
        k = (self.chip + 1 + i) % self.chips
        mine = self.part(k * 2 + self.core)
        self.slice_of(k * 2 + self.core, mine)
        self.to_core(k).wait_recv()
        mine[...] = (mine[...].astype(jnp.float32) + self.from_core[k].astype(jnp.float32)).astype(
            jnp.bfloat16
        )

        @pl.when(k != self.chip)
        def _():
            self.to_chip(k).start()

    def end(self):
        @pl.loop(1, self.chips)
        def _(i):
            self.came_chip(i).wait_recv()

        self.put_own.wait()
        self.drain()

    def drain(self):
        @pl.loop(0, self.chips)
        def _(k):
            self.to_core(k).wait_send()

            @pl.when(k != self.chip)
            def _():
                self.to_chip(k).wait_send()


class Loads:
    def __init__(self, sems, pairs):
        self.copies = [
            pltpu.make_async_copy(source, target, sems.at[i]) for i, (source, target) in enumerate(pairs)
        ]
        self.waited = set()
        for copy in self.copies:
            copy.start()

    def need(self, *which):
        for i in which:
            if i not in self.waited:
                self.waited.add(i)
                self.copies[i].wait()


class Tasks:
    def __init__(self):
        self.by_name = {}

    def add(self, name, phase, task):
        self.by_name[name, phase] = task

    def sum_and_share(self, phase, scatter, gather, total_b, finish):
        lines = scatter.at.lines
        for k in range(1, lines):
            self.add(f"A{k}", phase, functools.partial(scatter.low_step, k=k))
            self.add(f"B{k}", phase, functools.partial(scatter.high_step, k=k, total_b=total_b))
            self.add(f"l{k}", phase, functools.partial(gather.low_step, k=k))
        self.add("F", phase, finish)
        for k in range(lines):
            self.add(f"h{k}", phase, functools.partial(gather.high_step, k=k))
        self.add("E", phase, gather.end)

    def run(self, order):
        for name, phase, c in order:
            self.by_name[name, phase](c)


def in_turn(phase, lines, chunks):
    names = [f"{half}{k}" for k in range(1, lines) for half in "AB"] + ["F"]
    names += [f"l{k}" for k in range(1, lines)] + [f"h{k}" for k in range(lines)] + ["E"]
    return [(name, phase, c) for name in names for c in range(chunks)]


def unpack(order):
    return [(NAMES[code // 40], code // 8 % 5, code % 8) for code in order]


def rows_sum(values):
    return jnp.sum(values, axis=0, keepdims=True)


def mean_last(values):
    return jnp.mean(values, axis=-1, keepdims=True)


def dot_nn(a, b):
    return jnp.dot(a, b, preferred_element_type=jnp.float32)


def dot_nt(a, b):
    return lax.dot_general(a, b, (((1,), (1,)), ((), ())), preferred_element_type=jnp.float32)


def dot_tn(a, b):
    return lax.dot_general(a, b, (((0,), (0,)), ((), ())), preferred_element_type=jnp.float32)


def turn(values, cos_rows, sin_rows):
    return values * cos_rows + pltpu.roll(values, HD // 2, 1) * sin_rows


def front_tasks(
    tasks, batches, blocks, need_weights, lengths_ref, x_hbm, gain_ref, wq_ref, wk_ref, wv_ref, count_ref, width_ref, prob_ref,
    normed_hbm, query_ref, kv_hbm, heads_ref, ints_ref, floats_ref, cos_ref, sin_ref,
    x_mb, kv_own, kv_in, acc,
    sem_x, sem_normed, sem_own, sem_in, sem_send, sem_pass, sem_recv,
):
    blk, tp = lax.axis_index("blk"), lax.axis_index("tp")
    chips, chip, core = blocks // 2, blk // 2, blk % 2
    span, wide = x_hbm.shape[1], wq_ref.shape[1]
    heads = wide // HD
    scale = 1.0 / math.sqrt(HD)

    def slab(m):
        return pl.ds(pl.multiple_of(m * span, span), span)

    def get_x(m):
        return pltpu.make_async_copy(x_hbm.at[m], x_mb.at[m % 2], sem_x.at[m % 2])

    def put_normed(m):
        return pltpu.make_async_copy(x_mb.at[m % 2], normed_hbm.at[m], sem_normed.at[m % 2])

    def put_own(m):
        return pltpu.make_async_copy(kv_own.at[m], kv_hbm.at[m, blk], sem_own.at[m])

    def to_chip(m, k):
        return remote(
            kv_own.at[m], kv_hbm.at[m, blk], sem_send.at[m, k], sem_recv.at[m, blk], (k * 2 + core, tp)
        )

    def to_core(m):
        return remote(
            kv_own.at[m], kv_hbm.at[m, blk], sem_send.at[m, chip], sem_recv.at[m, blk], (chip * 2 + 1 - core, tp)
        )

    def pass_on(m, k):
        block = kv_hbm.at[m, k * 2 + core]
        return remote(
            block, block, sem_pass.at[m, k], sem_recv.at[m, k * 2 + core], (chip * 2 + 1 - core, tp)
        )

    def arrived(m, k):
        block = kv_hbm.at[m, k]
        return remote(block, block, sem_pass.at[m, 0], sem_recv.at[m, k], (blk, tp))

    def column(row):
        across = lax.broadcasted_iota(jnp.int32, (span, span), 1)
        down = lax.broadcasted_iota(jnp.int32, (span, span), 0)
        return jnp.sum(jnp.where(across == down, row.astype(jnp.float32), 0.0), axis=1, keepdims=True)

    def project(m):
        get_x(m).wait()
        if m + 1 < batches:
            if m >= 1:
                put_normed(m - 1).wait()
            get_x(m + 1).start()
        here = slab(m)
        x = x_mb[m % 2].astype(jnp.float32)
        scaled = x * lax.rsqrt(mean_last(x * x) + EPS)
        x_mb[m % 2] = (scaled * gain_ref[...]).astype(jnp.bfloat16)
        put_normed(m).start()
        rows = blk * span + lax.broadcasted_iota(jnp.int32, (span, 1), 0)
        begin, end = jnp.zeros((span, 1), jnp.int32), jnp.int32(0)
        for s in range(lengths_ref.shape[1]):
            length = lengths_ref[m, s]
            end = end + length
            begin = begin + jnp.where(rows >= end, length, 0)
        ints_ref[here, 0:1] = column(count_ref[m : m + 1, :]).astype(jnp.int32)
        ints_ref[here, 1:2] = column(width_ref[m : m + 1, :]).astype(jnp.int32)
        ints_ref[here, 2:3] = begin
        floats_ref[here, 0:1] = column(prob_ref[m : m + 1, :])
        lanes = lax.broadcasted_iota(jnp.int32, (1, HD), 1)
        half = HD // 2
        frequency = jnp.exp((lanes % half).astype(jnp.float32) * (-math.log(10000.0) / half))
        angles = (rows - begin).astype(jnp.float32) * frequency
        cos_rows = jnp.cos(angles)
        sin_rows = jnp.sin(angles) * jnp.where(lanes < half, -1.0, 1.0)
        cos_ref[here, :] = cos_rows
        sin_ref[here, :] = sin_rows
        normed = x_mb[m % 2]
        need_weights()
        query, key = dot_nn(normed, wq_ref[...]), dot_nn(normed, wk_ref[...])
        for h in range(heads):
            cols = slice(h * HD, (h + 1) * HD)
            query_ref[here, cols] = turn(query[:, cols], cos_rows, sin_rows).astype(jnp.bfloat16)
            kv_own[m, :, cols] = turn(key[:, cols], cos_rows, sin_rows).astype(jnp.bfloat16)
        kv_own[m, :, wide:] = dot_nn(normed, wv_ref[...]).astype(jnp.bfloat16)
        put_own(m).start()

        @pl.loop(chip + 1, chips)
        def _(k):
            to_chip(m, k).start()

        @pl.when(core == 0)
        def _():
            to_core(m).start()

    def pass_blocks(m):
        @pl.loop(0, chip)
        def _(k):
            arrived(m, k * 2 + core).wait_recv()
            pass_on(m, k).start()

    def get_kv(m, k):
        return pltpu.make_async_copy(kv_hbm.at[m, k], kv_in.at[k], sem_in.at[k])

    def attend(m):
        here = slab(m)
        q_rows = blk * span + lax.broadcasted_iota(jnp.int32, (span, span), 0)
        begin = ints_ref[here, 2:3]

        @pl.loop(0, blk)
        def _(k):
            @pl.when(k % 2 != core)
            def _():
                arrived(m, k).wait_recv()

            get_kv(m, k).start()

        def raw_scores(k, kv):
            k_rows = k * span + lax.broadcasted_iota(jnp.int32, (span, span), 1)
            allowed = (k_rows <= q_rows) & (k_rows >= begin)
            result = []
            for h in range(heads):
                cols = slice(h * HD, (h + 1) * HD)
                raw = dot_nt(query_ref[here, cols], kv[:, cols])
                result.append(jnp.where(allowed, raw * scale, NEG))
            return result

        def highest_of(k, kv):
            return tuple(functools.reduce(jnp.maximum, lane_tiles(score)) for score in raw_scores(k, kv))

        def weigh(k, kv, tops, sums):
            result, scores = [], raw_scores(k, kv)
            for h in range(heads):
                weights = jnp.exp(scores[h] - tops[h])
                result.append(sums[h] + sum(lane_tiles(weights)))
                acc[:, h * HD : (h + 1) * HD] += dot_nn(
                    weights.astype(jnp.bfloat16), kv[:, wide + h * HD : wide + (h + 1) * HD]
                )
            return tuple(result)

        highest = highest_of(blk, kv_own.at[m])

        def first(k, highest):
            get_kv(m, k).wait()
            return tuple(map(jnp.maximum, highest, highest_of(k, kv_in.at[k])))

        highest = lax.fori_loop(0, blk, first, highest)
        tops = [jnp.max(high, axis=-1, keepdims=True) for high in highest]
        acc[...] = jnp.zeros_like(acc)
        sums = weigh(blk, kv_own.at[m], tops, (jnp.zeros((span, LANE), jnp.float32),) * heads)
        sums = lax.fori_loop(0, blk, lambda k, sums: weigh(k, kv_in.at[k], tops, sums), sums)
        for h in range(heads):
            cols = slice(h * HD, (h + 1) * HD)
            row_sum = jnp.sum(sums[h], axis=-1, keepdims=True)
            floats_ref[here, 1 + h : 2 + h] = tops[h] + jnp.log(row_sum)
            heads_ref[here, cols] = jnp.where(
                tp * heads + h < ints_ref[here, 0:1], acc[:, cols] / row_sum, 0.0
            ).astype(jnp.bfloat16)

    def end():
        for m in range(batches):
            put_own(m).wait()
            if m >= batches - 2:
                put_normed(m).wait()

            @pl.loop(chip + 1, chips)
            def _(k):
                to_chip(m, k).wait_send()

            @pl.when(core == 0)
            def _():
                to_core(m).wait_send()

            @pl.loop(0, chip)
            def _(k):
                pass_on(m, k).wait_send()

    tasks.add("Q", 0, project)
    tasks.add("X", 0, pass_blocks)
    tasks.add("S", 0, attend)
    get_x(0).start()
    return end


def lane_tiles(values):
    return [values[:, i : i + LANE] for i in range(0, values.shape[1], LANE)]


def middle_kernel(
    lines, blocks, batches, chunks, chunk_rows, lengths_ref, tokens_hbm, x_hbm, grad_hbm, wq_hbm, wk_hbm, wv_hbm, wo_hbm, up_hbm,
    down_hbm, gain_ref, bias_ref, rms_ref, count_ref, width_ref, prob_ref, normed_hbm, kv_hbm, own_up, others_up, own_down, others_down, branch_hbm, feed_hbm, input_ref, resid_ref, sums_ref,
    query_ref, heads_ref, ints_ref, floats_ref, cos_ref, sin_ref,
    wq_ref, wk_ref, wv_ref, wo_ref, up_ref, down_ref, sem_load, x_own, g_own, g_all, own_branch, feed_part, lifted_ref, squared_ref, hidden_ref, normal_ref, inv_own, total,
    total_b, sem_in, sem_g, sem_feed, *rest,
):
    place = Place(lines)
    y, z, tp = place.y, place.z, place.tp
    spot = y * lines + z
    rows = chunk_rows // (2 * lines)
    width = gain_ref.shape[-1]
    units = up_ref.shape[1]
    s1, s2 = Scatter(place, CUT_SUM, *rest[:5], *rest[5:7]), Scatter(place, CUT_SUM, *rest[:5], *rest[7:9])
    a1 = Gather(place, CUT_SHARE, lambda c: lifted_ref.at[c, y, z], lifted_ref, None, *rest[10:12])
    a2 = Gather(place, CUT_SHARE, lambda c: own_branch.at[c], branch_hbm, *rest[12:15])
    share = width // blocks

    def up_slice(target, out):
        step = min(TILE, share)

        @pl.loop(0, share // step)
        def _(i):
            lanes = pl.ds(pl.multiple_of(target * share + i * step, step), step)
            lifted = lifted_ref[:, :, :, :, lanes].reshape(chunks * chunk_rows, step)
            out[pl.ds(pl.multiple_of(i * step, step), step), :] = dot_tn(lifted, hidden_ref[...]).astype(
                jnp.bfloat16
            )

    def down_slice(target, out):
        lanes = pl.ds(pl.multiple_of(target * share, share), share)

        @pl.loop(0, units // TILE)
        def _(i):
            cols = pl.ds(pl.multiple_of(i * TILE, TILE), TILE)
            grad = g_all[:, :, :, lanes].reshape(chunks * chunk_rows, share)
            out[cols, :] = dot_tn(squared_ref[:, cols], grad).astype(jnp.bfloat16)

    grad_up = BlockScatter(
        blocks, up_slice, lambda k: up_ref.at[pl.ds(pl.multiple_of(k * share, share), share), :], own_up, others_up,
        *rest[15:19],
    )
    grad_down = BlockScatter(
        blocks, down_slice, lambda k: down_ref.at[:, pl.ds(pl.multiple_of(k * share, share), share)], own_down, others_down,
        *rest[19:23],
    )

    get_x = pltpu.make_async_copy(tokens_hbm.at[:, spot], x_own, sem_in.at[0])
    get_g = pltpu.make_async_copy(grad_hbm.at[:, spot], g_own, sem_in.at[1])
    tasks = Tasks()
    front_end = front_tasks(
        tasks, batches, blocks, lambda: loads.need(0, 1, 2), lengths_ref, x_hbm, rms_ref, wq_ref, wk_ref, wv_ref, count_ref,
        width_ref, prob_ref, normed_hbm, query_ref, kv_hbm, heads_ref, ints_ref, floats_ref, cos_ref, sin_ref, *rest[23:],
    )
    sources = (wq_hbm, wk_hbm, wv_hbm, wo_hbm, up_hbm, down_hbm)
    loads = Loads(sem_load, list(zip(sources, (wq_ref, wk_ref, wv_ref, wo_ref, up_ref, down_ref), strict=True)))
    for copy in (get_x, get_g):
        copy.start()

    def get_grad(c):
        return pltpu.make_async_copy(grad_hbm.at[c], g_all.at[c], sem_g.at[c])

    def put_feed(c):
        return pltpu.make_async_copy(feed_part.at[c % FEED], feed_hbm.at[c], sem_feed.at[c])

    @pl.loop(0, chunks)
    def _(c):
        get_grad(c).start()

    greet("tp", "blk")
    sums_ref[...] = jnp.zeros_like(sums_ref)

    def own_rows(c):
        return pl.ds(pl.multiple_of(c * chunk_rows + spot * rows, rows), rows)

    def all_rows(c):
        return pl.ds(pl.multiple_of(c * chunk_rows, chunk_rows), chunk_rows)

    def tiled(n, body):
        @pl.loop(0, n // TILE)
        def _(i):
            body(pl.ds(pl.multiple_of(i * TILE, TILE), TILE))

    def put(part, c, cols, values):
        n = values.shape[0] // chunk_rows
        part[c : c + n, :, :, :, cols] = values.astype(jnp.bfloat16).reshape(n, 2, lines, rows, TILE)

    def project(c):
        loads.need(3)
        heads = heads_ref[all_rows(c), :]

        def one(cols):
            put(s1.part, c, cols, dot_nn(heads, wo_ref[:, cols]))

        tiled(width, one)
        s1.begin(c)

    first_norms = [get_x.wait, get_g.wait]

    def norm(c):
        while first_norms:
            first_norms.pop()()
        s1.finish(c, total)
        residual = x_own[c].astype(jnp.float32) + total[...]
        center = residual - mean_last(residual)
        inv_std = lax.rsqrt(mean_last(center * center) + EPS)
        normal = center * inv_std
        input_ref[c] = residual
        normal_ref[c] = normal
        inv_own[c] = jnp.broadcast_to(inv_std, (rows, LANE))
        lifted_ref[c, y, z] = (normal * gain_ref[...] + bias_ref[...]).astype(jnp.bfloat16)
        a1.begin(c)

    def feed(c):
        group = range(c, c + FEED)
        loads.need(4, 5)
        for i in group:
            a1.end(i)
            s1.drain(i)
            get_grad(i).wait()
        size = FEED * chunk_rows
        lifted = lifted_ref[c : c + FEED].reshape(size, width)
        span = pl.ds(c * chunk_rows, size)
        prob, limit = floats_ref[span, 0:1], (ints_ref[span, 1:2] + 1) * (FF // 4)
        g_all[c : c + FEED] = (
            g_all[c : c + FEED].astype(jnp.float32) * prob.reshape(FEED, 2 * lines, rows, 1)
        ).astype(jnp.bfloat16)

        def units_of(cols):
            active = jnp.maximum(dot_nn(lifted, up_ref[:, cols]), 0.0)
            ids = tp * units + cols.start + lax.broadcasted_iota(jnp.int32, (size, TILE), 1)
            mask = (ids < limit).astype(jnp.float32)
            squared_ref[span, cols] = (active * active * mask).astype(jnp.bfloat16)
            back = dot_nt(g_all[c : c + FEED].reshape(size, width), down_ref[cols, :])
            hidden_ref[span, cols] = (back * mask * 2.0 * active).astype(jnp.bfloat16)

        tiled(units, units_of)
        hidden = hidden_ref[span, :]

        def lift(cols):
            put(s2.part, c, cols, dot_nt(hidden, up_ref[cols, :]))

        tiled(width, lift)
        for i in group:
            s2.begin(i)
        squared = squared_ref[span, :]
        if c > 0:
            for i in range(FEED):
                put_feed(c - FEED + i).wait()

        def out(cols):
            put(feed_part, 0, cols, dot_nn(squared, down_ref[:, cols]))

        tiled(width, out)
        for i in group:
            put_feed(i).start()

    def norm_back(c):
        s2.finish(c, total)
        grad_lifted, normal = total[...], normal_ref[c]
        sums_ref[0:1, :] += rows_sum(grad_lifted * normal)
        sums_ref[1:2, :] += rows_sum(grad_lifted)
        g = grad_lifted * gain_ref[...]
        grad_resid = g_own[c].astype(jnp.float32) + inv_own[c][:, 0:1] * (
            g - mean_last(g) - normal * mean_last(g * normal)
        )
        resid_ref[c] = grad_resid
        own_branch[c] = grad_resid.astype(jnp.bfloat16)
        a2.begin(c)

    tasks.add("P", 1, project)
    tasks.sum_and_share(1, s1, a1, total_b, norm)
    tasks.add("P", 2, feed)
    tasks.sum_and_share(2, s2, a2, total_b, norm_back)
    steps = (grad_up.all_first, grad_down.all_first, grad_up.all_second, grad_down.all_second)
    tasks.add("W", 0, lambda k: steps[k]())
    tasks.add("Z", 0, lambda k: None)
    tasks.run(middle_order(lines, chunks, batches))
    front_end()

    for c in range(chunks - FEED, chunks):
        put_feed(c).wait()

    @pl.loop(0, chunks)
    def _(c):
        for part in (s2, a1, a2):
            part.drain(c)

    grad_up.end()
    grad_down.end()


def middle_order(lines, chunks, batches):
    if (lines, chunks, batches) == (4, 8, 4):
        return unpack(MIDDLE_ORDER)
    order = [(name, 0, m) for name in "QXS" for m in range(batches)]
    order += [("P", 1, c) for c in range(chunks)] + in_turn(1, lines, chunks)[:-chunks]
    order += [("P", 2, c) for c in range(0, chunks, FEED)] + in_turn(2, lines, chunks)
    return order + [("W", 0, k) for k in range(4)]


def middle(tokens, lengths, head_count, width_index, router_prob, norm_gain, w_query, w_key, w_value, grad_out, w_out,
           ln_gain, ln_bias, w_up, w_down):
    lines, blocks = lax.axis_size("tp") // 2, lax.axis_size("blk")
    batches, span, width = tokens.shape
    count, units, wide = batches * span, w_up.shape[1], w_query.shape[1]
    heads = wide // HD
    chunk_rows = CHUNK_ROWS
    chunks, rows = count // chunk_rows, chunk_rows // (2 * lines)
    share = width // blocks
    split = (chunks, 2 * lines, rows, width)
    full = (chunks, 2, lines, rows, width)
    any_space, vmem = pl.BlockSpec(memory_space=pl.ANY), pl.BlockSpec(memory_space=VMEM)
    bf16, f32 = jnp.bfloat16, jnp.float32
    dma = pltpu.SemaphoreType.DMA
    loads = (w_query, w_key, w_value, w_out, w_up, w_down)
    outs = pl.pallas_call(
        functools.partial(middle_kernel, lines, blocks, batches, chunks, chunk_rows),
        out_shape=[
            jax.ShapeDtypeStruct((batches, span, width), bf16),
            jax.ShapeDtypeStruct((batches, blocks, span, 2 * wide), bf16),
            *BlockScatter.outs(blocks, (share, units)),
            *BlockScatter.outs(blocks, (units, share)),
            jax.ShapeDtypeStruct(full, bf16),
            jax.ShapeDtypeStruct(full, bf16),
            jax.ShapeDtypeStruct((chunks, rows, width), f32),
            jax.ShapeDtypeStruct((chunks, rows, width), f32),
            jax.ShapeDtypeStruct((2, width), f32),
            jax.ShapeDtypeStruct((count, wide), bf16),
            jax.ShapeDtypeStruct((count, wide), bf16),
            jax.ShapeDtypeStruct((count, 3), jnp.int32),
            jax.ShapeDtypeStruct((count, 1 + heads), f32),
            jax.ShapeDtypeStruct((count, HD), f32),
            jax.ShapeDtypeStruct((count, HD), f32),
        ],
        in_specs=[pl.BlockSpec(memory_space=pltpu.SMEM)] + [any_space] * 9 + [vmem] * 6,
        out_specs=[any_space] * 8 + [vmem] * 9,
        scratch_shapes=[VMEM(load.shape, bf16) for load in loads]
        + [
            dma((len(loads),)),
            VMEM((chunks, rows, width), bf16),
            VMEM((chunks, rows, width), bf16),
            VMEM(split, bf16),
            VMEM((chunks, rows, width), bf16),
            VMEM((FEED,) + full[1:], bf16),
            VMEM(full, bf16),
            VMEM((count, units), bf16),
            VMEM((count, units), bf16),
            VMEM((chunks, rows, width), f32),
            VMEM((chunks, rows, LANE), f32),
            VMEM((rows, width), f32),
            VMEM((2, rows, width - CUT_SUM), f32),
            dma((2,)),
            dma((chunks,)),
            dma((chunks,)),
        ]
        + Scatter.scratch(chunks, lines, rows, width, CUT_SUM)
        + Scatter.semaphores(chunks, lines) * 2
        + Gather.scratch(chunks, lines) * 2
        + BlockScatter.scratch(blocks, (share, units))
        + BlockScatter.scratch(blocks, (units, share))
        + [
            VMEM((2, span, width), bf16),
            VMEM((batches, span, 2 * wide), bf16),
            VMEM((blocks, span, 2 * wide), bf16),
            VMEM((span, wide), f32),
            dma((2,)),
            dma((2,)),
            dma((batches,)),
            dma((blocks,)),
            dma((batches, blocks // 2)),
            dma((batches, blocks // 2)),
            dma((batches, blocks)),
        ],
        compiler_params=pltpu.CompilerParams(
            collective_id=1, has_side_effects=True, vmem_limit_bytes=VMEM_LIMIT
        ),
        cost_estimate=pl.CostEstimate(
            flops=2 * count * width * (4 * wide + 6 * units), bytes_accessed=40 * 2**20, transcendentals=0
        ),
    )(
        lengths, tokens.reshape(split), tokens, grad_out.reshape(split), *loads, ln_gain[None], ln_bias[None],
        norm_gain[None], head_count, width_index, router_prob,
    )
    return outs


def turn_back(grad, cos_rows, sin_rows):
    return grad * cos_rows - pltpu.roll(grad, HD // 2, 1) * sin_rows


def back_kernel(
    lines, blocks, batches, chunks, chunk_rows, tokens_hbm, kv_hbm, feed_hbm, branch_hbm, normed_hbm,
    input_hbm, resid_hbm, query_hbm, heads_hbm, wq_hbm, wk_hbm, wv_hbm, wo_hbm, cos_hbm, sin_hbm, floats_hbm,
    ints_ref, gain_ref, sums_ref, mixed_hbm, in_hbm, own_w, others_w, own_o, others_o,
    small_ref,
    input_ref, resid_ref, query_ref, heads_ref, wq_ref, wk_ref, wv_ref, wo_ref, cos_ref, sin_ref, floats_ref, sem_load,
    branch_ref, x_own, own_in, own_mixed, kv_mb, grad_mb, delta_mb, dq_mb, stage, own, came, pre, total, total_b,
    grad_w, small, small_blk, small_part, small_tp, sem_in, sem_branch, sem_feed, sem_kv, sem_send, sem_recv, sem_free, sem_blk, sem_tp,
    *rest,
):
    place = Place(lines)
    blk, tp, y, z = lax.axis_index("blk"), place.tp, place.y, place.z
    spot = y * lines + z
    rows = chunk_rows // (2 * lines)
    width = gain_ref.shape[-1]
    wide = query_ref.shape[1]
    heads = wide // HD
    span = query_ref.shape[0] // batches
    per = span // chunk_rows
    scale = 1.0 / math.sqrt(HD)
    s3, s4 = Scatter(place, CUT_SUM, *rest[0:7]), Scatter(place, CUT_SUM, *rest[7:14])
    a3 = Gather(place, CUT_SHARE, lambda c: own_mixed.at[c], mixed_hbm, *rest[14:17])
    a4 = Gather(place, CUT_SHARE, lambda c: own_in.at[c], in_hbm, *rest[17:20])

    get_x = pltpu.make_async_copy(tokens_hbm.at[:, spot], x_own, sem_in)
    get_x.start()

    def get_kv(step):
        source = kv_hbm.at[step // (blk + 1), step % (blk + 1)]
        return pltpu.make_async_copy(source, kv_mb.at[step % 2], sem_kv.at[step % 2])

    def get_feed(c):
        return pltpu.make_async_copy(feed_hbm.at[c], s3.part.at[c], sem_feed.at[c])

    def slab(m):
        return pl.ds(pl.multiple_of(m * span, span), span)

    ring = stage.shape[0]

    def get_branch(m):
        return pltpu.make_async_copy(branch_hbm.at[slab(m), :], branch_ref.at[slab(m), :], sem_branch.at[m])

    get_normed = pltpu.make_async_copy(normed_hbm, branch_ref, sem_branch.at[batches])
    waited = set()

    def need_branch(*which):
        for m in which:
            if m not in waited:
                waited.add(m)
                get_branch(m).wait()

    def to_owner(m, k):
        slot = (m * blk + k) % ring
        return remote(
            stage.at[slot], came.at[m % 2, blk], sem_send.at[slot], sem_recv.at[m % 2, blk], (k, tp)
        )

    def from_peer(m, k):
        return remote(stage.at[0], came.at[m % 2, k], sem_send.at[0], sem_recv.at[m % 2, k], (k, tp))

    def attend_back(m):
        need_branch(m)
        loads.need(*attend_loads)
        here = slab(m)
        grad = dot_nt(branch_ref[here, :], wo_ref[...]).astype(jnp.bfloat16)
        for h in range(heads):
            cols = slice(h * HD, (h + 1) * HD)
            head = tp * heads + h
            masked = jnp.where(head < ints_ref[here, 0:1], grad[:, cols].astype(jnp.float32), 0.0)
            grad_mb[:, cols] = masked.astype(jnp.bfloat16)
            delta = jnp.sum(masked * heads_ref[here, cols].astype(jnp.float32), axis=-1, keepdims=True)
            delta_mb[h] = jnp.broadcast_to(delta, (span, LANE))
        dq_mb[...] = jnp.zeros_like(dq_mb)
        q_rows = blk * span + lax.broadcasted_iota(jnp.int32, (span, span), 0)
        begin = ints_ref[here, 2:3]

        def pairs(k, out):
            step = m * (blk + 1) + k
            get_kv(step).wait()

            @pl.when(step + 1 < batches * (blk + 1))
            def _():
                get_kv(step + 1).start()

            k_rows = k * span + lax.broadcasted_iota(jnp.int32, (span, span), 1)
            allowed = (k_rows <= q_rows) & (k_rows >= begin)
            for h in range(heads):
                cols = slice(h * HD, (h + 1) * HD)
                q, g = query_ref[here, cols], grad_mb[:, cols]
                key = kv_mb[step % 2, :, cols]
                value = kv_mb[step % 2, :, wide + h * HD : wide + (h + 1) * HD]
                raw = dot_nt(q, key)
                prob = jnp.where(allowed, jnp.exp(raw * scale - floats_ref[here, 1 + h : 2 + h]), 0.0)
                grad_prob = dot_nt(g, value)
                grad_score = (prob * (grad_prob - delta_mb[h][:, 0:1]) * scale).astype(jnp.bfloat16)
                dq_mb[:, cols] += dot_nn(grad_score, key)
                out[:, cols] = dot_tn(grad_score, q).astype(jnp.bfloat16)
                out[:, wide + h * HD : wide + (h + 1) * HD] = dot_tn(prob.astype(jnp.bfloat16), g).astype(
                    jnp.bfloat16
                )

        @pl.loop(0, blk)
        def _(k):
            sent = m * blk + k

            @pl.when(sent >= ring)
            def _():
                to_owner((sent - ring) // blk, (sent - ring) % blk).wait_send()

            pairs(k, stage.at[sent % ring])

            @pl.when(m >= 2)
            def _():
                pl.semaphore_wait(sem_free.at[k], 1)

            to_owner(m, k).start()

        pairs(blk, own.at[m % 2])
        if m == batches - 1:
            get_normed.start()
        for h in range(heads):
            cols = slice(h * HD, (h + 1) * HD)
            pre[here, cols] = turn_back(dq_mb[:, cols], cos_ref[here, :], sin_ref[here, :]).astype(
                jnp.bfloat16
            )

    def gather_kv(m):
        here = slab(m)
        grad_w[...] = own[m % 2].astype(jnp.float32)

        @pl.loop(blk + 1, blocks)
        def _(k):
            from_peer(m, k).wait_recv()
            grad_w[...] += came[m % 2, k].astype(jnp.float32)

            @pl.when(m + 2 < batches)
            def _():
                pl.semaphore_signal(sem_free.at[blk], inc=1, device_id=(k, tp), device_id_type=MESH)

        for h in range(heads):
            cols = slice(h * HD, (h + 1) * HD)
            pre[here, wide + h * HD : wide + (h + 1) * HD] = turn_back(
                grad_w[:, cols], cos_ref[here, :], sin_ref[here, :]
            ).astype(jnp.bfloat16)
        pre[here, 2 * wide :] = grad_w[:, wide:].astype(jnp.bfloat16)

    def spread(c):
        loads.need(*spread_loads)
        here = pl.ds(pl.multiple_of(c * chunk_rows, chunk_rows), chunk_rows)

        @pl.loop(0, width // TILE)
        def _(i):
            cols = pl.ds(pl.multiple_of(i * TILE, TILE), TILE)
            grad = dot_nt(pre[here, :wide], wq_ref[cols, :])
            grad += dot_nt(pre[here, wide : 2 * wide], wk_ref[cols, :])
            grad += dot_nt(pre[here, 2 * wide :], wv_ref[cols, :])
            s4.part[c, :, :, :, cols] = grad.astype(jnp.bfloat16).reshape(2, lines, rows, TILE)

        s4.begin(c)

    def feed(c):
        get_feed(c).wait()
        s3.begin(c)

    def mix(c):
        loads.need(*mix_loads)
        s3.finish(c, total)
        prob = floats_ref[pl.ds(pl.multiple_of(c * chunk_rows + spot * rows, rows), rows), 0:1]
        own_mixed[c] = (input_ref[c] + prob * total[...]).astype(jnp.bfloat16)
        a3.begin(c)

    def last(c):
        loads.need(*last_loads)
        s4.finish(c, total)
        grad_normed, x = total[...], x_own[c].astype(jnp.float32)
        inv_rms = lax.rsqrt(mean_last(x * x) + EPS)
        scaled = x * inv_rms
        small[0:1, :] += rows_sum(grad_normed * scaled)
        s = grad_normed * gain_ref[...]
        grad_in = resid_ref[c] + inv_rms * (s - scaled * mean_last(s * scaled))
        own_in[c] = grad_in.astype(jnp.bfloat16)
        a4.begin(c)

    share = width // blocks

    def slice_of(target, out):
        step = min(TILE, share)

        @pl.loop(0, share // step)
        def _(i):
            lanes = pl.ds(pl.multiple_of(target * share + i * step, step), step)
            grad = dot_tn(branch_ref[:, lanes], pre[...]).astype(jnp.bfloat16)
            for k in range(3):
                out[k, pl.ds(pl.multiple_of(i * step, step), step), :] = grad[:, k * wide : (k + 1) * wide]

    def out_slice(target, out):
        lanes = pl.ds(pl.multiple_of(target * share, share), share)
        out[...] = dot_tn(heads_ref[...], branch_ref[:, lanes]).astype(jnp.bfloat16)

    part, out_part = rest[20], rest[25]
    weights = BlockScatter(blocks, slice_of, lambda k: part.at[k], own_w, others_w, *rest[21:25])
    out_weights = BlockScatter(blocks, out_slice, lambda k: out_part.at[k], own_o, others_o, *rest[26:30])
    ranks = 2 * lines

    def small_to_blk(k):
        peer = (blk + k) % blocks
        lanes = pl.ds(pl.multiple_of(peer * share, share), share)
        return remote(
            small.at[:, lanes], small_blk.at[k - 1], sem_blk.at[0, k], sem_blk.at[1, k], (peer, tp)
        )

    def small_to_tp(k):
        return remote(
            small_part, small_tp.at[k - 1], sem_tp.at[0, k], sem_tp.at[1, k], (blk, (tp + k) % ranks)
        )

    def small_first():
        for k in range(1, blocks):
            small_to_blk(k).start()

    def small_second():
        small_part[...] = small[:, pl.ds(pl.multiple_of(blk * share, share), share)]
        for k in range(1, blocks):
            small_to_blk(k).wait()
            small_part[...] += small_blk[k - 1]
        for k in range(1, ranks):
            small_to_tp(k).start()

    def small_third():
        small_ref[...] = small_part[...]
        for k in range(1, ranks):
            small_to_tp(k).wait()
            small_ref[...] += small_tp[k - 1]

    get_branch(0).start()
    attend_loads, mix_loads, last_loads, spread_loads = (2, 3, 7, 8, 9, 10), (0, 10), (1,), (4, 5, 6)
    refs = (input_ref, resid_ref, query_ref, heads_ref, wq_ref, wk_ref, wv_ref, wo_ref, cos_ref, sin_ref, floats_ref)
    sources = (
        input_hbm, resid_hbm, query_hbm, heads_hbm, wq_hbm, wk_hbm, wv_hbm, wo_hbm, cos_hbm, sin_hbm, floats_hbm,
    )
    loads = Loads(sem_load, list(zip(sources, refs, strict=True)))
    for m in range(1, batches):
        get_branch(m).start()

    @pl.loop(0, chunks)
    def _(c):
        get_feed(c).start()

    get_kv(0).start()
    greet("tp", "blk")
    get_x.wait()
    small[...] = jnp.zeros_like(small)
    small[1:3, :] = sums_ref[...]

    tasks = Tasks()
    tasks.add("P", 3, feed)
    tasks.sum_and_share(3, s3, a3, total_b, mix)
    tasks.add("T", 0, attend_back)
    tasks.add("K", 0, gather_kv)
    tasks.add("P", 4, spread)
    tasks.sum_and_share(4, s4, a4, total_b, last)

    def out_gradient(k):
        need_branch(*range(batches))
        loads.need(3)
        (out_weights.all_first, out_weights.all_second)[k]()

    def weight_gradients(k):
        if k == 0:
            get_normed.wait()
        (weights.all_first, weights.all_second)[k]()

    tasks.add("O", 0, out_gradient)
    tasks.add("V", 0, weight_gradients)
    tasks.add("M", 0, lambda k: (small_first, small_second, small_third)[k]())
    tasks.add("Z", 0, lambda k: None)
    tasks.run(back_order(lines, chunks, batches))

    @pl.loop(0, chunks)
    def _(c):
        for phase in (s3, s4, a3, a4):
            phase.drain(c)

    @pl.loop(jnp.maximum(batches * blk - ring, 0), batches * blk)
    def _(sent):
        to_owner(sent // blk, sent % blk).wait_send()

    weights.end()
    out_weights.end()


def back_order(lines, chunks, batches):
    if (lines, chunks, batches) == (4, 8, 4):
        return unpack(BACK_ORDER)
    order = [("O", 0, 0), ("O", 0, 1)] + [("P", 3, c) for c in range(chunks)] + in_turn(3, lines, chunks)
    order += [(name, 0, m) for m in range(batches) for name in "TK"]
    order += [("V", 0, 0), ("V", 0, 1)] + [("P", 4, c) for c in range(chunks)] + in_turn(4, lines, chunks)
    return order + [("M", 0, k) for k in range(3)]


def back(tokens, kv, feed_part, grad_branch, normed, own_input, own_resid, query, heads_out, w_query, w_key, w_value,
         w_out, norm_gain, ints, floats, cos_rows, sin_rows, ln_sums):
    lines, blocks = lax.axis_size("tp") // 2, lax.axis_size("blk")
    count, width = tokens.shape
    batches, wide = kv.shape[0], query.shape[1]
    chunk_rows = CHUNK_ROWS
    chunks, rows = count // chunk_rows, chunk_rows // (2 * lines)
    span = count // batches
    heads = wide // HD
    share = width // blocks
    any_space, vmem = pl.BlockSpec(memory_space=pl.ANY), pl.BlockSpec(memory_space=VMEM)
    bf16, f32 = jnp.bfloat16, jnp.float32
    dma = pltpu.SemaphoreType.DMA
    full = (chunks, 2, lines, rows, width)
    loads = (
        own_input, own_resid, query, heads_out, w_query, w_key, w_value, w_out, cos_rows, sin_rows, floats,
    )
    outs = pl.pallas_call(
        functools.partial(back_kernel, lines, blocks, batches, chunks, chunk_rows),
        out_shape=[jax.ShapeDtypeStruct(full, bf16)] * 2
        + BlockScatter.outs(blocks, (3, share, wide))
        + BlockScatter.outs(blocks, (wide, share))
        + [jax.ShapeDtypeStruct((8, share), f32)],
        in_specs=[any_space] * 16 + [vmem] * 3,
        out_specs=[any_space] * 6 + [vmem],
        scratch_shapes=[VMEM(load.shape, load.dtype) for load in loads]
        + [
            dma((len(loads),)),
            VMEM((count, width), bf16),
            VMEM((chunks, rows, width), bf16),
            VMEM((chunks, rows, width), bf16),
            VMEM((chunks, rows, width), bf16),
            VMEM((2, span, 2 * wide), bf16),
            VMEM((span, wide), bf16),
            VMEM((heads, span, LANE), f32),
            VMEM((span, wide), f32),
            VMEM((RING, span, 2 * wide), bf16),
            VMEM((2, span, 2 * wide), bf16),
            VMEM((2, blocks, span, 2 * wide), bf16),
            VMEM((count, 3 * wide), bf16),
            VMEM((rows, width), f32),
            VMEM((2, rows, width - CUT_SUM), f32),
            VMEM((span, 2 * wide), f32),
            VMEM((8, width), f32),
            VMEM((blocks - 1, 8, share), f32),
            VMEM((8, share), f32),
            VMEM((2 * lines - 1, 8, share), f32),
            dma(()),
            dma((batches + 1,)),
            dma((chunks,)),
            dma((2,)),
            dma((RING,)),
            dma((2, blocks)),
            pltpu.SemaphoreType.REGULAR((blocks,)),
            dma((2, blocks)),
            dma((2, 2 * lines)),
        ]
        + (Scatter.scratch(chunks, lines, rows, width, CUT_SUM) + Scatter.semaphores(chunks, lines)) * 2
        + Gather.scratch(chunks, lines) * 2
        + [VMEM((blocks, 3, share, wide), bf16)]
        + BlockScatter.scratch(blocks, (3, share, wide))
        + [VMEM((blocks, wide, share), bf16)]
        + BlockScatter.scratch(blocks, (wide, share)),
        compiler_params=pltpu.CompilerParams(
            collective_id=2, has_side_effects=True, vmem_limit_bytes=VMEM_LIMIT
        ),
        cost_estimate=pl.CostEstimate(
            flops=2 * count * width * wide * 7, bytes_accessed=40 * 2**20, transcendentals=0
        ),
    )(
        tokens.reshape(chunks, 2 * lines, rows, width), kv, feed_part, grad_branch, normed, *loads, ints,
        norm_gain[None], ln_sums,
    )
    return outs


def finish_kernel(pairs, copies, *refs):
    ins, refs = refs[: 2 * pairs + copies + 1], refs[2 * pairs + copies + 1 :]
    outs, scratch = refs[: pairs + copies + 5], refs[pairs + copies + 5 :]
    own, others, results = scratch[:pairs], scratch[pairs : 2 * pairs], scratch[2 * pairs : 3 * pairs]
    held = scratch[3 * pairs : 3 * pairs + copies]
    sem_load, sem_copy, sem_store = scratch[3 * pairs + copies :]
    loads = []
    for i in range(pairs):
        loads.append(pltpu.make_async_copy(ins[2 * i], own[i], sem_load.at[2 * i]))
        loads.append(pltpu.make_async_copy(ins[2 * i + 1], others[i], sem_load.at[2 * i + 1]))
    for load in loads:
        load.start()
    moves = []
    for i in range(copies):
        source, target = ins[2 * pairs + i], outs[pairs + 2 + i]
        moves += [
            (
                pltpu.make_async_copy(source.at[m], held[i].at[m], sem_copy.at[0, i, m]),
                pltpu.make_async_copy(held[i].at[m], target.at[m], sem_copy.at[1, i, m]),
            )
            for m in range(source.shape[0])
        ]
    for come, _ in moves:
        come.start()
    sums = ins[-1]
    for i in range(3):
        outs[pairs + 2 + copies + i][...] = sums[i : i + 1, :]
    stores = [go for _, go in moves]
    for come, go in moves[: len(moves) // 2]:
        come.wait()
        go.start()
    for i in range(pairs):
        loads[2 * i].wait()
        loads[2 * i + 1].wait()
        total = own[i][...].astype(jnp.float32)
        for k in range(others[i].shape[0]):
            total += others[i][k].astype(jnp.float32)
        results[i][...] = total
        targets = [(results[0].at[k], outs[k]) for k in range(3)] if i == 0 else [(results[i], outs[i + 2])]
        for k, (source, target) in enumerate(targets):
            stores.append(pltpu.make_async_copy(source, target, sem_store.at[k if i == 0 else i + 2]))
            stores[-1].start()
    for come, go in moves[len(moves) // 2 :]:
        come.wait()
        go.start()
    for copy in stores:
        copy.wait()


def finish(pairs, copies, sums):
    any_space, vmem = pl.BlockSpec(memory_space=pl.ANY), pl.BlockSpec(memory_space=VMEM)
    f32, share = jnp.float32, sums.shape[1]
    dma = pltpu.SemaphoreType.DMA
    return pl.pallas_call(
        functools.partial(finish_kernel, len(pairs), len(copies)),
        out_shape=[jax.ShapeDtypeStruct(pairs[0][0].shape[1:], f32)] * 3
        + [jax.ShapeDtypeStruct(own.shape, f32) for own, _ in pairs[1:]]
        + [jax.ShapeDtypeStruct(copy.shape, copy.dtype) for copy in copies]
        + [jax.ShapeDtypeStruct((1, share), f32)] * 3,
        in_specs=[any_space] * (2 * len(pairs) + len(copies)) + [vmem],
        out_specs=[any_space] * (len(pairs) + 2 + len(copies)) + [vmem] * 3,
        scratch_shapes=[VMEM(own.shape, own.dtype) for own, _ in pairs]
        + [VMEM(others.shape, others.dtype) for _, others in pairs]
        + [VMEM(own.shape, f32) for own, _ in pairs]
        + [VMEM(copy.shape, copy.dtype) for copy in copies]
        + [dma((2 * len(pairs),)), dma((2, len(copies), copies[0].shape[0])), dma((len(pairs) + 2,))],
        compiler_params=pltpu.CompilerParams(vmem_limit_bytes=VMEM_LIMIT),
        cost_estimate=pl.CostEstimate(flops=0, bytes_accessed=28 * 2**20, transcendentals=0),
    )(*[array for pair in pairs for array in pair], *copies, sums)


def local(
    tokens,
    lengths,
    head_count,
    width_index,
    router_prob,
    norm_gain,
    w_query,
    w_key,
    w_value,
    w_out,
    ln_gain,
    ln_bias,
    w_up,
    w_down,
    grad_out,
):
    batches, rows_dev, features = tokens.shape
    count = batches * rows_dev
    (
        normed, kv, own_up, others_up, own_down, others_down, grad_branch, feed_part, own_input, own_resid, ln_sums,
        query, heads_out, ints, floats, cos_rows, sin_rows,
    ) = middle(
        tokens, lengths, head_count, width_index, router_prob, norm_gain, w_query, w_key, w_value,
        grad_out.reshape(count, features), w_out, ln_gain, ln_bias, w_up, w_down,
    )
    flat = tokens.reshape(count, features)
    mixed_out, grad_in, own_w, others_w, own_out, others_out, sums = back(
        flat,
        kv,
        feed_part,
        grad_branch.reshape(count, features),
        normed.reshape(count, features),
        own_input,
        own_resid,
        query,
        heads_out,
        w_query,
        w_key,
        w_value,
        w_out,
        norm_gain,
        ints,
        floats,
        cos_rows,
        sin_rows,
        ln_sums,
    )
    grad_q, grad_k, grad_v, grad_out_w, grad_up, grad_down, mixed_out, grad_in, *sums = finish(
        [(own_w, others_w), (own_out, others_out), (own_up, others_up), (own_down, others_down)],
        [mixed_out.reshape(tokens.shape), grad_in.reshape(tokens.shape)],
        sums,
    )
    gain_sum, ln_gain_sum, ln_bias_sum = (total.reshape(-1) for total in sums)
    return (
        mixed_out, grad_in, gain_sum, grad_q, grad_k, grad_v, grad_out_w, ln_gain_sum, ln_bias_sum, grad_up, grad_down
    )


def solution(mesh):
    return jax.shard_map(
        local,
        mesh=mesh,
        in_specs=(
            P(None, "blk", None),
            P(),
            P(None, "blk"),
            P(None, "blk"),
            P(None, "blk"),
            P(),
            P(None, "tp"),
            P(None, "tp"),
            P(None, "tp"),
            P("tp", None),
            P(),
            P(),
            P(None, "tp"),
            P("tp", None),
            P(None, "blk", None),
        ),
        out_specs=(
            P(None, "blk", None),
            P(None, "blk", None),
            P("blk"),
            P("blk", "tp"),
            P("blk", "tp"),
            P("blk", "tp"),
            P("tp", "blk"),
            P("blk"),
            P("blk"),
            P("blk", "tp"),
            P("tp", "blk"),
        ),
        check_vma=False,
    )
```

```python
import functools
import math

import jax
import jax.numpy as jnp
from jax import lax
from jax.experimental import pallas as pl
from jax.experimental.pallas import tpu as pltpu
from jax.sharding import PartitionSpec as P

HD = 128
FF = 8192


EPS = 1e-05
NEG = -1e30
CHUNK_ROWS = 128
CUT_SUM = 1408
CUT_SHARE = 1408
CUT_SHARE_BACK = 1536
VMEM_LIMIT = 63 * 2**20
RING = 4
TILE = 1024
FEED = 2
NAMES = ("P", "A1", "A2", "A3", "B1", "B2", "B3", "F", "l1", "l2", "l3", "h0", "h1", "h2", "h3", "E", "W", "T", "K", "O", "V", "M", "Z", "Q", "X", "S")
MIDDLE_ORDER = (
    920, 921, 922, 960, 1000, 8, 961, 9, 1001, 48, 10, 962, 168, 923, 88, 11, 208, 169, 1002, 171,
    12, 248, 49, 963, 13, 209, 128, 172, 170, 1003, 89, 288, 249, 173, 14, 129, 211, 212, 328, 51,
    448, 174, 50, 213, 252, 210, 91, 289, 251, 214, 131, 53, 488, 368, 90, 15, 449, 253, 528, 130,
    329, 93, 291, 250, 52, 133, 175, 369, 293, 215, 409, 489, 408, 54, 255, 254, 92, 331, 290, 132,
    568, 55, 333, 529, 451, 292, 94, 453, 371, 450, 373, 330, 569, 16, 370, 95, 134, 491, 490, 410,
    176, 411, 294, 135, 56, 530, 531, 295, 332, 216, 452, 96, 413, 177, 334, 256, 57, 372, 570, 454,
    493, 335, 492, 455, 571, 136, 412, 18, 374, 217, 257, 375, 414, 533, 532, 97, 415, 296, 573,
    495, 494, 572, 137, 20, 178, 535, 575, 179, 534, 297, 574, 22, 180, 219, 640, 456, 59, 58, 457,
    337, 218, 336, 181, 641, 377, 220, 376, 182, 496, 99, 642, 221, 98, 536, 61, 259, 260, 222, 183,
    261, 139, 497, 258, 138, 63, 101, 223, 299, 537, 298, 416, 459, 141, 458, 103, 301, 417, 499,
    60, 263, 339, 461, 498, 643, 143, 341, 577, 539, 100, 262, 62, 538, 579, 379, 338, 303, 501,
    102, 576, 140, 541, 300, 581, 142, 381, 421, 378, 578, 340, 460, 343, 302, 383, 463, 616, 418,
    423, 342, 462, 380, 617, 382, 420, 500, 419, 621, 502, 422, 618, 619, 503, 543, 540, 580, 583,
    542, 620, 623, 582, 622, 880,
)
BACK_ORDER = (
    24, 25, 26, 680, 27, 185, 28, 29, 681, 225, 186, 65, 30, 187, 184, 760, 64, 761, 66, 189, 188,
    31, 720, 105, 229, 227, 682, 226, 190, 68, 228, 104, 106, 224, 69, 265, 32, 266, 269, 264, 191,
    145, 144, 305, 108, 268, 230, 146, 33, 231, 109, 304, 192, 67, 148, 149, 308, 309, 306, 232,
    465, 464, 721, 271, 193, 469, 107, 344, 468, 73, 267, 345, 272, 233, 34, 147, 346, 505, 35, 504,
    273, 508, 466, 113, 348, 385, 307, 386, 509, 349, 545, 544, 194, 548, 72, 384, 683, 71, 506,
    426, 389, 153, 112, 347, 722, 424, 152, 70, 467, 74, 195, 111, 234, 270, 388, 312, 313, 387,
    507, 274, 151, 110, 36, 235, 114, 75, 547, 311, 275, 150, 352, 473, 427, 549, 196, 37, 472, 353,
    428, 546, 310, 115, 392, 723, 154, 585, 513, 76, 236, 512, 471, 38, 197, 155, 116, 314, 276,
    350, 553, 586, 237, 39, 511, 552, 198, 470, 199, 351, 77, 551, 592, 277, 156, 593, 429, 390,
    432, 800, 238, 510, 78, 584, 239, 354, 117, 315, 474, 278, 316, 425, 118, 391, 279, 157, 801,
    355, 624, 589, 79, 514, 393, 395, 119, 394, 317, 475, 158, 356, 476, 159, 433, 625, 435, 515,
    555, 550, 430, 516, 554, 434, 587, 632, 357, 633, 319, 318, 477, 840, 591, 397, 556, 629, 595,
    588, 396, 431, 841, 479, 358, 359, 436, 627, 478, 590, 626, 594, 635, 628, 517, 630, 398, 437,
    596, 399, 518, 631, 557, 519, 438, 842, 558, 439, 559, 598, 597, 634, 638, 636, 637, 599, 639,
    880,
)


MESH = pl.DeviceIdType.MESH
VMEM = pltpu.VMEM
LANE = 128


def remote(src, dst, send, recv, device):
    return pltpu.make_async_remote_copy(
        src_ref=src, dst_ref=dst, send_sem=send, recv_sem=recv, device_id=device, device_id_type=MESH
    )


class Place:
    def __init__(self, lines):
        blk, tp = lax.axis_index("blk"), lax.axis_index("tp")
        self.lines, self.tp = lines, tp
        self.z, self.y = tp // 2, tp % 2
        self.other = 1 - self.y
        self.across = (blk, self.z * 2 + self.other)
        self.right = (blk, jnp.minimum(self.z + 1, lines - 1) * 2 + self.y)
        self.left = (blk, jnp.maximum(self.z - 1, 0) * 2 + self.y)
        self.has_right, self.has_left = self.z < lines - 1, self.z > 0


def greet(*axes):
    place = {axis: lax.axis_index(axis) for axis in ("blk", "tp")}
    peers = 0
    for axis in axes:
        size = lax.axis_size(axis)
        for k in range(1, size):
            peer = dict(place)
            peer[axis] = (place[axis] + k) % size
            pl.semaphore_signal(
                pltpu.get_barrier_semaphore(),
                inc=1,
                device_id=(peer["blk"], peer["tp"]),
                device_id_type=MESH,
            )
        peers += size - 1
    pl.semaphore_wait(pltpu.get_barrier_semaphore(), peers)


class Scatter:
    def __init__(self, place, cut, part, across_a, line_a, line_b, across_b, send, recv):
        self.at, self.cut, self.part = place, cut, part
        self.across_a, self.line_a, self.line_b, self.across_b = across_a, line_a, line_b, across_b
        self.send, self.recv = send, recv

    @staticmethod
    def scratch(chunks, lines, rows, width, cut):
        return [
            VMEM((chunks, 2, lines, rows, width), jnp.bfloat16),
            VMEM((chunks, lines, rows, cut), jnp.bfloat16),
            VMEM((chunks, lines + 1, rows, cut), jnp.bfloat16),
            VMEM((chunks, lines + 1, 2, rows, width - cut), jnp.bfloat16),
            VMEM((chunks, rows, width - cut), jnp.bfloat16),
        ]

    @staticmethod
    def semaphores(chunks, lines):
        return [
            pltpu.SemaphoreType.DMA((chunks, 2 * lines + 2)),
            pltpu.SemaphoreType.DMA((chunks, 2 * lines + 4)),
        ]

    def low(self, c, j):
        return self.part.at[c, self.at.y, j, :, : self.cut]

    def high(self, c, j):
        return self.part.at[c, :, j, :, self.cut :]

    def copy_across_a(self, c):
        return remote(
            self.part.at[c, self.at.other, :, :, : self.cut],
            self.across_a.at[c],
            self.send.at[c, 0],
            self.recv.at[c, 0],
            self.at.across,
        )

    def copy_across_b(self, c):
        return remote(
            self.part.at[c, self.at.other, self.at.z, :, self.cut :],
            self.across_b.at[c],
            self.send.at[c, 1],
            self.recv.at[c, 1],
            self.at.across,
        )

    def copy_line(self, c, j, slot, device, first):
        lines = self.at.lines
        if first:
            source, target, send, recv = self.low(c, j), self.line_a, 2, 2
        else:
            source, target, send, recv = self.high(c, j), self.line_b, 2 + lines, 3 + lines
        return remote(
            source, target.at[c, slot], self.send.at[c, send + j], self.recv.at[c, recv + slot], device
        )

    def to_right(self, c, j, first):
        return self.copy_line(c, j, j + 1, self.at.right, first)

    def to_left(self, c, j, first):
        return self.copy_line(c, j, j, self.at.left, first)

    def take(self, c, j, slot, first):
        self.copy_line(c, j, slot, self.at.right, first).wait_recv()
        view = self.low(c, j) if first else self.high(c, j)
        came = (self.line_a if first else self.line_b)[c, slot]
        view[...] = (view[...].astype(jnp.float32) + came.astype(jnp.float32)).astype(jnp.bfloat16)

    def line_starts(self, c, first):
        lines = self.at.lines

        @pl.when(self.at.z == 0)
        def _():
            for j in range(lines - 1, 0, -1):
                self.to_right(c, j, first).start()

        @pl.when(self.at.z == lines - 1)
        def _():
            for j in range(lines - 1):
                self.to_left(c, j, first).start()

    def line_hop(self, c, step, first):
        lines = self.at.lines

        @pl.when(self.at.z == step)
        def _():
            for j in range(lines - 1, step, -1):
                self.take(c, j, j + 1, first)
                self.to_right(c, j, first).start()

        @pl.when(self.at.z == lines - 1 - step)
        def _():
            for j in range(lines - 1 - step):
                self.take(c, j, j, first)
                self.to_left(c, j, first).start()

    def line_end(self, c, total, first):
        z = self.at.z
        buffer = self.line_a if first else self.line_b

        @pl.when(self.at.has_left)
        def _():
            self.copy_line(c, z, z + 1, self.at.right, first).wait_recv()
            total[...] += buffer[c, z + 1].astype(jnp.float32)

        @pl.when(self.at.has_right)
        def _():
            self.copy_line(c, z, z, self.at.right, first).wait_recv()
            total[...] += buffer[c, z].astype(jnp.float32)

    def begin(self, c):
        self.copy_across_a(c).start()
        self.line_starts(c, False)

    def low_step(self, c, k):
        if k > 1:
            return self.line_hop(c, k - 1, True)
        self.copy_across_a(c).wait_recv()
        mine = self.part.at[c, self.at.y, :, :, : self.cut]
        mine[...] = (mine[...].astype(jnp.float32) + self.across_a[c].astype(jnp.float32)).astype(
            jnp.bfloat16
        )
        self.line_starts(c, True)

    def high_step(self, c, k, total_b):
        if k < self.at.lines - 1:
            return self.line_hop(c, k, False)
        mine = self.high(c, self.at.z)
        total_b[...] = mine[...].astype(jnp.float32)
        self.line_end(c, total_b, False)
        mine[...] = total_b[...].astype(jnp.bfloat16)
        self.copy_across_b(c).start()

    def finish(self, c, total):
        y, z = self.at.y, self.at.z
        low, high = total.at[:, : self.cut], total.at[:, self.cut :]
        low[...] = self.low(c, z)[...].astype(jnp.float32)
        self.line_end(c, low, True)
        self.copy_across_b(c).wait_recv()
        high[...] = self.part[c, y, z, :, self.cut :].astype(jnp.float32) + self.across_b[c].astype(
            jnp.float32
        )

    def drain(self, c):
        self.copy_across_a(c).wait_send()
        self.copy_across_b(c).wait_send()
        for first in (True, False):
            for j in range(self.at.lines):

                @pl.when(self.at.z != j)
                def _(j=j, first=first):
                    self.to_right(c, j, first).wait_send()


class Gather:
    def __init__(self, place, cut, own, full, local, send, recv):
        self.at, self.cut, self.own, self.full = place, cut, own, full
        self.local, self.send, self.recv = local, send, recv

    @staticmethod
    def scratch(chunks, lines):
        return [
            pltpu.SemaphoreType.DMA((chunks,)),
            pltpu.SemaphoreType.DMA((chunks, 5 * lines + 1)),
            pltpu.SemaphoreType.DMA((chunks, 3 * lines + 1)),
        ]

    def low(self, c, j):
        target = self.full.at[c, self.at.y, j, :, : self.cut]
        return target, target

    def copy_low(self, c, j, way, mine):
        lines = self.at.lines
        target = self.full.at[c, self.at.y, j, :, : self.cut]
        source = self.own(c).at[:, : self.cut] if mine else target
        device = (self.at.right, self.at.left, self.at.across)[way]
        recv = j + (lines if way == 2 else 0)
        return remote(source, target, self.send.at[c, way * lines + j], self.recv.at[c, recv], device)

    def copy_high(self, c, j, way):
        lines = self.at.lines
        view = self.full.at[c, :, j, :, self.cut :]
        device = (self.at.right, self.at.left)[way]
        return remote(
            view, view, self.send.at[c, (3 + way) * lines + j], self.recv.at[c, 2 * lines + j], device
        )

    def copy_high_across(self, c):
        lines = self.at.lines
        return remote(
            self.own(c).at[:, self.cut :],
            self.full.at[c, self.at.y, self.at.z, :, self.cut :],
            self.send.at[c, 5 * lines],
            self.recv.at[c, 3 * lines],
            self.at.across,
        )

    def copy_local(self, c):
        return pltpu.make_async_copy(
            self.own(c), self.full.at[c, self.at.y, self.at.z], self.local.at[c]
        )

    def begin(self, c):
        z = self.at.z
        if self.local is not None:
            self.copy_local(c).start()

        @pl.when(self.at.has_right)
        def _():
            self.copy_low(c, z, 0, True).start()

        @pl.when(self.at.has_left)
        def _():
            self.copy_low(c, z, 1, True).start()

        self.copy_high_across(c).start()
        self.copy_low(c, z, 2, True).start()

    def low_step(self, c, k):
        z, lines = self.at.z, self.at.lines

        @pl.when(z >= k)
        def _():
            self.copy_low(c, z - k, 0, False).wait_recv()

            @pl.when(self.at.has_right)
            def _():
                self.copy_low(c, z - k, 0, False).start()

            self.copy_low(c, z - k, 2, False).start()

        @pl.when(z + k < lines)
        def _():
            self.copy_low(c, z + k, 0, False).wait_recv()

            @pl.when(self.at.has_left)
            def _():
                self.copy_low(c, z + k, 1, False).start()

            self.copy_low(c, z + k, 2, False).start()

    def high_step(self, c, k):
        z, lines = self.at.z, self.at.lines
        if k == 0:
            if self.local is not None:
                self.copy_local(c).wait()
            self.copy_high_across(c).wait_recv()

            @pl.when(self.at.has_right)
            def _():
                self.copy_high(c, z, 0).start()

            @pl.when(self.at.has_left)
            def _():
                self.copy_high(c, z, 1).start()

            return

        @pl.when(z >= k)
        def _():
            self.copy_high(c, z - k, 0).wait_recv()

            @pl.when(self.at.has_right)
            def _():
                self.copy_high(c, z - k, 0).start()

        @pl.when(z + k < lines)
        def _():
            self.copy_high(c, z + k, 0).wait_recv()

            @pl.when(self.at.has_left)
            def _():
                self.copy_high(c, z + k, 1).start()

    def end(self, c):
        for j in range(self.at.lines):
            target = self.full.at[c, self.at.other, j, :, : self.cut]
            remote(
                target,
                target,
                self.send.at[c, 2 * self.at.lines + j],
                self.recv.at[c, self.at.lines + j],
                self.at.across,
            ).wait_recv()

    def drain(self, c):
        lines, z = self.at.lines, self.at.z
        self.copy_high_across(c).wait_send()
        for j in range(lines):

            @pl.when(self.at.has_right & (z >= j))
            def _(j=j):
                self.copy_low(c, j, 0, False).wait_send()
                self.copy_high(c, j, 0).wait_send()

            @pl.when(self.at.has_left & (z <= j))
            def _(j=j):
                self.copy_low(c, j, 1, False).wait_send()
                self.copy_high(c, j, 1).wait_send()

            self.copy_low(c, j, 2, False).wait_send()


class BlockScatter:
    def __init__(self, blocks, slice_of, part, own_hbm, from_chip, from_core, send, recv, sem_own):
        self.blk, self.tp = lax.axis_index("blk"), lax.axis_index("tp")
        self.chips, self.chip, self.core = blocks // 2, self.blk // 2, self.blk % 2
        self.slice_of, self.part = slice_of, part
        self.from_core, self.from_chip, self.send, self.recv = from_core, from_chip, send, recv
        self.put_own = pltpu.make_async_copy(part(self.blk), own_hbm, sem_own)

    @staticmethod
    def scratch(blocks, shape):
        chips = blocks // 2
        return [
            VMEM((chips,) + shape, jnp.bfloat16),
            pltpu.SemaphoreType.DMA((2, chips)),
            pltpu.SemaphoreType.DMA((2, chips)),
            pltpu.SemaphoreType.DMA(()),
        ]

    @staticmethod
    def outs(blocks, shape):
        return [
            jax.ShapeDtypeStruct(shape, jnp.bfloat16),
            jax.ShapeDtypeStruct((blocks // 2 - 1,) + shape, jnp.bfloat16),
        ]

    def to_core(self, k):
        return remote(
            self.part(k * 2 + 1 - self.core),
            self.from_core.at[k],
            self.send.at[0, k],
            self.recv.at[0, k],
            (self.chip * 2 + 1 - self.core, self.tp),
        )

    def to_chip(self, k):
        return remote(
            self.part(k * 2 + self.core),
            self.from_chip.at[(self.chip - k + self.chips) % self.chips - 1],
            self.send.at[1, k],
            self.recv.at[1, (self.chip - k + self.chips) % self.chips],
            (k * 2 + self.core, self.tp),
        )

    def came_chip(self, i):
        k = (self.chip + i) % self.chips
        return remote(
            self.part(k * 2 + self.core),
            self.from_chip.at[i - 1],
            self.send.at[1, k],
            self.recv.at[1, i],
            (k * 2 + self.core, self.tp),
        )

    def all_first(self):
        @pl.loop(0, self.chips)
        def _(i):
            self.first(i)

    def all_second(self):
        @pl.loop(0, self.chips)
        def _(i):
            self.second(i)

        self.put_own.start()

    def first(self, i):
        k = (self.chip + 1 + i) % self.chips
        self.slice_of(k * 2 + 1 - self.core, self.part(k * 2 + 1 - self.core))
        self.to_core(k).start()

    def second(self, i):
        k = (self.chip + 1 + i) % self.chips
        mine = self.part(k * 2 + self.core)
        self.slice_of(k * 2 + self.core, mine)
        self.to_core(k).wait_recv()
        mine[...] = (mine[...].astype(jnp.float32) + self.from_core[k].astype(jnp.float32)).astype(
            jnp.bfloat16
        )

        @pl.when(k != self.chip)
        def _():
            self.to_chip(k).start()

    def end(self):
        @pl.loop(1, self.chips)
        def _(i):
            self.came_chip(i).wait_recv()

        self.put_own.wait()
        self.drain()

    def drain(self):
        @pl.loop(0, self.chips)
        def _(k):
            self.to_core(k).wait_send()

            @pl.when(k != self.chip)
            def _():
                self.to_chip(k).wait_send()


class Loads:
    def __init__(self, sems, pairs):
        self.copies = [
            pltpu.make_async_copy(source, target, sems.at[i]) for i, (source, target) in enumerate(pairs)
        ]
        self.waited = set()
        for copy in self.copies:
            copy.start()

    def need(self, *which):
        for i in which:
            if i not in self.waited:
                self.waited.add(i)
                self.copies[i].wait()


class Tasks:
    def __init__(self):
        self.by_name = {}

    def add(self, name, phase, task):
        self.by_name[name, phase] = task

    def sum_and_share(self, phase, scatter, gather, total_b, finish):
        lines = scatter.at.lines
        for k in range(1, lines):
            self.add(f"A{k}", phase, functools.partial(scatter.low_step, k=k))
            self.add(f"B{k}", phase, functools.partial(scatter.high_step, k=k, total_b=total_b))
            self.add(f"l{k}", phase, functools.partial(gather.low_step, k=k))
        self.add("F", phase, finish)
        for k in range(lines):
            self.add(f"h{k}", phase, functools.partial(gather.high_step, k=k))
        self.add("E", phase, gather.end)

    def run(self, order):
        for name, phase, c in order:
            self.by_name[name, phase](c)


def in_turn(phase, lines, chunks):
    names = [f"{half}{k}" for k in range(1, lines) for half in "AB"] + ["F"]
    names += [f"l{k}" for k in range(1, lines)] + [f"h{k}" for k in range(lines)] + ["E"]
    return [(name, phase, c) for name in names for c in range(chunks)]


def unpack(order):
    return [(NAMES[code // 40], code // 8 % 5, code % 8) for code in order]


def rows_sum(values):
    return jnp.sum(values, axis=0, keepdims=True)


def mean_last(values):
    return jnp.mean(values, axis=-1, keepdims=True)


def dot_nn(a, b):
    return jnp.dot(a, b, preferred_element_type=jnp.float32)


def dot_nt(a, b):
    return lax.dot_general(a, b, (((1,), (1,)), ((), ())), preferred_element_type=jnp.float32)


def dot_tn(a, b):
    return lax.dot_general(a, b, (((0,), (0,)), ((), ())), preferred_element_type=jnp.float32)


def turn(values, cos_rows, sin_rows):
    return values * cos_rows + pltpu.roll(values, HD // 2, 1) * sin_rows


def front_tasks(
    tasks, batches, blocks, need_weights, lengths_ref, x_hbm, gain_ref, wq_ref, wk_ref, wv_ref, count_ref, width_ref, prob_ref,
    normed_hbm, query_ref, kv_hbm, heads_ref, ints_ref, floats_ref, cos_ref, sin_ref,
    x_mb, kv_own, kv_in, acc,
    sem_x, sem_normed, sem_own, sem_in, sem_send, sem_pass, sem_recv,
):
    blk, tp = lax.axis_index("blk"), lax.axis_index("tp")
    chips, chip, core = blocks // 2, blk // 2, blk % 2
    span, wide = x_hbm.shape[1], wq_ref.shape[1]
    heads = wide // HD
    scale = 1.0 / math.sqrt(HD)

    def slab(m):
        return pl.ds(pl.multiple_of(m * span, span), span)

    def get_x(m):
        return pltpu.make_async_copy(x_hbm.at[m], x_mb.at[m % 2], sem_x.at[m % 2])

    def put_normed(m):
        return pltpu.make_async_copy(x_mb.at[m % 2], normed_hbm.at[m], sem_normed.at[m % 2])

    def put_own(m):
        return pltpu.make_async_copy(kv_own.at[m], kv_hbm.at[m, blk], sem_own.at[m])

    def to_chip(m, k):
        return remote(
            kv_own.at[m], kv_hbm.at[m, blk], sem_send.at[m, k], sem_recv.at[m, blk], (k * 2 + core, tp)
        )

    def to_core(m):
        return remote(
            kv_own.at[m], kv_hbm.at[m, blk], sem_send.at[m, chip], sem_recv.at[m, blk], (chip * 2 + 1 - core, tp)
        )

    def pass_on(m, k):
        block = kv_hbm.at[m, k * 2 + core]
        return remote(
            block, block, sem_pass.at[m, k], sem_recv.at[m, k * 2 + core], (chip * 2 + 1 - core, tp)
        )

    def arrived(m, k):
        block = kv_hbm.at[m, k]
        return remote(block, block, sem_pass.at[m, 0], sem_recv.at[m, k], (blk, tp))

    def column(row):
        across = lax.broadcasted_iota(jnp.int32, (span, span), 1)
        down = lax.broadcasted_iota(jnp.int32, (span, span), 0)
        return jnp.sum(jnp.where(across == down, row.astype(jnp.float32), 0.0), axis=1, keepdims=True)

    def project(m):
        get_x(m).wait()
        if m + 1 < batches:
            if m >= 1:
                put_normed(m - 1).wait()
            get_x(m + 1).start()
        here = slab(m)
        x = x_mb[m % 2].astype(jnp.float32)
        scaled = x * lax.rsqrt(mean_last(x * x) + EPS)
        x_mb[m % 2] = (scaled * gain_ref[...]).astype(jnp.bfloat16)
        put_normed(m).start()
        rows = blk * span + lax.broadcasted_iota(jnp.int32, (span, 1), 0)
        begin, end = jnp.zeros((span, 1), jnp.int32), jnp.int32(0)
        for s in range(lengths_ref.shape[1]):
            length = lengths_ref[m, s]
            end = end + length
            begin = begin + jnp.where(rows >= end, length, 0)
        ints_ref[here, 0:1] = column(count_ref[m : m + 1, :]).astype(jnp.int32)
        ints_ref[here, 1:2] = column(width_ref[m : m + 1, :]).astype(jnp.int32)
        ints_ref[here, 2:3] = begin
        floats_ref[here, 0:1] = column(prob_ref[m : m + 1, :])
        lanes = lax.broadcasted_iota(jnp.int32, (1, HD), 1)
        half = HD // 2
        frequency = jnp.exp((lanes % half).astype(jnp.float32) * (-math.log(10000.0) / half))
        angles = (rows - begin).astype(jnp.float32) * frequency
        cos_rows = jnp.cos(angles)
        sin_rows = jnp.sin(angles) * jnp.where(lanes < half, -1.0, 1.0)
        cos_ref[here, :] = cos_rows
        sin_ref[here, :] = sin_rows
        normed = x_mb[m % 2]
        need_weights()
        query, key = dot_nn(normed, wq_ref[...]), dot_nn(normed, wk_ref[...])
        for h in range(heads):
            cols = slice(h * HD, (h + 1) * HD)
            query_ref[here, cols] = turn(query[:, cols], cos_rows, sin_rows).astype(jnp.bfloat16)
            kv_own[m, :, cols] = turn(key[:, cols], cos_rows, sin_rows).astype(jnp.bfloat16)
        kv_own[m, :, wide:] = dot_nn(normed, wv_ref[...]).astype(jnp.bfloat16)
        put_own(m).start()

        @pl.loop(chip + 1, chips)
        def _(k):
            to_chip(m, k).start()

        @pl.when(core == 0)
        def _():
            to_core(m).start()

    def pass_blocks(m):
        @pl.loop(0, chip)
        def _(k):
            arrived(m, k * 2 + core).wait_recv()
            pass_on(m, k).start()

    def get_kv(m, k):
        return pltpu.make_async_copy(kv_hbm.at[m, k], kv_in.at[k], sem_in.at[k])

    def attend(m):
        here = slab(m)
        q_rows = blk * span + lax.broadcasted_iota(jnp.int32, (span, span), 0)
        begin = ints_ref[here, 2:3]

        @pl.loop(0, blk)
        def _(k):
            @pl.when(k % 2 != core)
            def _():
                arrived(m, k).wait_recv()

            get_kv(m, k).start()

        def raw_scores(k, kv):
            k_rows = k * span + lax.broadcasted_iota(jnp.int32, (span, span), 1)
            allowed = (k_rows <= q_rows) & (k_rows >= begin)
            result = []
            for h in range(heads):
                cols = slice(h * HD, (h + 1) * HD)
                raw = dot_nt(query_ref[here, cols], kv[:, cols])
                result.append(jnp.where(allowed, raw * scale, NEG))
            return result

        def highest_of(k, kv):
            return tuple(functools.reduce(jnp.maximum, lane_tiles(score)) for score in raw_scores(k, kv))

        def weigh(k, kv, tops, sums):
            result, scores = [], raw_scores(k, kv)
            for h in range(heads):
                weights = jnp.exp(scores[h] - tops[h])
                result.append(sums[h] + sum(lane_tiles(weights)))
                acc[:, h * HD : (h + 1) * HD] += dot_nn(
                    weights.astype(jnp.bfloat16), kv[:, wide + h * HD : wide + (h + 1) * HD]
                )
            return tuple(result)

        highest = highest_of(blk, kv_own.at[m])

        def first(k, highest):
            get_kv(m, k).wait()
            return tuple(map(jnp.maximum, highest, highest_of(k, kv_in.at[k])))

        highest = lax.fori_loop(0, blk, first, highest)
        tops = [jnp.max(high, axis=-1, keepdims=True) for high in highest]
        acc[...] = jnp.zeros_like(acc)
        sums = weigh(blk, kv_own.at[m], tops, (jnp.zeros((span, LANE), jnp.float32),) * heads)
        sums = lax.fori_loop(0, blk, lambda k, sums: weigh(k, kv_in.at[k], tops, sums), sums)
        for h in range(heads):
            cols = slice(h * HD, (h + 1) * HD)
            row_sum = jnp.sum(sums[h], axis=-1, keepdims=True)
            floats_ref[here, 1 + h : 2 + h] = tops[h] + jnp.log(row_sum)
            heads_ref[here, cols] = jnp.where(
                tp * heads + h < ints_ref[here, 0:1], acc[:, cols] / row_sum, 0.0
            ).astype(jnp.bfloat16)

    def end():
        for m in range(batches):
            put_own(m).wait()
            if m >= batches - 2:
                put_normed(m).wait()

            @pl.loop(chip + 1, chips)
            def _(k):
                to_chip(m, k).wait_send()

            @pl.when(core == 0)
            def _():
                to_core(m).wait_send()

            @pl.loop(0, chip)
            def _(k):
                pass_on(m, k).wait_send()

    tasks.add("Q", 0, project)
    tasks.add("X", 0, pass_blocks)
    tasks.add("S", 0, attend)
    get_x(0).start()
    return end


def lane_tiles(values):
    return [values[:, i : i + LANE] for i in range(0, values.shape[1], LANE)]


def middle_kernel(
    lines, blocks, batches, chunks, chunk_rows, lengths_ref, tokens_hbm, x_hbm, grad_hbm, wq_hbm, wk_hbm, wv_hbm, wo_hbm, up_hbm,
    down_hbm, gain_ref, bias_ref, rms_ref, count_ref, width_ref, prob_ref, normed_hbm, kv_hbm, own_up, others_up, own_down, others_down, branch_hbm, feed_hbm, input_ref, resid_ref, sums_ref,
    query_ref, heads_ref, ints_ref, floats_ref, cos_ref, sin_ref,
    wq_ref, wk_ref, wv_ref, wo_ref, up_ref, down_ref, sem_load, x_own, g_own, g_all, own_branch, feed_part, lifted_ref, squared_ref, hidden_ref, normal_ref, inv_own, total,
    total_b, sem_in, sem_g, sem_feed, *rest,
):
    place = Place(lines)
    y, z, tp = place.y, place.z, place.tp
    spot = y * lines + z
    rows = chunk_rows // (2 * lines)
    width = gain_ref.shape[-1]
    units = up_ref.shape[1]
    s1, s2 = Scatter(place, CUT_SUM, *rest[:5], *rest[5:7]), Scatter(place, CUT_SUM, *rest[:5], *rest[7:9])
    a1 = Gather(place, CUT_SHARE, lambda c: lifted_ref.at[c, y, z], lifted_ref, None, *rest[10:12])
    a2 = Gather(place, CUT_SHARE, lambda c: own_branch.at[c], branch_hbm, *rest[12:15])
    share = width // blocks

    def up_slice(target, out):
        step = min(TILE, share)

        @pl.loop(0, share // step)
        def _(i):
            lanes = pl.ds(pl.multiple_of(target * share + i * step, step), step)
            lifted = lifted_ref[:, :, :, :, lanes].reshape(chunks * chunk_rows, step)
            out[pl.ds(pl.multiple_of(i * step, step), step), :] = dot_tn(lifted, hidden_ref[...]).astype(
                jnp.bfloat16
            )

    def down_slice(target, out):
        lanes = pl.ds(pl.multiple_of(target * share, share), share)

        @pl.loop(0, units // TILE)
        def _(i):
            cols = pl.ds(pl.multiple_of(i * TILE, TILE), TILE)
            grad = g_all[:, :, :, lanes].reshape(chunks * chunk_rows, share)
            out[cols, :] = dot_tn(squared_ref[:, cols], grad).astype(jnp.bfloat16)

    grad_up = BlockScatter(
        blocks, up_slice, lambda k: up_ref.at[pl.ds(pl.multiple_of(k * share, share), share), :], own_up, others_up,
        *rest[15:19],
    )
    grad_down = BlockScatter(
        blocks, down_slice, lambda k: down_ref.at[:, pl.ds(pl.multiple_of(k * share, share), share)], own_down, others_down,
        *rest[19:23],
    )

    get_x = pltpu.make_async_copy(tokens_hbm.at[:, spot], x_own, sem_in.at[0])
    get_g = pltpu.make_async_copy(grad_hbm.at[:, spot], g_own, sem_in.at[1])
    tasks = Tasks()
    front_end = front_tasks(
        tasks, batches, blocks, lambda: loads.need(0, 1, 2), lengths_ref, x_hbm, rms_ref, wq_ref, wk_ref, wv_ref, count_ref,
        width_ref, prob_ref, normed_hbm, query_ref, kv_hbm, heads_ref, ints_ref, floats_ref, cos_ref, sin_ref, *rest[23:],
    )
    sources = (wq_hbm, wk_hbm, wv_hbm, wo_hbm, up_hbm, down_hbm)
    loads = Loads(sem_load, list(zip(sources, (wq_ref, wk_ref, wv_ref, wo_ref, up_ref, down_ref), strict=True)))
    for copy in (get_x, get_g):
        copy.start()

    def get_grad(c):
        return pltpu.make_async_copy(grad_hbm.at[c], g_all.at[c], sem_g.at[c])

    def put_feed(c):
        return pltpu.make_async_copy(feed_part.at[c % FEED], feed_hbm.at[c], sem_feed.at[c])

    @pl.loop(0, chunks)
    def _(c):
        get_grad(c).start()

    greet("tp", "blk")
    sums_ref[...] = jnp.zeros_like(sums_ref)

    def own_rows(c):
        return pl.ds(pl.multiple_of(c * chunk_rows + spot * rows, rows), rows)

    def all_rows(c):
        return pl.ds(pl.multiple_of(c * chunk_rows, chunk_rows), chunk_rows)

    def tiled(n, body):
        @pl.loop(0, n // TILE)
        def _(i):
            body(pl.ds(pl.multiple_of(i * TILE, TILE), TILE))

    def put(part, c, cols, values):
        n = values.shape[0] // chunk_rows
        part[c : c + n, :, :, :, cols] = values.astype(jnp.bfloat16).reshape(n, 2, lines, rows, TILE)

    def project(c):
        loads.need(3)
        heads = heads_ref[all_rows(c), :]

        def one(cols):
            put(s1.part, c, cols, dot_nn(heads, wo_ref[:, cols]))

        tiled(width, one)
        s1.begin(c)

    first_norms = [get_x.wait, get_g.wait]

    def norm(c):
        while first_norms:
            first_norms.pop()()
        s1.finish(c, total)
        residual = x_own[c].astype(jnp.float32) + total[...]
        center = residual - mean_last(residual)
        inv_std = lax.rsqrt(mean_last(center * center) + EPS)
        normal = center * inv_std
        input_ref[c] = residual
        normal_ref[c] = normal
        inv_own[c] = jnp.broadcast_to(inv_std, (rows, LANE))
        lifted_ref[c, y, z] = (normal * gain_ref[...] + bias_ref[...]).astype(jnp.bfloat16)
        a1.begin(c)

    def feed(c):
        group = range(c, c + FEED)
        loads.need(4, 5)
        for i in group:
            a1.end(i)
            s1.drain(i)
            get_grad(i).wait()
        size = FEED * chunk_rows
        lifted = lifted_ref[c : c + FEED].reshape(size, width)
        span = pl.ds(c * chunk_rows, size)
        prob, limit = floats_ref[span, 0:1], (ints_ref[span, 1:2] + 1) * (FF // 4)
        g_all[c : c + FEED] = (
            g_all[c : c + FEED].astype(jnp.float32) * prob.reshape(FEED, 2 * lines, rows, 1)
        ).astype(jnp.bfloat16)

        def units_of(cols):
            active = jnp.maximum(dot_nn(lifted, up_ref[:, cols]), 0.0)
            ids = tp * units + cols.start + lax.broadcasted_iota(jnp.int32, (size, TILE), 1)
            mask = (ids < limit).astype(jnp.float32)
            squared_ref[span, cols] = (active * active * mask).astype(jnp.bfloat16)
            back = dot_nt(g_all[c : c + FEED].reshape(size, width), down_ref[cols, :])
            hidden_ref[span, cols] = (back * mask * 2.0 * active).astype(jnp.bfloat16)

        tiled(units, units_of)
        hidden = hidden_ref[span, :]

        def lift(cols):
            put(s2.part, c, cols, dot_nt(hidden, up_ref[cols, :]))

        tiled(width, lift)
        for i in group:
            s2.begin(i)
        squared = squared_ref[span, :]
        if c > 0:
            for i in range(FEED):
                put_feed(c - FEED + i).wait()

        def out(cols):
            put(feed_part, 0, cols, dot_nn(squared, down_ref[:, cols]))

        tiled(width, out)
        for i in group:
            put_feed(i).start()

    def norm_back(c):
        s2.finish(c, total)
        grad_lifted, normal = total[...], normal_ref[c]
        sums_ref[0:1, :] += rows_sum(grad_lifted * normal)
        sums_ref[1:2, :] += rows_sum(grad_lifted)
        g = grad_lifted * gain_ref[...]
        grad_resid = g_own[c].astype(jnp.float32) + inv_own[c][:, 0:1] * (
            g - mean_last(g) - normal * mean_last(g * normal)
        )
        resid_ref[c] = grad_resid
        own_branch[c] = grad_resid.astype(jnp.bfloat16)
        a2.begin(c)

    tasks.add("P", 1, project)
    tasks.sum_and_share(1, s1, a1, total_b, norm)
    tasks.add("P", 2, feed)
    tasks.sum_and_share(2, s2, a2, total_b, norm_back)
    steps = (grad_up.all_first, grad_down.all_first, grad_up.all_second, grad_down.all_second)
    tasks.add("W", 0, lambda k: steps[k]())
    tasks.add("Z", 0, lambda k: None)
    tasks.run(middle_order(lines, chunks, batches))
    front_end()

    for c in range(chunks - FEED, chunks):
        put_feed(c).wait()

    @pl.loop(0, chunks)
    def _(c):
        for part in (s2, a1, a2):
            part.drain(c)

    grad_up.end()
    grad_down.end()


def middle_order(lines, chunks, batches):
    if (lines, chunks, batches) == (4, 8, 4):
        return unpack(MIDDLE_ORDER)
    order = [(name, 0, m) for name in "QXS" for m in range(batches)]
    order += [("P", 1, c) for c in range(chunks)] + in_turn(1, lines, chunks)[:-chunks]
    order += [("P", 2, c) for c in range(0, chunks, FEED)] + in_turn(2, lines, chunks)
    return order + [("W", 0, k) for k in range(4)]


def middle(tokens, lengths, head_count, width_index, router_prob, norm_gain, w_query, w_key, w_value, grad_out, w_out,
           ln_gain, ln_bias, w_up, w_down):
    lines, blocks = lax.axis_size("tp") // 2, lax.axis_size("blk")
    batches, span, width = tokens.shape
    count, units, wide = batches * span, w_up.shape[1], w_query.shape[1]
    heads = wide // HD
    chunk_rows = CHUNK_ROWS
    chunks, rows = count // chunk_rows, chunk_rows // (2 * lines)
    share = width // blocks
    split = (chunks, 2 * lines, rows, width)
    full = (chunks, 2, lines, rows, width)
    any_space, vmem = pl.BlockSpec(memory_space=pl.ANY), pl.BlockSpec(memory_space=VMEM)
    bf16, f32 = jnp.bfloat16, jnp.float32
    dma = pltpu.SemaphoreType.DMA
    loads = (w_query, w_key, w_value, w_out, w_up, w_down)
    outs = pl.pallas_call(
        functools.partial(middle_kernel, lines, blocks, batches, chunks, chunk_rows),
        out_shape=[
            jax.ShapeDtypeStruct((batches, span, width), bf16),
            jax.ShapeDtypeStruct((batches, blocks, span, 2 * wide), bf16),
            *BlockScatter.outs(blocks, (share, units)),
            *BlockScatter.outs(blocks, (units, share)),
            jax.ShapeDtypeStruct(full, bf16),
            jax.ShapeDtypeStruct(full, bf16),
            jax.ShapeDtypeStruct((chunks, rows, width), f32),
            jax.ShapeDtypeStruct((chunks, rows, width), f32),
            jax.ShapeDtypeStruct((2, width), f32),
            jax.ShapeDtypeStruct((count, wide), bf16),
            jax.ShapeDtypeStruct((count, wide), bf16),
            jax.ShapeDtypeStruct((count, 3), jnp.int32),
            jax.ShapeDtypeStruct((count, 1 + heads), f32),
            jax.ShapeDtypeStruct((count, HD), f32),
            jax.ShapeDtypeStruct((count, HD), f32),
        ],
        in_specs=[pl.BlockSpec(memory_space=pltpu.SMEM)] + [any_space] * 9 + [vmem] * 6,
        out_specs=[any_space] * 8 + [vmem] * 9,
        scratch_shapes=[VMEM(load.shape, bf16) for load in loads]
        + [
            dma((len(loads),)),
            VMEM((chunks, rows, width), bf16),
            VMEM((chunks, rows, width), bf16),
            VMEM(split, bf16),
            VMEM((chunks, rows, width), bf16),
            VMEM((FEED,) + full[1:], bf16),
            VMEM(full, bf16),
            VMEM((count, units), bf16),
            VMEM((count, units), bf16),
            VMEM((chunks, rows, width), f32),
            VMEM((chunks, rows, LANE), f32),
            VMEM((rows, width), f32),
            VMEM((2, rows, width - CUT_SUM), f32),
            dma((2,)),
            dma((chunks,)),
            dma((chunks,)),
        ]
        + Scatter.scratch(chunks, lines, rows, width, CUT_SUM)
        + Scatter.semaphores(chunks, lines) * 2
        + Gather.scratch(chunks, lines) * 2
        + BlockScatter.scratch(blocks, (share, units))
        + BlockScatter.scratch(blocks, (units, share))
        + [
            VMEM((2, span, width), bf16),
            VMEM((batches, span, 2 * wide), bf16),
            VMEM((blocks, span, 2 * wide), bf16),
            VMEM((span, wide), f32),
            dma((2,)),
            dma((2,)),
            dma((batches,)),
            dma((blocks,)),
            dma((batches, blocks // 2)),
            dma((batches, blocks // 2)),
            dma((batches, blocks)),
        ],
        compiler_params=pltpu.CompilerParams(
            collective_id=1, has_side_effects=True, vmem_limit_bytes=VMEM_LIMIT
        ),
        cost_estimate=pl.CostEstimate(
            flops=2 * count * width * (4 * wide + 6 * units), bytes_accessed=40 * 2**20, transcendentals=0
        ),
    )(
        lengths, tokens.reshape(split), tokens, grad_out.reshape(split), *loads, ln_gain[None], ln_bias[None],
        norm_gain[None], head_count, width_index, router_prob,
    )
    return outs


def turn_back(grad, cos_rows, sin_rows):
    return grad * cos_rows - pltpu.roll(grad, HD // 2, 1) * sin_rows


def back_kernel(
    lines, blocks, batches, chunks, chunk_rows, tokens_hbm, kv_hbm, feed_hbm, branch_hbm, normed_hbm,
    input_hbm, resid_hbm, query_hbm, heads_hbm, wq_hbm, wk_hbm, wv_hbm, wo_hbm, cos_hbm, sin_hbm, floats_hbm,
    ints_ref, gain_ref, sums_ref, mixed_hbm, in_hbm, own_w, others_w, own_o, others_o,
    small_ref,
    input_ref, resid_ref, query_ref, heads_ref, wq_ref, wk_ref, wv_ref, wo_ref, cos_ref, sin_ref, floats_ref, sem_load,
    branch_ref, x_own, own_in, own_mixed, kv_mb, grad_mb, delta_mb, dq_mb, stage, own, came, pre, total, total_b,
    grad_w, small, small_blk, small_part, small_tp, sem_in, sem_branch, sem_feed, sem_kv, sem_send, sem_recv, sem_free, sem_blk, sem_tp,
    *rest,
):
    place = Place(lines)
    blk, tp, y, z = lax.axis_index("blk"), place.tp, place.y, place.z
    spot = y * lines + z
    rows = chunk_rows // (2 * lines)
    width = gain_ref.shape[-1]
    wide = query_ref.shape[1]
    heads = wide // HD
    span = query_ref.shape[0] // batches
    per = span // chunk_rows
    scale = 1.0 / math.sqrt(HD)
    s3, s4 = Scatter(place, CUT_SUM, *rest[0:7]), Scatter(place, CUT_SUM, *rest[7:14])
    a3 = Gather(place, CUT_SHARE_BACK, lambda c: own_mixed.at[c], mixed_hbm, *rest[14:17])
    a4 = Gather(place, CUT_SHARE_BACK, lambda c: own_in.at[c], in_hbm, *rest[17:20])

    get_x = pltpu.make_async_copy(tokens_hbm.at[:, spot], x_own, sem_in)
    get_x.start()

    def get_kv(step):
        source = kv_hbm.at[step // (blk + 1), step % (blk + 1)]
        return pltpu.make_async_copy(source, kv_mb.at[step % 2], sem_kv.at[step % 2])

    def get_feed(c):
        return pltpu.make_async_copy(feed_hbm.at[c], s3.part.at[c], sem_feed.at[c])

    def slab(m):
        return pl.ds(pl.multiple_of(m * span, span), span)

    ring = stage.shape[0]

    def get_branch(m):
        return pltpu.make_async_copy(branch_hbm.at[slab(m), :], branch_ref.at[slab(m), :], sem_branch.at[m])

    get_normed = pltpu.make_async_copy(normed_hbm, branch_ref, sem_branch.at[batches])
    waited = set()

    def need_branch(*which):
        for m in which:
            if m not in waited:
                waited.add(m)
                get_branch(m).wait()

    def to_owner(m, k):
        slot = (m * blk + k) % ring
        return remote(
            stage.at[slot], came.at[m % 2, blk], sem_send.at[slot], sem_recv.at[m % 2, blk], (k, tp)
        )

    def from_peer(m, k):
        return remote(stage.at[0], came.at[m % 2, k], sem_send.at[0], sem_recv.at[m % 2, k], (k, tp))

    def attend_back(m):
        need_branch(m)
        loads.need(*attend_loads)
        here = slab(m)
        grad = dot_nt(branch_ref[here, :], wo_ref[...]).astype(jnp.bfloat16)
        for h in range(heads):
            cols = slice(h * HD, (h + 1) * HD)
            head = tp * heads + h
            masked = jnp.where(head < ints_ref[here, 0:1], grad[:, cols].astype(jnp.float32), 0.0)
            grad_mb[:, cols] = masked.astype(jnp.bfloat16)
            delta = jnp.sum(masked * heads_ref[here, cols].astype(jnp.float32), axis=-1, keepdims=True)
            delta_mb[h] = jnp.broadcast_to(delta, (span, LANE))
        dq_mb[...] = jnp.zeros_like(dq_mb)
        q_rows = blk * span + lax.broadcasted_iota(jnp.int32, (span, span), 0)
        begin = ints_ref[here, 2:3]

        def pairs(k, out):
            step = m * (blk + 1) + k
            get_kv(step).wait()

            @pl.when(step + 1 < batches * (blk + 1))
            def _():
                get_kv(step + 1).start()

            k_rows = k * span + lax.broadcasted_iota(jnp.int32, (span, span), 1)
            allowed = (k_rows <= q_rows) & (k_rows >= begin)
            for h in range(heads):
                cols = slice(h * HD, (h + 1) * HD)
                q, g = query_ref[here, cols], grad_mb[:, cols]
                key = kv_mb[step % 2, :, cols]
                value = kv_mb[step % 2, :, wide + h * HD : wide + (h + 1) * HD]
                raw = dot_nt(q, key)
                prob = jnp.where(allowed, jnp.exp(raw * scale - floats_ref[here, 1 + h : 2 + h]), 0.0)
                grad_prob = dot_nt(g, value)
                grad_score = (prob * (grad_prob - delta_mb[h][:, 0:1]) * scale).astype(jnp.bfloat16)
                dq_mb[:, cols] += dot_nn(grad_score, key)
                out[:, cols] = dot_tn(grad_score, q).astype(jnp.bfloat16)
                out[:, wide + h * HD : wide + (h + 1) * HD] = dot_tn(prob.astype(jnp.bfloat16), g).astype(
                    jnp.bfloat16
                )

        @pl.loop(0, blk)
        def _(k):
            sent = m * blk + k

            @pl.when(sent >= ring)
            def _():
                to_owner((sent - ring) // blk, (sent - ring) % blk).wait_send()

            pairs(k, stage.at[sent % ring])

            @pl.when(m >= 2)
            def _():
                pl.semaphore_wait(sem_free.at[k], 1)

            to_owner(m, k).start()

        pairs(blk, own.at[m % 2])
        if m == batches - 1:
            get_normed.start()
        for h in range(heads):
            cols = slice(h * HD, (h + 1) * HD)
            pre[here, cols] = turn_back(dq_mb[:, cols], cos_ref[here, :], sin_ref[here, :]).astype(
                jnp.bfloat16
            )

    def gather_kv(m):
        here = slab(m)
        grad_w[...] = own[m % 2].astype(jnp.float32)

        @pl.loop(blk + 1, blocks)
        def _(k):
            from_peer(m, k).wait_recv()
            grad_w[...] += came[m % 2, k].astype(jnp.float32)

            @pl.when(m + 2 < batches)
            def _():
                pl.semaphore_signal(sem_free.at[blk], inc=1, device_id=(k, tp), device_id_type=MESH)

        for h in range(heads):
            cols = slice(h * HD, (h + 1) * HD)
            pre[here, wide + h * HD : wide + (h + 1) * HD] = turn_back(
                grad_w[:, cols], cos_ref[here, :], sin_ref[here, :]
            ).astype(jnp.bfloat16)
        pre[here, 2 * wide :] = grad_w[:, wide:].astype(jnp.bfloat16)

    def spread(c):
        loads.need(*spread_loads)
        here = pl.ds(pl.multiple_of(c * chunk_rows, chunk_rows), chunk_rows)

        @pl.loop(0, width // TILE)
        def _(i):
            cols = pl.ds(pl.multiple_of(i * TILE, TILE), TILE)
            grad = dot_nt(pre[here, :wide], wq_ref[cols, :])
            grad += dot_nt(pre[here, wide : 2 * wide], wk_ref[cols, :])
            grad += dot_nt(pre[here, 2 * wide :], wv_ref[cols, :])
            s4.part[c, :, :, :, cols] = grad.astype(jnp.bfloat16).reshape(2, lines, rows, TILE)

        s4.begin(c)

    def feed(c):
        get_feed(c).wait()
        s3.begin(c)

    def mix(c):
        loads.need(*mix_loads)
        s3.finish(c, total)
        prob = floats_ref[pl.ds(pl.multiple_of(c * chunk_rows + spot * rows, rows), rows), 0:1]
        own_mixed[c] = (input_ref[c] + prob * total[...]).astype(jnp.bfloat16)
        a3.begin(c)

    def last(c):
        loads.need(*last_loads)
        s4.finish(c, total)
        grad_normed, x = total[...], x_own[c].astype(jnp.float32)
        inv_rms = lax.rsqrt(mean_last(x * x) + EPS)
        scaled = x * inv_rms
        small[0:1, :] += rows_sum(grad_normed * scaled)
        s = grad_normed * gain_ref[...]
        grad_in = resid_ref[c] + inv_rms * (s - scaled * mean_last(s * scaled))
        own_in[c] = grad_in.astype(jnp.bfloat16)
        a4.begin(c)

    share = width // blocks

    def slice_of(target, out):
        step = min(TILE, share)

        @pl.loop(0, share // step)
        def _(i):
            lanes = pl.ds(pl.multiple_of(target * share + i * step, step), step)
            grad = dot_tn(branch_ref[:, lanes], pre[...]).astype(jnp.bfloat16)
            for k in range(3):
                out[k, pl.ds(pl.multiple_of(i * step, step), step), :] = grad[:, k * wide : (k + 1) * wide]

    def out_slice(target, out):
        lanes = pl.ds(pl.multiple_of(target * share, share), share)
        out[...] = dot_tn(heads_ref[...], branch_ref[:, lanes]).astype(jnp.bfloat16)

    part, out_part = rest[20], rest[25]
    weights = BlockScatter(blocks, slice_of, lambda k: part.at[k], own_w, others_w, *rest[21:25])
    out_weights = BlockScatter(blocks, out_slice, lambda k: out_part.at[k], own_o, others_o, *rest[26:30])
    ranks = 2 * lines

    def small_to_blk(k):
        peer = (blk + k) % blocks
        lanes = pl.ds(pl.multiple_of(peer * share, share), share)
        return remote(
            small.at[:, lanes], small_blk.at[k - 1], sem_blk.at[0, k], sem_blk.at[1, k], (peer, tp)
        )

    def small_to_tp(k):
        return remote(
            small_part, small_tp.at[k - 1], sem_tp.at[0, k], sem_tp.at[1, k], (blk, (tp + k) % ranks)
        )

    def small_first():
        for k in range(1, blocks):
            small_to_blk(k).start()

    def small_second():
        small_part[...] = small[:, pl.ds(pl.multiple_of(blk * share, share), share)]
        for k in range(1, blocks):
            small_to_blk(k).wait()
            small_part[...] += small_blk[k - 1]
        for k in range(1, ranks):
            small_to_tp(k).start()

    def small_third():
        small_ref[...] = small_part[...]
        for k in range(1, ranks):
            small_to_tp(k).wait()
            small_ref[...] += small_tp[k - 1]

    get_branch(0).start()
    attend_loads, mix_loads, last_loads, spread_loads = (2, 3, 7, 8, 9, 10), (0, 10), (1,), (4, 5, 6)
    refs = (input_ref, resid_ref, query_ref, heads_ref, wq_ref, wk_ref, wv_ref, wo_ref, cos_ref, sin_ref, floats_ref)
    sources = (
        input_hbm, resid_hbm, query_hbm, heads_hbm, wq_hbm, wk_hbm, wv_hbm, wo_hbm, cos_hbm, sin_hbm, floats_hbm,
    )
    loads = Loads(sem_load, list(zip(sources, refs, strict=True)))
    for m in range(1, batches):
        get_branch(m).start()

    @pl.loop(0, chunks)
    def _(c):
        get_feed(c).start()

    get_kv(0).start()
    greet("tp", "blk")
    get_x.wait()
    small[...] = jnp.zeros_like(small)
    small[1:3, :] = sums_ref[...]

    tasks = Tasks()
    tasks.add("P", 3, feed)
    tasks.sum_and_share(3, s3, a3, total_b, mix)
    tasks.add("T", 0, attend_back)
    tasks.add("K", 0, gather_kv)
    tasks.add("P", 4, spread)
    tasks.sum_and_share(4, s4, a4, total_b, last)

    def out_gradient(k):
        need_branch(*range(batches))
        loads.need(3)
        (out_weights.all_first, out_weights.all_second)[k]()

    def weight_gradients(k):
        if k == 0:
            get_normed.wait()
        (weights.all_first, weights.all_second)[k]()

    tasks.add("O", 0, out_gradient)
    tasks.add("V", 0, weight_gradients)
    tasks.add("M", 0, lambda k: (small_first, small_second, small_third)[k]())
    tasks.add("Z", 0, lambda k: None)
    tasks.run(back_order(lines, chunks, batches))

    @pl.loop(0, chunks)
    def _(c):
        for phase in (s3, s4, a3, a4):
            phase.drain(c)

    @pl.loop(jnp.maximum(batches * blk - ring, 0), batches * blk)
    def _(sent):
        to_owner(sent // blk, sent % blk).wait_send()

    weights.end()
    out_weights.end()


def back_order(lines, chunks, batches):
    if (lines, chunks, batches) == (4, 8, 4):
        return unpack(BACK_ORDER)
    order = [("O", 0, 0), ("O", 0, 1)] + [("P", 3, c) for c in range(chunks)] + in_turn(3, lines, chunks)
    order += [(name, 0, m) for m in range(batches) for name in "TK"]
    order += [("V", 0, 0), ("V", 0, 1)] + [("P", 4, c) for c in range(chunks)] + in_turn(4, lines, chunks)
    return order + [("M", 0, k) for k in range(3)]


def back(tokens, kv, feed_part, grad_branch, normed, own_input, own_resid, query, heads_out, w_query, w_key, w_value,
         w_out, norm_gain, ints, floats, cos_rows, sin_rows, ln_sums):
    lines, blocks = lax.axis_size("tp") // 2, lax.axis_size("blk")
    count, width = tokens.shape
    batches, wide = kv.shape[0], query.shape[1]
    chunk_rows = CHUNK_ROWS
    chunks, rows = count // chunk_rows, chunk_rows // (2 * lines)
    span = count // batches
    heads = wide // HD
    share = width // blocks
    any_space, vmem = pl.BlockSpec(memory_space=pl.ANY), pl.BlockSpec(memory_space=VMEM)
    bf16, f32 = jnp.bfloat16, jnp.float32
    dma = pltpu.SemaphoreType.DMA
    full = (chunks, 2, lines, rows, width)
    loads = (
        own_input, own_resid, query, heads_out, w_query, w_key, w_value, w_out, cos_rows, sin_rows, floats,
    )
    outs = pl.pallas_call(
        functools.partial(back_kernel, lines, blocks, batches, chunks, chunk_rows),
        out_shape=[jax.ShapeDtypeStruct(full, bf16)] * 2
        + BlockScatter.outs(blocks, (3, share, wide))
        + BlockScatter.outs(blocks, (wide, share))
        + [jax.ShapeDtypeStruct((8, share), f32)],
        in_specs=[any_space] * 16 + [vmem] * 3,
        out_specs=[any_space] * 6 + [vmem],
        scratch_shapes=[VMEM(load.shape, load.dtype) for load in loads]
        + [
            dma((len(loads),)),
            VMEM((count, width), bf16),
            VMEM((chunks, rows, width), bf16),
            VMEM((chunks, rows, width), bf16),
            VMEM((chunks, rows, width), bf16),
            VMEM((2, span, 2 * wide), bf16),
            VMEM((span, wide), bf16),
            VMEM((heads, span, LANE), f32),
            VMEM((span, wide), f32),
            VMEM((RING, span, 2 * wide), bf16),
            VMEM((2, span, 2 * wide), bf16),
            VMEM((2, blocks, span, 2 * wide), bf16),
            VMEM((count, 3 * wide), bf16),
            VMEM((rows, width), f32),
            VMEM((2, rows, width - CUT_SUM), f32),
            VMEM((span, 2 * wide), f32),
            VMEM((8, width), f32),
            VMEM((blocks - 1, 8, share), f32),
            VMEM((8, share), f32),
            VMEM((2 * lines - 1, 8, share), f32),
            dma(()),
            dma((batches + 1,)),
            dma((chunks,)),
            dma((2,)),
            dma((RING,)),
            dma((2, blocks)),
            pltpu.SemaphoreType.REGULAR((blocks,)),
            dma((2, blocks)),
            dma((2, 2 * lines)),
        ]
        + (Scatter.scratch(chunks, lines, rows, width, CUT_SUM) + Scatter.semaphores(chunks, lines)) * 2
        + Gather.scratch(chunks, lines) * 2
        + [VMEM((blocks, 3, share, wide), bf16)]
        + BlockScatter.scratch(blocks, (3, share, wide))
        + [VMEM((blocks, wide, share), bf16)]
        + BlockScatter.scratch(blocks, (wide, share)),
        compiler_params=pltpu.CompilerParams(
            collective_id=2, has_side_effects=True, vmem_limit_bytes=VMEM_LIMIT
        ),
        cost_estimate=pl.CostEstimate(
            flops=2 * count * width * wide * 7, bytes_accessed=40 * 2**20, transcendentals=0
        ),
    )(
        tokens.reshape(chunks, 2 * lines, rows, width), kv, feed_part, grad_branch, normed, *loads, ints,
        norm_gain[None], ln_sums,
    )
    return outs


def finish_kernel(pairs, copies, *refs):
    ins, refs = refs[: 2 * pairs + copies + 1], refs[2 * pairs + copies + 1 :]
    outs, scratch = refs[: pairs + copies + 5], refs[pairs + copies + 5 :]
    own, others, results = scratch[:pairs], scratch[pairs : 2 * pairs], scratch[2 * pairs : 3 * pairs]
    held = scratch[3 * pairs : 3 * pairs + copies]
    sem_load, sem_copy, sem_store = scratch[3 * pairs + copies :]
    loads = []
    for i in range(pairs):
        loads.append(pltpu.make_async_copy(ins[2 * i], own[i], sem_load.at[2 * i]))
        loads.append(pltpu.make_async_copy(ins[2 * i + 1], others[i], sem_load.at[2 * i + 1]))
    for load in loads:
        load.start()
    moves = []
    for i in range(copies):
        source, target = ins[2 * pairs + i], outs[pairs + 2 + i]
        moves += [
            (
                pltpu.make_async_copy(source.at[m], held[i].at[m], sem_copy.at[0, i, m]),
                pltpu.make_async_copy(held[i].at[m], target.at[m], sem_copy.at[1, i, m]),
            )
            for m in range(source.shape[0])
        ]
    for come, _ in moves:
        come.start()
    sums = ins[-1]
    for i in range(3):
        outs[pairs + 2 + copies + i][...] = sums[i : i + 1, :]
    stores = [go for _, go in moves]
    for come, go in moves[: len(moves) // 2]:
        come.wait()
        go.start()
    for i in range(pairs):
        loads[2 * i].wait()
        loads[2 * i + 1].wait()
        total = own[i][...].astype(jnp.float32)
        for k in range(others[i].shape[0]):
            total += others[i][k].astype(jnp.float32)
        results[i][...] = total
        targets = [(results[0].at[k], outs[k]) for k in range(3)] if i == 0 else [(results[i], outs[i + 2])]
        for k, (source, target) in enumerate(targets):
            stores.append(pltpu.make_async_copy(source, target, sem_store.at[k if i == 0 else i + 2]))
            stores[-1].start()
    for come, go in moves[len(moves) // 2 :]:
        come.wait()
        go.start()
    for copy in stores:
        copy.wait()


def finish(pairs, copies, sums):
    any_space, vmem = pl.BlockSpec(memory_space=pl.ANY), pl.BlockSpec(memory_space=VMEM)
    f32, share = jnp.float32, sums.shape[1]
    dma = pltpu.SemaphoreType.DMA
    return pl.pallas_call(
        functools.partial(finish_kernel, len(pairs), len(copies)),
        out_shape=[jax.ShapeDtypeStruct(pairs[0][0].shape[1:], f32)] * 3
        + [jax.ShapeDtypeStruct(own.shape, f32) for own, _ in pairs[1:]]
        + [jax.ShapeDtypeStruct(copy.shape, copy.dtype) for copy in copies]
        + [jax.ShapeDtypeStruct((1, share), f32)] * 3,
        in_specs=[any_space] * (2 * len(pairs) + len(copies)) + [vmem],
        out_specs=[any_space] * (len(pairs) + 2 + len(copies)) + [vmem] * 3,
        scratch_shapes=[VMEM(own.shape, own.dtype) for own, _ in pairs]
        + [VMEM(others.shape, others.dtype) for _, others in pairs]
        + [VMEM(own.shape, f32) for own, _ in pairs]
        + [VMEM(copy.shape, copy.dtype) for copy in copies]
        + [dma((2 * len(pairs),)), dma((2, len(copies), copies[0].shape[0])), dma((len(pairs) + 2,))],
        compiler_params=pltpu.CompilerParams(vmem_limit_bytes=VMEM_LIMIT),
        cost_estimate=pl.CostEstimate(flops=0, bytes_accessed=28 * 2**20, transcendentals=0),
    )(*[array for pair in pairs for array in pair], *copies, sums)


def local(
    tokens,
    lengths,
    head_count,
    width_index,
    router_prob,
    norm_gain,
    w_query,
    w_key,
    w_value,
    w_out,
    ln_gain,
    ln_bias,
    w_up,
    w_down,
    grad_out,
):
    batches, rows_dev, features = tokens.shape
    count = batches * rows_dev
    (
        normed, kv, own_up, others_up, own_down, others_down, grad_branch, feed_part, own_input, own_resid, ln_sums,
        query, heads_out, ints, floats, cos_rows, sin_rows,
    ) = middle(
        tokens, lengths, head_count, width_index, router_prob, norm_gain, w_query, w_key, w_value,
        grad_out.reshape(count, features), w_out, ln_gain, ln_bias, w_up, w_down,
    )
    flat = tokens.reshape(count, features)
    mixed_out, grad_in, own_w, others_w, own_out, others_out, sums = back(
        flat,
        kv,
        feed_part,
        grad_branch.reshape(count, features),
        normed.reshape(count, features),
        own_input,
        own_resid,
        query,
        heads_out,
        w_query,
        w_key,
        w_value,
        w_out,
        norm_gain,
        ints,
        floats,
        cos_rows,
        sin_rows,
        ln_sums,
    )
    grad_q, grad_k, grad_v, grad_out_w, grad_up, grad_down, mixed_out, grad_in, *sums = finish(
        [(own_w, others_w), (own_out, others_out), (own_up, others_up), (own_down, others_down)],
        [mixed_out.reshape(tokens.shape), grad_in.reshape(tokens.shape)],
        sums,
    )
    gain_sum, ln_gain_sum, ln_bias_sum = (total.reshape(-1) for total in sums)
    return (
        mixed_out, grad_in, gain_sum, grad_q, grad_k, grad_v, grad_out_w, ln_gain_sum, ln_bias_sum, grad_up, grad_down
    )


def solution(mesh):
    return jax.shard_map(
        local,
        mesh=mesh,
        in_specs=(
            P(None, "blk", None),
            P(),
            P(None, "blk"),
            P(None, "blk"),
            P(None, "blk"),
            P(),
            P(None, "tp"),
            P(None, "tp"),
            P(None, "tp"),
            P("tp", None),
            P(),
            P(),
            P(None, "tp"),
            P("tp", None),
            P(None, "blk", None),
        ),
        out_specs=(
            P(None, "blk", None),
            P(None, "blk", None),
            P("blk"),
            P("blk", "tp"),
            P("blk", "tp"),
            P("blk", "tp"),
            P("tp", "blk"),
            P("blk"),
            P("blk"),
            P("blk", "tp"),
            P("tp", "blk"),
        ),
        check_vma=False,
    )
```

```python
import functools
import math

import jax
import jax.numpy as jnp
from jax import lax
from jax.experimental import pallas as pl
from jax.experimental.pallas import tpu as pltpu
from jax.sharding import PartitionSpec as P

HD = 128
FF = 8192


EPS = 1e-05
NEG = -1e30
CHUNK_ROWS = 128
CUT_SUM = 1408
CUT_SHARE = 1408
CUT_SHARE_BACK = 1536
VMEM_LIMIT = 63 * 2**20
RING = 4
TILE = 1024
FEED = 2
NAMES = ("P", "A1", "A2", "A3", "B1", "B2", "B3", "F", "l1", "l2", "l3", "h0", "h1", "h2", "h3", "E", "W", "T", "K", "O", "V", "M", "Z", "Q", "X", "S")
MIDDLE_ORDER = (
    920, 921, 922, 960, 1000, 8, 961, 9, 1001, 48, 10, 962, 168, 923, 88, 11, 208, 169, 1002, 171,
    12, 248, 49, 963, 13, 209, 128, 172, 170, 1003, 89, 288, 249, 173, 14, 129, 211, 212, 328, 51,
    448, 174, 50, 213, 252, 210, 91, 289, 251, 214, 131, 53, 488, 368, 90, 15, 449, 253, 528, 130,
    329, 93, 291, 250, 52, 133, 175, 369, 293, 215, 409, 489, 408, 54, 255, 254, 92, 331, 290, 132,
    568, 55, 333, 529, 451, 292, 94, 453, 371, 450, 373, 330, 569, 16, 370, 95, 134, 491, 490, 410,
    176, 411, 294, 135, 56, 530, 531, 295, 332, 216, 452, 96, 413, 177, 334, 256, 57, 372, 570, 454,
    493, 335, 492, 455, 571, 136, 412, 18, 374, 217, 257, 375, 414, 533, 532, 97, 415, 296, 573,
    495, 494, 572, 137, 20, 178, 535, 575, 179, 534, 297, 574, 22, 180, 219, 640, 456, 59, 58, 457,
    337, 218, 336, 181, 641, 377, 220, 376, 182, 496, 99, 642, 221, 98, 536, 61, 259, 260, 222, 183,
    261, 139, 497, 258, 138, 63, 101, 223, 299, 537, 298, 416, 459, 141, 458, 103, 301, 417, 499,
    60, 263, 339, 461, 498, 643, 143, 341, 577, 539, 100, 262, 62, 538, 579, 379, 338, 303, 501,
    102, 576, 140, 541, 300, 581, 142, 381, 421, 378, 578, 340, 460, 343, 302, 383, 463, 616, 418,
    423, 342, 462, 380, 617, 382, 420, 500, 419, 621, 502, 422, 618, 619, 503, 543, 540, 580, 583,
    542, 620, 623, 582, 622, 880,
)
BACK_ORDER = (
    24, 25, 26, 680, 27, 185, 28, 29, 681, 225, 186, 65, 30, 187, 184, 760, 64, 761, 66, 189, 188,
    31, 720, 105, 229, 227, 682, 226, 190, 68, 228, 104, 106, 224, 69, 265, 32, 266, 269, 264, 191,
    145, 144, 305, 108, 268, 230, 146, 33, 231, 109, 304, 192, 67, 148, 149, 308, 309, 306, 232,
    465, 464, 721, 271, 193, 469, 107, 344, 468, 73, 267, 345, 272, 233, 34, 147, 346, 505, 35, 504,
    273, 508, 466, 113, 348, 385, 307, 386, 509, 349, 545, 544, 194, 548, 72, 384, 683, 71, 506,
    426, 389, 153, 112, 347, 722, 424, 152, 70, 467, 74, 195, 111, 234, 270, 388, 312, 313, 387,
    507, 274, 151, 110, 36, 235, 114, 75, 547, 311, 275, 150, 352, 473, 427, 549, 196, 37, 472, 353,
    428, 546, 310, 115, 392, 723, 154, 585, 513, 76, 236, 512, 471, 38, 197, 155, 116, 314, 276,
    350, 553, 586, 237, 39, 511, 552, 198, 470, 199, 351, 77, 551, 592, 277, 156, 593, 429, 390,
    432, 800, 238, 510, 78, 584, 239, 354, 117, 315, 474, 278, 316, 425, 118, 391, 279, 157, 801,
    355, 624, 589, 79, 514, 393, 395, 119, 394, 317, 475, 158, 356, 476, 159, 433, 625, 435, 515,
    555, 550, 430, 516, 554, 434, 587, 632, 357, 633, 319, 318, 477, 840, 591, 397, 556, 629, 595,
    588, 396, 431, 841, 479, 358, 359, 436, 627, 478, 590, 626, 594, 635, 628, 517, 630, 398, 437,
    596, 399, 518, 631, 557, 519, 438, 842, 558, 439, 559, 598, 597, 634, 638, 636, 637, 599, 639,
    880,
)


MESH = pl.DeviceIdType.MESH
VMEM = pltpu.VMEM
LANE = 128


def remote(src, dst, send, recv, device):
    return pltpu.make_async_remote_copy(
        src_ref=src, dst_ref=dst, send_sem=send, recv_sem=recv, device_id=device, device_id_type=MESH
    )


class Place:
    def __init__(self, lines):
        blk, tp = lax.axis_index("blk"), lax.axis_index("tp")
        self.lines, self.tp = lines, tp
        self.z, self.y = tp // 2, tp % 2
        self.other = 1 - self.y
        self.across = (blk, self.z * 2 + self.other)
        self.right = (blk, jnp.minimum(self.z + 1, lines - 1) * 2 + self.y)
        self.left = (blk, jnp.maximum(self.z - 1, 0) * 2 + self.y)
        self.has_right, self.has_left = self.z < lines - 1, self.z > 0


def greet(*axes):
    place = {axis: lax.axis_index(axis) for axis in ("blk", "tp")}
    peers = 0
    for axis in axes:
        size = lax.axis_size(axis)
        for k in range(1, size):
            peer = dict(place)
            peer[axis] = (place[axis] + k) % size
            pl.semaphore_signal(
                pltpu.get_barrier_semaphore(),
                inc=1,
                device_id=(peer["blk"], peer["tp"]),
                device_id_type=MESH,
            )
        peers += size - 1
    pl.semaphore_wait(pltpu.get_barrier_semaphore(), peers)


class Scatter:
    def __init__(self, place, cut, part, across_a, line_a, line_b, across_b, send, recv):
        self.at, self.cut, self.part = place, cut, part
        self.across_a, self.line_a, self.line_b, self.across_b = across_a, line_a, line_b, across_b
        self.send, self.recv = send, recv

    @staticmethod
    def scratch(chunks, lines, rows, width, cut):
        return [
            VMEM((chunks, 2, lines, rows, width), jnp.bfloat16),
            VMEM((chunks, lines, rows, cut), jnp.bfloat16),
            VMEM((chunks, lines + 1, rows, cut), jnp.bfloat16),
            VMEM((chunks, lines + 1, 2, rows, width - cut), jnp.bfloat16),
            VMEM((chunks, rows, width - cut), jnp.bfloat16),
        ]

    @staticmethod
    def semaphores(chunks, lines):
        return [
            pltpu.SemaphoreType.DMA((chunks, 2 * lines + 2)),
            pltpu.SemaphoreType.DMA((chunks, 2 * lines + 4)),
        ]

    def low(self, c, j):
        return self.part.at[c, self.at.y, j, :, : self.cut]

    def high(self, c, j):
        return self.part.at[c, :, j, :, self.cut :]

    def copy_across_a(self, c):
        return remote(
            self.part.at[c, self.at.other, :, :, : self.cut],
            self.across_a.at[c],
            self.send.at[c, 0],
            self.recv.at[c, 0],
            self.at.across,
        )

    def copy_across_b(self, c):
        return remote(
            self.part.at[c, self.at.other, self.at.z, :, self.cut :],
            self.across_b.at[c],
            self.send.at[c, 1],
            self.recv.at[c, 1],
            self.at.across,
        )

    def copy_line(self, c, j, slot, device, first):
        lines = self.at.lines
        if first:
            source, target, send, recv = self.low(c, j), self.line_a, 2, 2
        else:
            source, target, send, recv = self.high(c, j), self.line_b, 2 + lines, 3 + lines
        return remote(
            source, target.at[c, slot], self.send.at[c, send + j], self.recv.at[c, recv + slot], device
        )

    def to_right(self, c, j, first):
        return self.copy_line(c, j, j + 1, self.at.right, first)

    def to_left(self, c, j, first):
        return self.copy_line(c, j, j, self.at.left, first)

    def take(self, c, j, slot, first):
        self.copy_line(c, j, slot, self.at.right, first).wait_recv()
        view = self.low(c, j) if first else self.high(c, j)
        came = (self.line_a if first else self.line_b)[c, slot]
        view[...] = (view[...].astype(jnp.float32) + came.astype(jnp.float32)).astype(jnp.bfloat16)

    def line_starts(self, c, first):
        lines = self.at.lines

        @pl.when(self.at.z == 0)
        def _():
            for j in range(lines - 1, 0, -1):
                self.to_right(c, j, first).start()

        @pl.when(self.at.z == lines - 1)
        def _():
            for j in range(lines - 1):
                self.to_left(c, j, first).start()

    def line_hop(self, c, step, first):
        lines = self.at.lines

        @pl.when(self.at.z == step)
        def _():
            for j in range(lines - 1, step, -1):
                self.take(c, j, j + 1, first)
                self.to_right(c, j, first).start()

        @pl.when(self.at.z == lines - 1 - step)
        def _():
            for j in range(lines - 1 - step):
                self.take(c, j, j, first)
                self.to_left(c, j, first).start()

    def line_end(self, c, total, first):
        z = self.at.z
        buffer = self.line_a if first else self.line_b

        @pl.when(self.at.has_left)
        def _():
            self.copy_line(c, z, z + 1, self.at.right, first).wait_recv()
            total[...] += buffer[c, z + 1].astype(jnp.float32)

        @pl.when(self.at.has_right)
        def _():
            self.copy_line(c, z, z, self.at.right, first).wait_recv()
            total[...] += buffer[c, z].astype(jnp.float32)

    def begin(self, c):
        self.copy_across_a(c).start()
        self.line_starts(c, False)

    def low_step(self, c, k):
        if k > 1:
            return self.line_hop(c, k - 1, True)
        self.copy_across_a(c).wait_recv()
        mine = self.part.at[c, self.at.y, :, :, : self.cut]
        mine[...] = (mine[...].astype(jnp.float32) + self.across_a[c].astype(jnp.float32)).astype(
            jnp.bfloat16
        )
        self.line_starts(c, True)

    def high_step(self, c, k, total_b):
        if k < self.at.lines - 1:
            return self.line_hop(c, k, False)
        mine = self.high(c, self.at.z)
        total_b[...] = mine[...].astype(jnp.float32)
        self.line_end(c, total_b, False)
        mine[...] = total_b[...].astype(jnp.bfloat16)
        self.copy_across_b(c).start()

    def finish(self, c, total):
        y, z = self.at.y, self.at.z
        low, high = total.at[:, : self.cut], total.at[:, self.cut :]
        low[...] = self.low(c, z)[...].astype(jnp.float32)
        self.line_end(c, low, True)
        self.copy_across_b(c).wait_recv()
        high[...] = self.part[c, y, z, :, self.cut :].astype(jnp.float32) + self.across_b[c].astype(
            jnp.float32
        )

    def drain(self, c):
        self.copy_across_a(c).wait_send()
        self.copy_across_b(c).wait_send()
        for first in (True, False):
            for j in range(self.at.lines):

                @pl.when(self.at.z != j)
                def _(j=j, first=first):
                    self.to_right(c, j, first).wait_send()


class Gather:
    def __init__(self, place, cut, own, full, local, send, recv):
        self.at, self.cut, self.own, self.full = place, cut, own, full
        self.local, self.send, self.recv = local, send, recv

    @staticmethod
    def scratch(chunks, lines):
        return [
            pltpu.SemaphoreType.DMA((chunks,)),
            pltpu.SemaphoreType.DMA((chunks, 5 * lines + 1)),
            pltpu.SemaphoreType.DMA((chunks, 3 * lines + 1)),
        ]

    def low(self, c, j):
        target = self.full.at[c, self.at.y, j, :, : self.cut]
        return target, target

    def copy_low(self, c, j, way, mine):
        lines = self.at.lines
        target = self.full.at[c, self.at.y, j, :, : self.cut]
        source = self.own(c).at[:, : self.cut] if mine else target
        device = (self.at.right, self.at.left, self.at.across)[way]
        recv = j + (lines if way == 2 else 0)
        return remote(source, target, self.send.at[c, way * lines + j], self.recv.at[c, recv], device)

    def copy_high(self, c, j, way):
        lines = self.at.lines
        view = self.full.at[c, :, j, :, self.cut :]
        device = (self.at.right, self.at.left)[way]
        return remote(
            view, view, self.send.at[c, (3 + way) * lines + j], self.recv.at[c, 2 * lines + j], device
        )

    def copy_high_across(self, c):
        lines = self.at.lines
        return remote(
            self.own(c).at[:, self.cut :],
            self.full.at[c, self.at.y, self.at.z, :, self.cut :],
            self.send.at[c, 5 * lines],
            self.recv.at[c, 3 * lines],
            self.at.across,
        )

    def copy_local(self, c):
        return pltpu.make_async_copy(
            self.own(c), self.full.at[c, self.at.y, self.at.z], self.local.at[c]
        )

    def begin(self, c):
        z = self.at.z
        if self.local is not None:
            self.copy_local(c).start()

        @pl.when(self.at.has_right)
        def _():
            self.copy_low(c, z, 0, True).start()

        @pl.when(self.at.has_left)
        def _():
            self.copy_low(c, z, 1, True).start()

        self.copy_high_across(c).start()
        self.copy_low(c, z, 2, True).start()

    def low_step(self, c, k):
        z, lines = self.at.z, self.at.lines

        @pl.when(z >= k)
        def _():
            self.copy_low(c, z - k, 0, False).wait_recv()

            @pl.when(self.at.has_right)
            def _():
                self.copy_low(c, z - k, 0, False).start()

            self.copy_low(c, z - k, 2, False).start()

        @pl.when(z + k < lines)
        def _():
            self.copy_low(c, z + k, 0, False).wait_recv()

            @pl.when(self.at.has_left)
            def _():
                self.copy_low(c, z + k, 1, False).start()

            self.copy_low(c, z + k, 2, False).start()

    def high_step(self, c, k):
        z, lines = self.at.z, self.at.lines
        if k == 0:
            if self.local is not None:
                self.copy_local(c).wait()
            self.copy_high_across(c).wait_recv()

            @pl.when(self.at.has_right)
            def _():
                self.copy_high(c, z, 0).start()

            @pl.when(self.at.has_left)
            def _():
                self.copy_high(c, z, 1).start()

            return

        @pl.when(z >= k)
        def _():
            self.copy_high(c, z - k, 0).wait_recv()

            @pl.when(self.at.has_right)
            def _():
                self.copy_high(c, z - k, 0).start()

        @pl.when(z + k < lines)
        def _():
            self.copy_high(c, z + k, 0).wait_recv()

            @pl.when(self.at.has_left)
            def _():
                self.copy_high(c, z + k, 1).start()

    def end(self, c):
        for j in range(self.at.lines):
            target = self.full.at[c, self.at.other, j, :, : self.cut]
            remote(
                target,
                target,
                self.send.at[c, 2 * self.at.lines + j],
                self.recv.at[c, self.at.lines + j],
                self.at.across,
            ).wait_recv()

    def drain(self, c):
        lines, z = self.at.lines, self.at.z
        self.copy_high_across(c).wait_send()
        for j in range(lines):

            @pl.when(self.at.has_right & (z >= j))
            def _(j=j):
                self.copy_low(c, j, 0, False).wait_send()
                self.copy_high(c, j, 0).wait_send()

            @pl.when(self.at.has_left & (z <= j))
            def _(j=j):
                self.copy_low(c, j, 1, False).wait_send()
                self.copy_high(c, j, 1).wait_send()

            self.copy_low(c, j, 2, False).wait_send()


class BlockScatter:
    def __init__(self, blocks, slice_of, part, own_hbm, from_chip, from_core, send, recv, sem_own):
        self.blk, self.tp = lax.axis_index("blk"), lax.axis_index("tp")
        self.chips, self.chip, self.core = blocks // 2, self.blk // 2, self.blk % 2
        self.slice_of, self.part = slice_of, part
        self.from_core, self.from_chip, self.send, self.recv = from_core, from_chip, send, recv
        self.put_own = pltpu.make_async_copy(part(self.blk), own_hbm, sem_own)

    @staticmethod
    def scratch(blocks, shape):
        chips = blocks // 2
        return [
            VMEM((chips,) + shape, jnp.bfloat16),
            pltpu.SemaphoreType.DMA((2, chips)),
            pltpu.SemaphoreType.DMA((2, chips)),
            pltpu.SemaphoreType.DMA(()),
        ]

    @staticmethod
    def outs(blocks, shape):
        return [
            jax.ShapeDtypeStruct(shape, jnp.bfloat16),
            jax.ShapeDtypeStruct((blocks // 2 - 1,) + shape, jnp.bfloat16),
        ]

    def to_core(self, k):
        return remote(
            self.part(k * 2 + 1 - self.core),
            self.from_core.at[k],
            self.send.at[0, k],
            self.recv.at[0, k],
            (self.chip * 2 + 1 - self.core, self.tp),
        )

    def to_chip(self, k):
        return remote(
            self.part(k * 2 + self.core),
            self.from_chip.at[(self.chip - k + self.chips) % self.chips - 1],
            self.send.at[1, k],
            self.recv.at[1, (self.chip - k + self.chips) % self.chips],
            (k * 2 + self.core, self.tp),
        )

    def came_chip(self, i):
        k = (self.chip + i) % self.chips
        return remote(
            self.part(k * 2 + self.core),
            self.from_chip.at[i - 1],
            self.send.at[1, k],
            self.recv.at[1, i],
            (k * 2 + self.core, self.tp),
        )

    def all_first(self):
        @pl.loop(0, self.chips)
        def _(i):
            self.first(i)

    def all_second(self):
        @pl.loop(0, self.chips)
        def _(i):
            self.second(i)

        self.put_own.start()

    def first(self, i):
        k = (self.chip + 1 + i) % self.chips
        self.slice_of(k * 2 + 1 - self.core, self.part(k * 2 + 1 - self.core))
        self.to_core(k).start()

    def second(self, i):
        k = (self.chip + 1 + i) % self.chips
        mine = self.part(k * 2 + self.core)
        self.slice_of(k * 2 + self.core, mine)
        self.to_core(k).wait_recv()
        mine[...] = (mine[...].astype(jnp.float32) + self.from_core[k].astype(jnp.float32)).astype(
            jnp.bfloat16
        )

        @pl.when(k != self.chip)
        def _():
            self.to_chip(k).start()

    def end(self):
        @pl.loop(1, self.chips)
        def _(i):
            self.came_chip(i).wait_recv()

        self.put_own.wait()
        self.drain()

    def drain(self):
        @pl.loop(0, self.chips)
        def _(k):
            self.to_core(k).wait_send()

            @pl.when(k != self.chip)
            def _():
                self.to_chip(k).wait_send()


class Loads:
    def __init__(self, sems, pairs):
        self.copies = [
            pltpu.make_async_copy(source, target, sems.at[i]) for i, (source, target) in enumerate(pairs)
        ]
        self.waited = set()
        for copy in self.copies:
            copy.start()

    def need(self, *which):
        for i in which:
            if i not in self.waited:
                self.waited.add(i)
                self.copies[i].wait()


class Tasks:
    def __init__(self):
        self.by_name = {}

    def add(self, name, phase, task):
        self.by_name[name, phase] = task

    def sum_and_share(self, phase, scatter, gather, total_b, finish):
        lines = scatter.at.lines
        for k in range(1, lines):
            self.add(f"A{k}", phase, functools.partial(scatter.low_step, k=k))
            self.add(f"B{k}", phase, functools.partial(scatter.high_step, k=k, total_b=total_b))
            self.add(f"l{k}", phase, functools.partial(gather.low_step, k=k))
        self.add("F", phase, finish)
        for k in range(lines):
            self.add(f"h{k}", phase, functools.partial(gather.high_step, k=k))
        self.add("E", phase, gather.end)

    def run(self, order):
        for name, phase, c in order:
            self.by_name[name, phase](c)


def in_turn(phase, lines, chunks):
    names = [f"{half}{k}" for k in range(1, lines) for half in "AB"] + ["F"]
    names += [f"l{k}" for k in range(1, lines)] + [f"h{k}" for k in range(lines)] + ["E"]
    return [(name, phase, c) for name in names for c in range(chunks)]


def unpack(order):
    return [(NAMES[code // 40], code // 8 % 5, code % 8) for code in order]


def rows_sum(values):
    return jnp.sum(values, axis=0, keepdims=True)


def mean_last(values):
    return jnp.mean(values, axis=-1, keepdims=True)


def dot_nn(a, b):
    return jnp.dot(a, b, preferred_element_type=jnp.float32)


def dot_nt(a, b):
    return lax.dot_general(a, b, (((1,), (1,)), ((), ())), preferred_element_type=jnp.float32)


def dot_tn(a, b):
    return lax.dot_general(a, b, (((0,), (0,)), ((), ())), preferred_element_type=jnp.float32)


def turn(values, cos_rows, sin_rows):
    return values * cos_rows + pltpu.roll(values, HD // 2, 1) * sin_rows


def front_tasks(
    tasks, batches, blocks, need_weights, lengths_ref, x_hbm, gain_ref, wq_ref, wk_ref, wv_ref, count_ref, width_ref, prob_ref,
    normed_hbm, query_ref, kv_hbm, heads_ref, ints_ref, floats_ref, cos_ref, sin_ref,
    x_mb, kv_own, kv_in, acc,
    sem_x, sem_normed, sem_own, sem_in, sem_send, sem_pass, sem_recv,
):
    blk, tp = lax.axis_index("blk"), lax.axis_index("tp")
    chips, chip, core = blocks // 2, blk // 2, blk % 2
    span, wide = x_hbm.shape[1], wq_ref.shape[1]
    heads = wide // HD
    scale = 1.0 / math.sqrt(HD)

    def slab(m):
        return pl.ds(pl.multiple_of(m * span, span), span)

    def get_x(m):
        return pltpu.make_async_copy(x_hbm.at[m], x_mb.at[m % 2], sem_x.at[m % 2])

    def put_normed(m):
        return pltpu.make_async_copy(x_mb.at[m % 2], normed_hbm.at[m], sem_normed.at[m % 2])

    def put_own(m):
        return pltpu.make_async_copy(kv_own.at[m], kv_hbm.at[m, blk], sem_own.at[m])

    def to_chip(m, k):
        return remote(
            kv_own.at[m], kv_hbm.at[m, blk], sem_send.at[m, k], sem_recv.at[m, blk], (k * 2 + core, tp)
        )

    def to_core(m):
        return remote(
            kv_own.at[m], kv_hbm.at[m, blk], sem_send.at[m, chip], sem_recv.at[m, blk], (chip * 2 + 1 - core, tp)
        )

    def pass_on(m, k):
        block = kv_hbm.at[m, k * 2 + core]
        return remote(
            block, block, sem_pass.at[m, k], sem_recv.at[m, k * 2 + core], (chip * 2 + 1 - core, tp)
        )

    def arrived(m, k):
        block = kv_hbm.at[m, k]
        return remote(block, block, sem_pass.at[m, 0], sem_recv.at[m, k], (blk, tp))

    def column(row):
        across = lax.broadcasted_iota(jnp.int32, (span, span), 1)
        down = lax.broadcasted_iota(jnp.int32, (span, span), 0)
        return jnp.sum(jnp.where(across == down, row.astype(jnp.float32), 0.0), axis=1, keepdims=True)

    def project(m):
        get_x(m).wait()
        if m + 1 < batches:
            if m >= 1:
                put_normed(m - 1).wait()
            get_x(m + 1).start()
        here = slab(m)
        x = x_mb[m % 2].astype(jnp.float32)
        scaled = x * lax.rsqrt(mean_last(x * x) + EPS)
        x_mb[m % 2] = (scaled * gain_ref[...]).astype(jnp.bfloat16)
        put_normed(m).start()
        rows = blk * span + lax.broadcasted_iota(jnp.int32, (span, 1), 0)
        begin, end = jnp.zeros((span, 1), jnp.int32), jnp.int32(0)
        for s in range(lengths_ref.shape[1]):
            length = lengths_ref[m, s]
            end = end + length
            begin = begin + jnp.where(rows >= end, length, 0)
        ints_ref[here, 0:1] = column(count_ref[m : m + 1, :]).astype(jnp.int32)
        ints_ref[here, 1:2] = column(width_ref[m : m + 1, :]).astype(jnp.int32)
        ints_ref[here, 2:3] = begin
        floats_ref[here, 0:1] = column(prob_ref[m : m + 1, :])
        lanes = lax.broadcasted_iota(jnp.int32, (1, HD), 1)
        half = HD // 2
        frequency = jnp.exp((lanes % half).astype(jnp.float32) * (-math.log(10000.0) / half))
        angles = (rows - begin).astype(jnp.float32) * frequency
        cos_rows = jnp.cos(angles)
        sin_rows = jnp.sin(angles) * jnp.where(lanes < half, -1.0, 1.0)
        cos_ref[here, :] = cos_rows
        sin_ref[here, :] = sin_rows
        normed = x_mb[m % 2]
        need_weights()
        query, key = dot_nn(normed, wq_ref[...]), dot_nn(normed, wk_ref[...])
        for h in range(heads):
            cols = slice(h * HD, (h + 1) * HD)
            query_ref[here, cols] = turn(query[:, cols], cos_rows, sin_rows).astype(jnp.bfloat16)
            kv_own[m, :, cols] = turn(key[:, cols], cos_rows, sin_rows).astype(jnp.bfloat16)
        kv_own[m, :, wide:] = dot_nn(normed, wv_ref[...]).astype(jnp.bfloat16)
        put_own(m).start()

        @pl.loop(chip + 1, chips)
        def _(k):
            to_chip(m, k).start()

        @pl.when(core == 0)
        def _():
            to_core(m).start()

    def pass_blocks(m):
        @pl.loop(0, chip)
        def _(k):
            arrived(m, k * 2 + core).wait_recv()
            pass_on(m, k).start()

    def get_kv(m, k):
        return pltpu.make_async_copy(kv_hbm.at[m, k], kv_in.at[k], sem_in.at[k])

    def attend(m):
        here = slab(m)
        q_rows = blk * span + lax.broadcasted_iota(jnp.int32, (span, span), 0)
        begin = ints_ref[here, 2:3]

        @pl.loop(0, blk)
        def _(k):
            @pl.when(k % 2 != core)
            def _():
                arrived(m, k).wait_recv()

            get_kv(m, k).start()

        def raw_scores(k, kv):
            k_rows = k * span + lax.broadcasted_iota(jnp.int32, (span, span), 1)
            allowed = (k_rows <= q_rows) & (k_rows >= begin)
            result = []
            for h in range(heads):
                cols = slice(h * HD, (h + 1) * HD)
                raw = dot_nt(query_ref[here, cols], kv[:, cols])
                result.append(jnp.where(allowed, raw * scale, NEG))
            return result

        def highest_of(k, kv):
            return tuple(functools.reduce(jnp.maximum, lane_tiles(score)) for score in raw_scores(k, kv))

        def weigh(k, kv, tops, sums):
            result, scores = [], raw_scores(k, kv)
            for h in range(heads):
                weights = jnp.exp(scores[h] - tops[h])
                result.append(sums[h] + sum(lane_tiles(weights)))
                acc[:, h * HD : (h + 1) * HD] += dot_nn(
                    weights.astype(jnp.bfloat16), kv[:, wide + h * HD : wide + (h + 1) * HD]
                )
            return tuple(result)

        highest = highest_of(blk, kv_own.at[m])

        def first(k, highest):
            get_kv(m, k).wait()
            return tuple(map(jnp.maximum, highest, highest_of(k, kv_in.at[k])))

        highest = lax.fori_loop(0, blk, first, highest)
        tops = [jnp.max(high, axis=-1, keepdims=True) for high in highest]
        acc[...] = jnp.zeros_like(acc)
        sums = weigh(blk, kv_own.at[m], tops, (jnp.zeros((span, LANE), jnp.float32),) * heads)
        sums = lax.fori_loop(0, blk, lambda k, sums: weigh(k, kv_in.at[k], tops, sums), sums)
        for h in range(heads):
            cols = slice(h * HD, (h + 1) * HD)
            row_sum = jnp.sum(sums[h], axis=-1, keepdims=True)
            floats_ref[here, 1 + h : 2 + h] = tops[h] + jnp.log(row_sum)
            heads_ref[here, cols] = jnp.where(
                tp * heads + h < ints_ref[here, 0:1], acc[:, cols] / row_sum, 0.0
            ).astype(jnp.bfloat16)

    def end():
        for m in range(batches):
            put_own(m).wait()
            if m >= batches - 2:
                put_normed(m).wait()

            @pl.loop(chip + 1, chips)
            def _(k):
                to_chip(m, k).wait_send()

            @pl.when(core == 0)
            def _():
                to_core(m).wait_send()

            @pl.loop(0, chip)
            def _(k):
                pass_on(m, k).wait_send()

    tasks.add("Q", 0, project)
    tasks.add("X", 0, pass_blocks)
    tasks.add("S", 0, attend)
    get_x(0).start()
    return end


def lane_tiles(values):
    return [values[:, i : i + LANE] for i in range(0, values.shape[1], LANE)]


def middle_kernel(
    lines, blocks, batches, chunks, chunk_rows, lengths_ref, tokens_hbm, x_hbm, grad_hbm, wq_hbm, wk_hbm, wv_hbm, wo_hbm, up_hbm,
    down_hbm, gain_ref, bias_ref, rms_ref, count_ref, width_ref, prob_ref, normed_hbm, kv_hbm, own_up, others_up, own_down, others_down, branch_hbm, feed_hbm, input_ref, resid_ref, sums_ref,
    query_ref, heads_ref, ints_ref, floats_ref, cos_ref, sin_ref,
    wq_ref, wk_ref, wv_ref, wo_ref, up_ref, down_ref, sem_load, x_own, g_own, g_all, own_branch, feed_part, lifted_ref, squared_ref, hidden_ref, normal_ref, inv_own, total,
    total_b, sem_in, sem_g, sem_feed, *rest,
):
    place = Place(lines)
    y, z, tp = place.y, place.z, place.tp
    spot = y * lines + z
    rows = chunk_rows // (2 * lines)
    width = gain_ref.shape[-1]
    units = up_ref.shape[1]
    s1, s2 = Scatter(place, CUT_SUM, *rest[:5], *rest[5:7]), Scatter(place, CUT_SUM, *rest[:5], *rest[7:9])
    a1 = Gather(place, CUT_SHARE, lambda c: lifted_ref.at[c, y, z], lifted_ref, None, *rest[10:12])
    a2 = Gather(place, CUT_SHARE, lambda c: own_branch.at[c], branch_hbm, *rest[12:15])
    share = width // blocks

    def up_slice(target, out):
        step = min(TILE, share)

        @pl.loop(0, share // step)
        def _(i):
            lanes = pl.ds(pl.multiple_of(target * share + i * step, step), step)
            lifted = lifted_ref[:, :, :, :, lanes].reshape(chunks * chunk_rows, step)
            out[pl.ds(pl.multiple_of(i * step, step), step), :] = dot_tn(lifted, hidden_ref[...]).astype(
                jnp.bfloat16
            )

    def down_slice(target, out):
        lanes = pl.ds(pl.multiple_of(target * share, share), share)

        @pl.loop(0, units // TILE)
        def _(i):
            cols = pl.ds(pl.multiple_of(i * TILE, TILE), TILE)
            grad = g_all[:, :, :, lanes].reshape(chunks * chunk_rows, share)
            out[cols, :] = dot_tn(squared_ref[:, cols], grad).astype(jnp.bfloat16)

    grad_up = BlockScatter(
        blocks, up_slice, lambda k: up_ref.at[pl.ds(pl.multiple_of(k * share, share), share), :], own_up, others_up,
        *rest[15:19],
    )
    grad_down = BlockScatter(
        blocks, down_slice, lambda k: down_ref.at[:, pl.ds(pl.multiple_of(k * share, share), share)], own_down, others_down,
        *rest[19:23],
    )

    get_x = pltpu.make_async_copy(tokens_hbm.at[:, spot], x_own, sem_in.at[0])
    get_g = pltpu.make_async_copy(grad_hbm.at[:, spot], g_own, sem_in.at[1])
    tasks = Tasks()
    front_end = front_tasks(
        tasks, batches, blocks, lambda: loads.need(0, 1, 2), lengths_ref, x_hbm, rms_ref, wq_ref, wk_ref, wv_ref, count_ref,
        width_ref, prob_ref, normed_hbm, query_ref, kv_hbm, heads_ref, ints_ref, floats_ref, cos_ref, sin_ref, *rest[23:],
    )
    sources = (wq_hbm, wk_hbm, wv_hbm, wo_hbm, up_hbm, down_hbm)
    loads = Loads(sem_load, list(zip(sources, (wq_ref, wk_ref, wv_ref, wo_ref, up_ref, down_ref), strict=True)))
    for copy in (get_x, get_g):
        copy.start()

    def get_grad(c):
        return pltpu.make_async_copy(grad_hbm.at[c], g_all.at[c], sem_g.at[c])

    def put_feed(c):
        return pltpu.make_async_copy(feed_part.at[c % FEED], feed_hbm.at[c], sem_feed.at[c])

    @pl.loop(0, chunks)
    def _(c):
        get_grad(c).start()

    greet("tp", "blk")
    sums_ref[...] = jnp.zeros_like(sums_ref)

    def own_rows(c):
        return pl.ds(pl.multiple_of(c * chunk_rows + spot * rows, rows), rows)

    def all_rows(c):
        return pl.ds(pl.multiple_of(c * chunk_rows, chunk_rows), chunk_rows)

    def tiled(n, body):
        @pl.loop(0, n // TILE)
        def _(i):
            body(pl.ds(pl.multiple_of(i * TILE, TILE), TILE))

    def put(part, c, cols, values):
        n = values.shape[0] // chunk_rows
        part[c : c + n, :, :, :, cols] = values.astype(jnp.bfloat16).reshape(n, 2, lines, rows, TILE)

    def project(c):
        if c % FEED:
            return
        loads.need(3)
        heads = heads_ref[pl.ds(c * chunk_rows, FEED * chunk_rows), :]

        def one(cols):
            put(s1.part, c, cols, dot_nn(heads, wo_ref[:, cols]))

        tiled(width, one)
        for i in range(c, c + FEED):
            s1.begin(i)

    first_norms = [get_x.wait, get_g.wait]

    def norm(c):
        while first_norms:
            first_norms.pop()()
        s1.finish(c, total)
        residual = x_own[c].astype(jnp.float32) + total[...]
        center = residual - mean_last(residual)
        inv_std = lax.rsqrt(mean_last(center * center) + EPS)
        normal = center * inv_std
        input_ref[c] = residual
        normal_ref[c] = normal
        inv_own[c] = jnp.broadcast_to(inv_std, (rows, LANE))
        lifted_ref[c, y, z] = (normal * gain_ref[...] + bias_ref[...]).astype(jnp.bfloat16)
        a1.begin(c)

    def feed(c):
        group = range(c, c + FEED)
        loads.need(4, 5)
        for i in group:
            a1.end(i)
            s1.drain(i)
            get_grad(i).wait()
        size = FEED * chunk_rows
        lifted = lifted_ref[c : c + FEED].reshape(size, width)
        span = pl.ds(c * chunk_rows, size)
        prob, limit = floats_ref[span, 0:1], (ints_ref[span, 1:2] + 1) * (FF // 4)
        g_all[c : c + FEED] = (
            g_all[c : c + FEED].astype(jnp.float32) * prob.reshape(FEED, 2 * lines, rows, 1)
        ).astype(jnp.bfloat16)

        def units_of(cols):
            active = jnp.maximum(dot_nn(lifted, up_ref[:, cols]), 0.0)
            ids = tp * units + cols.start + lax.broadcasted_iota(jnp.int32, (size, TILE), 1)
            mask = (ids < limit).astype(jnp.float32)
            squared_ref[span, cols] = (active * active * mask).astype(jnp.bfloat16)
            back = dot_nt(g_all[c : c + FEED].reshape(size, width), down_ref[cols, :])
            hidden_ref[span, cols] = (back * mask * 2.0 * active).astype(jnp.bfloat16)

        tiled(units, units_of)
        hidden = hidden_ref[span, :]

        def lift(cols):
            put(s2.part, c, cols, dot_nt(hidden, up_ref[cols, :]))

        tiled(width, lift)
        for i in group:
            s2.begin(i)
        squared = squared_ref[span, :]
        if c > 0:
            for i in range(FEED):
                put_feed(c - FEED + i).wait()

        def out(cols):
            put(feed_part, 0, cols, dot_nn(squared, down_ref[:, cols]))

        tiled(width, out)
        for i in group:
            put_feed(i).start()

    def norm_back(c):
        s2.finish(c, total)
        grad_lifted, normal = total[...], normal_ref[c]
        sums_ref[0:1, :] += rows_sum(grad_lifted * normal)
        sums_ref[1:2, :] += rows_sum(grad_lifted)
        g = grad_lifted * gain_ref[...]
        grad_resid = g_own[c].astype(jnp.float32) + inv_own[c][:, 0:1] * (
            g - mean_last(g) - normal * mean_last(g * normal)
        )
        resid_ref[c] = grad_resid
        own_branch[c] = grad_resid.astype(jnp.bfloat16)
        a2.begin(c)

    tasks.add("P", 1, project)
    tasks.sum_and_share(1, s1, a1, total_b, norm)
    tasks.add("P", 2, feed)
    tasks.sum_and_share(2, s2, a2, total_b, norm_back)
    steps = (grad_up.all_first, grad_down.all_first, grad_up.all_second, grad_down.all_second)
    tasks.add("W", 0, lambda k: steps[k]())
    tasks.add("Z", 0, lambda k: None)
    tasks.run(middle_order(lines, chunks, batches))
    front_end()

    for c in range(chunks - FEED, chunks):
        put_feed(c).wait()

    @pl.loop(0, chunks)
    def _(c):
        for part in (s2, a1, a2):
            part.drain(c)

    grad_up.end()
    grad_down.end()


def middle_order(lines, chunks, batches):
    if (lines, chunks, batches) == (4, 8, 4):
        return unpack(MIDDLE_ORDER)
    order = [(name, 0, m) for name in "QXS" for m in range(batches)]
    order += [("P", 1, c) for c in range(chunks)] + in_turn(1, lines, chunks)[:-chunks]
    order += [("P", 2, c) for c in range(0, chunks, FEED)] + in_turn(2, lines, chunks)
    return order + [("W", 0, k) for k in range(4)]


def middle(tokens, lengths, head_count, width_index, router_prob, norm_gain, w_query, w_key, w_value, grad_out, w_out,
           ln_gain, ln_bias, w_up, w_down):
    lines, blocks = lax.axis_size("tp") // 2, lax.axis_size("blk")
    batches, span, width = tokens.shape
    count, units, wide = batches * span, w_up.shape[1], w_query.shape[1]
    heads = wide // HD
    chunk_rows = CHUNK_ROWS
    chunks, rows = count // chunk_rows, chunk_rows // (2 * lines)
    share = width // blocks
    split = (chunks, 2 * lines, rows, width)
    full = (chunks, 2, lines, rows, width)
    any_space, vmem = pl.BlockSpec(memory_space=pl.ANY), pl.BlockSpec(memory_space=VMEM)
    bf16, f32 = jnp.bfloat16, jnp.float32
    dma = pltpu.SemaphoreType.DMA
    loads = (w_query, w_key, w_value, w_out, w_up, w_down)
    outs = pl.pallas_call(
        functools.partial(middle_kernel, lines, blocks, batches, chunks, chunk_rows),
        out_shape=[
            jax.ShapeDtypeStruct((batches, span, width), bf16),
            jax.ShapeDtypeStruct((batches, blocks, span, 2 * wide), bf16),
            *BlockScatter.outs(blocks, (share, units)),
            *BlockScatter.outs(blocks, (units, share)),
            jax.ShapeDtypeStruct(full, bf16),
            jax.ShapeDtypeStruct(full, bf16),
            jax.ShapeDtypeStruct((chunks, rows, width), f32),
            jax.ShapeDtypeStruct((chunks, rows, width), f32),
            jax.ShapeDtypeStruct((2, width), f32),
            jax.ShapeDtypeStruct((count, wide), bf16),
            jax.ShapeDtypeStruct((count, wide), bf16),
            jax.ShapeDtypeStruct((count, 3), jnp.int32),
            jax.ShapeDtypeStruct((count, 1 + heads), f32),
            jax.ShapeDtypeStruct((count, HD), f32),
            jax.ShapeDtypeStruct((count, HD), f32),
        ],
        in_specs=[pl.BlockSpec(memory_space=pltpu.SMEM)] + [any_space] * 9 + [vmem] * 6,
        out_specs=[any_space] * 8 + [vmem] * 9,
        scratch_shapes=[VMEM(load.shape, bf16) for load in loads]
        + [
            dma((len(loads),)),
            VMEM((chunks, rows, width), bf16),
            VMEM((chunks, rows, width), bf16),
            VMEM(split, bf16),
            VMEM((chunks, rows, width), bf16),
            VMEM((FEED,) + full[1:], bf16),
            VMEM(full, bf16),
            VMEM((count, units), bf16),
            VMEM((count, units), bf16),
            VMEM((chunks, rows, width), f32),
            VMEM((chunks, rows, LANE), f32),
            VMEM((rows, width), f32),
            VMEM((2, rows, width - CUT_SUM), f32),
            dma((2,)),
            dma((chunks,)),
            dma((chunks,)),
        ]
        + Scatter.scratch(chunks, lines, rows, width, CUT_SUM)
        + Scatter.semaphores(chunks, lines) * 2
        + Gather.scratch(chunks, lines) * 2
        + BlockScatter.scratch(blocks, (share, units))
        + BlockScatter.scratch(blocks, (units, share))
        + [
            VMEM((2, span, width), bf16),
            VMEM((batches, span, 2 * wide), bf16),
            VMEM((blocks, span, 2 * wide), bf16),
            VMEM((span, wide), f32),
            dma((2,)),
            dma((2,)),
            dma((batches,)),
            dma((blocks,)),
            dma((batches, blocks // 2)),
            dma((batches, blocks // 2)),
            dma((batches, blocks)),
        ],
        compiler_params=pltpu.CompilerParams(
            collective_id=1, has_side_effects=True, vmem_limit_bytes=VMEM_LIMIT
        ),
        cost_estimate=pl.CostEstimate(
            flops=2 * count * width * (4 * wide + 6 * units), bytes_accessed=40 * 2**20, transcendentals=0
        ),
    )(
        lengths, tokens.reshape(split), tokens, grad_out.reshape(split), *loads, ln_gain[None], ln_bias[None],
        norm_gain[None], head_count, width_index, router_prob,
    )
    return outs


def turn_back(grad, cos_rows, sin_rows):
    return grad * cos_rows - pltpu.roll(grad, HD // 2, 1) * sin_rows


def back_kernel(
    lines, blocks, batches, chunks, chunk_rows, tokens_hbm, kv_hbm, feed_hbm, branch_hbm, normed_hbm,
    input_hbm, resid_hbm, query_hbm, heads_hbm, wq_hbm, wk_hbm, wv_hbm, wo_hbm, cos_hbm, sin_hbm, floats_hbm,
    ints_ref, gain_ref, sums_ref, mixed_hbm, in_hbm, own_w, others_w, own_o, others_o,
    small_ref,
    input_ref, resid_ref, query_ref, heads_ref, wq_ref, wk_ref, wv_ref, wo_ref, cos_ref, sin_ref, floats_ref, sem_load,
    branch_ref, x_own, own_in, own_mixed, kv_mb, grad_mb, delta_mb, dq_mb, stage, own, came, pre, total, total_b,
    grad_w, small, small_blk, small_part, small_tp, sem_in, sem_branch, sem_feed, sem_kv, sem_send, sem_recv, sem_free, sem_blk, sem_tp,
    *rest,
):
    place = Place(lines)
    blk, tp, y, z = lax.axis_index("blk"), place.tp, place.y, place.z
    spot = y * lines + z
    rows = chunk_rows // (2 * lines)
    width = gain_ref.shape[-1]
    wide = query_ref.shape[1]
    heads = wide // HD
    span = query_ref.shape[0] // batches
    per = span // chunk_rows
    scale = 1.0 / math.sqrt(HD)
    s3, s4 = Scatter(place, CUT_SUM, *rest[0:7]), Scatter(place, CUT_SUM, *rest[7:14])
    a3 = Gather(place, CUT_SHARE_BACK, lambda c: own_mixed.at[c], mixed_hbm, *rest[14:17])
    a4 = Gather(place, CUT_SHARE_BACK, lambda c: own_in.at[c], in_hbm, *rest[17:20])

    get_x = pltpu.make_async_copy(tokens_hbm.at[:, spot], x_own, sem_in)
    get_x.start()

    def get_kv(step):
        source = kv_hbm.at[step // (blk + 1), step % (blk + 1)]
        return pltpu.make_async_copy(source, kv_mb.at[step % 2], sem_kv.at[step % 2])

    def get_feed(c):
        return pltpu.make_async_copy(feed_hbm.at[c], s3.part.at[c], sem_feed.at[c])

    def slab(m):
        return pl.ds(pl.multiple_of(m * span, span), span)

    ring = stage.shape[0]

    def get_branch(m):
        return pltpu.make_async_copy(branch_hbm.at[slab(m), :], branch_ref.at[slab(m), :], sem_branch.at[m])

    get_normed = pltpu.make_async_copy(normed_hbm, branch_ref, sem_branch.at[batches])
    waited = set()

    def need_branch(*which):
        for m in which:
            if m not in waited:
                waited.add(m)
                get_branch(m).wait()

    def to_owner(m, k):
        slot = (m * blk + k) % ring
        return remote(
            stage.at[slot], came.at[m % 2, blk], sem_send.at[slot], sem_recv.at[m % 2, blk], (k, tp)
        )

    def from_peer(m, k):
        return remote(stage.at[0], came.at[m % 2, k], sem_send.at[0], sem_recv.at[m % 2, k], (k, tp))

    def attend_back(m):
        need_branch(m)
        loads.need(*attend_loads)
        here = slab(m)
        grad = dot_nt(branch_ref[here, :], wo_ref[...]).astype(jnp.bfloat16)
        for h in range(heads):
            cols = slice(h * HD, (h + 1) * HD)
            head = tp * heads + h
            masked = jnp.where(head < ints_ref[here, 0:1], grad[:, cols].astype(jnp.float32), 0.0)
            grad_mb[:, cols] = masked.astype(jnp.bfloat16)
            delta = jnp.sum(masked * heads_ref[here, cols].astype(jnp.float32), axis=-1, keepdims=True)
            delta_mb[h] = jnp.broadcast_to(delta, (span, LANE))
        dq_mb[...] = jnp.zeros_like(dq_mb)
        q_rows = blk * span + lax.broadcasted_iota(jnp.int32, (span, span), 0)
        begin = ints_ref[here, 2:3]

        def pairs(k, out):
            step = m * (blk + 1) + k
            get_kv(step).wait()

            @pl.when(step + 1 < batches * (blk + 1))
            def _():
                get_kv(step + 1).start()

            k_rows = k * span + lax.broadcasted_iota(jnp.int32, (span, span), 1)
            allowed = (k_rows <= q_rows) & (k_rows >= begin)
            for h in range(heads):
                cols = slice(h * HD, (h + 1) * HD)
                q, g = query_ref[here, cols], grad_mb[:, cols]
                key = kv_mb[step % 2, :, cols]
                value = kv_mb[step % 2, :, wide + h * HD : wide + (h + 1) * HD]
                raw = dot_nt(q, key)
                prob = jnp.where(allowed, jnp.exp(raw * scale - floats_ref[here, 1 + h : 2 + h]), 0.0)
                grad_prob = dot_nt(g, value)
                grad_score = (prob * (grad_prob - delta_mb[h][:, 0:1]) * scale).astype(jnp.bfloat16)
                dq_mb[:, cols] += dot_nn(grad_score, key)
                out[:, cols] = dot_tn(grad_score, q).astype(jnp.bfloat16)
                out[:, wide + h * HD : wide + (h + 1) * HD] = dot_tn(prob.astype(jnp.bfloat16), g).astype(
                    jnp.bfloat16
                )

        @pl.loop(0, blk)
        def _(k):
            sent = m * blk + k

            @pl.when(sent >= ring)
            def _():
                to_owner((sent - ring) // blk, (sent - ring) % blk).wait_send()

            pairs(k, stage.at[sent % ring])

            @pl.when(m >= 2)
            def _():
                pl.semaphore_wait(sem_free.at[k], 1)

            to_owner(m, k).start()

        pairs(blk, own.at[m % 2])
        if m == batches - 1:
            get_normed.start()
        for h in range(heads):
            cols = slice(h * HD, (h + 1) * HD)
            pre[here, cols] = turn_back(dq_mb[:, cols], cos_ref[here, :], sin_ref[here, :]).astype(
                jnp.bfloat16
            )

    def gather_kv(m):
        here = slab(m)
        grad_w[...] = own[m % 2].astype(jnp.float32)

        @pl.loop(blk + 1, blocks)
        def _(k):
            from_peer(m, k).wait_recv()
            grad_w[...] += came[m % 2, k].astype(jnp.float32)

            @pl.when(m + 2 < batches)
            def _():
                pl.semaphore_signal(sem_free.at[blk], inc=1, device_id=(k, tp), device_id_type=MESH)

        for h in range(heads):
            cols = slice(h * HD, (h + 1) * HD)
            pre[here, wide + h * HD : wide + (h + 1) * HD] = turn_back(
                grad_w[:, cols], cos_ref[here, :], sin_ref[here, :]
            ).astype(jnp.bfloat16)
        pre[here, 2 * wide :] = grad_w[:, wide:].astype(jnp.bfloat16)

    def spread(c):
        loads.need(*spread_loads)
        here = pl.ds(pl.multiple_of(c * chunk_rows, chunk_rows), chunk_rows)

        @pl.loop(0, width // TILE)
        def _(i):
            cols = pl.ds(pl.multiple_of(i * TILE, TILE), TILE)
            grad = dot_nt(pre[here, :wide], wq_ref[cols, :])
            grad += dot_nt(pre[here, wide : 2 * wide], wk_ref[cols, :])
            grad += dot_nt(pre[here, 2 * wide :], wv_ref[cols, :])
            s4.part[c, :, :, :, cols] = grad.astype(jnp.bfloat16).reshape(2, lines, rows, TILE)

        s4.begin(c)

    def feed(c):
        get_feed(c).wait()
        s3.begin(c)

    def mix(c):
        loads.need(*mix_loads)
        s3.finish(c, total)
        prob = floats_ref[pl.ds(pl.multiple_of(c * chunk_rows + spot * rows, rows), rows), 0:1]
        own_mixed[c] = (input_ref[c] + prob * total[...]).astype(jnp.bfloat16)
        a3.begin(c)

    def last(c):
        loads.need(*last_loads)
        s4.finish(c, total)
        grad_normed, x = total[...], x_own[c].astype(jnp.float32)
        inv_rms = lax.rsqrt(mean_last(x * x) + EPS)
        scaled = x * inv_rms
        small[0:1, :] += rows_sum(grad_normed * scaled)
        s = grad_normed * gain_ref[...]
        grad_in = resid_ref[c] + inv_rms * (s - scaled * mean_last(s * scaled))
        own_in[c] = grad_in.astype(jnp.bfloat16)
        a4.begin(c)

    share = width // blocks

    def slice_of(target, out):
        step = min(TILE, share)

        @pl.loop(0, share // step)
        def _(i):
            lanes = pl.ds(pl.multiple_of(target * share + i * step, step), step)
            grad = dot_tn(branch_ref[:, lanes], pre[...]).astype(jnp.bfloat16)
            for k in range(3):
                out[k, pl.ds(pl.multiple_of(i * step, step), step), :] = grad[:, k * wide : (k + 1) * wide]

    def out_slice(target, out):
        lanes = pl.ds(pl.multiple_of(target * share, share), share)
        out[...] = dot_tn(heads_ref[...], branch_ref[:, lanes]).astype(jnp.bfloat16)

    part, out_part = rest[20], rest[25]
    weights = BlockScatter(blocks, slice_of, lambda k: part.at[k], own_w, others_w, *rest[21:25])
    out_weights = BlockScatter(blocks, out_slice, lambda k: out_part.at[k], own_o, others_o, *rest[26:30])
    ranks = 2 * lines

    def small_to_blk(k):
        peer = (blk + k) % blocks
        lanes = pl.ds(pl.multiple_of(peer * share, share), share)
        return remote(
            small.at[:, lanes], small_blk.at[k - 1], sem_blk.at[0, k], sem_blk.at[1, k], (peer, tp)
        )

    def small_to_tp(k):
        return remote(
            small_part, small_tp.at[k - 1], sem_tp.at[0, k], sem_tp.at[1, k], (blk, (tp + k) % ranks)
        )

    def small_first():
        for k in range(1, blocks):
            small_to_blk(k).start()

    def small_second():
        small_part[...] = small[:, pl.ds(pl.multiple_of(blk * share, share), share)]
        for k in range(1, blocks):
            small_to_blk(k).wait()
            small_part[...] += small_blk[k - 1]
        for k in range(1, ranks):
            small_to_tp(k).start()

    def small_third():
        small_ref[...] = small_part[...]
        for k in range(1, ranks):
            small_to_tp(k).wait()
            small_ref[...] += small_tp[k - 1]

    get_branch(0).start()
    attend_loads, mix_loads, last_loads, spread_loads = (2, 3, 7, 8, 9, 10), (0, 10), (1,), (4, 5, 6)
    refs = (input_ref, resid_ref, query_ref, heads_ref, wq_ref, wk_ref, wv_ref, wo_ref, cos_ref, sin_ref, floats_ref)
    sources = (
        input_hbm, resid_hbm, query_hbm, heads_hbm, wq_hbm, wk_hbm, wv_hbm, wo_hbm, cos_hbm, sin_hbm, floats_hbm,
    )
    loads = Loads(sem_load, list(zip(sources, refs, strict=True)))
    for m in range(1, batches):
        get_branch(m).start()

    @pl.loop(0, chunks)
    def _(c):
        get_feed(c).start()

    get_kv(0).start()
    greet("tp", "blk")
    get_x.wait()
    small[...] = jnp.zeros_like(small)
    small[1:3, :] = sums_ref[...]

    tasks = Tasks()
    tasks.add("P", 3, feed)
    tasks.sum_and_share(3, s3, a3, total_b, mix)
    tasks.add("T", 0, attend_back)
    tasks.add("K", 0, gather_kv)
    tasks.add("P", 4, spread)
    tasks.sum_and_share(4, s4, a4, total_b, last)

    def out_gradient(k):
        need_branch(*range(batches))
        loads.need(3)
        (out_weights.all_first, out_weights.all_second)[k]()

    def weight_gradients(k):
        if k == 0:
            get_normed.wait()
        (weights.all_first, weights.all_second)[k]()

    tasks.add("O", 0, out_gradient)
    tasks.add("V", 0, weight_gradients)
    tasks.add("M", 0, lambda k: (small_first, small_second, small_third)[k]())
    tasks.add("Z", 0, lambda k: None)
    tasks.run(back_order(lines, chunks, batches))

    @pl.loop(0, chunks)
    def _(c):
        for phase in (s3, s4, a3, a4):
            phase.drain(c)

    @pl.loop(jnp.maximum(batches * blk - ring, 0), batches * blk)
    def _(sent):
        to_owner(sent // blk, sent % blk).wait_send()

    weights.end()
    out_weights.end()


def back_order(lines, chunks, batches):
    if (lines, chunks, batches) == (4, 8, 4):
        return unpack(BACK_ORDER)
    order = [("O", 0, 0), ("O", 0, 1)] + [("P", 3, c) for c in range(chunks)] + in_turn(3, lines, chunks)
    order += [(name, 0, m) for m in range(batches) for name in "TK"]
    order += [("V", 0, 0), ("V", 0, 1)] + [("P", 4, c) for c in range(chunks)] + in_turn(4, lines, chunks)
    return order + [("M", 0, k) for k in range(3)]


def back(tokens, kv, feed_part, grad_branch, normed, own_input, own_resid, query, heads_out, w_query, w_key, w_value,
         w_out, norm_gain, ints, floats, cos_rows, sin_rows, ln_sums):
    lines, blocks = lax.axis_size("tp") // 2, lax.axis_size("blk")
    count, width = tokens.shape
    batches, wide = kv.shape[0], query.shape[1]
    chunk_rows = CHUNK_ROWS
    chunks, rows = count // chunk_rows, chunk_rows // (2 * lines)
    span = count // batches
    heads = wide // HD
    share = width // blocks
    any_space, vmem = pl.BlockSpec(memory_space=pl.ANY), pl.BlockSpec(memory_space=VMEM)
    bf16, f32 = jnp.bfloat16, jnp.float32
    dma = pltpu.SemaphoreType.DMA
    full = (chunks, 2, lines, rows, width)
    loads = (
        own_input, own_resid, query, heads_out, w_query, w_key, w_value, w_out, cos_rows, sin_rows, floats,
    )
    outs = pl.pallas_call(
        functools.partial(back_kernel, lines, blocks, batches, chunks, chunk_rows),
        out_shape=[jax.ShapeDtypeStruct(full, bf16)] * 2
        + BlockScatter.outs(blocks, (3, share, wide))
        + BlockScatter.outs(blocks, (wide, share))
        + [jax.ShapeDtypeStruct((8, share), f32)],
        in_specs=[any_space] * 16 + [vmem] * 3,
        out_specs=[any_space] * 6 + [vmem],
        scratch_shapes=[VMEM(load.shape, load.dtype) for load in loads]
        + [
            dma((len(loads),)),
            VMEM((count, width), bf16),
            VMEM((chunks, rows, width), bf16),
            VMEM((chunks, rows, width), bf16),
            VMEM((chunks, rows, width), bf16),
            VMEM((2, span, 2 * wide), bf16),
            VMEM((span, wide), bf16),
            VMEM((heads, span, LANE), f32),
            VMEM((span, wide), f32),
            VMEM((RING, span, 2 * wide), bf16),
            VMEM((2, span, 2 * wide), bf16),
            VMEM((2, blocks, span, 2 * wide), bf16),
            VMEM((count, 3 * wide), bf16),
            VMEM((rows, width), f32),
            VMEM((2, rows, width - CUT_SUM), f32),
            VMEM((span, 2 * wide), f32),
            VMEM((8, width), f32),
            VMEM((blocks - 1, 8, share), f32),
            VMEM((8, share), f32),
            VMEM((2 * lines - 1, 8, share), f32),
            dma(()),
            dma((batches + 1,)),
            dma((chunks,)),
            dma((2,)),
            dma((RING,)),
            dma((2, blocks)),
            pltpu.SemaphoreType.REGULAR((blocks,)),
            dma((2, blocks)),
            dma((2, 2 * lines)),
        ]
        + (Scatter.scratch(chunks, lines, rows, width, CUT_SUM) + Scatter.semaphores(chunks, lines)) * 2
        + Gather.scratch(chunks, lines) * 2
        + [VMEM((blocks, 3, share, wide), bf16)]
        + BlockScatter.scratch(blocks, (3, share, wide))
        + [VMEM((blocks, wide, share), bf16)]
        + BlockScatter.scratch(blocks, (wide, share)),
        compiler_params=pltpu.CompilerParams(
            collective_id=2, has_side_effects=True, vmem_limit_bytes=VMEM_LIMIT
        ),
        cost_estimate=pl.CostEstimate(
            flops=2 * count * width * wide * 7, bytes_accessed=40 * 2**20, transcendentals=0
        ),
    )(
        tokens.reshape(chunks, 2 * lines, rows, width), kv, feed_part, grad_branch, normed, *loads, ints,
        norm_gain[None], ln_sums,
    )
    return outs


def finish_kernel(pairs, copies, *refs):
    ins, refs = refs[: 2 * pairs + copies + 1], refs[2 * pairs + copies + 1 :]
    outs, scratch = refs[: pairs + copies + 5], refs[pairs + copies + 5 :]
    own, others, results = scratch[:pairs], scratch[pairs : 2 * pairs], scratch[2 * pairs : 3 * pairs]
    held = scratch[3 * pairs : 3 * pairs + copies]
    sem_load, sem_copy, sem_store = scratch[3 * pairs + copies :]
    loads = []
    for i in range(pairs):
        loads.append(pltpu.make_async_copy(ins[2 * i], own[i], sem_load.at[2 * i]))
        loads.append(pltpu.make_async_copy(ins[2 * i + 1], others[i], sem_load.at[2 * i + 1]))
    for load in loads:
        load.start()
    moves = []
    for i in range(copies):
        source, target = ins[2 * pairs + i], outs[pairs + 2 + i]
        moves += [
            (
                pltpu.make_async_copy(source.at[m], held[i].at[m], sem_copy.at[0, i, m]),
                pltpu.make_async_copy(held[i].at[m], target.at[m], sem_copy.at[1, i, m]),
            )
            for m in range(source.shape[0])
        ]
    for come, _ in moves:
        come.start()
    sums = ins[-1]
    for i in range(3):
        outs[pairs + 2 + copies + i][...] = sums[i : i + 1, :]
    stores = [go for _, go in moves]
    for come, go in moves[: len(moves) // 2]:
        come.wait()
        go.start()
    for i in range(pairs):
        loads[2 * i].wait()
        loads[2 * i + 1].wait()
        total = own[i][...].astype(jnp.float32)
        for k in range(others[i].shape[0]):
            total += others[i][k].astype(jnp.float32)
        results[i][...] = total
        targets = [(results[0].at[k], outs[k]) for k in range(3)] if i == 0 else [(results[i], outs[i + 2])]
        for k, (source, target) in enumerate(targets):
            stores.append(pltpu.make_async_copy(source, target, sem_store.at[k if i == 0 else i + 2]))
            stores[-1].start()
    for come, go in moves[len(moves) // 2 :]:
        come.wait()
        go.start()
    for copy in stores:
        copy.wait()


def finish(pairs, copies, sums):
    any_space, vmem = pl.BlockSpec(memory_space=pl.ANY), pl.BlockSpec(memory_space=VMEM)
    f32, share = jnp.float32, sums.shape[1]
    dma = pltpu.SemaphoreType.DMA
    return pl.pallas_call(
        functools.partial(finish_kernel, len(pairs), len(copies)),
        out_shape=[jax.ShapeDtypeStruct(pairs[0][0].shape[1:], f32)] * 3
        + [jax.ShapeDtypeStruct(own.shape, f32) for own, _ in pairs[1:]]
        + [jax.ShapeDtypeStruct(copy.shape, copy.dtype) for copy in copies]
        + [jax.ShapeDtypeStruct((1, share), f32)] * 3,
        in_specs=[any_space] * (2 * len(pairs) + len(copies)) + [vmem],
        out_specs=[any_space] * (len(pairs) + 2 + len(copies)) + [vmem] * 3,
        scratch_shapes=[VMEM(own.shape, own.dtype) for own, _ in pairs]
        + [VMEM(others.shape, others.dtype) for _, others in pairs]
        + [VMEM(own.shape, f32) for own, _ in pairs]
        + [VMEM(copy.shape, copy.dtype) for copy in copies]
        + [dma((2 * len(pairs),)), dma((2, len(copies), copies[0].shape[0])), dma((len(pairs) + 2,))],
        compiler_params=pltpu.CompilerParams(vmem_limit_bytes=VMEM_LIMIT),
        cost_estimate=pl.CostEstimate(flops=0, bytes_accessed=28 * 2**20, transcendentals=0),
    )(*[array for pair in pairs for array in pair], *copies, sums)


def local(
    tokens,
    lengths,
    head_count,
    width_index,
    router_prob,
    norm_gain,
    w_query,
    w_key,
    w_value,
    w_out,
    ln_gain,
    ln_bias,
    w_up,
    w_down,
    grad_out,
):
    batches, rows_dev, features = tokens.shape
    count = batches * rows_dev
    (
        normed, kv, own_up, others_up, own_down, others_down, grad_branch, feed_part, own_input, own_resid, ln_sums,
        query, heads_out, ints, floats, cos_rows, sin_rows,
    ) = middle(
        tokens, lengths, head_count, width_index, router_prob, norm_gain, w_query, w_key, w_value,
        grad_out.reshape(count, features), w_out, ln_gain, ln_bias, w_up, w_down,
    )
    flat = tokens.reshape(count, features)
    mixed_out, grad_in, own_w, others_w, own_out, others_out, sums = back(
        flat,
        kv,
        feed_part,
        grad_branch.reshape(count, features),
        normed.reshape(count, features),
        own_input,
        own_resid,
        query,
        heads_out,
        w_query,
        w_key,
        w_value,
        w_out,
        norm_gain,
        ints,
        floats,
        cos_rows,
        sin_rows,
        ln_sums,
    )
    grad_q, grad_k, grad_v, grad_out_w, grad_up, grad_down, mixed_out, grad_in, *sums = finish(
        [(own_w, others_w), (own_out, others_out), (own_up, others_up), (own_down, others_down)],
        [mixed_out.reshape(tokens.shape), grad_in.reshape(tokens.shape)],
        sums,
    )
    gain_sum, ln_gain_sum, ln_bias_sum = (total.reshape(-1) for total in sums)
    return (
        mixed_out, grad_in, gain_sum, grad_q, grad_k, grad_v, grad_out_w, ln_gain_sum, ln_bias_sum, grad_up, grad_down
    )


def solution(mesh):
    return jax.shard_map(
        local,
        mesh=mesh,
        in_specs=(
            P(None, "blk", None),
            P(),
            P(None, "blk"),
            P(None, "blk"),
            P(None, "blk"),
            P(),
            P(None, "tp"),
            P(None, "tp"),
            P(None, "tp"),
            P("tp", None),
            P(),
            P(),
            P(None, "tp"),
            P("tp", None),
            P(None, "blk", None),
        ),
        out_specs=(
            P(None, "blk", None),
            P(None, "blk", None),
            P("blk"),
            P("blk", "tp"),
            P("blk", "tp"),
            P("blk", "tp"),
            P("tp", "blk"),
            P("blk"),
            P("blk"),
            P("blk", "tp"),
            P("tp", "blk"),
        ),
        check_vma=False,
    )
```
